32 devices in a mesh: tm: 8 (over z, core), depth: 4 (over y, x).
Axes of the slice: x: 2, y: 2, z: 4, core: 2. Of those that a mesh axis runs over, the one named last changes fastest.
Arguments:
- raw: bfloat16 [128, 32, 128], P('tm', 'depth'), may hold values from -6 to 6
- stream: bfloat16 [128, 32, 2048], P('tm', 'depth'), may hold values from -6 to 6
- conv_w: bfloat16 [3, 128, 2048], replicated, may hold values from -0.3125 to 0.3125
- gain: float32 [2048], replicated, may hold values from 0.1 to 1.9
- w_qkv: bfloat16 [2048, 3072], P('tm', 'depth'), may hold values from -4 to 4
- mask: int32 [4, 8, 5], P('depth', 'tm'), may hold values from 0 to 1, as said below
Outputs:
- context: bfloat16 [128, 32, 1024], P('tm', 'depth')
The draws below stay inside these ranges and needn't reach their ends.
Inputs may be any that keep to these rules, and one draw needn't show every extreme that they name: mask[p, i, 2] = 1 for every block; mask[p, i, e] = 0 wherever i + e - 2 lies outside 0 to 7.
All inputs are finite; a program needn't handle non-finite values.
Results may differ from the reference program's by a relative error of at most 0.012.
The reference program's roundings to bfloat16 on the way (of `normed`, `projected` and `weights`) count: a program that leaves them out, or rounds other values in their place, can miss the bound.
Values may be sent and summed in bfloat16 or wider, within the bound.
No kernel may reach another device: no remote copies, remote signals or barrier semaphores. Data moves between devices by JAX's collectives and lax.ppermute only.
A program may use at most 64 MiB of HBM per device.

```python
import math
import jax
import jax.numpy as jnp
from jax import lax

D = 2048
HEADS = 8
HD = 128
F_IN = 128
BT = 16
PP = 8
NT = 128
NP = 32
NTB = 8
RB = 2
KSPAN = 5
N_DEPTH = 4


def draw_w_qkv(key, part):
    head_cols = HEADS * HD
    first_key = jax.random.fold_in(jax.random.fold_in(key, 11), 0)
    scales = jnp.concatenate([jnp.full((2 * head_cols,), 2.0, jnp.float32), jnp.ones((head_cols,), jnp.float32)]) / math.sqrt(D)
    matrix = jax.random.normal(first_key, (D, 3 * head_cols), jnp.float32) * scales
    return jnp.clip(matrix, -4.0, 4.0).astype(jnp.bfloat16)


def draw_mask(key, part):
    level_key, coin_key = jax.random.split(jax.random.fold_in(key, 5))
    levels = jax.random.randint(level_key, (N_DEPTH, NTB, 1), 0, 5)
    coin_draws = jax.random.randint(coin_key, (N_DEPTH, NTB, KSPAN), 0, 4)
    offsets = jnp.arange(KSPAN, dtype=jnp.int32)[None, None, :] - RB
    blocks = jnp.arange(NTB, dtype=jnp.int32)[None, :, None] + offsets
    inside = (blocks >= 0) & (blocks < NTB)
    chosen = (coin_draws < levels) | (offsets == 0)
    return jnp.where(inside & chosen, 1, 0).astype(jnp.int32)


def block_scale(key, extent, pieces, low, largest):
    factor_of, own = 1.0, jax.random.fold_in(key, 6)
    for dim, parts in pieces:
        draws = jnp.exp(jax.random.uniform(jax.random.fold_in(own, dim), (parts,), jnp.float32, low / len(pieces), largest / len(pieces)))
        factor_of = factor_of * jnp.repeat(draws, extent[dim] // parts).reshape([-1 if axis == dim else 1 for axis in range(len(extent))])
    return factor_of


def noise(own_key, extent, width, limit, shards=(), kind=jnp.bfloat16):
    loudness = block_scale(own_key, extent, shards, -0.22, 0.18) if shards else 1.0
    values = jax.random.normal(own_key, extent, jnp.float32) * width * loudness
    return jnp.minimum(jnp.maximum(values, -limit), limit).astype(kind)


def setup_inputs(seed: int = 0) -> dict:
    seeds = jax.random.split(jax.random.key(seed), 7)
    return {
        "raw": noise(seeds[0], (NT, NP, F_IN), 1.0, 6.0, ((0, 8), (1, 4))),
        "stream": noise(seeds[1], (NT, NP, D), 1.0, 6.0, ((0, 8), (1, 4))),
        "conv_w": noise(seeds[2], (3, F_IN, D), (3 * F_IN) ** -0.5, 0.3125),
        "gain": jnp.clip(1.0 + 0.18 * jax.random.normal(seeds[3], (D,), jnp.float32), 0.1, 1.9),
        "w_qkv": draw_w_qkv(jax.random.fold_in(seeds[6], 71), 0),
        "mask": draw_mask(jax.random.fold_in(seeds[6], 71), 0),
    }


def attend(query_block, key_rows, value_rows, allowed):
    inv_root = 1.0 / math.sqrt(HD)
    scores = jnp.einsum('qhd,khd->hqk', query_block.astype(jnp.float32), key_rows.astype(jnp.float32)) * inv_root
    scores = jnp.where(allowed[None, None, :], scores, -1e+30)
    row_max = lax.optimization_barrier(jnp.max(scores, axis=-1, keepdims=True))
    powers = jnp.exp(scores - row_max)
    weights = (powers / lax.optimization_barrier(jnp.sum(powers, axis=-1, keepdims=True))).astype(jnp.bfloat16)
    result = jnp.einsum('hqk,khd->qhd', weights.astype(jnp.float32), value_rows.astype(jnp.float32))
    return result.reshape(query_block.shape[0], HEADS * HD).astype(jnp.bfloat16)

def reference(raw, stream, conv_w, gain, w_qkv, mask):
    tokens_all = NT * NP
    padded = jnp.pad(raw, ((0, 0), (1, 1), (0, 0)))
    embedded = stream.reshape(tokens_all, D).astype(jnp.float32)
    for offset in range(3):
        window = padded[:, offset:offset + NP].reshape(tokens_all, F_IN)
        embedded = embedded + jnp.dot(window, conv_w[offset], preferred_element_type=jnp.float32)
    normed = (embedded * lax.rsqrt(lax.optimization_barrier(jnp.mean(embedded * embedded, axis=-1, keepdims=True)) + 1e-05) * gain).astype(jnp.bfloat16)
    projected = jnp.dot(normed, w_qkv, preferred_element_type=jnp.float32).astype(jnp.bfloat16)
    block_rows = BT * PP
    head_cols = HEADS * HD
    width_all = 3 * head_cols
    blocked = projected.reshape(NTB, BT, N_DEPTH, PP, width_all).transpose(2, 0, 1, 3, 4).reshape(N_DEPTH, NTB, block_rows, width_all)
    queries = blocked[..., :head_cols]
    keyvals = jnp.pad(blocked[..., head_cols:], ((0, 0), (RB, RB), (0, 0), (0, 0)))
    mask_int = mask.astype(jnp.int32)

    def one_block(index):
        index = index.astype(jnp.int32)
        zero = jnp.zeros((), jnp.int32)
        depth_index = (index // NTB).astype(jnp.int32)
        time_index = (index % NTB).astype(jnp.int32)
        query_block = lax.dynamic_slice(queries, (depth_index, time_index, zero, zero), (1, 1, block_rows, head_cols)).reshape(block_rows, HEADS, HD)
        neighbourhood = lax.dynamic_slice(keyvals, (depth_index, time_index, zero, zero), (1, KSPAN, block_rows, 2 * head_cols)).reshape(KSPAN * block_rows, 2 * head_cols)
        key_rows = neighbourhood[:, :head_cols].reshape(KSPAN * block_rows, HEADS, HD)
        value_rows = neighbourhood[:, head_cols:].reshape(KSPAN * block_rows, HEADS, HD)
        row_mask = lax.dynamic_slice(mask_int, (depth_index, time_index, zero), (1, 1, KSPAN)).reshape(KSPAN)
        allowed = jnp.repeat(row_mask, block_rows) > 0
        return attend(query_block, key_rows, value_rows, allowed)
    results = lax.map(one_block, jnp.arange(N_DEPTH * NTB, dtype=jnp.int32))
    return results.reshape(N_DEPTH, NTB, BT, PP, head_cols).transpose(1, 2, 0, 3, 4).reshape(NT, NP, head_cols)
```

```python
import functools
import math

import jax
import jax.numpy as jnp
from jax import lax
from jax.experimental import pallas as pl
from jax.experimental.pallas import tpu as pltpu
from jax.sharding import PartitionSpec as P

HEADS = 8
HD = 128
BT = 16
PP = 8
RD = 2
VMEM = pltpu.VMEM
SMEM = pltpu.SMEM


def padded_2(value, sides, width):
    for axis, dim in sides:
        devices, length = (lax.axis_size(axis), value.shape[dim])
        up = [(i, (i + 1) % devices) for i in range(devices - 1)]
        down = [(j, i) for i, j in up]
        last = lax.slice_in_dim(value, length - width, length, axis=dim)
        leading = lax.slice_in_dim(value, 0, width, axis=dim)
        before = lax.ppermute(last, axis, up)
        after = lax.ppermute(leading, axis, down)
        value = jnp.concatenate([before, value, after], axis=dim)
    return value


def normed_tokens(raw, stream, conv_w, gain):
    time_len, site_len, feat_len = raw.shape
    tok_rows = time_len * site_len
    padded = padded_2(raw, (("depth", 1),), 1)
    embedded = stream.reshape(tok_rows, stream.shape[2]).astype(jnp.float32)
    for offset in range(3):
        window = padded[:, offset : offset + site_len].reshape(tok_rows, feat_len)
        embedded = embedded + jnp.dot(window, conv_w[offset], preferred_element_type=jnp.float32)
    scale = lax.rsqrt(jnp.mean(embedded * embedded, axis=-1, keepdims=True) + 1e-05)
    return (embedded * scale * gain).astype(jnp.bfloat16)


def hop(value, fn, zs):
    pairs = []
    for z in range(zs):
        for core in range(2):
            for depth in range(4):
                to = fn(z, core, depth)
                if to is not None:
                    pairs.append(((2 * z + core) * 4 + depth, (2 * to[0] + to[1]) * 4 + to[2]))
    return lax.ppermute(value, ("tm", "depth"), pairs)


def swap_core(value, zs):
    return hop(value, lambda z, c, d: (z, 1 - c, d), zs)


def swap_depth(value, bits, zs):
    return hop(value, lambda z, c, d: (z, c, d ^ bits), zs)


def move_z(value, by, zs, first=0, last=None):
    last = zs if last is None else last
    return hop(value, lambda z, c, d: (z + by, c, d) if 0 <= z + by < zs and first <= z < last else None, zs)


def project_kernel(zs, place, *refs):
    x_refs, shards = refs[:2], refs[2 : 2 + 2 * zs - 1]
    q_ref, kv_ref, w_full = refs[2 + 2 * zs - 1 :]
    z, core = place[0], place[1]
    rows = shards[0].shape[0]
    for r in range(-(zs - 1), zs):
        source = z - r

        @pl.when((source >= 0) & (source < zs))
        def _():
            at = pl.ds(pl.multiple_of(source * rows, rows), rows)
            for part in range(3):
                third = pl.multiple_of(place[2 + part] * HD, HD)
                w_full[at, pl.ds(third, HD)] = shards[r + zs - 1][:, part * HD : (part + 1) * HD]

    block = x_refs[0].shape[1]
    for rel in range(2):
        u = core ^ rel

        def body(step, carry):
            pair = x_refs[rel][pl.ds(2 * step, 2)].reshape(2 * block, x_refs[rel].shape[2])
            out = jnp.dot(pair, w_full[...], preferred_element_type=jnp.float32)
            out = out.astype(jnp.bfloat16).reshape(2, block, 3 * HD)
            at = pl.ds(pl.multiple_of(u * block, block), block)
            q_ref[pl.ds(2 * step, 2), at, :] = out[:, :, :HD]
            kv_ref[pl.ds(2 * step, 2), at, :] = out[:, :, HD:]
            return carry

        lax.fori_loop(0, 2, body, 0)


def attend_kernel(place, mask, q_ref, before, own, after, keep_ref, send_ref):
    core = place[1]
    block = q_ref.shape[1] // 2
    inv_root = 1.0 / math.sqrt(HD)

    def body(r, carry):
        q = q_ref[r]
        scores = []
        for side, kv in enumerate((before, own, after)):
            s = lax.dot_general(q, kv[r][:, :HD], (((1,), (1,)), ((), ())), preferred_element_type=jnp.float32)
            s = (s * inv_root).reshape(2, block, 2, block)
            rows = []
            for u in range(2):
                cols = []
                for v in range(2):
                    entry = 2 * side + v - u
                    piece = s[u, :, v]
                    if 0 <= entry <= 4:
                        flag = mask[((u ^ core) * 4 + r) * 5 + entry]
                        piece = jnp.where(flag > 0, piece, -1e30)
                    else:
                        piece = jnp.full_like(piece, -1e30)
                    cols.append(piece)
                rows.append(jnp.concatenate(cols, axis=1))
            scores.append(jnp.concatenate(rows, axis=0))
        top = functools.reduce(jnp.maximum, [jnp.max(s, axis=1, keepdims=True) for s in scores])
        powers = [jnp.exp(s - top) for s in scores]
        total = functools.reduce(jnp.add, [jnp.sum(p, axis=1, keepdims=True) for p in powers])
        inverse = 1.0 / total
        result = jnp.zeros((2 * block, HD), jnp.float32)
        for p, kv in zip(powers, (before, own, after)):
            w = (p * inverse).astype(jnp.bfloat16)
            result += jnp.dot(w, kv[r][:, HD:], preferred_element_type=jnp.float32)
        result = result.astype(jnp.bfloat16)
        for u in range(2):

            @pl.when(core == u)
            def _():
                keep_ref[r] = result[u * block : (u + 1) * block]
                send_ref[r] = result[(1 - u) * block : (2 - u) * block]

        return carry

    lax.fori_loop(0, 4, body, 0)


def gather_kernel(place, own, x, y, diagonal, out_ref):
    core, depth = place[1], place[5]
    for r, ref in enumerate((own, x, y, diagonal)):
        for rel in range(2):
            at = pl.multiple_of((2 * (depth ^ r) + (core ^ rel)) * HD, HD)
            out_ref[:, pl.ds(at, HD)] = ref[:, rel * HD : (rel + 1) * HD]


def vmem_call(kernel, outs, scratch=(), smem=1, total=1, limit=40):
    return pl.pallas_call(
        kernel,
        out_shape=outs,
        in_specs=[pl.BlockSpec(memory_space=SMEM)] * smem + [pl.BlockSpec(memory_space=VMEM)] * (total - smem),
        out_specs=jax.tree.map(lambda _: pl.BlockSpec(memory_space=VMEM), outs),
        scratch_shapes=list(scratch),
        compiler_params=pltpu.CompilerParams(vmem_limit_bytes=limit * 2**20),
    )


def plane_device(raw, stream, conv_w, gain, w_qkv, mask):
    zs = lax.axis_size("tm") // 2
    tm, depth = lax.axis_index("tm"), lax.axis_index("depth")
    z, core = tm // 2, tm % 2
    time_len, site_len, _ = raw.shape
    block = time_len * site_len
    width = stream.shape[2]

    rows = w_qkv.shape[0]
    grouped = w_qkv.reshape(rows, 3, 2, HD)
    keep = lax.dynamic_index_in_dim(grouped, core, 2, keepdims=False)
    send = lax.dynamic_index_in_dim(grouped, 1 - core, 2, keepdims=False)
    received = swap_core(send, zs)
    first = core == 0
    both = jnp.concatenate([jnp.where(first, keep, received), jnp.where(first, received, keep)], axis=0)
    parts = [hop(both[:, k], lambda z, c, d, k=k: (z, c, (k - d) % 4), zs) for k in range(3)]
    shard = jnp.concatenate(parts, axis=1)
    thirds = [(3 * ((k - depth) % 4) + k) // 4 for k in range(3)]

    normed = normed_tokens(raw, stream, conv_w, gain)

    ahead, back = [shard], [shard]
    for r in range(1, zs):
        ahead.append(move_z(ahead[-1], 1, zs, first=r - 1))
        back.append(move_z(back[-1], -1, zs, last=zs - r + 1))
    shards = back[:0:-1] + ahead

    own_tokens = jnp.stack([normed] + [swap_depth(normed, bits, zs) for bits in (1, 2, 3)])
    other_tokens = swap_core(own_tokens, zs)

    flags = mask.reshape(1, mask.shape[2])
    flags = jnp.concatenate([flags] + [swap_depth(flags, bits, zs) for bits in (1, 2, 3)])
    flags = jnp.concatenate([flags, swap_core(flags, zs)]).reshape(-1)

    place = jnp.stack([z, core] + thirds + [depth]).astype(jnp.int32)
    bf16 = jnp.bfloat16
    q, kv = vmem_call(
        functools.partial(project_kernel, zs),
        (jax.ShapeDtypeStruct((4, 2 * block, HD), bf16), jax.ShapeDtypeStruct((4, 2 * block, 2 * HD), bf16)),
        scratch=[VMEM((width, 3 * HD), bf16)],
        total=3 + 2 * zs - 1,
    )(place, own_tokens, other_tokens, *shards)

    before = move_z(kv, 1, zs)
    after = move_z(kv, -1, zs)
    piece = jax.ShapeDtypeStruct((4, block, HD), bf16)
    kept, sent = vmem_call(attend_kernel, (piece, piece), smem=2, total=6)(place, flags, q, before, kv, after)
    pair = jnp.concatenate([kept, swap_core(sent, zs)], axis=2)
    pieces = [pair[0]] + [swap_depth(pair[bits], bits, zs) for bits in (1, 2, 3)]
    context = vmem_call(gather_kernel, jax.ShapeDtypeStruct((block, HEADS * HD), bf16), total=5)(place, *pieces)
    return context.reshape(time_len, site_len, HEADS * HD)


def from_behind(value, axis, by):
    devices = lax.axis_size(axis)
    pairs = [(i, i + by) for i in range(devices) if 0 <= i + by < devices]
    return lax.ppermute(value, axis, pairs)


def head_attend(query_head, key_head, value_head, allowed):
    inv_root = 1.0 / math.sqrt(HD)
    scores = (
        jnp.einsum("qd,kd->qk", query_head, key_head, preferred_element_type=jnp.float32) * inv_root
    )
    scores = jnp.where(allowed, scores, -1e30)
    row_max = jnp.max(scores, axis=-1, keepdims=True)
    powers = jnp.exp(scores - row_max)
    weights = (powers / jnp.sum(powers, axis=-1, keepdims=True)).astype(jnp.bfloat16)
    return jnp.dot(weights, value_head, preferred_element_type=jnp.float32).astype(jnp.bfloat16)


def per_device(raw, stream, conv_w, gain, w_qkv, mask):
    time_len, site_len, _ = raw.shape
    tok_rows = time_len * site_len
    normed = normed_tokens(raw, stream, conv_w, gain)
    columns = lax.all_gather(w_qkv, "depth", axis=1, tiled=True)
    projected = jnp.dot(
        normed,
        lax.all_gather(columns, "tm", axis=0, tiled=True),
        preferred_element_type=jnp.float32,
    ).astype(jnp.bfloat16)
    head_cols = projected.shape[1] // 3
    queries = projected[:, :head_cols]
    keyvals = projected[:, head_cols:]
    earlier = []
    later = []
    moving_back = keyvals
    moving_ahead = keyvals
    for hop_index in range(RD):
        moving_back = from_behind(moving_back, "tm", 1)
        moving_ahead = from_behind(moving_ahead, "tm", -1)
        earlier.insert(0, moving_back)
        later.append(moving_ahead)
    gathered = jnp.concatenate(earlier + [keyvals] + later, axis=0)
    block_rows = BT * PP
    own_blocks = tok_rows // block_rows
    span_blocks = gathered.shape[0] // block_rows
    local_mask = mask[0]
    query_ids = jnp.arange(own_blocks, dtype=jnp.int32)[:, None]
    key_ids = jnp.arange(span_blocks, dtype=jnp.int32)[None, :]
    entry_ids = key_ids - query_ids
    picks = entry_ids[:, :, None] == jnp.arange(local_mask.shape[1], dtype=jnp.int32)[None, None, :]
    block_allowed = jnp.sum(jnp.where(picks, local_mask[:, None, :], 0), axis=-1) > 0
    allowed = jnp.repeat(jnp.repeat(block_allowed, block_rows, axis=0), block_rows, axis=1)
    query_heads = queries.reshape(tok_rows, HEADS, HD).transpose(1, 0, 2)
    key_heads = gathered[:, :head_cols].reshape(gathered.shape[0], HEADS, HD).transpose(1, 0, 2)
    value_heads = gathered[:, head_cols:].reshape(gathered.shape[0], HEADS, HD).transpose(1, 0, 2)
    context = lax.map(
        lambda operands: head_attend(operands[0], operands[1], operands[2], allowed),
        (query_heads, key_heads, value_heads),
    )
    return context.transpose(1, 0, 2).reshape(time_len, site_len, head_cols)


def solution(mesh):
    in_specs = (
        P("tm", "depth", None),
        P("tm", "depth", None),
        P(),
        P(),
        P("tm", "depth"),
        P("depth", "tm", None),
    )
    out_specs = P("tm", "depth", None)
    fits = mesh.shape["depth"] == 4 and mesh.shape["tm"] % 2 == 0
    return jax.shard_map(
        plane_device if fits else per_device, mesh=mesh, in_specs=in_specs, out_specs=out_specs, check_vma=False
    )
```

```python
import functools
import math

import jax
import jax.numpy as jnp
from jax import lax
from jax.experimental import pallas as pl
from jax.experimental.pallas import tpu as pltpu
from jax.sharding import PartitionSpec as P

HEADS = 8
HD = 128
BT = 16
PP = 8
RD = 2
VMEM = pltpu.VMEM
SMEM = pltpu.SMEM


def padded_2(value, sides, width):
    for axis, dim in sides:
        devices, length = (lax.axis_size(axis), value.shape[dim])
        up = [(i, (i + 1) % devices) for i in range(devices - 1)]
        down = [(j, i) for i, j in up]
        last = lax.slice_in_dim(value, length - width, length, axis=dim)
        leading = lax.slice_in_dim(value, 0, width, axis=dim)
        before = lax.ppermute(last, axis, up)
        after = lax.ppermute(leading, axis, down)
        value = jnp.concatenate([before, value, after], axis=dim)
    return value


def normed_tokens(raw, stream, conv_w, gain):
    time_len, site_len, feat_len = raw.shape
    tok_rows = time_len * site_len
    padded = padded_2(raw, (("depth", 1),), 1)
    embedded = stream.reshape(tok_rows, stream.shape[2]).astype(jnp.float32)
    for offset in range(3):
        window = padded[:, offset : offset + site_len].reshape(tok_rows, feat_len)
        embedded = embedded + jnp.dot(window, conv_w[offset], preferred_element_type=jnp.float32)
    scale = lax.rsqrt(jnp.mean(embedded * embedded, axis=-1, keepdims=True) + 1e-05)
    return (embedded * scale * gain).astype(jnp.bfloat16)


def hop(value, fn, zs):
    pairs = []
    for z in range(zs):
        for core in range(2):
            for depth in range(4):
                to = fn(z, core, depth)
                if to is not None:
                    pairs.append(((2 * z + core) * 4 + depth, (2 * to[0] + to[1]) * 4 + to[2]))
    return lax.ppermute(value, ("tm", "depth"), pairs)


def swap_core(value, zs):
    return hop(value, lambda z, c, d: (z, 1 - c, d), zs)


def swap_depth(value, bits, zs):
    return hop(value, lambda z, c, d: (z, c, d ^ bits), zs)


def move_z(value, by, zs, first=0, last=None):
    last = zs if last is None else last
    return hop(value, lambda z, c, d: (z + by, c, d) if 0 <= z + by < zs and first <= z < last else None, zs)


def partial_kernel(zs, place, *refs):
    near = 2 * (zs - 2) + 1
    x_refs, shards, acc_ref = refs[:8], refs[8 : 8 + near], refs[8 + near]
    z = place[0] >> 1
    rows, block = shards[0].shape[0], x_refs[0].shape[0]

    def add(source, shard, fresh):
        at = pl.ds(pl.multiple_of(source * rows, rows), rows)
        for rel in range(2):
            x = jnp.concatenate([ref[:, at] for ref in x_refs[4 * rel : 4 * rel + 4]], axis=0)
            value = jnp.dot(x, shard[...], preferred_element_type=jnp.float32)
            here = slice(4 * rel * block, 4 * (rel + 1) * block)
            acc_ref[here] = value if fresh else acc_ref[here] + value

    add(z, shards[zs - 2], True)
    for r in range(-(zs - 2), zs - 1):
        if r:
            pl.when((z - r >= 0) & (z - r < zs))(functools.partial(add, z - r, shards[r + zs - 2], False))


def project_kernel(zs, place, *refs):
    x_refs, (from_last, from_first, acc_in, q_ref, kv_ref, acc_ref) = refs[:8], refs[8:]
    z, core, depth = place[0] >> 1, place[0] & 1, place[1]
    turn = jnp.where(depth == 3, 0, depth)
    rows, block = from_last.shape[0], x_refs[0].shape[0]
    for rel in range(2):
        u = core ^ rel
        here = slice(4 * rel * block, 4 * (rel + 1) * block)
        acc_ref[here] = acc_in[here]
        for edge, source, shard in ((0, zs - 1, from_last), (zs - 1, 0, from_first)):

            @pl.when(z == edge)
            def _(source=source, shard=shard):
                x = jnp.concatenate(
                    [ref[:, source * rows : (source + 1) * rows] for ref in x_refs[4 * rel : 4 * rel + 4]], axis=0
                )
                acc_ref[here] += jnp.dot(x, shard[...], preferred_element_type=jnp.float32)

        at = pl.ds(pl.multiple_of(u * block, block), block)
        for r in range(4):
            mine = slice((4 * rel + r) * block, (4 * rel + r + 1) * block)
            for third, (ref, column) in enumerate(((q_ref, 0), (kv_ref, 0), (kv_ref, HD))):
                at_group = third + turn
                at_group = jnp.where(at_group >= 3, at_group - 3, at_group)
                lanes = pl.ds(pl.multiple_of(at_group * HD, HD), HD)
                ref[r, at, column : column + HD] = acc_ref[mine, lanes].astype(jnp.bfloat16)


def attend_kernel(place, mask, q_ref, before, own, after, keep_ref, send_ref):
    core = place[0] & 1
    block = q_ref.shape[1] // 2
    inv_root = 1.0 / math.sqrt(HD)
    for r in range(4):
        for u in range(2):
            q = q_ref[r, u * block : (u + 1) * block]
            spans = ((before, u, 2), (own, 0, 2), (after, 0, 1 + u))
            scores, entry = [], 0
            for ref, first, last in spans:
                k = ref[r, first * block : last * block, :HD]
                s = lax.dot_general(q, k, (((1,), (1,)), ((), ())), preferred_element_type=jnp.float32)
                for v in range(last - first):
                    flag = mask[((u ^ core) * 4 + r) * 5 + entry]
                    scores.append(jnp.where(flag > 0, s[:, v * block : (v + 1) * block] * inv_root, -1e30))
                    entry += 1
            top = jnp.max(functools.reduce(jnp.maximum, scores), axis=1, keepdims=True)
            powers = [jnp.exp(s - top) for s in scores]
            inverse = 1.0 / jnp.sum(functools.reduce(jnp.add, powers), axis=1, keepdims=True)
            weights = [(p * inverse).astype(jnp.bfloat16) for p in powers]
            result, entry = jnp.zeros((block, HD), jnp.float32), 0
            for ref, first, last in spans:
                w = jnp.concatenate(weights[entry : entry + last - first], axis=1)
                entry += last - first
                result += jnp.dot(w, ref[r, first * block : last * block, HD:], preferred_element_type=jnp.float32)
            result = result.astype(jnp.bfloat16)

            @pl.when(core == u)
            def _():
                keep_ref[r] = result

            @pl.when(core != u)
            def _():
                send_ref[r] = result


def gather_kernel(place, own, x, y, diagonal, out_ref):
    core, depth = place[0] & 1, place[1]
    for r, ref in enumerate((own, x, y, diagonal)):
        for rel in range(2):
            at = pl.multiple_of((2 * (depth ^ r) + (core ^ rel)) * HD, HD)
            out_ref[:, pl.ds(at, HD)] = ref[:, rel * HD : (rel + 1) * HD]


def vmem_call(kernel, outs, scratch=(), smem=1, total=1, limit=40):
    return pl.pallas_call(
        kernel,
        out_shape=outs,
        in_specs=[pl.BlockSpec(memory_space=SMEM)] * smem + [pl.BlockSpec(memory_space=VMEM)] * (total - smem),
        out_specs=jax.tree.map(lambda _: pl.BlockSpec(memory_space=VMEM), outs),
        scratch_shapes=list(scratch),
        compiler_params=pltpu.CompilerParams(vmem_limit_bytes=limit * 2**20),
    )


def after(value, *others):
    return lax.optimization_barrier((value, *others))[0]


def plane_device(raw, stream, conv_w, gain, w_qkv, mask):
    zs = lax.axis_size("tm") // 2
    tm, depth = lax.axis_index("tm"), lax.axis_index("depth")
    core = tm & 1
    time_len, site_len, _ = raw.shape
    block = time_len * site_len
    bf16, f32 = jnp.bfloat16, jnp.float32

    pair = 2 * HD
    low, mid, high = (w_qkv[:, k * pair : (k + 1) * pair] for k in range(3))
    mid = lax.optimization_barrier(mid)
    even = (depth & 1) == 0
    from_y = swap_depth(jnp.where(even, high, low), 2, zs)
    from_x = swap_depth(mid, 1, zs)
    groups = [jnp.where(even, low, from_y), from_x, jnp.where(even, from_y, high)]
    first = core == 0
    keep = jnp.concatenate([jnp.where(first, g[:, :HD], g[:, HD:]) for g in groups], axis=1)
    send = jnp.concatenate([jnp.where(first, g[:, HD:], g[:, :HD]) for g in groups], axis=1)
    received = swap_core(send, zs)
    shard = jnp.concatenate([jnp.where(first, keep, received), jnp.where(first, received, keep)], axis=0)

    ahead, back = [shard], [shard]
    for r in range(1, zs):
        ahead.append(move_z(ahead[-1], 1, zs, first=r - 1))
        back.append(move_z(back[-1], -1, zs, last=zs - r + 1))

    normed = normed_tokens(raw, stream, conv_w, gain)
    tokens = [normed] + [swap_depth(normed, bits, zs) for bits in (1, 2, 3)]
    tokens += [swap_core(t, zs) for t in tokens]

    flags = after(mask.reshape(1, mask.shape[2]), tokens[1])
    flags = jnp.concatenate([flags] + [swap_depth(flags, bits, zs) for bits in (1, 2, 3)])
    flags = jnp.concatenate([flags, swap_core(flags, zs)]).reshape(-1)

    place = jnp.stack([tm, depth]).astype(jnp.int32)
    near = back[-2:0:-1] + ahead[:-1]
    total = vmem_call(
        functools.partial(partial_kernel, zs), jax.ShapeDtypeStruct((8 * block, 3 * HD), f32), total=9 + len(near)
    )(place, *tokens, *near)
    total = after(total, flags)
    q, kv = vmem_call(
        functools.partial(project_kernel, zs),
        (jax.ShapeDtypeStruct((4, 2 * block, HD), bf16), jax.ShapeDtypeStruct((4, 2 * block, 2 * HD), bf16)),
        scratch=[VMEM((8 * block, 3 * HD), f32)],
        total=12,
    )(place, *tokens, back[-1], ahead[-1], total)

    piece = jax.ShapeDtypeStruct((4, block, HD), bf16)
    kept, sent = vmem_call(attend_kernel, (piece, piece), smem=2, total=6)(
        place, flags, q, move_z(kv, 1, zs), kv, move_z(kv, -1, zs)
    )
    pairs = jnp.concatenate([kept, swap_core(sent, zs)], axis=2)
    pieces = [pairs[0]] + [swap_depth(pairs[bits], bits, zs) for bits in (1, 2, 3)]
    context = vmem_call(gather_kernel, jax.ShapeDtypeStruct((block, HEADS * HD), bf16), total=5)(place, *pieces)
    return context.reshape(time_len, site_len, HEADS * HD)


def from_behind(value, axis, by):
    devices = lax.axis_size(axis)
    pairs = [(i, i + by) for i in range(devices) if 0 <= i + by < devices]
    return lax.ppermute(value, axis, pairs)


def head_attend(query_head, key_head, value_head, allowed):
    inv_root = 1.0 / math.sqrt(HD)
    scores = (
        jnp.einsum("qd,kd->qk", query_head, key_head, preferred_element_type=jnp.float32) * inv_root
    )
    scores = jnp.where(allowed, scores, -1e30)
    row_max = jnp.max(scores, axis=-1, keepdims=True)
    powers = jnp.exp(scores - row_max)
    weights = (powers / jnp.sum(powers, axis=-1, keepdims=True)).astype(jnp.bfloat16)
    return jnp.dot(weights, value_head, preferred_element_type=jnp.float32).astype(jnp.bfloat16)


def per_device(raw, stream, conv_w, gain, w_qkv, mask):
    time_len, site_len, _ = raw.shape
    tok_rows = time_len * site_len
    normed = normed_tokens(raw, stream, conv_w, gain)
    columns = lax.all_gather(w_qkv, "depth", axis=1, tiled=True)
    projected = jnp.dot(
        normed,
        lax.all_gather(columns, "tm", axis=0, tiled=True),
        preferred_element_type=jnp.float32,
    ).astype(jnp.bfloat16)
    head_cols = projected.shape[1] // 3
    queries = projected[:, :head_cols]
    keyvals = projected[:, head_cols:]
    earlier = []
    later = []
    moving_back = keyvals
    moving_ahead = keyvals
    for hop_index in range(RD):
        moving_back = from_behind(moving_back, "tm", 1)
        moving_ahead = from_behind(moving_ahead, "tm", -1)
        earlier.insert(0, moving_back)
        later.append(moving_ahead)
    gathered = jnp.concatenate(earlier + [keyvals] + later, axis=0)
    block_rows = BT * PP
    own_blocks = tok_rows // block_rows
    span_blocks = gathered.shape[0] // block_rows
    local_mask = mask[0]
    query_ids = jnp.arange(own_blocks, dtype=jnp.int32)[:, None]
    key_ids = jnp.arange(span_blocks, dtype=jnp.int32)[None, :]
    entry_ids = key_ids - query_ids
    picks = entry_ids[:, :, None] == jnp.arange(local_mask.shape[1], dtype=jnp.int32)[None, None, :]
    block_allowed = jnp.sum(jnp.where(picks, local_mask[:, None, :], 0), axis=-1) > 0
    allowed = jnp.repeat(jnp.repeat(block_allowed, block_rows, axis=0), block_rows, axis=1)
    query_heads = queries.reshape(tok_rows, HEADS, HD).transpose(1, 0, 2)
    key_heads = gathered[:, :head_cols].reshape(gathered.shape[0], HEADS, HD).transpose(1, 0, 2)
    value_heads = gathered[:, head_cols:].reshape(gathered.shape[0], HEADS, HD).transpose(1, 0, 2)
    context = lax.map(
        lambda operands: head_attend(operands[0], operands[1], operands[2], allowed),
        (query_heads, key_heads, value_heads),
    )
    return context.transpose(1, 0, 2).reshape(time_len, site_len, head_cols)


def solution(mesh):
    in_specs = (
        P("tm", "depth", None),
        P("tm", "depth", None),
        P(),
        P(),
        P("tm", "depth"),
        P("depth", "tm", None),
    )
    out_specs = P("tm", "depth", None)
    fits = mesh.shape["depth"] == 4 and mesh.shape["tm"] % 2 == 0
    return jax.shard_map(
        plane_device if fits else per_device, mesh=mesh, in_specs=in_specs, out_specs=out_specs, check_vma=False
    )
```

```python
import functools
import math

import jax
import jax.numpy as jnp
from jax import lax
from jax.experimental import pallas as pl
from jax.experimental.pallas import tpu as pltpu
from jax.sharding import PartitionSpec as P

HEADS = 8
HD = 128
BT = 16
PP = 8
RD = 2
VMEM = pltpu.VMEM
SMEM = pltpu.SMEM


def padded_2(value, sides, width):
    for axis, dim in sides:
        devices, length = (lax.axis_size(axis), value.shape[dim])
        up = [(i, (i + 1) % devices) for i in range(devices - 1)]
        down = [(j, i) for i, j in up]
        last = lax.slice_in_dim(value, length - width, length, axis=dim)
        leading = lax.slice_in_dim(value, 0, width, axis=dim)
        before = lax.ppermute(last, axis, up)
        after = lax.ppermute(leading, axis, down)
        value = jnp.concatenate([before, value, after], axis=dim)
    return value


def normed_tokens(padded, stream, conv_w, gain):
    time_len, site_len, width = stream.shape
    tok_rows = time_len * site_len
    embedded = stream.reshape(tok_rows, width).astype(jnp.float32)
    for offset in range(3):
        window = padded[:, offset : offset + site_len].reshape(tok_rows, padded.shape[2])
        embedded = embedded + jnp.dot(window, conv_w[offset], preferred_element_type=jnp.float32)
    scale = lax.rsqrt(jnp.mean(embedded * embedded, axis=-1, keepdims=True) + 1e-05)
    return (embedded * scale * gain).astype(jnp.bfloat16)


def hop(value, fn):
    pairs = []
    for z in range(4):
        for core in range(2):
            for depth in range(4):
                to = fn(z, core, depth)
                if to is not None:
                    pairs.append(((2 * z + core) * 4 + depth, (2 * to[0] + to[1]) * 4 + to[2]))
    return lax.ppermute(value, ("tm", "depth"), pairs)


def swap_core(value):
    return hop(value, lambda z, c, d: (z, 1 - c, d))


def swap_depth(value, bits):
    return hop(value, lambda z, c, d: (z, c, d ^ bits))


def after(value, *others):
    return lax.optimization_barrier((value, *others))[0]


def move_z(value, by, only=range(4)):
    return hop(value, lambda z, c, d: (z + by, c, d) if z in only and 0 <= z + by < 4 else None)


def split_kernel(place, w_ref, x_ref, y_ref, keep_ref):
    pair = 2 * HD
    even = (place[1] & 1) == 0
    low, high = w_ref[:, :pair], w_ref[:, 2 * pair :]
    x_ref[...] = w_ref[:, pair : 2 * pair]
    y_ref[...] = jnp.where(even, high, low)
    keep_ref[...] = jnp.where(even, low, high)


def sort_kernel(place, kept, from_x, from_y, keep_ref, send_ref):
    first, even = (place[0] & 1) == 0, (place[1] & 1) == 0
    low = jnp.where(even, kept[...], from_y[...])
    high = jnp.where(even, from_y[...], kept[...])
    for k, group in enumerate((low, from_x[...], high)):
        here = slice(k * HD, (k + 1) * HD)
        keep_ref[:, here] = jnp.where(first, group[:, :HD], group[:, HD:])
        send_ref[:, here] = jnp.where(first, group[:, HD:], group[:, :HD])


def embed_kernel(place, raw, beside, across, stream, conv_w, gain, out_ref, acc_ref):
    time_len, site_len, feat_len = raw.shape
    depth = place[1]
    even = (depth & 1) == 0
    side, far = beside[:time_len].astype(jnp.float32), across[:time_len].astype(jnp.float32)
    before = jnp.where(even, jnp.where(depth == 2, far, 0.0), side)
    behind = jnp.where(even, side, jnp.where(depth == 1, far, 0.0))
    sites = raw[...].astype(jnp.float32)
    padded = jnp.concatenate([before[:, None], sites, behind[:, None]], axis=1)
    tok_rows = time_len * site_len
    windows = [padded[:, j : j + site_len].reshape(tok_rows, feat_len).astype(jnp.bfloat16) for j in range(3)]
    total = jnp.zeros((tok_rows, 1), jnp.float32)
    width, step = stream.shape[1], 512
    for at in range(0, width, step):
        here = slice(at, at + step)
        part = stream[:, here].astype(jnp.float32)
        for j in range(3):
            part += jnp.dot(windows[j], conv_w[j, :, here], preferred_element_type=jnp.float32)
        acc_ref[:, here] = part
        total += jnp.sum(part * part, axis=1, keepdims=True)
    scale = lax.rsqrt(total / width + 1e-05)
    out_ref[...] = (acc_ref[...] * scale * gain[...]).astype(jnp.bfloat16)


def columns(x_refs, source, rows):
    at = pl.ds(pl.multiple_of(source * rows, rows), rows)
    return jnp.concatenate([ref[:, at] for ref in x_refs], axis=0)


def partial_kernel(place, *refs):
    x_refs, (own, far, near, acc_ref) = refs[:-4], refs[-4:]
    z = place[0] >> 1
    rows = own.shape[0]
    value = jnp.dot(columns(x_refs, z, rows), own[...], preferred_element_type=jnp.float32)
    value += jnp.dot(columns(x_refs, z ^ 2, rows), far[...], preferred_element_type=jnp.float32)
    value += jnp.dot(columns(x_refs, z ^ 1, rows), near[...], preferred_element_type=jnp.float32)
    acc_ref[...] = value


def project_kernel(place, *refs):
    x_refs, (own, far, near, last, acc_in, q_ref, kv_ref, acc_ref, both_ref) = refs[:10], refs[10:]
    z, core, depth = place[0] >> 1, place[0] & 1, place[1]
    rows, block = own.shape[0], x_refs[0].shape[0]
    turn = jnp.where(depth == 3, 0, depth)
    half = x_refs[6].shape[1]
    for i in range(4):
        both_ref[(i // 2) * block : (i // 2 + 1) * block, (i % 2) * half : (i % 2 + 1) * half] = x_refs[6 + i][...]
    diagonals = [both_ref]
    value = jnp.dot(columns(diagonals, z, rows), own[...], preferred_element_type=jnp.float32)
    value += jnp.dot(columns(diagonals, z ^ 2, rows), far[...], preferred_element_type=jnp.float32)
    value += jnp.dot(columns(diagonals, z ^ 1, rows), near[...], preferred_element_type=jnp.float32)
    value += jnp.dot(columns(diagonals, z ^ 3, rows), last[...], preferred_element_type=jnp.float32)
    acc_ref[6 * block :] = value
    x = columns(x_refs[:6], z ^ 3, rows)
    value = jnp.dot(x, last[...], preferred_element_type=jnp.float32)
    acc_ref[: 6 * block] = acc_in[...] + value
    for rel in range(2):
        at = pl.ds(pl.multiple_of((core ^ rel) * block, block), block)
        for r in range(4):
            row = 3 * rel + r if r < 3 else 6 + rel
            mine = slice(row * block, (row + 1) * block)
            for third, (ref, column) in enumerate(((q_ref, 0), (kv_ref, 0), (kv_ref, HD))):
                group = third + turn
                group = jnp.where(group >= 3, group - 3, group)
                lanes = pl.ds(pl.multiple_of(group * HD, HD), HD)
                ref[r, at, column : column + HD] = acc_ref[mine, lanes].astype(jnp.bfloat16)


def attend_kernel(place, mask, q_ref, before, own, behind, keep_ref, send_ref):
    core = place[0] & 1
    block = q_ref.shape[1] // 2
    inv_root = 1.0 / math.sqrt(HD)
    for r in range(4):
        results = []
        for u in range(2):
            q = q_ref[r, u * block : (u + 1) * block]
            spans = ((before, u, 2), (own, 0, 2), (behind, 0, 1 + u))
            scores, entry = [], 0
            for ref, first, last in spans:
                k = ref[r, first * block : last * block, :HD]
                s = lax.dot_general(q, k, (((1,), (1,)), ((), ())), preferred_element_type=jnp.float32)
                for v in range(last - first):
                    flag = mask[((u ^ core) * 4 + r) * 5 + entry]
                    scores.append(jnp.where(flag > 0, s[:, v * block : (v + 1) * block] * inv_root, -1e30))
                    entry += 1
            top = jnp.max(functools.reduce(jnp.maximum, scores), axis=1, keepdims=True)
            powers = [jnp.exp(s - top) for s in scores]
            inverse = 1.0 / jnp.sum(functools.reduce(jnp.add, powers), axis=1, keepdims=True)
            weights = [(p * inverse).astype(jnp.bfloat16) for p in powers]
            result, entry = jnp.zeros((block, HD), jnp.float32), 0
            for ref, first, last in spans:
                w = jnp.concatenate(weights[entry : entry + last - first], axis=1)
                entry += last - first
                result += jnp.dot(w, ref[r, first * block : last * block, HD:], preferred_element_type=jnp.float32)
            results.append(result.astype(jnp.bfloat16))
        keep_ref[r] = jnp.where(core == 0, results[0], results[1])
        send_ref[r] = jnp.where(core == 0, results[1], results[0])


def gather_kernel(place, own, x, y, diagonal, out_ref):
    core, depth = place[0] & 1, place[1]
    for r, ref in enumerate((own, x, y, diagonal)):
        for rel in range(2):
            at = pl.multiple_of((2 * (depth ^ r) + (core ^ rel)) * HD, HD)
            out_ref[:, pl.ds(at, HD)] = ref[:, rel * HD : (rel + 1) * HD]


def vmem_call(kernel, outs, scratch=(), smem=1, total=1, limit=40, macs=0):
    return pl.pallas_call(
        kernel,
        out_shape=outs,
        in_specs=[pl.BlockSpec(memory_space=SMEM)] * smem + [pl.BlockSpec(memory_space=VMEM)] * (total - smem),
        out_specs=jax.tree.map(lambda _: pl.BlockSpec(memory_space=VMEM), outs),
        scratch_shapes=list(scratch),
        cost_estimate=pl.CostEstimate(flops=2 * macs, bytes_accessed=0, transcendentals=0),
        compiler_params=pltpu.CompilerParams(vmem_limit_bytes=limit * 2**20),
    )


def plane_device(raw, stream, conv_w, gain, w_qkv, mask):
    tm, depth = lax.axis_index("tm"), lax.axis_index("depth")
    first = (tm & 1) == 0
    time_len, site_len, feat_len = raw.shape
    block = time_len * site_len
    bf16, f32 = jnp.bfloat16, jnp.float32

    place = jnp.stack([tm, depth]).astype(jnp.int32)
    pair = jax.ShapeDtypeStruct((w_qkv.shape[0], 2 * HD), bf16)
    triple = jax.ShapeDtypeStruct((w_qkv.shape[0], 3 * HD), bf16)

    to_x, to_y, kept = vmem_call(split_kernel, (pair,) * 3, total=2)(place, w_qkv)
    from_y, from_x = swap_depth(to_y, 2), swap_depth(to_x, 1)
    keep, send = vmem_call(sort_kernel, (triple,) * 2, total=4)(place, kept, from_x, from_y)
    received = swap_core(send)
    shard = jnp.concatenate([jnp.where(first, keep, received), jnp.where(first, received, keep)], axis=0)
    far = hop(shard, lambda z, c, d: (z ^ 2, c, d))
    near = hop(shard, lambda z, c, d: (z ^ 1, c, d))
    far, near = lax.optimization_barrier((far, near))
    last = hop(far, lambda z, c, d: (z ^ 1, c, d))

    flags = jnp.pad(mask.reshape(1, mask.shape[2]), ((0, 0), (0, feat_len - mask.shape[2]))).astype(bf16)
    edges = [jnp.where(depth == at, raw[:, -1], raw[:, 0]) for at in (depth & 2, 1)]
    beside = swap_depth(jnp.concatenate([edges[0], flags]), 1)
    across = swap_depth(jnp.concatenate([edges[1], flags]), 3)
    flags = jnp.concatenate([flags, beside[time_len:], swap_depth(flags, 2), across[time_len:]])
    flags = jnp.concatenate([flags, swap_core(flags)])[:, : mask.shape[2]].astype(jnp.int32).reshape(-1)

    width = stream.shape[2]
    normed = vmem_call(
        embed_kernel,
        jax.ShapeDtypeStruct((block, width), bf16),
        scratch=[VMEM((block, width), f32)],
        total=7,
        macs=block * 3 * feat_len * width,
    )(place, raw, beside, across, stream.reshape(block, width), conv_w, gain.reshape(1, width))
    normed = after(normed, flags)
    from_x, from_y = swap_depth(normed, 1), swap_depth(normed, 2)
    half = width // 2
    left, right = swap_depth(from_x[:, :half], 2), swap_depth(from_y[:, half:], 1)

    rows = shard.shape[0]
    tokens = [normed, from_x, from_y]
    other = [swap_core(after(t, far)) for t in tokens]
    total = vmem_call(
        partial_kernel, jax.ShapeDtypeStruct((6 * block, 3 * HD), f32), total=10, macs=6 * block * 3 * rows * 3 * HD
    )(place, *tokens, *other, shard, far, near)
    left, right = after(left, total), after(right, total)
    q, kv = vmem_call(
        project_kernel,
        (jax.ShapeDtypeStruct((4, 2 * block, HD), bf16), jax.ShapeDtypeStruct((4, 2 * block, 2 * HD), bf16)),
        scratch=[VMEM((8 * block, 3 * HD), f32), VMEM((2 * block, width), bf16)],
        total=16,
        macs=14 * block * rows * 3 * HD,
    )(place, *tokens, *other, left, right, swap_core(left), swap_core(right), shard, far, near, last, total)

    piece = jax.ShapeDtypeStruct((4, block, HD), bf16)
    kept, sent = vmem_call(attend_kernel, (piece, piece), smem=2, total=6, macs=8 * block * 10 * block * HD)(
        place, flags, q, move_z(kv, 1), kv, move_z(kv, -1)
    )
    pairs = jnp.concatenate([kept, swap_core(sent)], axis=2)
    pieces = [pairs[0]] + [swap_depth(pairs[bits], bits) for bits in (1, 2, 3)]
    context = vmem_call(gather_kernel, jax.ShapeDtypeStruct((block, HEADS * HD), bf16), total=5)(place, *pieces)
    return context.reshape(time_len, site_len, HEADS * HD)


def from_behind(value, axis, by):
    devices = lax.axis_size(axis)
    pairs = [(i, i + by) for i in range(devices) if 0 <= i + by < devices]
    return lax.ppermute(value, axis, pairs)


def head_attend(query_head, key_head, value_head, allowed):
    inv_root = 1.0 / math.sqrt(HD)
    scores = (
        jnp.einsum("qd,kd->qk", query_head, key_head, preferred_element_type=jnp.float32) * inv_root
    )
    scores = jnp.where(allowed, scores, -1e30)
    row_max = jnp.max(scores, axis=-1, keepdims=True)
    powers = jnp.exp(scores - row_max)
    weights = (powers / jnp.sum(powers, axis=-1, keepdims=True)).astype(jnp.bfloat16)
    return jnp.dot(weights, value_head, preferred_element_type=jnp.float32).astype(jnp.bfloat16)


def per_device(raw, stream, conv_w, gain, w_qkv, mask):
    time_len, site_len, _ = raw.shape
    tok_rows = time_len * site_len
    normed = normed_tokens(padded_2(raw, (("depth", 1),), 1), stream, conv_w, gain)
    columns = lax.all_gather(w_qkv, "depth", axis=1, tiled=True)
    projected = jnp.dot(
        normed,
        lax.all_gather(columns, "tm", axis=0, tiled=True),
        preferred_element_type=jnp.float32,
    ).astype(jnp.bfloat16)
    head_cols = projected.shape[1] // 3
    queries = projected[:, :head_cols]
    keyvals = projected[:, head_cols:]
    earlier = []
    later = []
    moving_back = keyvals
    moving_ahead = keyvals
    for hop_index in range(RD):
        moving_back = from_behind(moving_back, "tm", 1)
        moving_ahead = from_behind(moving_ahead, "tm", -1)
        earlier.insert(0, moving_back)
        later.append(moving_ahead)
    gathered = jnp.concatenate(earlier + [keyvals] + later, axis=0)
    block_rows = BT * PP
    own_blocks = tok_rows // block_rows
    span_blocks = gathered.shape[0] // block_rows
    local_mask = mask[0]
    query_ids = jnp.arange(own_blocks, dtype=jnp.int32)[:, None]
    key_ids = jnp.arange(span_blocks, dtype=jnp.int32)[None, :]
    entry_ids = key_ids - query_ids
    picks = entry_ids[:, :, None] == jnp.arange(local_mask.shape[1], dtype=jnp.int32)[None, None, :]
    block_allowed = jnp.sum(jnp.where(picks, local_mask[:, None, :], 0), axis=-1) > 0
    allowed = jnp.repeat(jnp.repeat(block_allowed, block_rows, axis=0), block_rows, axis=1)
    query_heads = queries.reshape(tok_rows, HEADS, HD).transpose(1, 0, 2)
    key_heads = gathered[:, :head_cols].reshape(gathered.shape[0], HEADS, HD).transpose(1, 0, 2)
    value_heads = gathered[:, head_cols:].reshape(gathered.shape[0], HEADS, HD).transpose(1, 0, 2)
    context = lax.map(
        lambda operands: head_attend(operands[0], operands[1], operands[2], allowed),
        (query_heads, key_heads, value_heads),
    )
    return context.transpose(1, 0, 2).reshape(time_len, site_len, head_cols)


def solution(mesh):
    in_specs = (
        P("tm", "depth", None),
        P("tm", "depth", None),
        P(),
        P(),
        P("tm", "depth"),
        P("depth", "tm", None),
    )
    out_specs = P("tm", "depth", None)
    fits = mesh.shape["depth"] == 4 and mesh.shape["tm"] == 8
    return jax.shard_map(
        plane_device if fits else per_device, mesh=mesh, in_specs=in_specs, out_specs=out_specs, check_vma=False
    )
```

```python
import functools
import math

import jax
import jax.numpy as jnp
from jax import lax
from jax.experimental import pallas as pl
from jax.experimental.pallas import tpu as pltpu
from jax.sharding import PartitionSpec as P

HEADS = 8
HD = 128
BT = 16
PP = 8
RD = 2
VMEM = pltpu.VMEM
SMEM = pltpu.SMEM


def padded_2(value, sides, width):
    for axis, dim in sides:
        devices, length = (lax.axis_size(axis), value.shape[dim])
        up = [(i, (i + 1) % devices) for i in range(devices - 1)]
        down = [(j, i) for i, j in up]
        last = lax.slice_in_dim(value, length - width, length, axis=dim)
        leading = lax.slice_in_dim(value, 0, width, axis=dim)
        before = lax.ppermute(last, axis, up)
        after = lax.ppermute(leading, axis, down)
        value = jnp.concatenate([before, value, after], axis=dim)
    return value


def normed_tokens(padded, stream, conv_w, gain):
    time_len, site_len, width = stream.shape
    tok_rows = time_len * site_len
    embedded = stream.reshape(tok_rows, width).astype(jnp.float32)
    for offset in range(3):
        window = padded[:, offset : offset + site_len].reshape(tok_rows, padded.shape[2])
        embedded = embedded + jnp.dot(window, conv_w[offset], preferred_element_type=jnp.float32)
    scale = lax.rsqrt(jnp.mean(embedded * embedded, axis=-1, keepdims=True) + 1e-05)
    return (embedded * scale * gain).astype(jnp.bfloat16)


PAIR = 2 * HD
EXTRA = 16


def hop(value, fn):
    pairs = []
    for z in range(4):
        for core in range(2):
            for depth in range(4):
                to = fn(z, core, depth)
                if to is not None:
                    pairs.append(((2 * z + core) * 4 + depth, (2 * to[0] + to[1]) * 4 + to[2]))
    return lax.ppermute(value, ("tm", "depth"), pairs)


def swap_core(value):
    return hop(value, lambda z, c, d: (z, 1 - c, d))


def swap_depth(value, bits):
    return hop(value, lambda z, c, d: (z, c, d ^ bits))


def swap_z(value, bits):
    return hop(value, lambda z, c, d: (z ^ bits, c, d))


def move_z(value, by):
    return hop(value, lambda z, c, d: (z + by, c, d) if 0 <= z + by < 4 else None)


def after(value, *others):
    return lax.optimization_barrier((value, *others))[0]


def where_am_i():
    tm = lax.axis_index("tm")
    return tm >> 1, tm & 1, lax.axis_index("depth")


def split_kernel(mask, w, raw, to_x, to_y, to_across, keep, sites, sems):
    _, _, depth = where_am_i()
    odd = depth & 1
    size = w.shape[0]
    copies = [pltpu.make_async_copy(raw, sites, sems.at[3])]
    for i, (at, ref) in enumerate(
        ((PAIR, to_x.at[:size]), ((1 - odd) * 2 * PAIR, to_y.at[:size]), (odd * 2 * PAIR, keep))
    ):
        at = at if isinstance(at, int) else pl.multiple_of(at, PAIR)
        copies.append(pltpu.make_async_copy(w.at[:, pl.ds(at, PAIR)], ref, sems.at[i]))
    for copy in copies:
        copy.start()
    lane = lax.broadcasted_iota(jnp.int32, (EXTRA, HD), 1)
    flags = jnp.zeros((EXTRA, HD), jnp.int32)
    for entry in range(mask.shape[0]):
        flags = jnp.where(lane == entry, mask[entry], flags)
    flags = flags.astype(jnp.float32).astype(jnp.bfloat16)
    copies[0].wait()
    values = sites[...].astype(jnp.float32)
    first, last = values[:, 0], values[:, values.shape[1] - 1]
    for ref, use_last, at in ((to_x, odd == 0, size), (to_across, depth == 1, 0)):
        ref[at : at + EXTRA, :HD] = jnp.where(use_last, last, first).astype(jnp.bfloat16)
        ref[at : at + EXTRA, HD:] = flags
    to_y[size:, :HD] = flags
    to_y[size:, HD:] = flags
    for copy in copies[1:]:
        copy.wait()


def sort_kernel(kept, from_x, from_y, across, to_y, keep_ref, send_ref, flags_ref):
    _, core, depth = where_am_i()
    first, even = core == 0, (depth & 1) == 0
    size = kept.shape[0]
    low = jnp.where(even, kept[...], from_y[:size])
    high = jnp.where(even, from_y[:size], kept[...])
    for k, group in enumerate((low, from_x[:size], high)):
        here = slice(k * HD, (k + 1) * HD)
        keep_ref[:, here] = jnp.where(first, group[:, :HD], group[:, HD:])
        send_ref[:size, here] = jnp.where(first, group[:, HD:], group[:, :HD])
    row = lax.broadcasted_iota(jnp.int32, (EXTRA, HD), 0)
    flags = to_y[size:, :HD].astype(jnp.float32)
    for r, value in ((1, from_x[size:, HD:]), (2, from_y[size:, :HD]), (3, across[:, HD:])):
        flags = jnp.where(row == r, value.astype(jnp.float32), flags)
    flags = flags.astype(jnp.bfloat16)
    flags_ref[...] = flags
    for k in range(3):
        send_ref[size:, k * HD : (k + 1) * HD] = flags


def embed_kernel(from_x, across, gain, raw, stream, conv_w, out_ref, acc, sites, tokens, weights, sems):
    time_len, site_len, feat_len = raw.shape
    _, _, depth = where_am_i()
    even = (depth & 1) == 0
    rows, width = stream.shape
    parts = weights.shape[0]
    step = width // parts
    first = pltpu.make_async_copy(raw, sites, sems.at[2 * parts])
    first.start()
    copies = []
    for i in range(parts):
        here = pl.ds(i * step, step)
        pair = (
            pltpu.make_async_copy(conv_w.at[:, :, here], weights.at[i], sems.at[2 * i]),
            pltpu.make_async_copy(stream.at[:, here], tokens.at[i], sems.at[2 * i + 1]),
        )
        for copy in pair:
            copy.start()
        copies.append(pair)
    side = from_x[from_x.shape[0] - EXTRA :, :HD].astype(jnp.float32)
    far = across[:, :HD].astype(jnp.float32)
    before = jnp.where(even, jnp.where(depth == 2, far, 0.0), side)
    behind = jnp.where(even, side, jnp.where(depth == 1, far, 0.0))
    first.wait()
    padded = jnp.concatenate([before[:, None], sites[...].astype(jnp.float32), behind[:, None]], axis=1)
    windows = [padded[:, j : j + site_len].reshape(rows, feat_len).astype(jnp.bfloat16) for j in range(3)]
    windows = jnp.concatenate(windows, axis=1)
    total = jnp.zeros((rows, 1), jnp.float32)
    for i, pair in enumerate(copies):
        for copy in pair:
            copy.wait()
        part = jnp.dot(windows, weights[i].reshape(3 * feat_len, step), preferred_element_type=jnp.float32)
        part += tokens[i].astype(jnp.float32)
        acc[:, i * step : (i + 1) * step] = part
        total += jnp.sum(part * part, axis=1, keepdims=True)
    scale = lax.rsqrt(total / width + 1e-05)
    out_ref[...] = (acc[...] * scale * gain[...]).astype(jnp.bfloat16)


def take(refs, source, core, rows):
    half = rows // 2
    cuts = [pl.ds(pl.multiple_of(source * rows + c * half, half), half) for c in (core, 1 - core)]
    return jnp.concatenate([jnp.concatenate([ref[:, at] for at in cuts], axis=1) for ref in refs], axis=0)


def partial_kernel(*refs):
    x_refs, (own, far, near, acc_ref) = refs[:4], refs[4:]
    z, core, _ = where_am_i()
    w = jnp.concatenate([own[...], far[...], near[...]], axis=0)
    x = [take(x_refs, source, core, own.shape[0]) for source in (z, z ^ 2, z ^ 1)]
    acc_ref[...] = jnp.dot(jnp.concatenate(x, axis=1), w, preferred_element_type=jnp.float32)


def project_kernel(*refs):
    early, late, (own, far, near, last, acc_in, q_ref, k_ref, v_ref, acc_ref, x_all) = refs[:4], refs[4:12], refs[12:]
    z, core, depth = where_am_i()
    rows, block, half = last.shape[0], late[0].shape[0], late[0].shape[1]
    for i, ref in enumerate(late):
        x_all[(i // 2) * block : (i // 2 + 1) * block, (i % 2) * half : (i % 2 + 1) * half] = ref[...]
    w = jnp.concatenate([own[...], far[...], near[...], last[...]], axis=0)
    x = [take([x_all], source, core, rows) for source in (z, z ^ 2, z ^ 1, z ^ 3)]
    acc_ref[4 * block :] = jnp.dot(jnp.concatenate(x, axis=1), w, preferred_element_type=jnp.float32)
    x = take(early, z ^ 3, core, rows)
    acc_ref[: 4 * block] = acc_in[...] + jnp.dot(x, last[...], preferred_element_type=jnp.float32)
    order = ((0, 1, 2, 6), (3, 4, 5, 7))
    turn = jnp.where(depth == 3, 0, depth)
    for rel in range(2):
        at = pl.ds(pl.multiple_of((core ^ rel) * block, block), block)
        for r in range(4):
            row = order[rel][r]
            mine = slice(row * block, (row + 1) * block)
            for third, ref in enumerate((q_ref, k_ref, v_ref)):
                group = third + turn
                group = jnp.where(group >= 3, group - 3, group)
                lanes = pl.ds(pl.multiple_of(group * HD, HD), HD)
                ref[r, at, :] = acc_ref[mine, lanes].astype(jnp.bfloat16)


def spans(u):
    return ((0, u, 2), (1, 0, 2), (2, 0, 1 + u))


def weigh_kernel(q_ref, before, own, behind, own_flags, other_flags, out_ref):
    _, core, _ = where_am_i()
    block = q_ref.shape[1] // 2
    inv_root = 1.0 / math.sqrt(HD)
    flags = [own_flags[...].astype(jnp.float32), other_flags[...].astype(jnp.float32)]
    flags = [jnp.where(core == u, flags[0], flags[1]) for u in range(2)]
    bias = [(f - 1.0) * 1e30 for f in flags]
    keys = (before, own, behind)
    for r in range(4):
        for u in range(2):
            q = q_ref[r, u * block : (u + 1) * block]
            scores = []
            for side, first, last in spans(u):
                k = keys[side][r, first * block : last * block]
                s = lax.dot_general(q, k, (((1,), (1,)), ((), ())), preferred_element_type=jnp.float32)
                for v in range(last - first):
                    entry = len(scores)
                    shut = jnp.broadcast_to(bias[u][r : r + 1, entry : entry + 1], (block, block))
                    scores.append(s[:, v * block : (v + 1) * block] * inv_root + shut)
            top = jnp.max(functools.reduce(jnp.maximum, scores), axis=1, keepdims=True)
            powers = [jnp.exp(s - top) for s in scores]
            inverse = 1.0 / jnp.sum(functools.reduce(jnp.add, powers), axis=1, keepdims=True)
            for entry, p in enumerate(powers):
                here = slice(entry * block, (entry + 1) * block)
                out_ref[r, u * block : (u + 1) * block, here] = (p * inverse).astype(jnp.bfloat16)


def mix_kernel(r, weights, before, own, behind, out_ref):
    block = weights.shape[1] // 2
    values = (before, own, behind)
    for u in range(2):
        w = weights[r, u * block : (u + 1) * block]
        v = [values[side][r, first * block : last * block] for side, first, last in spans(u)]
        result = jnp.dot(w, jnp.concatenate(v, axis=0), preferred_element_type=jnp.float32)
        out_ref[u * block : (u + 1) * block] = result.astype(jnp.bfloat16)


def gather_kernel(*refs):
    out_ref = refs[-1]
    _, core, depth = where_am_i()
    block = out_ref.shape[0]
    mine = pl.ds(pl.multiple_of(core * block, block), block)
    for i, ref in enumerate(refs[:-1]):
        r, rel = i >> 1, i & 1
        at = pl.multiple_of((2 * (depth ^ r) + (core ^ rel)) * HD, HD)
        out_ref[:, pl.ds(at, HD)] = ref[mine, :]


def call(kernel, outs, places, scratch=(), macs=0):
    spaces = {"s": SMEM, "v": VMEM, "a": pl.ANY}
    return pl.pallas_call(
        kernel,
        out_shape=outs,
        in_specs=[pl.BlockSpec(memory_space=spaces[place]) for place in places],
        out_specs=jax.tree.map(lambda _: pl.BlockSpec(memory_space=VMEM), outs),
        scratch_shapes=list(scratch),
        cost_estimate=pl.CostEstimate(flops=2 * macs, bytes_accessed=0, transcendentals=0),
        compiler_params=pltpu.CompilerParams(vmem_limit_bytes=({2: 60, 3: 58}.get(places.count("a"), 40)) * 2**20),
    )


def plane_device(raw, stream, conv_w, gain, w_qkv, mask):
    time_len, site_len, feat_len = raw.shape
    block, width = time_len * site_len, stream.shape[2]
    half, size = width // 2, w_qkv.shape[0]
    bf16, f32 = jnp.bfloat16, jnp.float32

    def array(*shape, kind=bf16):
        return jax.ShapeDtypeStruct(shape, kind)

    to_x, to_y, to_across, kept = call(
        split_kernel,
        (array(size + EXTRA, PAIR), array(size + EXTRA, PAIR), array(EXTRA, PAIR), array(size, PAIR)),
        "saa",
        scratch=[VMEM(raw.shape, bf16), pltpu.SemaphoreType.DMA((4,))],
    )(mask.reshape(mask.shape[2]), w_qkv, raw)
    from_x, from_y, across = swap_depth(to_x, 1), swap_depth(to_y, 2), swap_depth(to_across, 3)
    keep, send, flags = call(
        sort_kernel, (array(size, 3 * HD), array(size + EXTRA, 3 * HD), array(EXTRA, HD)), "v" * 5
    )(kept, from_x, from_y, across, to_y)
    received = swap_core(send)
    other_flags = received[size:, :HD]
    shard = jnp.concatenate([keep, received[:size]], axis=0)
    far, near = swap_z(shard, 2), swap_z(shard, 1)

    parts = 4
    normed = call(
        embed_kernel,
        array(block, width),
        "vvvaaa",
        scratch=[
            VMEM((block, width), f32),
            VMEM(raw.shape, bf16),
            VMEM((parts, block, width // parts), bf16),
            VMEM((parts, 3, feat_len, width // parts), bf16),
            pltpu.SemaphoreType.DMA((2 * parts + 1,)),
        ],
        macs=block * 3 * feat_len * width,
    )(from_x, across, gain.reshape(1, width), raw, stream.reshape(block, width), conv_w)
    normed = after(normed, received)
    beside, above = swap_depth(normed, 1), swap_depth(normed, 2)
    opposite = swap_core(normed)
    far, near, opposite = lax.optimization_barrier((far, near, opposite))
    last = swap_z(far, 1)
    halves = [t[:, i * half : (i + 1) * half] for t in (after(beside, far), after(above, far)) for i in range(2)]
    diagonal = [swap_depth(halves[0], 2), swap_depth(halves[3], 1)]
    rows = 2 * size
    early = (normed, beside, above, opposite)
    total = call(partial_kernel, array(4 * block, 3 * HD, kind=f32), "v" * 7, macs=4 * block * 3 * rows * 3 * HD)(
        *early, shard, far, near
    )
    diagonal = [after(t, total) for t in diagonal]
    late = [swap_core(t) for t in halves] + diagonal + [swap_core(t) for t in diagonal]
    one_head = array(4, 2 * block, HD)
    q, k, v = call(
        project_kernel,
        (one_head,) * 3,
        "v" * 17,
        scratch=[VMEM((8 * block, 3 * HD), f32), VMEM((4 * block, width), bf16)],
        macs=20 * block * rows * 3 * HD,
    )(*early, *late, shard, far, near, last, total)

    weights = call(weigh_kernel, array(4, 2 * block, 5 * block), "v" * 6, macs=8 * block * 5 * block * HD)(
        q, move_z(k, 1), k, move_z(k, -1), flags, other_flags
    )
    values = (move_z(v, 1), v, move_z(v, -1))
    pieces = {}
    for r in (3, 1, 2, 0):
        mixed = call(functools.partial(mix_kernel, r), array(2 * block, HD), "vvvv", macs=2 * block * 5 * block * HD)(
            weights, *values
        )
        pieces[r] = swap_depth(mixed, r) if r else mixed
    both = [t for r in range(4) for t in (pieces[r], swap_core(pieces[r]))]
    context = call(gather_kernel, array(block, HEADS * HD), "v" * 8)(*both)
    return context.reshape(time_len, site_len, HEADS * HD)


def from_behind(value, axis, by):
    devices = lax.axis_size(axis)
    pairs = [(i, i + by) for i in range(devices) if 0 <= i + by < devices]
    return lax.ppermute(value, axis, pairs)


def head_attend(query_head, key_head, value_head, allowed):
    inv_root = 1.0 / math.sqrt(HD)
    scores = (
        jnp.einsum("qd,kd->qk", query_head, key_head, preferred_element_type=jnp.float32) * inv_root
    )
    scores = jnp.where(allowed, scores, -1e30)
    row_max = jnp.max(scores, axis=-1, keepdims=True)
    powers = jnp.exp(scores - row_max)
    weights = (powers / jnp.sum(powers, axis=-1, keepdims=True)).astype(jnp.bfloat16)
    return jnp.dot(weights, value_head, preferred_element_type=jnp.float32).astype(jnp.bfloat16)


def per_device(raw, stream, conv_w, gain, w_qkv, mask):
    time_len, site_len, _ = raw.shape
    tok_rows = time_len * site_len
    normed = normed_tokens(padded_2(raw, (("depth", 1),), 1), stream, conv_w, gain)
    columns = lax.all_gather(w_qkv, "depth", axis=1, tiled=True)
    projected = jnp.dot(
        normed,
        lax.all_gather(columns, "tm", axis=0, tiled=True),
        preferred_element_type=jnp.float32,
    ).astype(jnp.bfloat16)
    head_cols = projected.shape[1] // 3
    queries = projected[:, :head_cols]
    keyvals = projected[:, head_cols:]
    earlier = []
    later = []
    moving_back = keyvals
    moving_ahead = keyvals
    for hop_index in range(RD):
        moving_back = from_behind(moving_back, "tm", 1)
        moving_ahead = from_behind(moving_ahead, "tm", -1)
        earlier.insert(0, moving_back)
        later.append(moving_ahead)
    gathered = jnp.concatenate(earlier + [keyvals] + later, axis=0)
    block_rows = BT * PP
    own_blocks = tok_rows // block_rows
    span_blocks = gathered.shape[0] // block_rows
    local_mask = mask[0]
    query_ids = jnp.arange(own_blocks, dtype=jnp.int32)[:, None]
    key_ids = jnp.arange(span_blocks, dtype=jnp.int32)[None, :]
    entry_ids = key_ids - query_ids
    picks = entry_ids[:, :, None] == jnp.arange(local_mask.shape[1], dtype=jnp.int32)[None, None, :]
    block_allowed = jnp.sum(jnp.where(picks, local_mask[:, None, :], 0), axis=-1) > 0
    allowed = jnp.repeat(jnp.repeat(block_allowed, block_rows, axis=0), block_rows, axis=1)
    query_heads = queries.reshape(tok_rows, HEADS, HD).transpose(1, 0, 2)
    key_heads = gathered[:, :head_cols].reshape(gathered.shape[0], HEADS, HD).transpose(1, 0, 2)
    value_heads = gathered[:, head_cols:].reshape(gathered.shape[0], HEADS, HD).transpose(1, 0, 2)
    context = lax.map(
        lambda operands: head_attend(operands[0], operands[1], operands[2], allowed),
        (query_heads, key_heads, value_heads),
    )
    return context.transpose(1, 0, 2).reshape(time_len, site_len, head_cols)


def solution(mesh):
    in_specs = (
        P("tm", "depth", None),
        P("tm", "depth", None),
        P(),
        P(),
        P("tm", "depth"),
        P("depth", "tm", None),
    )
    out_specs = P("tm", "depth", None)
    fits = mesh.shape["depth"] == 4 and mesh.shape["tm"] == 8
    return jax.shard_map(
        plane_device if fits else per_device, mesh=mesh, in_specs=in_specs, out_specs=out_specs, check_vma=False
    )
```

```python
import functools
import math

import jax
import jax.numpy as jnp
from jax import lax
from jax.experimental import pallas as pl
from jax.experimental.pallas import tpu as pltpu
from jax.sharding import PartitionSpec as P

HEADS = 8
HD = 128
BT = 16
PP = 8
RD = 2
VMEM = pltpu.VMEM
SMEM = pltpu.SMEM


def padded_2(value, sides, width):
    for axis, dim in sides:
        devices, length = (lax.axis_size(axis), value.shape[dim])
        up = [(i, (i + 1) % devices) for i in range(devices - 1)]
        down = [(j, i) for i, j in up]
        last = lax.slice_in_dim(value, length - width, length, axis=dim)
        leading = lax.slice_in_dim(value, 0, width, axis=dim)
        before = lax.ppermute(last, axis, up)
        after = lax.ppermute(leading, axis, down)
        value = jnp.concatenate([before, value, after], axis=dim)
    return value


def normed_tokens(padded, stream, conv_w, gain):
    time_len, site_len, width = stream.shape
    tok_rows = time_len * site_len
    embedded = stream.reshape(tok_rows, width).astype(jnp.float32)
    for offset in range(3):
        window = padded[:, offset : offset + site_len].reshape(tok_rows, padded.shape[2])
        embedded = embedded + jnp.dot(window, conv_w[offset], preferred_element_type=jnp.float32)
    scale = lax.rsqrt(jnp.mean(embedded * embedded, axis=-1, keepdims=True) + 1e-05)
    return (embedded * scale * gain).astype(jnp.bfloat16)


PAIR = 2 * HD
V_ORDER = (3, 1, 2, 0)
EXTRA = 16


def hop(value, fn):
    pairs = []
    for z in range(4):
        for core in range(2):
            for depth in range(4):
                to = fn(z, core, depth)
                if to is not None:
                    pairs.append(((2 * z + core) * 4 + depth, (2 * to[0] + to[1]) * 4 + to[2]))
    return lax.ppermute(value, ("tm", "depth"), pairs)


def swap_core(value):
    return hop(value, lambda z, c, d: (z, 1 - c, d))


def swap_depth(value, bits):
    return hop(value, lambda z, c, d: (z, c, d ^ bits))


def swap_z(value, bits):
    return hop(value, lambda z, c, d: (z ^ bits, c, d))


def swap_middle(value):
    return hop(value, lambda z, c, d: (z ^ 3, c, d) if z in (1, 2) else None)


def after(value, *others):
    return lax.optimization_barrier((value, *others))[0]


def where_am_i():
    tm = lax.axis_index("tm")
    return tm >> 1, tm & 1, lax.axis_index("depth")


def split_kernel(mask, w, raw, to_x, to_y, to_across, keep, sites, sems):
    _, _, depth = where_am_i()
    odd = depth & 1
    size = w.shape[0]
    copies = [pltpu.make_async_copy(raw, sites, sems.at[3])]
    for i, (at, ref) in enumerate(
        ((PAIR, to_x.at[:size]), ((1 - odd) * 2 * PAIR, to_y.at[:size]), (odd * 2 * PAIR, keep))
    ):
        at = at if isinstance(at, int) else pl.multiple_of(at, PAIR)
        copies.append(pltpu.make_async_copy(w.at[:, pl.ds(at, PAIR)], ref, sems.at[i]))
    for copy in copies:
        copy.start()
    lane = lax.broadcasted_iota(jnp.int32, (EXTRA, HD), 1)
    flags = jnp.zeros((EXTRA, HD), jnp.int32)
    for entry in range(mask.shape[0]):
        flags = jnp.where(lane == entry, mask[entry], flags)
    flags = flags.astype(jnp.float32).astype(jnp.bfloat16)
    copies[0].wait()
    values = sites[...].astype(jnp.float32)
    first, last = values[:, 0], values[:, values.shape[1] - 1]
    for ref, use_last, at in ((to_x, odd == 0, size), (to_across, depth == 1, 0)):
        ref[at : at + EXTRA, :HD] = jnp.where(use_last, last, first).astype(jnp.bfloat16)
        ref[at : at + EXTRA, HD:] = flags
    to_y[size:, :HD] = flags
    to_y[size:, HD:] = flags
    for copy in copies[1:]:
        copy.wait()


def sort_kernel(kept, from_x, from_y, across, to_y, keep_ref, send_ref, flags_ref):
    _, core, depth = where_am_i()
    first, even = core == 0, (depth & 1) == 0
    size = kept.shape[0]
    low = jnp.where(even, kept[...], from_y[:size])
    high = jnp.where(even, from_y[:size], kept[...])
    for k, group in enumerate((low, from_x[:size], high)):
        here = slice(k * HD, (k + 1) * HD)
        keep_ref[:, here] = jnp.where(first, group[:, :HD], group[:, HD:])
        send_ref[:size, here] = jnp.where(first, group[:, HD:], group[:, :HD])
    row = lax.broadcasted_iota(jnp.int32, (EXTRA, HD), 0)
    flags = to_y[size:, :HD].astype(jnp.float32)
    for r, value in ((1, from_x[size:, HD:]), (2, from_y[size:, :HD]), (3, across[:, HD:])):
        flags = jnp.where(row == r, value.astype(jnp.float32), flags)
    flags = flags.astype(jnp.bfloat16)
    flags_ref[...] = flags
    for k in range(3):
        send_ref[size:, k * HD : (k + 1) * HD] = flags


def load_kernel(*refs):
    count = (len(refs) - 1) // 2
    copies = [pltpu.make_async_copy(refs[i], refs[count + i], refs[-1].at[i]) for i in range(count)]
    for copy in copies:
        copy.start()
    for copy in copies:
        copy.wait()


def embed_kernel(from_x, across, gain, raw, stream, conv_w, out_ref, acc):
    time_len, site_len, feat_len = raw.shape
    _, _, depth = where_am_i()
    even = (depth & 1) == 0
    rows, width = stream.shape
    side = from_x[from_x.shape[0] - EXTRA :, :HD].astype(jnp.float32)
    far = across[:, :HD].astype(jnp.float32)
    before = jnp.where(even, jnp.where(depth == 2, far, 0.0), side)
    behind = jnp.where(even, side, jnp.where(depth == 1, far, 0.0))
    padded = jnp.concatenate([before[:, None], raw[...].astype(jnp.float32), behind[:, None]], axis=1)
    windows = [padded[:, j : j + site_len].reshape(rows, feat_len).astype(jnp.bfloat16) for j in range(3)]
    windows = jnp.concatenate(windows, axis=1)
    total, step = jnp.zeros((rows, 1), jnp.float32), width // 4
    for at in range(0, width, step):
        here = slice(at, at + step)
        part = jnp.dot(windows, conv_w[:, here], preferred_element_type=jnp.float32)
        part += stream[:, here].astype(jnp.float32)
        acc[:, here] = part
        total += jnp.sum(part * part, axis=1, keepdims=True)
    scale = lax.rsqrt(total / width + 1e-05)
    out_ref[...] = (acc[...] * scale * gain[...]).astype(jnp.bfloat16)


def take(refs, source, core, rows):
    half = rows // 2
    cuts = [pl.ds(pl.multiple_of(source * rows + c * half, half), half) for c in (core, 1 - core)]
    return jnp.concatenate([jnp.concatenate([ref[:, at] for at in cuts], axis=1) for ref in refs], axis=0)


def partial_kernel(*refs):
    x_refs, (own, far, near, acc_ref) = refs[:6], refs[6:]
    z, core, _ = where_am_i()
    w = jnp.concatenate([ref[...] for ref in (own, far, near)], axis=0)
    x = [take(x_refs, source, core, own.shape[0]) for source in (z, z ^ 2, z ^ 1)]
    acc_ref[...] = jnp.dot(jnp.concatenate(x, axis=1), w, preferred_element_type=jnp.float32)


def project_kernel(*refs):
    early, late, (own, far, near, last, acc_in) = refs[:6], refs[6:10], refs[10:15]
    q_ref, k_ref, v_first, v_second, acc_ref, x_all = refs[15:]
    z, core, depth = where_am_i()
    rows, block, half = own.shape[0], late[0].shape[0], late[0].shape[1]
    for i, ref in enumerate(late):
        x_all[(i // 2) * block : (i // 2 + 1) * block, (i % 2) * half : (i % 2 + 1) * half] = ref[...]
    w = jnp.concatenate([ref[...] for ref in (own, far, near, last)], axis=0)
    x = [take([x_all], source, core, rows) for source in (z, z ^ 2, z ^ 1, z ^ 3)]
    acc_ref[6 * block :] = jnp.dot(jnp.concatenate(x, axis=1), w, preferred_element_type=jnp.float32)
    x = take(early, z ^ 3, core, rows)
    acc_ref[: 6 * block] = acc_in[...] + jnp.dot(x, last[...], preferred_element_type=jnp.float32)
    order = ((0, 1, 2, 6), (3, 4, 5, 7))
    turn = jnp.where(depth == 3, 0, depth)
    for rel in range(2):
        at = pl.ds(pl.multiple_of((core ^ rel) * block, block), block)
        for r in range(4):
            row = order[rel][r]
            mine = slice(row * block, (row + 1) * block)
            v_at = V_ORDER.index(r)
            targets = (q_ref.at[r], k_ref.at[r], (v_first, v_second)[v_at // 2].at[v_at % 2])
            for third, ref in enumerate(targets):
                group = third + turn
                group = jnp.where(group >= 3, group - 3, group)
                lanes = pl.ds(pl.multiple_of(group * HD, HD), HD)
                ref[at, :] = acc_ref[mine, lanes].astype(jnp.bfloat16)


def spans(u):
    return ((0, u, 2), (1, 0, 2), (2, 0, 1 + u))


def neighbours(outer, own, middle, index):
    z, _, _ = where_am_i()
    odd = (z & 1) == 1
    outer, middle = outer[index], middle[index]
    return jnp.where(odd, outer, middle), own[index], jnp.where(odd, middle, outer)


def weigh_kernel(q_ref, outer, own, middle, own_flags, other_flags, out_ref):
    _, core, _ = where_am_i()
    block = q_ref.shape[1] // 2
    inv_root = 1.0 / math.sqrt(HD)
    flags = [own_flags[...].astype(jnp.float32), other_flags[...].astype(jnp.float32)]
    flags = [jnp.where(core == u, flags[0], flags[1]) for u in range(2)]
    bias = [(f - 1.0) * 1e30 for f in flags]
    for r in range(4):
        keys = neighbours(outer, own, middle, r)
        for u in range(2):
            q = q_ref[r, u * block : (u + 1) * block]
            scores = []
            for side, first, last in spans(u):
                k = keys[side][first * block : last * block]
                s = lax.dot_general(q, k, (((1,), (1,)), ((), ())), preferred_element_type=jnp.float32)
                for v in range(last - first):
                    entry = len(scores)
                    shut = jnp.broadcast_to(bias[u][r : r + 1, entry : entry + 1], (block, block))
                    scores.append(s[:, v * block : (v + 1) * block] * inv_root + shut)
            top = jnp.max(functools.reduce(jnp.maximum, scores), axis=1, keepdims=True)
            powers = [jnp.exp(s - top) for s in scores]
            inverse = 1.0 / jnp.sum(functools.reduce(jnp.add, powers), axis=1, keepdims=True)
            for entry, p in enumerate(powers):
                here = slice(entry * block, (entry + 1) * block)
                out_ref[r, u * block : (u + 1) * block, here] = (p * inverse).astype(jnp.bfloat16)


def mix_kernel(r, weights, outer, own, middle, out_ref):
    block = weights.shape[1] // 2
    values = neighbours(outer, own, middle, V_ORDER.index(r) % 2)
    for u in range(2):
        w = weights[r, u * block : (u + 1) * block]
        v = [values[side][first * block : last * block] for side, first, last in spans(u)]
        result = jnp.dot(w, jnp.concatenate(v, axis=0), preferred_element_type=jnp.float32)
        out_ref[u * block : (u + 1) * block] = result.astype(jnp.bfloat16)


def gather_kernel(*refs):
    out_ref = refs[-1]
    _, core, depth = where_am_i()
    block = out_ref.shape[0]
    mine = pl.ds(pl.multiple_of(core * block, block), block)
    for i, ref in enumerate(refs[:-1]):
        r, rel = i >> 1, i & 1
        at = pl.multiple_of((2 * (depth ^ r) + (core ^ rel)) * HD, HD)
        out_ref[:, pl.ds(at, HD)] = ref[mine, :]


def call(kernel, outs, places, scratch=(), macs=0):
    spaces = {"s": SMEM, "v": VMEM, "h": pltpu.HBM}
    return pl.pallas_call(
        kernel,
        out_shape=outs,
        in_specs=[pl.BlockSpec(memory_space=spaces[place]) for place in places],
        out_specs=jax.tree.map(lambda _: pl.BlockSpec(memory_space=VMEM), outs),
        scratch_shapes=list(scratch),
        cost_estimate=pl.CostEstimate(flops=2 * macs, bytes_accessed=0, transcendentals=0),
        compiler_params=pltpu.CompilerParams(vmem_limit_bytes=32 * 2**20),
    )


def plane_device(raw, stream, conv_w, gain, w_qkv, mask):
    time_len, site_len, feat_len = raw.shape
    block, width = time_len * site_len, stream.shape[2]
    half, size = width // 2, w_qkv.shape[0]
    bf16, f32 = jnp.bfloat16, jnp.float32

    def array(*shape, kind=bf16):
        return jax.ShapeDtypeStruct(shape, kind)

    to_x, to_y, to_across, kept = call(
        split_kernel,
        (array(size + EXTRA, PAIR), array(size + EXTRA, PAIR), array(EXTRA, PAIR), array(size, PAIR)),
        "shh",
        scratch=[VMEM(raw.shape, bf16), pltpu.SemaphoreType.DMA((4,))],
    )(mask.reshape(mask.shape[2]), w_qkv, raw)
    from_x, from_y, across = swap_depth(to_x, 1), swap_depth(to_y, 2), swap_depth(to_across, 3)
    operands = (after(raw, to_x), stream.reshape(block, width), conv_w.reshape(3 * feat_len, width))
    operands = call(
        load_kernel, tuple(array(*t.shape) for t in operands), "hhh", scratch=[pltpu.SemaphoreType.DMA((3,))]
    )(*operands)
    kept, *operands = lax.optimization_barrier((kept, *operands))
    keep, send, flags = call(
        sort_kernel, (array(size, 3 * HD), array(size + EXTRA, 3 * HD), array(EXTRA, HD)), "v" * 5
    )(kept, from_x, from_y, across, to_y)
    received = swap_core(send)
    other_flags = received[size:, :HD]
    shard = jnp.concatenate([keep, received[:size]], axis=0)
    far, near = swap_z(shard, 2), swap_z(shard, 1)

    normed = call(
        embed_kernel,
        array(block, width),
        "v" * 6,
        scratch=[VMEM((block, width), f32)],
        macs=block * 3 * feat_len * width,
    )(from_x, across, gain.reshape(1, width), *operands)
    normed = after(normed, received)
    beside, above = swap_depth(normed, 1), swap_depth(normed, 2)
    opposite = swap_core(normed)
    far, near, opposite, beside, above = lax.optimization_barrier((far, near, opposite, beside, above))
    early = (normed, beside, above, opposite, swap_core(beside), swap_core(above))
    last = swap_z(far, 1)
    diagonal = [swap_depth(early[1][:, :half], 2), swap_depth(early[2][:, half:], 1)]
    rows = 2 * size
    total = call(partial_kernel, array(6 * block, 3 * HD, kind=f32), "v" * 9, macs=6 * block * 3 * rows * 3 * HD)(
        *early, shard, far, near
    )
    last, total, *diagonal = lax.optimization_barrier((last, total, *diagonal))
    late = diagonal + [swap_core(t) for t in diagonal]
    one_head, half_head = array(4, 2 * block, HD), array(2, 2 * block, HD)
    q, k, *v = call(
        project_kernel,
        (one_head, one_head, half_head, half_head),
        "v" * 15,
        scratch=[VMEM((8 * block, 3 * HD), f32), VMEM((2 * block, width), bf16)],
        macs=14 * block * rows * 3 * HD,
    )(*early, *late, shard, far, near, last, total)

    weights = call(weigh_kernel, array(4, 2 * block, 5 * block), "v" * 6, macs=8 * block * 5 * block * HD)(
        q, swap_z(k, 1), k, swap_middle(k), flags, other_flags
    )
    values = [(swap_z(t, 1), t, swap_middle(t)) for t in v]
    pieces = {}
    for r in V_ORDER:
        mixed = call(functools.partial(mix_kernel, r), array(2 * block, HD), "vvvv", macs=2 * block * 5 * block * HD)(
            weights, *values[V_ORDER.index(r) // 2]
        )
        pieces[r] = swap_depth(mixed, r) if r else mixed
    both = [t for r in range(4) for t in (pieces[r], swap_core(pieces[r]))]
    context = call(gather_kernel, array(block, HEADS * HD), "v" * 8)(*both)
    return context.reshape(time_len, site_len, HEADS * HD)


def from_behind(value, axis, by):
    devices = lax.axis_size(axis)
    pairs = [(i, i + by) for i in range(devices) if 0 <= i + by < devices]
    return lax.ppermute(value, axis, pairs)


def head_attend(query_head, key_head, value_head, allowed):
    inv_root = 1.0 / math.sqrt(HD)
    scores = (
        jnp.einsum("qd,kd->qk", query_head, key_head, preferred_element_type=jnp.float32) * inv_root
    )
    scores = jnp.where(allowed, scores, -1e30)
    row_max = jnp.max(scores, axis=-1, keepdims=True)
    powers = jnp.exp(scores - row_max)
    weights = (powers / jnp.sum(powers, axis=-1, keepdims=True)).astype(jnp.bfloat16)
    return jnp.dot(weights, value_head, preferred_element_type=jnp.float32).astype(jnp.bfloat16)


def per_device(raw, stream, conv_w, gain, w_qkv, mask):
    time_len, site_len, _ = raw.shape
    tok_rows = time_len * site_len
    normed = normed_tokens(padded_2(raw, (("depth", 1),), 1), stream, conv_w, gain)
    columns = lax.all_gather(w_qkv, "depth", axis=1, tiled=True)
    projected = jnp.dot(
        normed,
        lax.all_gather(columns, "tm", axis=0, tiled=True),
        preferred_element_type=jnp.float32,
    ).astype(jnp.bfloat16)
    head_cols = projected.shape[1] // 3
    queries = projected[:, :head_cols]
    keyvals = projected[:, head_cols:]
    earlier = []
    later = []
    moving_back = keyvals
    moving_ahead = keyvals
    for hop_index in range(RD):
        moving_back = from_behind(moving_back, "tm", 1)
        moving_ahead = from_behind(moving_ahead, "tm", -1)
        earlier.insert(0, moving_back)
        later.append(moving_ahead)
    gathered = jnp.concatenate(earlier + [keyvals] + later, axis=0)
    block_rows = BT * PP
    own_blocks = tok_rows // block_rows
    span_blocks = gathered.shape[0] // block_rows
    local_mask = mask[0]
    query_ids = jnp.arange(own_blocks, dtype=jnp.int32)[:, None]
    key_ids = jnp.arange(span_blocks, dtype=jnp.int32)[None, :]
    entry_ids = key_ids - query_ids
    picks = entry_ids[:, :, None] == jnp.arange(local_mask.shape[1], dtype=jnp.int32)[None, None, :]
    block_allowed = jnp.sum(jnp.where(picks, local_mask[:, None, :], 0), axis=-1) > 0
    allowed = jnp.repeat(jnp.repeat(block_allowed, block_rows, axis=0), block_rows, axis=1)
    query_heads = queries.reshape(tok_rows, HEADS, HD).transpose(1, 0, 2)
    key_heads = gathered[:, :head_cols].reshape(gathered.shape[0], HEADS, HD).transpose(1, 0, 2)
    value_heads = gathered[:, head_cols:].reshape(gathered.shape[0], HEADS, HD).transpose(1, 0, 2)
    context = lax.map(
        lambda operands: head_attend(operands[0], operands[1], operands[2], allowed),
        (query_heads, key_heads, value_heads),
    )
    return context.transpose(1, 0, 2).reshape(time_len, site_len, head_cols)


def solution(mesh):
    in_specs = (
        P("tm", "depth", None),
        P("tm", "depth", None),
        P(),
        P(),
        P("tm", "depth"),
        P("depth", "tm", None),
    )
    out_specs = P("tm", "depth", None)
    fits = mesh.shape["depth"] == 4 and mesh.shape["tm"] == 8
    return jax.shard_map(
        plane_device if fits else per_device, mesh=mesh, in_specs=in_specs, out_specs=out_specs, check_vma=False
    )
```

```python
import functools
import math

import jax
import jax.numpy as jnp
from jax import lax
from jax.experimental import pallas as pl
from jax.experimental.pallas import tpu as pltpu
from jax.sharding import PartitionSpec as P

HEADS = 8
HD = 128
BT = 16
PP = 8
RD = 2
VMEM = pltpu.VMEM
SMEM = pltpu.SMEM


def padded_2(value, sides, width):
    for axis, dim in sides:
        devices, length = (lax.axis_size(axis), value.shape[dim])
        up = [(i, (i + 1) % devices) for i in range(devices - 1)]
        down = [(j, i) for i, j in up]
        last = lax.slice_in_dim(value, length - width, length, axis=dim)
        leading = lax.slice_in_dim(value, 0, width, axis=dim)
        before = lax.ppermute(last, axis, up)
        after = lax.ppermute(leading, axis, down)
        value = jnp.concatenate([before, value, after], axis=dim)
    return value


def normed_tokens(padded, stream, conv_w, gain):
    time_len, site_len, width = stream.shape
    tok_rows = time_len * site_len
    embedded = stream.reshape(tok_rows, width).astype(jnp.float32)
    for offset in range(3):
        window = padded[:, offset : offset + site_len].reshape(tok_rows, padded.shape[2])
        embedded = embedded + jnp.dot(window, conv_w[offset], preferred_element_type=jnp.float32)
    scale = lax.rsqrt(jnp.mean(embedded * embedded, axis=-1, keepdims=True) + 1e-05)
    return (embedded * scale * gain).astype(jnp.bfloat16)


PAIR = 2 * HD
V_ORDER = (3, 1, 2, 0)
EXTRA = 16


def hop(value, fn):
    pairs = []
    for z in range(4):
        for core in range(2):
            for depth in range(4):
                to = fn(z, core, depth)
                if to is not None:
                    pairs.append(((2 * z + core) * 4 + depth, (2 * to[0] + to[1]) * 4 + to[2]))
    return lax.ppermute(value, ("tm", "depth"), pairs)


def swap_core(value):
    return hop(value, lambda z, c, d: (z, 1 - c, d))


def swap_depth(value, bits):
    return hop(value, lambda z, c, d: (z, c, d ^ bits))


def swap_z(value, bits):
    return hop(value, lambda z, c, d: (z ^ bits, c, d))


def swap_middle(value):
    return hop(value, lambda z, c, d: (z ^ 3, c, d) if z in (1, 2) else None)


def after(value, *others):
    return lax.optimization_barrier((value, *others))[0]


def where_am_i():
    tm = lax.axis_index("tm")
    return tm >> 1, tm & 1, lax.axis_index("depth")


def edge_kernel(mask, raw, to_x, to_across, flags_ref):
    _, _, depth = where_am_i()
    odd = depth & 1
    lane = lax.broadcasted_iota(jnp.int32, (EXTRA, HD), 1)
    flags = jnp.zeros((EXTRA, HD), jnp.int32)
    for entry in range(mask.shape[0]):
        flags = jnp.where(lane == entry, mask[entry], flags)
    flags = flags.astype(jnp.float32).astype(jnp.bfloat16)
    flags_ref[...] = flags
    values = raw[...].astype(jnp.float32)
    first, last = values[:, 0], values[:, values.shape[1] - 1]
    for ref, use_last in ((to_x, odd == 0), (to_across, depth == 1)):
        ref[:EXTRA] = jnp.where(use_last, last, first).astype(jnp.bfloat16)
        ref[EXTRA:] = flags


def split_kernel(w, to_x, to_y, keep):
    _, _, depth = where_am_i()
    even = (depth & 1) == 0
    low, high = w[:, :PAIR], w[:, 2 * PAIR :]
    to_x[...] = w[:, PAIR : 2 * PAIR]
    to_y[: w.shape[0]] = jnp.where(even, high, low)
    keep[...] = jnp.where(even, low, high)


def split_far_kernel(w, flags, to_x, to_y, keep):
    split_kernel(w, to_x, to_y, keep)
    to_y[w.shape[0] :, :HD] = flags[...]
    to_y[w.shape[0] :, HD:] = flags[...]


def sorted_groups(kept, from_x, from_y):
    _, core, depth = where_am_i()
    first, even = core == 0, (depth & 1) == 0
    size = kept.shape[0]
    low = jnp.where(even, kept[...], from_y[:size])
    high = jnp.where(even, from_y[:size], kept[...])
    groups = (low, from_x[:size], high)
    turn = jnp.where(depth == 3, 0, depth)
    for third in range(3):
        group = jnp.where(turn == 0, groups[third], jnp.where(turn == 1, groups[(third + 1) % 3], groups[(third + 2) % 3]))
        yield third, jnp.where(first, group[:, :HD], group[:, HD:]), jnp.where(first, group[:, HD:], group[:, :HD])


def sort_kernel(kept, from_x, from_y, out_ref):
    for third, mine, other in sorted_groups(kept, from_x, from_y):
        out_ref[:, third * HD : (third + 1) * HD] = mine
        out_ref[:, (3 + third) * HD : (4 + third) * HD] = other


def sort_far_kernel(kept, from_x, from_y, edge_x, edge_across, own_flags, q_ref, kv_ref, send_ref, flags_ref):
    for third, mine, other in sorted_groups(kept, from_x, from_y):
        send_ref[:, third * HD : (third + 1) * HD] = other
        if third:
            kv_ref[:, (third - 1) * HD : third * HD] = mine
        else:
            q_ref[...] = mine
    row = lax.broadcasted_iota(jnp.int32, (EXTRA, HD), 0)
    flags = own_flags[...].astype(jnp.float32)
    for r, value in ((1, edge_x[EXTRA:]), (2, from_y[kept.shape[0] :, :HD]), (3, edge_across[EXTRA:])):
        flags = jnp.where(row == r, value.astype(jnp.float32), flags)
    flags = flags.astype(jnp.bfloat16)
    for k in range(3):
        flags_ref[:, k * HD : (k + 1) * HD] = flags


def embed_kernel(edge_x, edge_across, gain, raw, stream, conv_w, out_ref, acc):
    time_len, site_len, feat_len = raw.shape
    _, _, depth = where_am_i()
    even = (depth & 1) == 0
    rows, width = stream.shape
    side, far = edge_x[:time_len].astype(jnp.float32), edge_across[:time_len].astype(jnp.float32)
    before = jnp.where(even, jnp.where(depth == 2, far, 0.0), side)
    behind = jnp.where(even, side, jnp.where(depth == 1, far, 0.0))
    padded = jnp.concatenate([before[:, None], raw[...].astype(jnp.float32), behind[:, None]], axis=1)
    windows = [padded[:, j : j + site_len].reshape(rows, feat_len).astype(jnp.bfloat16) for j in range(3)]
    windows = jnp.concatenate(windows, axis=1)
    total, step = jnp.zeros((rows, 1), jnp.float32), width // 4
    for at in range(0, width, step):
        here = slice(at, at + step)
        part = jnp.dot(windows, conv_w[:, here], preferred_element_type=jnp.float32)
        part += stream[:, here].astype(jnp.float32)
        acc[:, here] = part
        total += jnp.sum(part * part, axis=1, keepdims=True)
    scale = lax.rsqrt(total / width + 1e-05)
    out_ref[...] = (acc[...] * scale * gain[...]).astype(jnp.bfloat16)


def take(refs, source, core, rows):
    half = rows // 2
    cuts = [pl.ds(pl.multiple_of(source * rows + c * half, half), half) for c in (core, 1 - core)]
    return jnp.concatenate([jnp.concatenate([ref[:, at] for at in cuts], axis=1) for ref in refs], axis=0)


def three_shards(x_refs, own, near, received, far_q, far_kv):
    z, core, _ = where_am_i()
    size, width = own.shape[0], 3 * HD
    w = [own[:, :width], received[:size], jnp.concatenate([far_q[...], far_kv[...]], axis=1)]
    w = jnp.concatenate(w + [near[:, :width], received[size : 2 * size]], axis=0)
    x = [take(x_refs, source, core, 2 * size) for source in (z, z ^ 2, z ^ 1)]
    return jnp.dot(jnp.concatenate(x, axis=1), w, preferred_element_type=jnp.float32)


def partial_kernel(*refs):
    refs[-1][...] = three_shards(refs[:6], *refs[6:-1])


def diagonal_kernel(*refs):
    pieces, weights, (acc_ref, x_ref) = refs[:6], refs[6:-2], refs[-2:]
    block, half = pieces[0].shape
    corners = ((0, 0), (0, half), (block, 0), (block + block // 2, 0), (block, half), (block + block // 2, half))
    for (row, at), ref in zip(corners, pieces):
        x_ref[row : row + ref.shape[0], at : at + half] = ref[...]
    acc_ref[...] = three_shards([x_ref], *weights)


ROW_ORDER = ((0, 1, 2, 6), (3, 4, 5, 7))


def finish(x_refs, last, acc_in, acc_diagonal, columns):
    z, core, _ = where_am_i()
    value = jnp.dot(take(x_refs, z ^ 3, core, last.shape[0]), last[...], preferred_element_type=jnp.float32)
    early = acc_in.shape[0]
    return (
        (acc_in[:, columns] + value[:early]).astype(jnp.bfloat16),
        (acc_diagonal[:, columns] + value[early:]).astype(jnp.bfloat16),
    )


def finish_kernel(columns, *refs):
    x_refs, (last, acc_in, acc_diagonal), out_refs = refs[:7], refs[7:10], refs[10:]
    _, core, _ = where_am_i()
    block = x_refs[0].shape[0]
    values = jnp.concatenate(finish(x_refs, last, acc_in, acc_diagonal, columns), axis=0)
    for rel in range(2):
        at = pl.ds(pl.multiple_of((core ^ rel) * block, block), block)
        for r in range(4):
            row = ROW_ORDER[rel][r]
            value = values[row * block : (row + 1) * block]
            out_refs[0][r, at, :] = value[:, :HD]
            if len(out_refs) > 1:
                v_at = V_ORDER.index(r)
                out_refs[1 + v_at // 2][v_at % 2, at, :] = value[:, HD:]


def spans(u):
    return ((0, u, 2), (1, 0, 2), (2, 0, 1 + u))


def neighbours(outer, own, middle, index):
    z, _, _ = where_am_i()
    odd = (z & 1) == 1
    outer, middle = outer[index], middle[index]
    return jnp.where(odd, outer, middle), own[index], jnp.where(odd, middle, outer)


def weigh_kernel(q_ref, outer, own, middle, own_flags, received, out_ref):
    _, core, _ = where_am_i()
    block = q_ref.shape[1] // 2
    inv_root = 1.0 / math.sqrt(HD)
    flags = [own_flags[:, :HD].astype(jnp.float32), received[-EXTRA:, :HD].astype(jnp.float32)]
    flags = [jnp.where(core == u, flags[0], flags[1]) for u in range(2)]
    bias = [(f - 1.0) * 1e30 for f in flags]
    for r in range(4):
        keys = neighbours(outer, own, middle, r)
        for u in range(2):
            q = q_ref[r, u * block : (u + 1) * block]
            scores = []
            for side, first, last in spans(u):
                k = keys[side][first * block : last * block]
                s = lax.dot_general(q, k, (((1,), (1,)), ((), ())), preferred_element_type=jnp.float32)
                for v in range(last - first):
                    entry = len(scores)
                    shut = jnp.broadcast_to(bias[u][r : r + 1, entry : entry + 1], (block, block))
                    scores.append(s[:, v * block : (v + 1) * block] * inv_root + shut)
            top = jnp.max(functools.reduce(jnp.maximum, scores), axis=1, keepdims=True)
            powers = [jnp.exp(s - top) for s in scores]
            inverse = 1.0 / jnp.sum(functools.reduce(jnp.add, powers), axis=1, keepdims=True)
            for entry, p in enumerate(powers):
                here = slice(entry * block, (entry + 1) * block)
                out_ref[r, u * block : (u + 1) * block, here] = (p * inverse).astype(jnp.bfloat16)


def mix_kernel(r, weights, outer, own, middle, out_ref):
    block = weights.shape[1] // 2
    values = neighbours(outer, own, middle, V_ORDER.index(r) % 2)
    for u in range(2):
        w = weights[r, u * block : (u + 1) * block]
        v = [values[side][first * block : last * block] for side, first, last in spans(u)]
        result = jnp.dot(w, jnp.concatenate(v, axis=0), preferred_element_type=jnp.float32)
        out_ref[u * block : (u + 1) * block] = result.astype(jnp.bfloat16)


def gather_kernel(*refs):
    out_ref = refs[-1]
    _, core, depth = where_am_i()
    block = out_ref.shape[0]
    mine = pl.ds(pl.multiple_of(core * block, block), block)
    for i, ref in enumerate(refs[:-1]):
        r, rel = i >> 1, i & 1
        at = pl.multiple_of((2 * (depth ^ r) + (core ^ rel)) * HD, HD)
        out_ref[:, pl.ds(at, HD)] = ref[mine, :]


def call(kernel, outs, places, scratch=(), macs=0):
    spaces = {"s": SMEM, "v": VMEM}
    return pl.pallas_call(
        kernel,
        out_shape=outs,
        in_specs=[pl.BlockSpec(memory_space=spaces[place]) for place in places],
        out_specs=jax.tree.map(lambda _: pl.BlockSpec(memory_space=VMEM), outs),
        scratch_shapes=list(scratch),
        cost_estimate=pl.CostEstimate(flops=2 * macs, bytes_accessed=0, transcendentals=0),
        compiler_params=pltpu.CompilerParams(vmem_limit_bytes=32 * 2**20),
    )


def plane_device(raw, stream, conv_w, gain, w_qkv, mask):
    time_len, site_len, feat_len = raw.shape
    block, width = time_len * site_len, stream.shape[2]
    half, size = width // 2, w_qkv.shape[0]
    bf16, f32 = jnp.bfloat16, jnp.float32

    def array(*shape, kind=bf16):
        return jax.ShapeDtypeStruct(shape, kind)

    far_raw = swap_z(w_qkv, 2)

    cut, cut_more = array(size, PAIR), array(size + EXTRA, PAIR)
    to_x, to_y, kept = call(split_kernel, (cut,) * 3, "v")(w_qkv)
    own = call(sort_kernel, array(size, 6 * HD), "vvv")(kept, swap_depth(to_x, 1), swap_depth(to_y, 2))
    near = swap_z(own, 1)

    edge_x, edge_across, own_flags = call(
        edge_kernel, (array(2 * EXTRA, HD), array(2 * EXTRA, HD), array(EXTRA, HD)), "sv"
    )(mask.reshape(mask.shape[2]), raw)
    edge_x, edge_across = swap_depth(edge_x, 1), swap_depth(edge_across, 3)
    normed = call(
        embed_kernel,
        array(block, width),
        "v" * 6,
        scratch=[VMEM((block, width), f32)],
        macs=block * 3 * feat_len * width,
    )(
        edge_x,
        edge_across,
        gain.reshape(1, width),
        raw,
        stream.reshape(block, width),
        conv_w.reshape(3 * feat_len, width),
    )
    beside, above = swap_depth(normed, 1), swap_depth(normed, 2)

    to_x, to_y, kept = call(split_far_kernel, (cut, cut_more, cut), "vv")(far_raw, own_flags)
    from_x, from_y = swap_depth(to_x, 1), swap_depth(to_y, 2)
    from_x, from_y, near, beside, above = lax.optimization_barrier((from_x, from_y, near, beside, above))
    keep_q, keep_kv, send, flags = call(
        sort_far_kernel,
        (array(size, HD), array(size, PAIR), array(size, 3 * HD), array(EXTRA, 3 * HD)),
        "v" * 6,
    )(kept, from_x, from_y, edge_x, edge_across, own_flags)
    received = swap_core(send)
    far_q = jnp.concatenate([keep_q, received[:, :HD]], axis=0)
    far_kv = jnp.concatenate([keep_kv, received[:, HD:]], axis=0)
    last_kv = swap_z(far_kv, 1)
    last_q = swap_z(far_q, 1)
    received = swap_core(jnp.concatenate([own[:, 3 * HD :], near[:, 3 * HD :], flags], axis=0))
    weights = (own, near, received, far_q, far_kv)
    opposite = swap_core(after(normed, near))

    diagonal = [swap_depth(beside[:, :half], 2), swap_depth(above[:, half:], 1)]
    early = (normed, beside, above, opposite, swap_core(beside), swap_core(above))
    rows = 2 * size
    total = call(partial_kernel, array(6 * block, 3 * HD, kind=f32), "v" * 11, macs=6 * block * 3 * rows * 3 * HD)(
        *early, *weights
    )
    diagonal = [after(t, total) for t in diagonal]
    diagonal += [swap_core(t[i * block // 2 : (i + 1) * block // 2]) for t in diagonal for i in range(2)]
    total_diagonal, diagonal = call(
        diagonal_kernel,
        (array(2 * block, 3 * HD, kind=f32), array(2 * block, width)),
        "v" * 11,
        macs=2 * block * 3 * rows * 3 * HD,
    )(*diagonal, *weights)
    one_head, half_head = array(4, 2 * block, HD), array(2, 2 * block, HD)
    k, *v = call(
        functools.partial(finish_kernel, slice(HD, 3 * HD)),
        (one_head, half_head, half_head),
        "v" * 10,
        macs=8 * block * rows * 2 * HD,
    )(*early, diagonal, last_kv, total, total_diagonal)
    (q,) = call(functools.partial(finish_kernel, slice(0, HD)), (one_head,), "v" * 10, macs=8 * block * rows * HD)(
        *early, diagonal, last_q, total, total_diagonal
    )

    weights = call(weigh_kernel, array(4, 2 * block, 5 * block), "v" * 6, macs=8 * block * 5 * block * HD)(
        q, swap_z(k, 1), k, swap_middle(k), flags, received
    )
    values = [(swap_z(t, 1), t, swap_middle(t)) for t in v]
    pieces = {}
    for r in V_ORDER:
        mixed = call(functools.partial(mix_kernel, r), array(2 * block, HD), "vvvv", macs=2 * block * 5 * block * HD)(
            weights, *values[V_ORDER.index(r) // 2]
        )
        pieces[r] = swap_depth(mixed, r) if r else mixed
    both = [t for r in range(4) for t in (pieces[r], swap_core(pieces[r]))]
    context = call(gather_kernel, array(block, HEADS * HD), "v" * 8)(*both)
    return context.reshape(time_len, site_len, HEADS * HD)


def from_behind(value, axis, by):
    devices = lax.axis_size(axis)
    pairs = [(i, i + by) for i in range(devices) if 0 <= i + by < devices]
    return lax.ppermute(value, axis, pairs)


def head_attend(query_head, key_head, value_head, allowed):
    inv_root = 1.0 / math.sqrt(HD)
    scores = (
        jnp.einsum("qd,kd->qk", query_head, key_head, preferred_element_type=jnp.float32) * inv_root
    )
    scores = jnp.where(allowed, scores, -1e30)
    row_max = jnp.max(scores, axis=-1, keepdims=True)
    powers = jnp.exp(scores - row_max)
    weights = (powers / jnp.sum(powers, axis=-1, keepdims=True)).astype(jnp.bfloat16)
    return jnp.dot(weights, value_head, preferred_element_type=jnp.float32).astype(jnp.bfloat16)


def per_device(raw, stream, conv_w, gain, w_qkv, mask):
    time_len, site_len, _ = raw.shape
    tok_rows = time_len * site_len
    normed = normed_tokens(padded_2(raw, (("depth", 1),), 1), stream, conv_w, gain)
    columns = lax.all_gather(w_qkv, "depth", axis=1, tiled=True)
    projected = jnp.dot(
        normed,
        lax.all_gather(columns, "tm", axis=0, tiled=True),
        preferred_element_type=jnp.float32,
    ).astype(jnp.bfloat16)
    head_cols = projected.shape[1] // 3
    queries = projected[:, :head_cols]
    keyvals = projected[:, head_cols:]
    earlier = []
    later = []
    moving_back = keyvals
    moving_ahead = keyvals
    for hop_index in range(RD):
        moving_back = from_behind(moving_back, "tm", 1)
        moving_ahead = from_behind(moving_ahead, "tm", -1)
        earlier.insert(0, moving_back)
        later.append(moving_ahead)
    gathered = jnp.concatenate(earlier + [keyvals] + later, axis=0)
    block_rows = BT * PP
    own_blocks = tok_rows // block_rows
    span_blocks = gathered.shape[0] // block_rows
    local_mask = mask[0]
    query_ids = jnp.arange(own_blocks, dtype=jnp.int32)[:, None]
    key_ids = jnp.arange(span_blocks, dtype=jnp.int32)[None, :]
    entry_ids = key_ids - query_ids
    picks = entry_ids[:, :, None] == jnp.arange(local_mask.shape[1], dtype=jnp.int32)[None, None, :]
    block_allowed = jnp.sum(jnp.where(picks, local_mask[:, None, :], 0), axis=-1) > 0
    allowed = jnp.repeat(jnp.repeat(block_allowed, block_rows, axis=0), block_rows, axis=1)
    query_heads = queries.reshape(tok_rows, HEADS, HD).transpose(1, 0, 2)
    key_heads = gathered[:, :head_cols].reshape(gathered.shape[0], HEADS, HD).transpose(1, 0, 2)
    value_heads = gathered[:, head_cols:].reshape(gathered.shape[0], HEADS, HD).transpose(1, 0, 2)
    context = lax.map(
        lambda operands: head_attend(operands[0], operands[1], operands[2], allowed),
        (query_heads, key_heads, value_heads),
    )
    return context.transpose(1, 0, 2).reshape(time_len, site_len, head_cols)


def solution(mesh):
    in_specs = (
        P("tm", "depth", None),
        P("tm", "depth", None),
        P(),
        P(),
        P("tm", "depth"),
        P("depth", "tm", None),
    )
    out_specs = P("tm", "depth", None)
    fits = mesh.shape["depth"] == 4 and mesh.shape["tm"] == 8
    return jax.shard_map(
        plane_device if fits else per_device, mesh=mesh, in_specs=in_specs, out_specs=out_specs, check_vma=False
    )
```

```python
import functools
import math

import jax
import jax.numpy as jnp
from jax import lax
from jax.experimental import pallas as pl
from jax.experimental.pallas import tpu as pltpu
from jax.sharding import PartitionSpec as P

HEADS = 8
HD = 128
BT = 16
PP = 8
RD = 2
VMEM = pltpu.VMEM
SMEM = pltpu.SMEM


def padded_2(value, sides, width):
    for axis, dim in sides:
        devices, length = (lax.axis_size(axis), value.shape[dim])
        up = [(i, (i + 1) % devices) for i in range(devices - 1)]
        down = [(j, i) for i, j in up]
        last = lax.slice_in_dim(value, length - width, length, axis=dim)
        leading = lax.slice_in_dim(value, 0, width, axis=dim)
        before = lax.ppermute(last, axis, up)
        after = lax.ppermute(leading, axis, down)
        value = jnp.concatenate([before, value, after], axis=dim)
    return value


def normed_tokens(padded, stream, conv_w, gain):
    time_len, site_len, width = stream.shape
    tok_rows = time_len * site_len
    embedded = stream.reshape(tok_rows, width).astype(jnp.float32)
    for offset in range(3):
        window = padded[:, offset : offset + site_len].reshape(tok_rows, padded.shape[2])
        embedded = embedded + jnp.dot(window, conv_w[offset], preferred_element_type=jnp.float32)
    scale = lax.rsqrt(jnp.mean(embedded * embedded, axis=-1, keepdims=True) + 1e-05)
    return (embedded * scale * gain).astype(jnp.bfloat16)


PAIR = 2 * HD
V_ORDER = (3, 1, 2, 0)
EXTRA = 16


def hop(value, fn):
    pairs = []
    for z in range(4):
        for core in range(2):
            for depth in range(4):
                to = fn(z, core, depth)
                if to is not None:
                    pairs.append(((2 * z + core) * 4 + depth, (2 * to[0] + to[1]) * 4 + to[2]))
    return lax.ppermute(value, ("tm", "depth"), pairs)


def swap_core(value):
    return hop(value, lambda z, c, d: (z, 1 - c, d))


def swap_depth(value, bits):
    return hop(value, lambda z, c, d: (z, c, d ^ bits))


def swap_z(value, bits):
    return hop(value, lambda z, c, d: (z ^ bits, c, d))


def swap_middle(value):
    return hop(value, lambda z, c, d: (z ^ 3, c, d) if z in (1, 2) else None)


def after(value, *others):
    return lax.optimization_barrier((value, *others))[0]


def where_am_i():
    tm = lax.axis_index("tm")
    return tm >> 1, tm & 1, lax.axis_index("depth")


def edge_kernel(mask, raw, to_x, to_across, flags_ref, sites_ref):
    _, _, depth = where_am_i()
    odd = depth & 1
    lane = lax.broadcasted_iota(jnp.int32, (EXTRA, HD), 1)
    flags = jnp.zeros((EXTRA, HD), jnp.int32)
    for entry in range(mask.shape[0]):
        flags = jnp.where(lane == entry, mask[entry], flags)
    flags = flags.astype(jnp.float32).astype(jnp.bfloat16)
    flags_ref[...] = flags
    sites_ref[...] = raw[...]
    values = raw[...].astype(jnp.float32)
    first, last = values[:, 0], values[:, values.shape[1] - 1]
    for ref, use_last in ((to_x, odd == 0), (to_across, depth == 1)):
        ref[:EXTRA] = jnp.where(use_last, last, first).astype(jnp.bfloat16)
        ref[EXTRA:] = flags


def split_kernel(w, to_x, to_y, keep):
    _, _, depth = where_am_i()
    even = (depth & 1) == 0
    low, high = w[:, :PAIR], w[:, 2 * PAIR :]
    to_x[...] = w[:, PAIR : 2 * PAIR]
    to_y[: w.shape[0]] = jnp.where(even, high, low)
    keep[...] = jnp.where(even, low, high)


def split_far_kernel(w, flags, to_y, keep):
    _, _, depth = where_am_i()
    even = (depth & 1) == 0
    low, high = w[:, :PAIR], w[:, 2 * PAIR :]
    to_y[: w.shape[0]] = jnp.where(even, high, low)
    keep[...] = jnp.where(even, low, high)
    to_y[w.shape[0] :, :HD] = flags[...]
    to_y[w.shape[0] :, HD:] = flags[...]


def sorted_groups(kept, from_x, from_y):
    _, core, depth = where_am_i()
    first, even = core == 0, (depth & 1) == 0
    size = kept.shape[0]
    low = jnp.where(even, kept[...], from_y[:size])
    high = jnp.where(even, from_y[:size], kept[...])
    groups = (low, from_x[:size], high)
    turn = jnp.where(depth == 3, 0, depth)
    for third in range(3):
        group = jnp.where(turn == 0, groups[third], jnp.where(turn == 1, groups[(third + 1) % 3], groups[(third + 2) % 3]))
        yield third, jnp.where(first, group[:, :HD], group[:, HD:]), jnp.where(first, group[:, HD:], group[:, :HD])


def sort_kernel(kept, from_x, from_y, out_ref):
    for third, mine, other in sorted_groups(kept, from_x, from_y):
        out_ref[:, third * HD : (third + 1) * HD] = mine
        out_ref[:, (3 + third) * HD : (4 + third) * HD] = other


def sort_far_kernel(kept, from_x, from_y, edge_x, edge_across, own_flags, keep_ref, send_ref, flags_ref):
    for third, mine, other in sorted_groups(kept, from_x, from_y):
        send_ref[:, third * HD : (third + 1) * HD] = other
        keep_ref[:, third * HD : (third + 1) * HD] = mine
    row = lax.broadcasted_iota(jnp.int32, (EXTRA, HD), 0)
    flags = own_flags[...].astype(jnp.float32)
    for r, value in ((1, edge_x[EXTRA:]), (2, from_y[kept.shape[0] :, :HD]), (3, edge_across[EXTRA:])):
        flags = jnp.where(row == r, value.astype(jnp.float32), flags)
    flags = flags.astype(jnp.bfloat16)
    for k in range(3):
        flags_ref[:, k * HD : (k + 1) * HD] = flags


def embed_kernel(edge_x, edge_across, raw, gain, stream, conv_w, out_ref, acc, tokens, weights, sems):
    time_len, site_len, feat_len = raw.shape
    _, _, depth = where_am_i()
    even = (depth & 1) == 0
    rows, width = stream.shape
    parts = weights.shape[0]
    step = width // parts
    copies = []
    for i in range(parts):
        here = pl.ds(i * step, step)
        copies.append(pltpu.make_async_copy(conv_w.at[:, here], weights.at[i], sems.at[2 * i]))
        copies.append(pltpu.make_async_copy(stream.at[:, here], tokens.at[i], sems.at[2 * i + 1]))
    for copy in copies:
        copy.start()
    side, far = edge_x[:time_len].astype(jnp.float32), edge_across[:time_len].astype(jnp.float32)
    before = jnp.where(even, jnp.where(depth == 2, far, 0.0), side)
    behind = jnp.where(even, side, jnp.where(depth == 1, far, 0.0))
    padded = jnp.concatenate([before[:, None], raw[...].astype(jnp.float32), behind[:, None]], axis=1)
    windows = [padded[:, j : j + site_len].reshape(rows, feat_len).astype(jnp.bfloat16) for j in range(3)]
    windows = jnp.concatenate(windows, axis=1)
    total = jnp.zeros((rows, 1), jnp.float32)
    for i in range(parts):
        copies[2 * i].wait()
        copies[2 * i + 1].wait()
        part = jnp.dot(windows, weights[i], preferred_element_type=jnp.float32) + tokens[i].astype(jnp.float32)
        acc[:, i * step : (i + 1) * step] = part
        total += jnp.sum(part * part, axis=1, keepdims=True)
    scale = lax.rsqrt(total / width + 1e-05)
    out_ref[...] = (acc[...] * scale * gain[...]).astype(jnp.bfloat16)


def take(refs, source, core, rows):
    half = rows // 2
    cuts = [pl.ds(pl.multiple_of(source * rows + c * half, half), half) for c in (core, 1 - core)]
    return jnp.concatenate([jnp.concatenate([ref[:, at] for at in cuts], axis=1) for ref in refs], axis=0)


def three_shards(x_refs, own, near, received, far):
    z, core, _ = where_am_i()
    size, width = own.shape[0], 3 * HD
    w = [own[:, :width], received[:size], far[...]]
    w = jnp.concatenate(w + [near[:, :width], received[size : 2 * size]], axis=0)
    x = [take(x_refs, source, core, 2 * size) for source in (z, z ^ 2, z ^ 1)]
    return jnp.dot(jnp.concatenate(x, axis=1), w, preferred_element_type=jnp.float32)


def partial_kernel(*refs):
    refs[-1][...] = three_shards(refs[:2], *refs[2:-1])


def diagonal_kernel(*refs):
    pieces, weights, (acc_ref, x_ref) = refs[:6], refs[6:-2], refs[-2:]
    block, half = pieces[0].shape
    corners = ((0, 0), (0, half), (block, 0), (block + block // 2, 0), (block, half), (block + block // 2, half))
    for (row, at), ref in zip(corners, pieces):
        x_ref[row : row + ref.shape[0], at : at + half] = ref[...]
    acc_ref[...] = three_shards([x_ref], *weights)


ROW_ORDER = ((0, 1, 2, 6), (3, 4, 5, 7))


def finish_kernel(*refs):
    x_refs, (last, acc_in, acc_diagonal, q_ref, k_ref, v_first, v_second) = refs[:3], refs[3:]
    z, core, _ = where_am_i()
    block, early = q_ref.shape[1] // 2, acc_in.shape[0]
    value = jnp.dot(take(x_refs, z ^ 3, core, last.shape[0]), last[...], preferred_element_type=jnp.float32)
    value = [acc_in[...] + value[:early], acc_diagonal[...] + value[early:]]
    value = jnp.concatenate(value, axis=0).astype(jnp.bfloat16)
    for rel in range(2):
        at = pl.ds(pl.multiple_of((core ^ rel) * block, block), block)
        for r in range(4):
            row = ROW_ORDER[rel][r]
            mine = value[row * block : (row + 1) * block]
            v_at = V_ORDER.index(r)
            q_ref[r, at, :] = mine[:, :HD]
            k_ref[r, at, :] = mine[:, HD:PAIR]
            (v_first, v_second)[v_at // 2][v_at % 2, at, :] = mine[:, PAIR:]


def spans(u):
    return ((0, u, 2), (1, 0, 2), (2, 0, 1 + u))


def neighbours(outer, own, middle, index):
    z, _, _ = where_am_i()
    odd = (z & 1) == 1
    outer, middle = outer[index], middle[index]
    return jnp.where(odd, outer, middle), own[index], jnp.where(odd, middle, outer)


def weigh_kernel(q_ref, outer, own, middle, own_flags, received, out_ref):
    _, core, _ = where_am_i()
    block = q_ref.shape[1] // 2
    inv_root = 1.0 / math.sqrt(HD)
    flags = [own_flags[:, :HD].astype(jnp.float32), received[-EXTRA:, :HD].astype(jnp.float32)]
    flags = [jnp.where(core == u, flags[0], flags[1]) for u in range(2)]
    bias = [(f - 1.0) * 1e30 for f in flags]
    for r in range(4):
        keys = neighbours(outer, own, middle, r)
        for u in range(2):
            q = q_ref[r, u * block : (u + 1) * block]
            scores = []
            for side, first, last in spans(u):
                k = keys[side][first * block : last * block]
                s = lax.dot_general(q, k, (((1,), (1,)), ((), ())), preferred_element_type=jnp.float32)
                for v in range(last - first):
                    entry = len(scores)
                    shut = jnp.broadcast_to(bias[u][r : r + 1, entry : entry + 1], (block, block))
                    scores.append(s[:, v * block : (v + 1) * block] * inv_root + shut)
            top = jnp.max(functools.reduce(jnp.maximum, scores), axis=1, keepdims=True)
            powers = [jnp.exp(s - top) for s in scores]
            inverse = 1.0 / jnp.sum(functools.reduce(jnp.add, powers), axis=1, keepdims=True)
            for entry, p in enumerate(powers):
                here = slice(entry * block, (entry + 1) * block)
                out_ref[r, u * block : (u + 1) * block, here] = (p * inverse).astype(jnp.bfloat16)


def mix_kernel(r, weights, outer, own, middle, out_ref):
    block = weights.shape[1] // 2
    values = neighbours(outer, own, middle, V_ORDER.index(r) % 2)
    for u in range(2):
        w = weights[r, u * block : (u + 1) * block]
        v = [values[side][first * block : last * block] for side, first, last in spans(u)]
        result = jnp.dot(w, jnp.concatenate(v, axis=0), preferred_element_type=jnp.float32)
        out_ref[u * block : (u + 1) * block] = result.astype(jnp.bfloat16)


def gather_kernel(*refs):
    out_ref = refs[-1]
    _, core, depth = where_am_i()
    block = out_ref.shape[0]
    mine = pl.ds(pl.multiple_of(core * block, block), block)
    for i, ref in enumerate(refs[:-1]):
        r, rel = i >> 1, i & 1
        at = pl.multiple_of((2 * (depth ^ r) + (core ^ rel)) * HD, HD)
        out_ref[:, pl.ds(at, HD)] = ref[mine, :]


def call(kernel, outs, places, scratch=(), macs=0, limit=32):
    spaces = {"s": SMEM, "v": VMEM, "a": pl.ANY}
    return pl.pallas_call(
        kernel,
        out_shape=outs,
        in_specs=[pl.BlockSpec(memory_space=spaces[place]) for place in places],
        out_specs=jax.tree.map(lambda _: pl.BlockSpec(memory_space=VMEM), outs),
        scratch_shapes=list(scratch),
        cost_estimate=pl.CostEstimate(flops=2 * macs, bytes_accessed=0, transcendentals=0),
        compiler_params=pltpu.CompilerParams(vmem_limit_bytes=limit * 2**20),
    )


def plane_device(raw, stream, conv_w, gain, w_qkv, mask):
    time_len, site_len, feat_len = raw.shape
    block, width = time_len * site_len, stream.shape[2]
    half, size = width // 2, w_qkv.shape[0]
    bf16, f32 = jnp.bfloat16, jnp.float32

    def array(*shape, kind=bf16):
        return jax.ShapeDtypeStruct(shape, kind)

    far_raw = swap_z(w_qkv, 2)

    cut, cut_more = array(size, PAIR), array(size + EXTRA, PAIR)
    to_x, to_y, kept = call(split_kernel, (cut,) * 3, "v")(w_qkv)
    own = call(sort_kernel, array(size, 6 * HD), "vvv")(kept, swap_depth(to_x, 1), swap_depth(to_y, 2))
    near = swap_z(own, 1)

    edge_x, edge_across, own_flags, sites = call(
        edge_kernel, (array(2 * EXTRA, HD), array(2 * EXTRA, HD), array(EXTRA, HD), array(*raw.shape)), "sv"
    )(mask.reshape(mask.shape[2]), raw)
    edge_x, edge_across = swap_depth(edge_x, 1), swap_depth(edge_across, 3)
    parts = 4
    normed = call(
        embed_kernel,
        array(block, width),
        "vvvvaa",
        scratch=[
            VMEM((block, width), f32),
            VMEM((parts, block, width // parts), bf16),
            VMEM((parts, 3 * feat_len, width // parts), bf16),
            pltpu.SemaphoreType.DMA((2 * parts,)),
        ],
        macs=block * 3 * feat_len * width,
        limit=53,
    )(
        edge_x,
        edge_across,
        sites,
        gain.reshape(1, width),
        stream.reshape(block, width),
        conv_w.reshape(3 * feat_len, width),
    )
    beside, above = swap_depth(normed, 1), swap_depth(normed, 2)

    to_y, kept = call(split_far_kernel, (cut_more, cut), "vv")(far_raw, own_flags)
    to_x = far_raw[:, PAIR : 2 * PAIR]
    from_x, from_y = swap_depth(to_x, 1), swap_depth(to_y, 2)
    keep, send, flags = call(
        sort_far_kernel,
        (array(size, 3 * HD), array(size, 3 * HD), array(EXTRA, 3 * HD)),
        "v" * 6,
    )(kept, from_x, from_y, edge_x, edge_across, own_flags)
    send, near, beside, above = lax.optimization_barrier((send, near, beside, above))
    far = jnp.concatenate([keep, swap_core(send)], axis=0)
    last = swap_z(far, 1)
    stack = jnp.concatenate([normed, beside, above], axis=0)
    far, near, stack = lax.optimization_barrier((far, near, stack))
    received = swap_core(jnp.concatenate([own[:, 3 * HD :], near[:, 3 * HD :], flags], axis=0))
    weights = (own, near, received, far)
    early = (stack, swap_core(stack))

    diagonal = [swap_depth(beside[:, :half], 2), swap_depth(above[:, half:], 1)]
    rows = 2 * size
    total = call(partial_kernel, array(6 * block, 3 * HD, kind=f32), "v" * 6, macs=6 * block * 3 * rows * 3 * HD)(
        *early, *weights
    )
    diagonal = [after(t, total) for t in diagonal]
    diagonal += [swap_core(t[i * block // 2 : (i + 1) * block // 2]) for t in diagonal for i in range(2)]
    total_diagonal, diagonal = call(
        diagonal_kernel,
        (array(2 * block, 3 * HD, kind=f32), array(2 * block, width)),
        "v" * 10,
        macs=2 * block * 3 * rows * 3 * HD,
    )(*diagonal, *weights)
    one_head, half_head = array(4, 2 * block, HD), array(2, 2 * block, HD)
    q, k, *v = call(
        finish_kernel, (one_head, one_head, half_head, half_head), "v" * 6, macs=8 * block * rows * 3 * HD
    )(*early, diagonal, last, total, total_diagonal)

    weights = call(weigh_kernel, array(4, 2 * block, 5 * block), "v" * 6, macs=8 * block * 5 * block * HD)(
        q, swap_z(k, 1), k, swap_middle(k), flags, received
    )
    values = [(swap_z(t, 1), t, swap_middle(t)) for t in v]
    pieces = {}
    for r in V_ORDER:
        mixed = call(functools.partial(mix_kernel, r), array(2 * block, HD), "vvvv", macs=2 * block * 5 * block * HD)(
            weights, *values[V_ORDER.index(r) // 2]
        )
        pieces[r] = swap_depth(mixed, r) if r else mixed
    both = [t for r in range(4) for t in (pieces[r], swap_core(pieces[r]))]
    context = call(gather_kernel, array(block, HEADS * HD), "v" * 8)(*both)
    return context.reshape(time_len, site_len, HEADS * HD)


def from_behind(value, axis, by):
    devices = lax.axis_size(axis)
    pairs = [(i, i + by) for i in range(devices) if 0 <= i + by < devices]
    return lax.ppermute(value, axis, pairs)


def head_attend(query_head, key_head, value_head, allowed):
    inv_root = 1.0 / math.sqrt(HD)
    scores = (
        jnp.einsum("qd,kd->qk", query_head, key_head, preferred_element_type=jnp.float32) * inv_root
    )
    scores = jnp.where(allowed, scores, -1e30)
    row_max = jnp.max(scores, axis=-1, keepdims=True)
    powers = jnp.exp(scores - row_max)
    weights = (powers / jnp.sum(powers, axis=-1, keepdims=True)).astype(jnp.bfloat16)
    return jnp.dot(weights, value_head, preferred_element_type=jnp.float32).astype(jnp.bfloat16)


def per_device(raw, stream, conv_w, gain, w_qkv, mask):
    time_len, site_len, _ = raw.shape
    tok_rows = time_len * site_len
    normed = normed_tokens(padded_2(raw, (("depth", 1),), 1), stream, conv_w, gain)
    columns = lax.all_gather(w_qkv, "depth", axis=1, tiled=True)
    projected = jnp.dot(
        normed,
        lax.all_gather(columns, "tm", axis=0, tiled=True),
        preferred_element_type=jnp.float32,
    ).astype(jnp.bfloat16)
    head_cols = projected.shape[1] // 3
    queries = projected[:, :head_cols]
    keyvals = projected[:, head_cols:]
    earlier = []
    later = []
    moving_back = keyvals
    moving_ahead = keyvals
    for hop_index in range(RD):
        moving_back = from_behind(moving_back, "tm", 1)
        moving_ahead = from_behind(moving_ahead, "tm", -1)
        earlier.insert(0, moving_back)
        later.append(moving_ahead)
    gathered = jnp.concatenate(earlier + [keyvals] + later, axis=0)
    block_rows = BT * PP
    own_blocks = tok_rows // block_rows
    span_blocks = gathered.shape[0] // block_rows
    local_mask = mask[0]
    query_ids = jnp.arange(own_blocks, dtype=jnp.int32)[:, None]
    key_ids = jnp.arange(span_blocks, dtype=jnp.int32)[None, :]
    entry_ids = key_ids - query_ids
    picks = entry_ids[:, :, None] == jnp.arange(local_mask.shape[1], dtype=jnp.int32)[None, None, :]
    block_allowed = jnp.sum(jnp.where(picks, local_mask[:, None, :], 0), axis=-1) > 0
    allowed = jnp.repeat(jnp.repeat(block_allowed, block_rows, axis=0), block_rows, axis=1)
    query_heads = queries.reshape(tok_rows, HEADS, HD).transpose(1, 0, 2)
    key_heads = gathered[:, :head_cols].reshape(gathered.shape[0], HEADS, HD).transpose(1, 0, 2)
    value_heads = gathered[:, head_cols:].reshape(gathered.shape[0], HEADS, HD).transpose(1, 0, 2)
    context = lax.map(
        lambda operands: head_attend(operands[0], operands[1], operands[2], allowed),
        (query_heads, key_heads, value_heads),
    )
    return context.transpose(1, 0, 2).reshape(time_len, site_len, head_cols)


def solution(mesh):
    in_specs = (
        P("tm", "depth", None),
        P("tm", "depth", None),
        P(),
        P(),
        P("tm", "depth"),
        P("depth", "tm", None),
    )
    out_specs = P("tm", "depth", None)
    fits = mesh.shape["depth"] == 4 and mesh.shape["tm"] == 8
    return jax.shard_map(
        plane_device if fits else per_device, mesh=mesh, in_specs=in_specs, out_specs=out_specs, check_vma=False
    )
```

```python
import functools
import math

import jax
import jax.numpy as jnp
from jax import lax
from jax.experimental import pallas as pl
from jax.experimental.pallas import tpu as pltpu
from jax.sharding import PartitionSpec as P

HEADS = 8
HD = 128
BT = 16
PP = 8
RD = 2
VMEM = pltpu.VMEM
SMEM = pltpu.SMEM


def padded_2(value, sides, width):
    for axis, dim in sides:
        devices, length = (lax.axis_size(axis), value.shape[dim])
        up = [(i, (i + 1) % devices) for i in range(devices - 1)]
        down = [(j, i) for i, j in up]
        last = lax.slice_in_dim(value, length - width, length, axis=dim)
        leading = lax.slice_in_dim(value, 0, width, axis=dim)
        before = lax.ppermute(last, axis, up)
        after = lax.ppermute(leading, axis, down)
        value = jnp.concatenate([before, value, after], axis=dim)
    return value


def normed_tokens(padded, stream, conv_w, gain):
    time_len, site_len, width = stream.shape
    tok_rows = time_len * site_len
    embedded = stream.reshape(tok_rows, width).astype(jnp.float32)
    for offset in range(3):
        window = padded[:, offset : offset + site_len].reshape(tok_rows, padded.shape[2])
        embedded = embedded + jnp.dot(window, conv_w[offset], preferred_element_type=jnp.float32)
    scale = lax.rsqrt(jnp.mean(embedded * embedded, axis=-1, keepdims=True) + 1e-05)
    return (embedded * scale * gain).astype(jnp.bfloat16)


PAIR = 2 * HD
V_ORDER = (3, 1, 2, 0)
EXTRA = 16


def hop(value, fn):
    pairs = []
    for z in range(4):
        for core in range(2):
            for depth in range(4):
                to = fn(z, core, depth)
                if to is not None:
                    pairs.append(((2 * z + core) * 4 + depth, (2 * to[0] + to[1]) * 4 + to[2]))
    return lax.ppermute(value, ("tm", "depth"), pairs)


def swap_core(value):
    return hop(value, lambda z, c, d: (z, 1 - c, d))


def swap_depth(value, bits):
    return hop(value, lambda z, c, d: (z, c, d ^ bits))


def swap_z(value, bits):
    return hop(value, lambda z, c, d: (z ^ bits, c, d))


def swap_middle(value):
    return hop(value, lambda z, c, d: (z ^ 3, c, d) if z in (1, 2) else None)


def after(value, *others):
    return lax.optimization_barrier((value, *others))[0]


def where_am_i():
    tm = lax.axis_index("tm")
    return tm >> 1, tm & 1, lax.axis_index("depth")


def edge_kernel(mask, raw, to_x, to_across, flags_ref, sites_ref):
    _, _, depth = where_am_i()
    odd = depth & 1
    lane = lax.broadcasted_iota(jnp.int32, (EXTRA, HD), 1)
    flags = jnp.zeros((EXTRA, HD), jnp.int32)
    for entry in range(mask.shape[0]):
        flags = jnp.where(lane == entry, mask[entry], flags)
    flags = flags.astype(jnp.float32).astype(jnp.bfloat16)
    flags_ref[...] = flags
    sites_ref[...] = raw[...]
    values = raw[...].astype(jnp.float32)
    first, last = values[:, 0], values[:, values.shape[1] - 1]
    for ref, use_last in ((to_x, odd == 0), (to_across, depth == 1)):
        ref[:EXTRA] = jnp.where(use_last, last, first).astype(jnp.bfloat16)
        ref[EXTRA:] = flags


def split_kernel(w, to_x, to_y, keep):
    _, _, depth = where_am_i()
    even = (depth & 1) == 0
    low, high = w[:, :PAIR], w[:, 2 * PAIR :]
    to_x[...] = w[:, PAIR : 2 * PAIR]
    to_y[: w.shape[0]] = jnp.where(even, high, low)
    keep[...] = jnp.where(even, low, high)


def sorted_groups(kept, from_x, from_y):
    _, core, depth = where_am_i()
    first, even = core == 0, (depth & 1) == 0
    size = kept.shape[0]
    low = jnp.where(even, kept[...], from_y[:size])
    high = jnp.where(even, from_y[:size], kept[...])
    groups = (low, from_x[:size], high)
    turn = jnp.where(depth == 3, 0, depth)
    for third in range(3):
        group = jnp.where(turn == 0, groups[third], jnp.where(turn == 1, groups[(third + 1) % 3], groups[(third + 2) % 3]))
        yield third, jnp.where(first, group[:, :HD], group[:, HD:]), jnp.where(first, group[:, HD:], group[:, :HD])


def sort_kernel(kept, from_x, from_y, out_ref):
    for third, mine, other in sorted_groups(kept, from_x, from_y):
        out_ref[:, third * HD : (third + 1) * HD] = mine
        out_ref[:, (3 + third) * HD : (4 + third) * HD] = other


def sort_far_kernel(kept, from_x, from_y, edge_x, edge_across, own_flags, keep_ref, send_ref, flags_ref):
    for third, mine, other in sorted_groups(kept, from_x, from_y):
        send_ref[:, third * HD : (third + 1) * HD] = other
        keep_ref[:, third * HD : (third + 1) * HD] = mine
    row = lax.broadcasted_iota(jnp.int32, (EXTRA, HD), 0)
    flags = own_flags[...].astype(jnp.float32)
    for r, value in ((1, edge_x[EXTRA:]), (2, from_y[kept.shape[0] :, :HD]), (3, edge_across[EXTRA:])):
        flags = jnp.where(row == r, value.astype(jnp.float32), flags)
    flags = flags.astype(jnp.bfloat16)
    for k in range(3):
        flags_ref[:, k * HD : (k + 1) * HD] = flags


def embed_kernel(edge_x, edge_across, raw, gain, stream, conv_w, out_ref, acc, tokens, weights, sems):
    time_len, site_len, feat_len = raw.shape
    _, _, depth = where_am_i()
    even = (depth & 1) == 0
    rows, width = stream.shape
    parts = weights.shape[0]
    step = width // parts
    copies = []
    for i in range(parts):
        here = pl.ds(i * step, step)
        copies.append(pltpu.make_async_copy(conv_w.at[:, here], weights.at[i], sems.at[2 * i]))
        copies.append(pltpu.make_async_copy(stream.at[:, here], tokens.at[i], sems.at[2 * i + 1]))
    for copy in copies:
        copy.start()
    side, far = edge_x[:time_len].astype(jnp.float32), edge_across[:time_len].astype(jnp.float32)
    before = jnp.where(even, jnp.where(depth == 2, far, 0.0), side)
    behind = jnp.where(even, side, jnp.where(depth == 1, far, 0.0))
    padded = jnp.concatenate([before[:, None], raw[...].astype(jnp.float32), behind[:, None]], axis=1)
    windows = [padded[:, j : j + site_len].reshape(rows, feat_len).astype(jnp.bfloat16) for j in range(3)]
    windows = jnp.concatenate(windows, axis=1)
    total = jnp.zeros((rows, 1), jnp.float32)
    for i in range(parts):
        copies[2 * i].wait()
        copies[2 * i + 1].wait()
        part = jnp.dot(windows, weights[i], preferred_element_type=jnp.float32) + tokens[i].astype(jnp.float32)
        acc[:, i * step : (i + 1) * step] = part
        total += jnp.sum(part * part, axis=1, keepdims=True)
    scale = lax.rsqrt(total / width + 1e-05)
    out_ref[...] = (acc[...] * scale * gain[...]).astype(jnp.bfloat16)


def take(refs, source, core, rows):
    half = rows // 2
    cuts = [pl.ds(pl.multiple_of(source * rows + c * half, half), half) for c in (core, 1 - core)]
    return jnp.concatenate([jnp.concatenate([ref[:, at] for at in cuts], axis=1) for ref in refs], axis=0)


def three_shards(x_refs, own, near, received, far):
    z, core, _ = where_am_i()
    size, width = own.shape[0], 3 * HD
    w = [own[:, :width], received[:size], far[...]]
    w = jnp.concatenate(w + [near[:, :width], received[size : 2 * size]], axis=0)
    x = [take(x_refs, source, core, 2 * size) for source in (z, z ^ 2, z ^ 1)]
    return jnp.dot(jnp.concatenate(x, axis=1), w, preferred_element_type=jnp.float32)


def partial_kernel(*refs):
    refs[-1][...] = three_shards(refs[:2], *refs[2:-1])


def diagonal_kernel(*refs):
    pieces, weights, (acc_ref, x_ref) = refs[:6], refs[6:-2], refs[-2:]
    block, half = pieces[0].shape
    corners = ((0, 0), (0, half), (block, 0), (block + block // 2, 0), (block, half), (block + block // 2, half))
    for (row, at), ref in zip(corners, pieces):
        x_ref[row : row + ref.shape[0], at : at + half] = ref[...]
    acc_ref[...] = three_shards([x_ref], *weights)


ROW_ORDER = ((0, 1, 2, 6), (3, 4, 5, 7))


def finish_kernel(*refs):
    x_refs, (last, acc_in, acc_diagonal, q_ref, k_ref, v_first, v_second) = refs[:3], refs[3:]
    z, core, _ = where_am_i()
    block, early = q_ref.shape[1] // 2, acc_in.shape[0]
    value = jnp.dot(take(x_refs, z ^ 3, core, last.shape[0]), last[...], preferred_element_type=jnp.float32)
    value = [acc_in[...] + value[:early], acc_diagonal[...] + value[early:]]
    value = jnp.concatenate(value, axis=0).astype(jnp.bfloat16)
    for rel in range(2):
        at = pl.ds(pl.multiple_of((core ^ rel) * block, block), block)
        for r in range(4):
            row = ROW_ORDER[rel][r]
            mine = value[row * block : (row + 1) * block]
            v_at = V_ORDER.index(r)
            q_ref[r, at, :] = mine[:, :HD]
            k_ref[r, at, :] = mine[:, HD:PAIR]
            (v_first, v_second)[v_at // 2][v_at % 2, at, :] = mine[:, PAIR:]


def spans(u):
    return ((0, u, 2), (1, 0, 2), (2, 0, 1 + u))


def neighbours(outer, own, middle, index):
    z, _, _ = where_am_i()
    odd = (z & 1) == 1
    outer, middle = outer[index], middle[index]
    return jnp.where(odd, outer, middle), own[index], jnp.where(odd, middle, outer)


def weigh_kernel(q_ref, outer, own, middle, own_flags, received, out_ref):
    _, core, _ = where_am_i()
    block = q_ref.shape[1] // 2
    inv_root = 1.0 / math.sqrt(HD)
    flags = [own_flags[:, :HD].astype(jnp.float32), received[-EXTRA:, :HD].astype(jnp.float32)]
    flags = [jnp.where(core == u, flags[0], flags[1]) for u in range(2)]
    bias = [(f - 1.0) * 1e30 for f in flags]
    for r in range(4):
        keys = neighbours(outer, own, middle, r)
        for u in range(2):
            q = q_ref[r, u * block : (u + 1) * block]
            scores = []
            for side, first, last in spans(u):
                k = keys[side][first * block : last * block]
                s = lax.dot_general(q, k, (((1,), (1,)), ((), ())), preferred_element_type=jnp.float32)
                for v in range(last - first):
                    entry = len(scores)
                    shut = jnp.broadcast_to(bias[u][r : r + 1, entry : entry + 1], (block, block))
                    scores.append(s[:, v * block : (v + 1) * block] * inv_root + shut)
            top = jnp.max(functools.reduce(jnp.maximum, scores), axis=1, keepdims=True)
            powers = [jnp.exp(s - top) for s in scores]
            inverse = 1.0 / jnp.sum(functools.reduce(jnp.add, powers), axis=1, keepdims=True)
            for entry, p in enumerate(powers):
                here = slice(entry * block, (entry + 1) * block)
                out_ref[r, u * block : (u + 1) * block, here] = (p * inverse).astype(jnp.bfloat16)


def mix_kernel(r, weights, outer, own, middle, keep_ref, send_ref):
    _, core, _ = where_am_i()
    block = weights.shape[1] // 2
    values = neighbours(outer, own, middle, V_ORDER.index(r) % 2)
    results = []
    for u in range(2):
        w = weights[r, u * block : (u + 1) * block]
        v = [values[side][first * block : last * block] for side, first, last in spans(u)]
        result = jnp.dot(w, jnp.concatenate(v, axis=0), preferred_element_type=jnp.float32)
        results.append(result.astype(jnp.bfloat16))
    keep_ref[...] = jnp.where(core == 0, results[0], results[1])
    send_ref[...] = jnp.where(core == 0, results[1], results[0])


def gather_kernel(*refs):
    out_ref = refs[-1]
    _, core, depth = where_am_i()
    for i, ref in enumerate(refs[:-1]):
        r, rel = i >> 1, i & 1
        at = pl.multiple_of((2 * (depth ^ r) + (core ^ rel)) * HD, HD)
        out_ref[:, pl.ds(at, HD)] = ref[...]


def call(kernel, outs, places, scratch=(), macs=0, limit=32):
    spaces = {"s": SMEM, "v": VMEM, "a": pl.ANY}
    return pl.pallas_call(
        kernel,
        out_shape=outs,
        in_specs=[pl.BlockSpec(memory_space=spaces[place]) for place in places],
        out_specs=jax.tree.map(lambda _: pl.BlockSpec(memory_space=VMEM), outs),
        scratch_shapes=list(scratch),
        cost_estimate=pl.CostEstimate(flops=2 * macs, bytes_accessed=0, transcendentals=0),
        compiler_params=pltpu.CompilerParams(vmem_limit_bytes=limit * 2**20),
    )


def plane_device(raw, stream, conv_w, gain, w_qkv, mask):
    time_len, site_len, feat_len = raw.shape
    block, width = time_len * site_len, stream.shape[2]
    half, size = width // 2, w_qkv.shape[0]
    bf16, f32 = jnp.bfloat16, jnp.float32

    def array(*shape, kind=bf16):
        return jax.ShapeDtypeStruct(shape, kind)

    far_raw = swap_z(w_qkv, 2)

    cut = array(size, PAIR)
    to_x, to_y, kept = call(split_kernel, (cut,) * 3, "v")(w_qkv)
    own = call(sort_kernel, array(size, 6 * HD), "vvv")(kept, swap_depth(to_x, 1), swap_depth(to_y, 2))
    near = swap_z(own, 1)

    edge_x, edge_across, own_flags, sites = call(
        edge_kernel, (array(2 * EXTRA, HD), array(2 * EXTRA, HD), array(EXTRA, HD), array(*raw.shape)), "sv"
    )(mask.reshape(mask.shape[2]), raw)
    edge_x, edge_across = swap_depth(edge_x, 1), swap_depth(edge_across, 3)
    parts = 4
    normed = call(
        embed_kernel,
        array(block, width),
        "vvvvaa",
        scratch=[
            VMEM((block, width), f32),
            VMEM((parts, block, width // parts), bf16),
            VMEM((parts, 3 * feat_len, width // parts), bf16),
            pltpu.SemaphoreType.DMA((2 * parts,)),
        ],
        macs=block * 3 * feat_len * width,
        limit=53,
    )(
        edge_x,
        edge_across,
        sites,
        gain.reshape(1, width),
        stream.reshape(block, width),
        conv_w.reshape(3 * feat_len, width),
    )
    beside, above = swap_depth(normed, 1), swap_depth(normed, 2)

    even = (lax.axis_index("depth") & 1) == 0
    low, to_x, high = (far_raw[:, k * PAIR : (k + 1) * PAIR] for k in range(3))
    kept = jnp.where(even, low, high)
    to_y = jnp.concatenate([jnp.where(even, high, low), jnp.concatenate([own_flags, own_flags], axis=1)], axis=0)
    from_x, from_y = swap_depth(to_x, 1), swap_depth(to_y, 2)
    keep, send, flags = call(
        sort_far_kernel,
        (array(size, 3 * HD), array(size, 3 * HD), array(EXTRA, 3 * HD)),
        "v" * 6,
    )(kept, from_x, from_y, edge_x, edge_across, own_flags)
    send, near, beside, above = lax.optimization_barrier((send, near, beside, above))
    far = jnp.concatenate([keep, swap_core(send)], axis=0)
    last = swap_z(far, 1)
    stack = jnp.concatenate([normed, beside, above], axis=0)
    far, near, stack = lax.optimization_barrier((far, near, stack))
    received = swap_core(jnp.concatenate([own[:, 3 * HD :], near[:, 3 * HD :], flags], axis=0))
    weights = (own, near, received, far)
    early = (stack, swap_core(stack))

    diagonal = [swap_depth(beside[:, :half], 2), swap_depth(above[:, half:], 1)]
    rows = 2 * size
    total = call(partial_kernel, array(6 * block, 3 * HD, kind=f32), "v" * 6, macs=6 * block * 3 * rows * 3 * HD)(
        *early, *weights
    )
    diagonal = [after(t, total) for t in diagonal]
    diagonal += [swap_core(t[i * block // 2 : (i + 1) * block // 2]) for t in diagonal for i in range(2)]
    total_diagonal, diagonal = call(
        diagonal_kernel,
        (array(2 * block, 3 * HD, kind=f32), array(2 * block, width)),
        "v" * 10,
        macs=2 * block * 3 * rows * 3 * HD,
    )(*diagonal, *weights)
    one_head, half_head = array(4, 2 * block, HD), array(2, 2 * block, HD)
    q, k, *v = call(
        finish_kernel, (one_head, one_head, half_head, half_head), "v" * 6, macs=8 * block * rows * 3 * HD
    )(*early, diagonal, last, total, total_diagonal)

    weights = call(weigh_kernel, array(4, 2 * block, 5 * block), "v" * 6, macs=8 * block * 5 * block * HD)(
        q, swap_z(k, 1), k, swap_middle(k), flags, received
    )
    values = [(swap_z(t, 1), t, swap_middle(t)) for t in v]
    pieces = {}
    for r in V_ORDER:
        kept, sent = call(
            functools.partial(mix_kernel, r), (array(block, HD),) * 2, "vvvv", macs=2 * block * 5 * block * HD
        )(weights, *values[V_ORDER.index(r) // 2])
        sent = hop(sent, lambda z, c, d, r=r: (z, 1 - c, d ^ r))
        pieces[r] = (swap_depth(kept, r) if r else kept, sent)
    both = [t for r in range(4) for t in pieces[r]]
    context = call(gather_kernel, array(block, HEADS * HD), "v" * 8)(*both)
    return context.reshape(time_len, site_len, HEADS * HD)


def from_behind(value, axis, by):
    devices = lax.axis_size(axis)
    pairs = [(i, i + by) for i in range(devices) if 0 <= i + by < devices]
    return lax.ppermute(value, axis, pairs)


def head_attend(query_head, key_head, value_head, allowed):
    inv_root = 1.0 / math.sqrt(HD)
    scores = (
        jnp.einsum("qd,kd->qk", query_head, key_head, preferred_element_type=jnp.float32) * inv_root
    )
    scores = jnp.where(allowed, scores, -1e30)
    row_max = jnp.max(scores, axis=-1, keepdims=True)
    powers = jnp.exp(scores - row_max)
    weights = (powers / jnp.sum(powers, axis=-1, keepdims=True)).astype(jnp.bfloat16)
    return jnp.dot(weights, value_head, preferred_element_type=jnp.float32).astype(jnp.bfloat16)


def per_device(raw, stream, conv_w, gain, w_qkv, mask):
    time_len, site_len, _ = raw.shape
    tok_rows = time_len * site_len
    normed = normed_tokens(padded_2(raw, (("depth", 1),), 1), stream, conv_w, gain)
    columns = lax.all_gather(w_qkv, "depth", axis=1, tiled=True)
    projected = jnp.dot(
        normed,
        lax.all_gather(columns, "tm", axis=0, tiled=True),
        preferred_element_type=jnp.float32,
    ).astype(jnp.bfloat16)
    head_cols = projected.shape[1] // 3
    queries = projected[:, :head_cols]
    keyvals = projected[:, head_cols:]
    earlier = []
    later = []
    moving_back = keyvals
    moving_ahead = keyvals
    for hop_index in range(RD):
        moving_back = from_behind(moving_back, "tm", 1)
        moving_ahead = from_behind(moving_ahead, "tm", -1)
        earlier.insert(0, moving_back)
        later.append(moving_ahead)
    gathered = jnp.concatenate(earlier + [keyvals] + later, axis=0)
    block_rows = BT * PP
    own_blocks = tok_rows // block_rows
    span_blocks = gathered.shape[0] // block_rows
    local_mask = mask[0]
    query_ids = jnp.arange(own_blocks, dtype=jnp.int32)[:, None]
    key_ids = jnp.arange(span_blocks, dtype=jnp.int32)[None, :]
    entry_ids = key_ids - query_ids
    picks = entry_ids[:, :, None] == jnp.arange(local_mask.shape[1], dtype=jnp.int32)[None, None, :]
    block_allowed = jnp.sum(jnp.where(picks, local_mask[:, None, :], 0), axis=-1) > 0
    allowed = jnp.repeat(jnp.repeat(block_allowed, block_rows, axis=0), block_rows, axis=1)
    query_heads = queries.reshape(tok_rows, HEADS, HD).transpose(1, 0, 2)
    key_heads = gathered[:, :head_cols].reshape(gathered.shape[0], HEADS, HD).transpose(1, 0, 2)
    value_heads = gathered[:, head_cols:].reshape(gathered.shape[0], HEADS, HD).transpose(1, 0, 2)
    context = lax.map(
        lambda operands: head_attend(operands[0], operands[1], operands[2], allowed),
        (query_heads, key_heads, value_heads),
    )
    return context.transpose(1, 0, 2).reshape(time_len, site_len, head_cols)


def solution(mesh):
    in_specs = (
        P("tm", "depth", None),
        P("tm", "depth", None),
        P(),
        P(),
        P("tm", "depth"),
        P("depth", "tm", None),
    )
    out_specs = P("tm", "depth", None)
    fits = mesh.shape["depth"] == 4 and mesh.shape["tm"] == 8
    return jax.shard_map(
        plane_device if fits else per_device, mesh=mesh, in_specs=in_specs, out_specs=out_specs, check_vma=False
    )
```

```python
import functools
import math

import jax
import jax.numpy as jnp
from jax import lax
from jax.experimental import pallas as pl
from jax.experimental.pallas import tpu as pltpu
from jax.sharding import PartitionSpec as P

HEADS = 8
HD = 128
BT = 16
PP = 8
RD = 2
VMEM = pltpu.VMEM
SMEM = pltpu.SMEM


def padded_2(value, sides, width):
    for axis, dim in sides:
        devices, length = (lax.axis_size(axis), value.shape[dim])
        up = [(i, (i + 1) % devices) for i in range(devices - 1)]
        down = [(j, i) for i, j in up]
        last = lax.slice_in_dim(value, length - width, length, axis=dim)
        leading = lax.slice_in_dim(value, 0, width, axis=dim)
        before = lax.ppermute(last, axis, up)
        after = lax.ppermute(leading, axis, down)
        value = jnp.concatenate([before, value, after], axis=dim)
    return value


def normed_tokens(padded, stream, conv_w, gain):
    time_len, site_len, width = stream.shape
    tok_rows = time_len * site_len
    embedded = stream.reshape(tok_rows, width).astype(jnp.float32)
    for offset in range(3):
        window = padded[:, offset : offset + site_len].reshape(tok_rows, padded.shape[2])
        embedded = embedded + jnp.dot(window, conv_w[offset], preferred_element_type=jnp.float32)
    scale = lax.rsqrt(jnp.mean(embedded * embedded, axis=-1, keepdims=True) + 1e-05)
    return (embedded * scale * gain).astype(jnp.bfloat16)


PAIR = 2 * HD
V_ORDER = (3, 1, 2, 0)
EXTRA = 16


def hop(value, fn):
    pairs = []
    for z in range(4):
        for core in range(2):
            for depth in range(4):
                to = fn(z, core, depth)
                if to is not None:
                    pairs.append(((2 * z + core) * 4 + depth, (2 * to[0] + to[1]) * 4 + to[2]))
    return lax.ppermute(value, ("tm", "depth"), pairs)


def swap_core(value):
    return hop(value, lambda z, c, d: (z, 1 - c, d))


def swap_depth(value, bits):
    return hop(value, lambda z, c, d: (z, c, d ^ bits))


def swap_z(value, bits):
    return hop(value, lambda z, c, d: (z ^ bits, c, d))


def swap_middle(value):
    return hop(value, lambda z, c, d: (z ^ 3, c, d) if z in (1, 2) else None)


def after(value, *others):
    return lax.optimization_barrier((value, *others))[0]


def where_am_i():
    tm = lax.axis_index("tm")
    return tm >> 1, tm & 1, lax.axis_index("depth")


def split_kernel(mask, w, raw, to_x, to_y, to_across, keep, flags_ref):
    _, _, depth = where_am_i()
    even = (depth & 1) == 0
    size, half = w.shape[0], raw.shape[0] // 2
    low, high = w[:, :PAIR], w[:, 2 * PAIR :]
    to_x[:size] = w[:, PAIR : 2 * PAIR]
    to_y[:size] = jnp.where(even, high, low)
    keep[...] = jnp.where(even, low, high)
    lane = lax.broadcasted_iota(jnp.int32, (EXTRA, HD), 1)
    flags = jnp.zeros((EXTRA, HD), jnp.int32)
    for entry in range(mask.shape[0]):
        flags = jnp.where(lane == entry, mask[entry], flags)
    flags = flags.astype(jnp.float32).astype(jnp.bfloat16)
    flags_ref[...] = flags
    at = to_across.shape[0] - EXTRA - half
    for i in range(2):
        to_across[:at, i * HD : (i + 1) * HD] = raw[:at]
    for ref, at in ((to_x, size), (to_y, size), (to_across, at)):
        for i in range(2):
            here = slice(i * HD, (i + 1) * HD)
            ref[at : at + half, here] = raw[i * half : (i + 1) * half]
            ref[at + half :, here] = flags


def sorted_groups(kept, from_x, from_y):
    _, core, depth = where_am_i()
    first, even = core == 0, (depth & 1) == 0
    size = kept.shape[0]
    low = jnp.where(even, kept[...], from_y[:size])
    high = jnp.where(even, from_y[:size], kept[...])
    groups = (low, from_x[:size], high)
    turn = jnp.where(depth == 3, 0, depth)
    for third in range(3):
        group = jnp.where(turn == 0, groups[third], jnp.where(turn == 1, groups[(third + 1) % 3], groups[(third + 2) % 3]))
        yield third, jnp.where(first, group[:, :HD], group[:, HD:]), jnp.where(first, group[:, HD:], group[:, :HD])


def sort_kernel(kept, from_x, from_y, out_ref):
    for third, mine, other in sorted_groups(kept, from_x, from_y):
        out_ref[:, third * HD : (third + 1) * HD] = mine
        out_ref[:, (3 + third) * HD : (4 + third) * HD] = other


def sort_far_kernel(kept, from_x, from_y, plane_x, plane_y, across, own_flags, keep_ref, send_ref, flags_ref):
    for third, mine, other in sorted_groups(kept, from_x, from_y):
        send_ref[:, third * HD : (third + 1) * HD] = other
        keep_ref[:, third * HD : (third + 1) * HD] = mine
    row = lax.broadcasted_iota(jnp.int32, (EXTRA, HD), 0)
    flags = own_flags[...].astype(jnp.float32)
    for r, ref in enumerate((plane_x, plane_y, across)):
        flags = jnp.where(row == r + 1, ref[ref.shape[0] - EXTRA :, :HD].astype(jnp.float32), flags)
    flags = flags.astype(jnp.bfloat16)
    for k in range(3):
        flags_ref[:, k * HD : (k + 1) * HD] = flags


def embed_kernel(rs, raw, plane_x, plane_y, across, conv_w, gain, *refs):
    streams, (out_ref, acc) = refs[: len(rs)], refs[-2:]
    for ref in refs[len(rs) : -2]:
        out_ref[: ref.shape[0]] = ref[...]
    _, _, depth = where_am_i()
    rows, width = raw.shape[0], conv_w.shape[1]
    raws = [raw[...]]
    for ref in (plane_x, plane_y, across):
        at = ref.shape[0] - EXTRA - rows // 2
        raws.append(jnp.concatenate([ref[at : at + rows // 2, :HD], ref[at : at + rows // 2, HD:]], axis=0))
    raws = [value.astype(jnp.float32).reshape(rows // PP, PP, HD) for value in raws]
    done = out_ref.shape[0] - len(rs) * rows
    for i, r in enumerate(rs):
        place = depth ^ r
        even = (place & 1) == 0
        side, far = raws[r ^ 1], raws[r ^ 3]
        before = jnp.where(even, jnp.where(place == 2, far[:, PP - 1 :], 0.0), side[:, PP - 1 :])
        behind = jnp.where(even, side[:, :1], jnp.where(place == 1, far[:, :1], 0.0))
        padded = jnp.concatenate([before, raws[r], behind], axis=1)
        windows = [padded[:, j : j + PP].reshape(rows, HD).astype(jnp.bfloat16) for j in range(3)]
        windows = jnp.concatenate(windows, axis=1)
        total, step = jnp.zeros((rows, 1), jnp.float32), width // 4
        for at in range(0, width, step):
            here = slice(at, at + step)
            part = jnp.dot(windows, conv_w[:, here], preferred_element_type=jnp.float32)
            part += streams[i][:, here].astype(jnp.float32)
            acc[:, here] = part
            total += jnp.sum(part * part, axis=1, keepdims=True)
        scale = lax.rsqrt(total / width + 1e-05)
        out_ref[done + i * rows : done + (i + 1) * rows] = (acc[...] * scale * gain[...]).astype(jnp.bfloat16)


def take(refs, source, core, rows):
    half = rows // 2
    cuts = [pl.ds(pl.multiple_of(source * rows + c * half, half), half) for c in (core, 1 - core)]
    return jnp.concatenate([jnp.concatenate([ref[:, at] for at in cuts], axis=1) for ref in refs], axis=0)


def three_shards(x_refs, own, near, received, far):
    z, core, _ = where_am_i()
    size, width = own.shape[0], 3 * HD
    w = [own[:, :width], received[:size], far[...]]
    w = jnp.concatenate(w + [near[:, :width], received[size : 2 * size]], axis=0)
    x = [take(x_refs, source, core, 2 * size) for source in (z, z ^ 2, z ^ 1)]
    return jnp.dot(jnp.concatenate(x, axis=1), w, preferred_element_type=jnp.float32)


def partial_kernel(*refs):
    refs[-1][...] = three_shards(refs[:2], *refs[2:-1])


def diagonal_kernel(mine, top, bottom, *refs):
    weights, (acc_ref, x_ref) = refs[:-2], refs[-2:]
    at = 0
    for ref in (mine, top, bottom):
        x_ref[at : at + ref.shape[0]] = ref[...]
        at += ref.shape[0]
    acc_ref[...] = three_shards([x_ref], *weights)


ROW_ORDER = ((0, 1, 2, 6), (3, 4, 5, 7))


def finish_kernel(*refs):
    x_refs, (last, acc_in, acc_diagonal, q_ref, k_ref, v_first, v_second) = refs[:3], refs[3:]
    z, core, _ = where_am_i()
    block, early = q_ref.shape[1] // 2, acc_in.shape[0]
    value = jnp.dot(take(x_refs, z ^ 3, core, last.shape[0]), last[...], preferred_element_type=jnp.float32)
    value = [acc_in[...] + value[:early], acc_diagonal[...] + value[early:]]
    value = jnp.concatenate(value, axis=0).astype(jnp.bfloat16)
    for rel in range(2):
        at = pl.ds(pl.multiple_of((core ^ rel) * block, block), block)
        for r in range(4):
            row = ROW_ORDER[rel][r]
            mine = value[row * block : (row + 1) * block]
            v_at = V_ORDER.index(r)
            q_ref[r, at, :] = mine[:, :HD]
            k_ref[r, at, :] = mine[:, HD:PAIR]
            (v_first, v_second)[v_at // 2][v_at % 2, at, :] = mine[:, PAIR:]


def spans(u):
    return ((0, u, 2), (1, 0, 2), (2, 0, 1 + u))


def neighbours(outer, own, middle, index):
    z, _, _ = where_am_i()
    odd = (z & 1) == 1
    outer, middle = outer[index], middle[index]
    return jnp.where(odd, outer, middle), own[index], jnp.where(odd, middle, outer)


def weigh_kernel(q_ref, outer, own, middle, own_flags, received, out_ref):
    _, core, _ = where_am_i()
    block = q_ref.shape[1] // 2
    inv_root = 1.0 / math.sqrt(HD)
    flags = [own_flags[:, :HD].astype(jnp.float32), received[-EXTRA:, :HD].astype(jnp.float32)]
    flags = [jnp.where(core == u, flags[0], flags[1]) for u in range(2)]
    bias = [(f - 1.0) * 1e30 for f in flags]
    for r in range(4):
        keys = neighbours(outer, own, middle, r)
        for u in range(2):
            q = q_ref[r, u * block : (u + 1) * block]
            scores = []
            for side, first, last in spans(u):
                k = keys[side][first * block : last * block]
                s = lax.dot_general(q, k, (((1,), (1,)), ((), ())), preferred_element_type=jnp.float32)
                for v in range(last - first):
                    entry = len(scores)
                    shut = jnp.broadcast_to(bias[u][r : r + 1, entry : entry + 1], (block, block))
                    scores.append(s[:, v * block : (v + 1) * block] * inv_root + shut)
            top = jnp.max(functools.reduce(jnp.maximum, scores), axis=1, keepdims=True)
            powers = [jnp.exp(s - top) for s in scores]
            inverse = 1.0 / jnp.sum(functools.reduce(jnp.add, powers), axis=1, keepdims=True)
            for entry, p in enumerate(powers):
                here = slice(entry * block, (entry + 1) * block)
                out_ref[r, u * block : (u + 1) * block, here] = (p * inverse).astype(jnp.bfloat16)


def mix_kernel(r, weights, outer, own, middle, keep_ref, send_ref):
    _, core, _ = where_am_i()
    block = weights.shape[1] // 2
    values = neighbours(outer, own, middle, V_ORDER.index(r) % 2)
    results = []
    for u in range(2):
        w = weights[r, u * block : (u + 1) * block]
        v = [values[side][first * block : last * block] for side, first, last in spans(u)]
        result = jnp.dot(w, jnp.concatenate(v, axis=0), preferred_element_type=jnp.float32)
        results.append(result.astype(jnp.bfloat16))
    keep_ref[...] = jnp.where(core == 0, results[0], results[1])
    send_ref[...] = jnp.where(core == 0, results[1], results[0])


def gather_kernel(*refs):
    out_ref = refs[-1]
    _, core, depth = where_am_i()
    for i, ref in enumerate(refs[:-1]):
        r, rel = i >> 1, i & 1
        at = pl.multiple_of((2 * (depth ^ r) + (core ^ rel)) * HD, HD)
        out_ref[:, pl.ds(at, HD)] = ref[...]


def call(kernel, outs, places, scratch=(), macs=0, limit=32):
    spaces = {"s": SMEM, "v": VMEM, "a": pl.ANY}
    return pl.pallas_call(
        kernel,
        out_shape=outs,
        in_specs=[pl.BlockSpec(memory_space=spaces[place]) for place in places],
        out_specs=jax.tree.map(lambda _: pl.BlockSpec(memory_space=VMEM), outs),
        scratch_shapes=list(scratch),
        cost_estimate=pl.CostEstimate(flops=2 * macs, bytes_accessed=0, transcendentals=0),
        compiler_params=pltpu.CompilerParams(vmem_limit_bytes=limit * 2**20),
    )


def plane_device(raw, stream, conv_w, gain, w_qkv, mask):
    time_len, site_len, feat_len = raw.shape
    block, width = time_len * site_len, stream.shape[2]
    half, size = width // 2, w_qkv.shape[0]
    bf16, f32 = jnp.bfloat16, jnp.float32

    def array(*shape, kind=bf16):
        return jax.ShapeDtypeStruct(shape, kind)

    far_raw = swap_z(w_qkv, 2)

    raw, stream = raw.reshape(block, feat_len), stream.reshape(block, width)
    conv_w, gain = conv_w.reshape(3 * feat_len, width), gain.reshape(1, width)
    more = block // 2 + EXTRA
    *to, kept, own_flags = call(
        split_kernel,
        (array(size + more, PAIR), array(size + more, PAIR), array(block, PAIR), array(size, PAIR), array(EXTRA, HD)),
        "svv",
    )(mask.reshape(mask.shape[2]), w_qkv, raw)
    plane = [swap_depth(t, r) for t, r in zip(to, (1, 2, 3))]
    own = call(sort_kernel, array(size, 6 * HD), "vvv")(kept, *plane[:2])
    near = swap_z(own, 1)

    def embed(rs, *streams, finished=()):
        return call(
            functools.partial(embed_kernel, rs),
            array((len(rs) + len(finished)) * block, width),
            "v" * (6 + len(streams) + len(finished)),
            scratch=[VMEM((block, width), f32)],
            macs=len(rs) * block * 3 * feat_len * width,
        )(raw, *plane, conv_w, gain, *streams, *finished)

    tied = after(stream, plane[2])
    beside, above = swap_depth(tied, 1), swap_depth(tied, 2)
    normed = embed((0,), stream)

    even = (lax.axis_index("depth") & 1) == 0
    low, to_x, high = (far_raw[:, k * PAIR : (k + 1) * PAIR] for k in range(3))
    kept, to_y = jnp.where(even, low, high), jnp.where(even, high, low)
    from_x, from_y = swap_depth(to_x, 1), swap_depth(to_y, 2)
    beside, above = after(beside, to_x), after(above, to_y)
    stack = embed((1, 2), beside, above, finished=(normed,))
    from_x, from_y, stack, near = lax.optimization_barrier((from_x, from_y, stack, near))
    keep, send, flags = call(
        sort_far_kernel,
        (array(size, 3 * HD), array(size, 3 * HD), array(EXTRA, 3 * HD)),
        "v" * 7,
    )(kept, from_x, from_y, *plane, own_flags)
    diagonal = swap_depth(beside[:, :half], 2), swap_depth(above[:, half:], 1)
    far = jnp.concatenate([keep, swap_core(send)], axis=0)
    last = swap_z(far, 1)
    far, near = lax.optimization_barrier((far, near))
    received = swap_core(jnp.concatenate([own[:, 3 * HD :], near[:, 3 * HD :], flags], axis=0))
    weights = (own, near, received, far)
    early = (stack, swap_core(stack))
    rows = 2 * size
    total = call(partial_kernel, array(6 * block, 3 * HD, kind=f32), "v" * 6, macs=6 * block * 3 * rows * 3 * HD)(
        *early, *weights
    )
    diagonal = embed((3,), after(jnp.concatenate(diagonal, axis=1), total))
    swapped = [swap_core(diagonal[i * block // 2 : (i + 1) * block // 2]) for i in range(2)]
    total_diagonal, diagonal = call(
        diagonal_kernel,
        (array(2 * block, 3 * HD, kind=f32), array(2 * block, width)),
        "v" * 7,
        macs=2 * block * 3 * rows * 3 * HD,
    )(diagonal, *swapped, *weights)
    one_head, half_head = array(4, 2 * block, HD), array(2, 2 * block, HD)
    q, k, *v = call(
        finish_kernel, (one_head, one_head, half_head, half_head), "v" * 6, macs=8 * block * rows * 3 * HD
    )(*early, diagonal, last, total, total_diagonal)

    weights = call(weigh_kernel, array(4, 2 * block, 5 * block), "v" * 6, macs=8 * block * 5 * block * HD)(
        q, swap_z(k, 1), k, swap_middle(k), flags, received
    )
    values = [(swap_z(t, 1), t, swap_middle(t)) for t in v]
    pieces = {}
    for r in V_ORDER:
        kept, sent = call(
            functools.partial(mix_kernel, r), (array(block, HD),) * 2, "vvvv", macs=2 * block * 5 * block * HD
        )(weights, *values[V_ORDER.index(r) // 2])
        sent = hop(sent, lambda z, c, d, r=r: (z, 1 - c, d ^ r))
        pieces[r] = (swap_depth(kept, r) if r else kept, sent)
    both = [t for r in range(4) for t in pieces[r]]
    context = call(gather_kernel, array(block, HEADS * HD), "v" * 8)(*both)
    return context.reshape(time_len, site_len, HEADS * HD)


def from_behind(value, axis, by):
    devices = lax.axis_size(axis)
    pairs = [(i, i + by) for i in range(devices) if 0 <= i + by < devices]
    return lax.ppermute(value, axis, pairs)


def head_attend(query_head, key_head, value_head, allowed):
    inv_root = 1.0 / math.sqrt(HD)
    scores = (
        jnp.einsum("qd,kd->qk", query_head, key_head, preferred_element_type=jnp.float32) * inv_root
    )
    scores = jnp.where(allowed, scores, -1e30)
    row_max = jnp.max(scores, axis=-1, keepdims=True)
    powers = jnp.exp(scores - row_max)
    weights = (powers / jnp.sum(powers, axis=-1, keepdims=True)).astype(jnp.bfloat16)
    return jnp.dot(weights, value_head, preferred_element_type=jnp.float32).astype(jnp.bfloat16)


def per_device(raw, stream, conv_w, gain, w_qkv, mask):
    time_len, site_len, _ = raw.shape
    tok_rows = time_len * site_len
    normed = normed_tokens(padded_2(raw, (("depth", 1),), 1), stream, conv_w, gain)
    columns = lax.all_gather(w_qkv, "depth", axis=1, tiled=True)
    projected = jnp.dot(
        normed,
        lax.all_gather(columns, "tm", axis=0, tiled=True),
        preferred_element_type=jnp.float32,
    ).astype(jnp.bfloat16)
    head_cols = projected.shape[1] // 3
    queries = projected[:, :head_cols]
    keyvals = projected[:, head_cols:]
    earlier = []
    later = []
    moving_back = keyvals
    moving_ahead = keyvals
    for hop_index in range(RD):
        moving_back = from_behind(moving_back, "tm", 1)
        moving_ahead = from_behind(moving_ahead, "tm", -1)
        earlier.insert(0, moving_back)
        later.append(moving_ahead)
    gathered = jnp.concatenate(earlier + [keyvals] + later, axis=0)
    block_rows = BT * PP
    own_blocks = tok_rows // block_rows
    span_blocks = gathered.shape[0] // block_rows
    local_mask = mask[0]
    query_ids = jnp.arange(own_blocks, dtype=jnp.int32)[:, None]
    key_ids = jnp.arange(span_blocks, dtype=jnp.int32)[None, :]
    entry_ids = key_ids - query_ids
    picks = entry_ids[:, :, None] == jnp.arange(local_mask.shape[1], dtype=jnp.int32)[None, None, :]
    block_allowed = jnp.sum(jnp.where(picks, local_mask[:, None, :], 0), axis=-1) > 0
    allowed = jnp.repeat(jnp.repeat(block_allowed, block_rows, axis=0), block_rows, axis=1)
    query_heads = queries.reshape(tok_rows, HEADS, HD).transpose(1, 0, 2)
    key_heads = gathered[:, :head_cols].reshape(gathered.shape[0], HEADS, HD).transpose(1, 0, 2)
    value_heads = gathered[:, head_cols:].reshape(gathered.shape[0], HEADS, HD).transpose(1, 0, 2)
    context = lax.map(
        lambda operands: head_attend(operands[0], operands[1], operands[2], allowed),
        (query_heads, key_heads, value_heads),
    )
    return context.transpose(1, 0, 2).reshape(time_len, site_len, head_cols)


def solution(mesh):
    in_specs = (
        P("tm", "depth", None),
        P("tm", "depth", None),
        P(),
        P(),
        P("tm", "depth"),
        P("depth", "tm", None),
    )
    out_specs = P("tm", "depth", None)
    fits = mesh.shape["depth"] == 4 and mesh.shape["tm"] == 8
    return jax.shard_map(
        plane_device if fits else per_device, mesh=mesh, in_specs=in_specs, out_specs=out_specs, check_vma=False
    )
```

```python
import functools
import math

import jax
import jax.numpy as jnp
from jax import lax
from jax.experimental import pallas as pl
from jax.experimental.pallas import tpu as pltpu
from jax.sharding import PartitionSpec as P

HEADS = 8
HD = 128
BT = 16
PP = 8
RD = 2
VMEM = pltpu.VMEM
SMEM = pltpu.SMEM


def padded_2(value, sides, width):
    for axis, dim in sides:
        devices, length = (lax.axis_size(axis), value.shape[dim])
        up = [(i, (i + 1) % devices) for i in range(devices - 1)]
        down = [(j, i) for i, j in up]
        last = lax.slice_in_dim(value, length - width, length, axis=dim)
        leading = lax.slice_in_dim(value, 0, width, axis=dim)
        before = lax.ppermute(last, axis, up)
        after = lax.ppermute(leading, axis, down)
        value = jnp.concatenate([before, value, after], axis=dim)
    return value


def normed_tokens(padded, stream, conv_w, gain):
    time_len, site_len, width = stream.shape
    tok_rows = time_len * site_len
    embedded = stream.reshape(tok_rows, width).astype(jnp.float32)
    for offset in range(3):
        window = padded[:, offset : offset + site_len].reshape(tok_rows, padded.shape[2])
        embedded = embedded + jnp.dot(window, conv_w[offset], preferred_element_type=jnp.float32)
    scale = lax.rsqrt(jnp.mean(embedded * embedded, axis=-1, keepdims=True) + 1e-05)
    return (embedded * scale * gain).astype(jnp.bfloat16)


PAIR = 2 * HD
V_ORDER = (3, 1, 2, 0)
EXTRA = 16


def hop(value, fn):
    pairs = []
    for z in range(4):
        for core in range(2):
            for depth in range(4):
                to = fn(z, core, depth)
                if to is not None:
                    pairs.append(((2 * z + core) * 4 + depth, (2 * to[0] + to[1]) * 4 + to[2]))
    return lax.ppermute(value, ("tm", "depth"), pairs)


def swap_core(value):
    return hop(value, lambda z, c, d: (z, 1 - c, d))


def swap_depth(value, bits):
    return hop(value, lambda z, c, d: (z, c, d ^ bits))


def swap_z(value, bits):
    return hop(value, lambda z, c, d: (z ^ bits, c, d))


def swap_middle(value):
    return hop(value, lambda z, c, d: (z ^ 3, c, d) if z in (1, 2) else None)


def after(value, *others):
    return lax.optimization_barrier((value, *others))[0]


def where_am_i():
    tm = lax.axis_index("tm")
    return tm >> 1, tm & 1, lax.axis_index("depth")


def split_kernel(mask, w, raw, to_x, to_y, to_across, keep, flags_ref):
    _, _, depth = where_am_i()
    even = (depth & 1) == 0
    size, half = w.shape[0], raw.shape[0] // 2
    low, high = w[:, :PAIR], w[:, 2 * PAIR :]
    to_x[:size] = w[:, PAIR : 2 * PAIR]
    to_y[:size] = jnp.where(even, high, low)
    keep[...] = jnp.where(even, low, high)
    lane = lax.broadcasted_iota(jnp.int32, (EXTRA, HD), 1)
    flags = jnp.zeros((EXTRA, HD), jnp.int32)
    for entry in range(mask.shape[0]):
        flags = jnp.where(lane == entry, mask[entry], flags)
    flags = flags.astype(jnp.float32).astype(jnp.bfloat16)
    flags_ref[...] = flags
    at = to_across.shape[0] - EXTRA - half
    for i in range(2):
        to_across[:at, i * HD : (i + 1) * HD] = raw[:at]
    for ref, at in ((to_x, size), (to_y, size), (to_across, at)):
        for i in range(2):
            here = slice(i * HD, (i + 1) * HD)
            ref[at : at + half, here] = raw[i * half : (i + 1) * half]
            ref[at + half :, here] = flags


def sorted_groups(kept, from_x, from_y):
    _, core, depth = where_am_i()
    first, even = core == 0, (depth & 1) == 0
    size = kept.shape[0]
    low = jnp.where(even, kept[...], from_y[:size])
    high = jnp.where(even, from_y[:size], kept[...])
    groups = (low, from_x[:size], high)
    turn = jnp.where(depth == 3, 0, depth)
    for third in range(3):
        group = jnp.where(turn == 0, groups[third], jnp.where(turn == 1, groups[(third + 1) % 3], groups[(third + 2) % 3]))
        yield third, jnp.where(first, group[:, :HD], group[:, HD:]), jnp.where(first, group[:, HD:], group[:, :HD])


def sort_kernel(kept, from_x, from_y, out_ref):
    for third, mine, other in sorted_groups(kept, from_x, from_y):
        out_ref[:, third * HD : (third + 1) * HD] = mine
        out_ref[:, (3 + third) * HD : (4 + third) * HD] = other


def sort_far_kernel(kept, from_x, from_y, plane_x, plane_y, across, own_flags, keep_ref, send_ref, flags_ref):
    for third, mine, other in sorted_groups(kept, from_x, from_y):
        send_ref[:, third * HD : (third + 1) * HD] = other
        keep_ref[:, third * HD : (third + 1) * HD] = mine
    row = lax.broadcasted_iota(jnp.int32, (EXTRA, HD), 0)
    flags = own_flags[...].astype(jnp.float32)
    for r, ref in enumerate((plane_x, plane_y, across)):
        flags = jnp.where(row == r + 1, ref[ref.shape[0] - EXTRA :, :HD].astype(jnp.float32), flags)
    flags = flags.astype(jnp.bfloat16)
    for k in range(3):
        flags_ref[:, k * HD : (k + 1) * HD] = flags


def embed_kernel(rs, more, raw, plane_x, plane_y, across, conv_w, gain, *refs):
    count = len(rs)
    streams, finished, (out_ref, *onward, acc) = refs[:count], refs[count : count + more], refs[count + more :]
    for ref in finished:
        out_ref[: ref.shape[0]] = ref[...]
    for i, ref in enumerate(onward):
        half = ref.shape[1]
        ref[...] = streams[i][:, i * half : (i + 1) * half]
    _, _, depth = where_am_i()
    rows, width = raw.shape[0], conv_w.shape[1]
    raws = [raw[...]]
    for ref in (plane_x, plane_y, across):
        at = ref.shape[0] - EXTRA - rows // 2
        raws.append(jnp.concatenate([ref[at : at + rows // 2, :HD], ref[at : at + rows // 2, HD:]], axis=0))
    raws = [value.astype(jnp.float32).reshape(rows // PP, PP, HD) for value in raws]
    done = out_ref.shape[0] - len(rs) * rows
    for i, r in enumerate(rs):
        place = depth ^ r
        even = (place & 1) == 0
        side, far = raws[r ^ 1], raws[r ^ 3]
        before = jnp.where(even, jnp.where(place == 2, far[:, PP - 1 :], 0.0), side[:, PP - 1 :])
        behind = jnp.where(even, side[:, :1], jnp.where(place == 1, far[:, :1], 0.0))
        padded = jnp.concatenate([before, raws[r], behind], axis=1)
        windows = [padded[:, j : j + PP].reshape(rows, HD).astype(jnp.bfloat16) for j in range(3)]
        windows = jnp.concatenate(windows, axis=1)
        total, step = jnp.zeros((rows, 1), jnp.float32), width // 4
        for at in range(0, width, step):
            here = slice(at, at + step)
            part = jnp.dot(windows, conv_w[:, here], preferred_element_type=jnp.float32)
            part += streams[i][:, here].astype(jnp.float32)
            acc[:, here] = part
            total += jnp.sum(part * part, axis=1, keepdims=True)
        scale = lax.rsqrt(total / width + 1e-05)
        out_ref[done + i * rows : done + (i + 1) * rows] = (acc[...] * scale * gain[...]).astype(jnp.bfloat16)


def take(refs, source, core, rows):
    half = rows // 2
    cuts = [pl.ds(pl.multiple_of(source * rows + c * half, half), half) for c in (core, 1 - core)]
    return jnp.concatenate([jnp.concatenate([ref[:, at] for at in cuts], axis=1) for ref in refs], axis=0)


def three_shards(x_refs, own, near, received, far):
    z, core, _ = where_am_i()
    size, width = own.shape[0], 3 * HD
    w = [own[:, :width], received[:size], far[...]]
    w = jnp.concatenate(w + [near[:, :width], received[size : 2 * size]], axis=0)
    x = [take(x_refs, source, core, 2 * size) for source in (z, z ^ 2, z ^ 1)]
    return jnp.dot(jnp.concatenate(x, axis=1), w, preferred_element_type=jnp.float32)


def partial_kernel(*refs):
    refs[-1][...] = three_shards(refs[:2], *refs[2:-1])


def diagonal_kernel(mine, top, bottom, *refs):
    weights, (acc_ref, x_ref) = refs[:-2], refs[-2:]
    at = 0
    for ref in (mine, top, bottom):
        x_ref[at : at + ref.shape[0]] = ref[...]
        at += ref.shape[0]
    acc_ref[...] = three_shards([x_ref], *weights)


ROW_ORDER = ((0, 1, 2, 6), (3, 4, 5, 7))


def finish_kernel(*refs):
    x_refs, (last, acc_in, acc_diagonal, q_ref, k_ref, v_first, v_second) = refs[:3], refs[3:]
    z, core, _ = where_am_i()
    block, early = q_ref.shape[1] // 2, acc_in.shape[0]
    value = jnp.dot(take(x_refs, z ^ 3, core, last.shape[0]), last[...], preferred_element_type=jnp.float32)
    value = [acc_in[...] + value[:early], acc_diagonal[...] + value[early:]]
    value = jnp.concatenate(value, axis=0).astype(jnp.bfloat16)
    for rel in range(2):
        at = pl.ds(pl.multiple_of((core ^ rel) * block, block), block)
        for r in range(4):
            row = ROW_ORDER[rel][r]
            mine = value[row * block : (row + 1) * block]
            v_at = V_ORDER.index(r)
            q_ref[r, at, :] = mine[:, :HD]
            k_ref[r, at, :] = mine[:, HD:PAIR]
            (v_first, v_second)[v_at // 2][v_at % 2, at, :] = mine[:, PAIR:]


def spans(u):
    return ((0, u, 2), (1, 0, 2), (2, 0, 1 + u))


def neighbours(outer, own, middle, index):
    z, _, _ = where_am_i()
    odd = (z & 1) == 1
    outer, middle = outer[index], middle[index]
    return jnp.where(odd, outer, middle), own[index], jnp.where(odd, middle, outer)


def weigh_kernel(q_ref, outer, own, middle, own_flags, received, out_ref):
    _, core, _ = where_am_i()
    block = q_ref.shape[1] // 2
    inv_root = 1.0 / math.sqrt(HD)
    flags = [own_flags[:, :HD].astype(jnp.float32), received[-EXTRA:, :HD].astype(jnp.float32)]
    flags = [jnp.where(core == u, flags[0], flags[1]) for u in range(2)]
    bias = [(f - 1.0) * 1e30 for f in flags]
    for r in range(4):
        keys = neighbours(outer, own, middle, r)
        for u in range(2):
            q = q_ref[r, u * block : (u + 1) * block]
            scores = []
            for side, first, last in spans(u):
                k = keys[side][first * block : last * block]
                s = lax.dot_general(q, k, (((1,), (1,)), ((), ())), preferred_element_type=jnp.float32)
                for v in range(last - first):
                    entry = len(scores)
                    shut = jnp.broadcast_to(bias[u][r : r + 1, entry : entry + 1], (block, block))
                    scores.append(s[:, v * block : (v + 1) * block] * inv_root + shut)
            top = jnp.max(functools.reduce(jnp.maximum, scores), axis=1, keepdims=True)
            powers = [jnp.exp(s - top) for s in scores]
            inverse = 1.0 / jnp.sum(functools.reduce(jnp.add, powers), axis=1, keepdims=True)
            for entry, p in enumerate(powers):
                here = slice(entry * block, (entry + 1) * block)
                out_ref[r, u * block : (u + 1) * block, here] = (p * inverse).astype(jnp.bfloat16)


def mix_kernel(r, weights, outer, own, middle, keep_ref, send_ref):
    _, core, _ = where_am_i()
    block = weights.shape[1] // 2
    values = neighbours(outer, own, middle, V_ORDER.index(r) % 2)
    results = []
    for u in range(2):
        w = weights[r, u * block : (u + 1) * block]
        v = [values[side][first * block : last * block] for side, first, last in spans(u)]
        result = jnp.dot(w, jnp.concatenate(v, axis=0), preferred_element_type=jnp.float32)
        results.append(result.astype(jnp.bfloat16))
    keep_ref[...] = jnp.where(core == 0, results[0], results[1])
    send_ref[...] = jnp.where(core == 0, results[1], results[0])


def gather_kernel(*refs):
    out_ref = refs[-1]
    _, core, depth = where_am_i()
    for i, ref in enumerate(refs[:-1]):
        r, rel = i >> 1, i & 1
        at = pl.multiple_of((2 * (depth ^ r) + (core ^ rel)) * HD, HD)
        out_ref[:, pl.ds(at, HD)] = ref[...]


def call(kernel, outs, places, scratch=(), macs=0, limit=32):
    spaces = {"s": SMEM, "v": VMEM, "a": pl.ANY}
    return pl.pallas_call(
        kernel,
        out_shape=outs,
        in_specs=[pl.BlockSpec(memory_space=spaces[place]) for place in places],
        out_specs=jax.tree.map(lambda _: pl.BlockSpec(memory_space=VMEM), outs),
        scratch_shapes=list(scratch),
        cost_estimate=pl.CostEstimate(flops=2 * macs, bytes_accessed=0, transcendentals=0),
        compiler_params=pltpu.CompilerParams(vmem_limit_bytes=limit * 2**20),
    )


def plane_device(raw, stream, conv_w, gain, w_qkv, mask):
    time_len, site_len, feat_len = raw.shape
    block, width = time_len * site_len, stream.shape[2]
    half, size = width // 2, w_qkv.shape[0]
    bf16, f32 = jnp.bfloat16, jnp.float32

    def array(*shape, kind=bf16):
        return jax.ShapeDtypeStruct(shape, kind)

    far_raw = swap_z(w_qkv, 2)

    raw, stream = raw.reshape(block, feat_len), stream.reshape(block, width)
    conv_w, gain = conv_w.reshape(3 * feat_len, width), gain.reshape(1, width)
    more = block // 2 + EXTRA
    *to, kept, own_flags = call(
        split_kernel,
        (array(size + more, PAIR), array(size + more, PAIR), array(block, PAIR), array(size, PAIR), array(EXTRA, HD)),
        "svv",
    )(mask.reshape(mask.shape[2]), w_qkv, raw)
    plane = [swap_depth(t, r) for t, r in zip(to, (1, 2, 3))]
    own = call(sort_kernel, array(size, 6 * HD), "vvv")(kept, *plane[:2])
    near = swap_z(own, 1)

    def embed(rs, *streams, finished=()):
        out = (array((len(rs) + len(finished)) * block, width),) + (array(block, half),) * (len(rs) - 1) * 2
        return call(
            functools.partial(embed_kernel, rs, len(finished)),
            out,
            "v" * (6 + len(streams) + len(finished)),
            scratch=[VMEM((block, width), f32)],
            macs=len(rs) * block * 3 * feat_len * width,
        )(raw, *plane, conv_w, gain, *streams, *finished)

    tied = after(stream, plane[2])
    beside, above = swap_depth(tied, 1), swap_depth(tied, 2)
    (normed,) = embed((0,), stream)
    far_raw = after(far_raw, normed)

    even = (lax.axis_index("depth") & 1) == 0
    low, to_x, high = (far_raw[:, k * PAIR : (k + 1) * PAIR] for k in range(3))
    kept, to_y = jnp.where(even, low, high), jnp.where(even, high, low)
    from_x, from_y = swap_depth(to_x, 1), swap_depth(to_y, 2)
    beside, above = after(beside, to_x), after(above, to_y)
    stack, *diagonal = embed((1, 2), beside, above, finished=(normed,))
    from_x, from_y, stack, near = lax.optimization_barrier((from_x, from_y, stack, near))
    keep, send, flags = call(
        sort_far_kernel,
        (array(size, 3 * HD), array(size, 3 * HD), array(EXTRA, 3 * HD)),
        "v" * 7,
    )(kept, from_x, from_y, *plane, own_flags)
    diagonal = swap_depth(diagonal[0], 2), swap_depth(diagonal[1], 1)
    far = jnp.concatenate([keep, swap_core(send)], axis=0)
    last = swap_z(far, 1)
    far, near, stack = lax.optimization_barrier((far, near, stack))
    received = swap_core(jnp.concatenate([own[:, 3 * HD :], near[:, 3 * HD :], flags], axis=0))
    weights = (own, near, received, far)
    piece = block // 2
    early = (stack, swap_core(stack))
    rows = 2 * size
    total = call(partial_kernel, array(6 * block, 3 * HD, kind=f32), "v" * 6, macs=6 * block * 3 * rows * 3 * HD)(
        *early, *weights
    )
    (diagonal,) = embed((3,), after(jnp.concatenate(diagonal, axis=1), total))
    swapped = [swap_core(diagonal[:piece]), swap_core(diagonal[piece:])]
    total_diagonal, diagonal = call(
        diagonal_kernel,
        (array(2 * block, 3 * HD, kind=f32), array(2 * block, width)),
        "v" * 7,
        macs=2 * block * 3 * rows * 3 * HD,
    )(diagonal, *swapped, *weights)
    one_head, half_head = array(4, 2 * block, HD), array(2, 2 * block, HD)
    q, k, *v = call(
        finish_kernel, (one_head, one_head, half_head, half_head), "v" * 6, macs=8 * block * rows * 3 * HD
    )(*early, diagonal, last, total, total_diagonal)

    weights = call(weigh_kernel, array(4, 2 * block, 5 * block), "v" * 6, macs=8 * block * 5 * block * HD)(
        q, swap_z(k, 1), k, swap_middle(k), flags, received
    )
    values = [(swap_z(t, 1), t, swap_middle(t)) for t in v]
    pieces = {}
    for r in V_ORDER:
        kept, sent = call(
            functools.partial(mix_kernel, r), (array(block, HD),) * 2, "vvvv", macs=2 * block * 5 * block * HD
        )(weights, *values[V_ORDER.index(r) // 2])
        sent = hop(sent, lambda z, c, d, r=r: (z, 1 - c, d ^ r))
        pieces[r] = (swap_depth(kept, r) if r else kept, sent)
    both = [t for r in range(4) for t in pieces[r]]
    context = call(gather_kernel, array(block, HEADS * HD), "v" * 8)(*both)
    return context.reshape(time_len, site_len, HEADS * HD)


def from_behind(value, axis, by):
    devices = lax.axis_size(axis)
    pairs = [(i, i + by) for i in range(devices) if 0 <= i + by < devices]
    return lax.ppermute(value, axis, pairs)


def head_attend(query_head, key_head, value_head, allowed):
    inv_root = 1.0 / math.sqrt(HD)
    scores = (
        jnp.einsum("qd,kd->qk", query_head, key_head, preferred_element_type=jnp.float32) * inv_root
    )
    scores = jnp.where(allowed, scores, -1e30)
    row_max = jnp.max(scores, axis=-1, keepdims=True)
    powers = jnp.exp(scores - row_max)
    weights = (powers / jnp.sum(powers, axis=-1, keepdims=True)).astype(jnp.bfloat16)
    return jnp.dot(weights, value_head, preferred_element_type=jnp.float32).astype(jnp.bfloat16)


def per_device(raw, stream, conv_w, gain, w_qkv, mask):
    time_len, site_len, _ = raw.shape
    tok_rows = time_len * site_len
    normed = normed_tokens(padded_2(raw, (("depth", 1),), 1), stream, conv_w, gain)
    columns = lax.all_gather(w_qkv, "depth", axis=1, tiled=True)
    projected = jnp.dot(
        normed,
        lax.all_gather(columns, "tm", axis=0, tiled=True),
        preferred_element_type=jnp.float32,
    ).astype(jnp.bfloat16)
    head_cols = projected.shape[1] // 3
    queries = projected[:, :head_cols]
    keyvals = projected[:, head_cols:]
    earlier = []
    later = []
    moving_back = keyvals
    moving_ahead = keyvals
    for hop_index in range(RD):
        moving_back = from_behind(moving_back, "tm", 1)
        moving_ahead = from_behind(moving_ahead, "tm", -1)
        earlier.insert(0, moving_back)
        later.append(moving_ahead)
    gathered = jnp.concatenate(earlier + [keyvals] + later, axis=0)
    block_rows = BT * PP
    own_blocks = tok_rows // block_rows
    span_blocks = gathered.shape[0] // block_rows
    local_mask = mask[0]
    query_ids = jnp.arange(own_blocks, dtype=jnp.int32)[:, None]
    key_ids = jnp.arange(span_blocks, dtype=jnp.int32)[None, :]
    entry_ids = key_ids - query_ids
    picks = entry_ids[:, :, None] == jnp.arange(local_mask.shape[1], dtype=jnp.int32)[None, None, :]
    block_allowed = jnp.sum(jnp.where(picks, local_mask[:, None, :], 0), axis=-1) > 0
    allowed = jnp.repeat(jnp.repeat(block_allowed, block_rows, axis=0), block_rows, axis=1)
    query_heads = queries.reshape(tok_rows, HEADS, HD).transpose(1, 0, 2)
    key_heads = gathered[:, :head_cols].reshape(gathered.shape[0], HEADS, HD).transpose(1, 0, 2)
    value_heads = gathered[:, head_cols:].reshape(gathered.shape[0], HEADS, HD).transpose(1, 0, 2)
    context = lax.map(
        lambda operands: head_attend(operands[0], operands[1], operands[2], allowed),
        (query_heads, key_heads, value_heads),
    )
    return context.transpose(1, 0, 2).reshape(time_len, site_len, head_cols)


def solution(mesh):
    in_specs = (
        P("tm", "depth", None),
        P("tm", "depth", None),
        P(),
        P(),
        P("tm", "depth"),
        P("depth", "tm", None),
    )
    out_specs = P("tm", "depth", None)
    fits = mesh.shape["depth"] == 4 and mesh.shape["tm"] == 8
    return jax.shard_map(
        plane_device if fits else per_device, mesh=mesh, in_specs=in_specs, out_specs=out_specs, check_vma=False
    )
```

```python
import functools
import math

import jax
import jax.numpy as jnp
from jax import lax
from jax.experimental import pallas as pl
from jax.experimental.pallas import tpu as pltpu
from jax.sharding import PartitionSpec as P

HEADS = 8
HD = 128
BT = 16
PP = 8
RD = 2
VMEM = pltpu.VMEM
SMEM = pltpu.SMEM


def padded_2(value, sides, width):
    for axis, dim in sides:
        devices, length = (lax.axis_size(axis), value.shape[dim])
        up = [(i, (i + 1) % devices) for i in range(devices - 1)]
        down = [(j, i) for i, j in up]
        last = lax.slice_in_dim(value, length - width, length, axis=dim)
        leading = lax.slice_in_dim(value, 0, width, axis=dim)
        before = lax.ppermute(last, axis, up)
        after = lax.ppermute(leading, axis, down)
        value = jnp.concatenate([before, value, after], axis=dim)
    return value


def normed_tokens(padded, stream, conv_w, gain):
    time_len, site_len, width = stream.shape
    tok_rows = time_len * site_len
    embedded = stream.reshape(tok_rows, width).astype(jnp.float32)
    for offset in range(3):
        window = padded[:, offset : offset + site_len].reshape(tok_rows, padded.shape[2])
        embedded = embedded + jnp.dot(window, conv_w[offset], preferred_element_type=jnp.float32)
    scale = lax.rsqrt(jnp.mean(embedded * embedded, axis=-1, keepdims=True) + 1e-05)
    return (embedded * scale * gain).astype(jnp.bfloat16)


PAIR = 2 * HD
V_ORDER = (3, 1, 2, 0)
EXTRA = 16


def hop(value, fn):
    pairs = []
    for z in range(4):
        for core in range(2):
            for depth in range(4):
                to = fn(z, core, depth)
                if to is not None:
                    pairs.append(((2 * z + core) * 4 + depth, (2 * to[0] + to[1]) * 4 + to[2]))
    return lax.ppermute(value, ("tm", "depth"), pairs)


def swap_core(value):
    return hop(value, lambda z, c, d: (z, 1 - c, d))


def swap_depth(value, bits):
    return hop(value, lambda z, c, d: (z, c, d ^ bits))


def swap_z(value, bits):
    return hop(value, lambda z, c, d: (z ^ bits, c, d))


def swap_middle(value):
    return hop(value, lambda z, c, d: (z ^ 3, c, d) if z in (1, 2) else None)


def after(value, *others):
    return lax.optimization_barrier((value, *others))[0]


def where_am_i():
    tm = lax.axis_index("tm")
    return tm >> 1, tm & 1, lax.axis_index("depth")


def split_kernel(mask, w, raw, to_x, to_y, to_across, keep, flags_ref):
    _, _, depth = where_am_i()
    even = (depth & 1) == 0
    size, half = w.shape[0], raw.shape[0] // 2
    low, high = w[:, :PAIR], w[:, 2 * PAIR :]
    to_x[:size] = w[:, PAIR : 2 * PAIR]
    to_y[:size] = jnp.where(even, high, low)
    keep[...] = jnp.where(even, low, high)
    lane = lax.broadcasted_iota(jnp.int32, (EXTRA, HD), 1)
    flags = jnp.zeros((EXTRA, HD), jnp.int32)
    for entry in range(mask.shape[0]):
        flags = jnp.where(lane == entry, mask[entry], flags)
    flags = flags.astype(jnp.float32).astype(jnp.bfloat16)
    flags_ref[...] = flags
    at = to_across.shape[0] - EXTRA - half
    for i in range(2):
        to_across[:at, i * HD : (i + 1) * HD] = raw[:at]
    for ref, at in ((to_x, size), (to_y, size), (to_across, at)):
        for i in range(2):
            here = slice(i * HD, (i + 1) * HD)
            ref[at : at + half, here] = raw[i * half : (i + 1) * half]
            ref[at + half :, here] = flags


def sorted_groups(kept, from_x, from_y):
    _, core, depth = where_am_i()
    first, even = core == 0, (depth & 1) == 0
    size = kept.shape[0]
    low = jnp.where(even, kept[...], from_y[:size])
    high = jnp.where(even, from_y[:size], kept[...])
    groups = (low, from_x[:size], high)
    turn = jnp.where(depth == 3, 0, depth)
    for third in range(3):
        group = jnp.where(turn == 0, groups[third], jnp.where(turn == 1, groups[(third + 1) % 3], groups[(third + 2) % 3]))
        yield third, jnp.where(first, group[:, :HD], group[:, HD:]), jnp.where(first, group[:, HD:], group[:, :HD])


def sort_kernel(kept, from_x, from_y, out_ref):
    for third, mine, other in sorted_groups(kept, from_x, from_y):
        out_ref[:, third * HD : (third + 1) * HD] = mine
        out_ref[:, (3 + third) * HD : (4 + third) * HD] = other


def sort_far_kernel(kept, from_x, from_y, plane_x, plane_y, across, own_flags, keep_ref, send_ref, flags_ref):
    for third, mine, other in sorted_groups(kept, from_x, from_y):
        send_ref[:, third * HD : (third + 1) * HD] = other
        keep_ref[:, third * HD : (third + 1) * HD] = mine
    row = lax.broadcasted_iota(jnp.int32, (EXTRA, HD), 0)
    flags = own_flags[...].astype(jnp.float32)
    for r, ref in enumerate((plane_x, plane_y, across)):
        flags = jnp.where(row == r + 1, ref[ref.shape[0] - EXTRA :, :HD].astype(jnp.float32), flags)
    flags = flags.astype(jnp.bfloat16)
    for k in range(3):
        flags_ref[:, k * HD : (k + 1) * HD] = flags


def embed_kernel(rs, more, raw, plane_x, plane_y, across, conv_w, gain, *refs):
    count = len(rs)
    streams, finished, (out_ref, *onward, acc) = refs[:count], refs[count : count + more], refs[count + more :]
    for ref in finished:
        out_ref[: ref.shape[0]] = ref[...]
    for i, ref in enumerate(onward):
        half = ref.shape[1]
        ref[...] = streams[i][:, i * half : (i + 1) * half]
    _, _, depth = where_am_i()
    rows, width = raw.shape[0], conv_w.shape[1]
    raws = [raw[...]]
    for ref in (plane_x, plane_y, across):
        at = ref.shape[0] - EXTRA - rows // 2
        raws.append(jnp.concatenate([ref[at : at + rows // 2, :HD], ref[at : at + rows // 2, HD:]], axis=0))
    raws = [value.astype(jnp.float32).reshape(rows // PP, PP, HD) for value in raws]
    done = out_ref.shape[0] - len(rs) * rows
    for i, r in enumerate(rs):
        place = depth ^ r
        even = (place & 1) == 0
        side, far = raws[r ^ 1], raws[r ^ 3]
        before = jnp.where(even, jnp.where(place == 2, far[:, PP - 1 :], 0.0), side[:, PP - 1 :])
        behind = jnp.where(even, side[:, :1], jnp.where(place == 1, far[:, :1], 0.0))
        padded = jnp.concatenate([before, raws[r], behind], axis=1)
        windows = [padded[:, j : j + PP].reshape(rows, HD).astype(jnp.bfloat16) for j in range(3)]
        windows = jnp.concatenate(windows, axis=1)
        total, step = jnp.zeros((rows, 1), jnp.float32), width // 4
        for at in range(0, width, step):
            here = slice(at, at + step)
            part = jnp.dot(windows, conv_w[:, here], preferred_element_type=jnp.float32)
            part += streams[i][:, here].astype(jnp.float32)
            acc[:, here] = part
            total += jnp.sum(part * part, axis=1, keepdims=True)
        scale = lax.rsqrt(total / width + 1e-05)
        out_ref[done + i * rows : done + (i + 1) * rows] = (acc[...] * scale * gain[...]).astype(jnp.bfloat16)


def take(refs, source, core, rows):
    half = rows // 2
    cuts = [pl.ds(pl.multiple_of(source * rows + c * half, half), half) for c in (core, 1 - core)]
    return jnp.concatenate([jnp.concatenate([ref[:, at] for at in cuts], axis=1) for ref in refs], axis=0)


def three_shards(x_refs, own, near, received, far):
    z, core, _ = where_am_i()
    size, width = own.shape[0], 3 * HD
    w = [own[:, :width], received[:size], far[...]]
    w = jnp.concatenate(w + [near[:, :width], received[size : 2 * size]], axis=0)
    x = [take(x_refs, source, core, 2 * size) for source in (z, z ^ 2, z ^ 1)]
    return jnp.dot(jnp.concatenate(x, axis=1), w, preferred_element_type=jnp.float32)


def partial_kernel(*refs):
    refs[-1][...] = three_shards(refs[:2], *refs[2:-1])


def diagonal_kernel(mine, top, bottom, *refs):
    weights, (acc_ref, x_ref) = refs[:-2], refs[-2:]
    at = 0
    for ref in (mine, top, bottom):
        x_ref[at : at + ref.shape[0]] = ref[...]
        at += ref.shape[0]
    acc_ref[...] = three_shards([x_ref], *weights)


ROW_ORDER = ((0, 1, 2, 6), (3, 4, 5, 7))


def finish_kernel(*refs):
    x_refs, (last, acc_in, acc_diagonal, q_ref, k_ref, v_first, v_second) = refs[:3], refs[3:]
    z, core, _ = where_am_i()
    block, early = q_ref.shape[1] // 2, acc_in.shape[0]
    value = jnp.dot(take(x_refs, z ^ 3, core, last.shape[0]), last[...], preferred_element_type=jnp.float32)
    value = [acc_in[...] + value[:early], acc_diagonal[...] + value[early:]]
    value = jnp.concatenate(value, axis=0).astype(jnp.bfloat16)
    for rel in range(2):
        at = pl.ds(pl.multiple_of((core ^ rel) * block, block), block)
        for r in range(4):
            row = ROW_ORDER[rel][r]
            mine = value[row * block : (row + 1) * block]
            v_at = V_ORDER.index(r)
            q_ref[r, at, :] = mine[:, :HD]
            k_ref[r, at, :] = mine[:, HD:PAIR]
            (v_first, v_second)[v_at // 2][v_at % 2, at, :] = mine[:, PAIR:]


def spans(u):
    return ((0, u, 2), (1, 0, 2), (2, 0, 1 + u))


def neighbours(outer, own, middle, index):
    z, _, _ = where_am_i()
    odd = (z & 1) == 1
    outer, middle = outer[index], middle[index]
    return jnp.where(odd, outer, middle), own[index], jnp.where(odd, middle, outer)


def weigh_kernel(q_ref, outer, own, middle, own_flags, received, out_ref):
    _, core, _ = where_am_i()
    block = q_ref.shape[1] // 2
    inv_root = 1.0 / math.sqrt(HD)
    flags = [own_flags[:, :HD].astype(jnp.float32), received[-EXTRA:, :HD].astype(jnp.float32)]
    flags = [jnp.where(core == u, flags[0], flags[1]) for u in range(2)]
    bias = [(f - 1.0) * 1e30 for f in flags]
    for r in range(4):
        keys = neighbours(outer, own, middle, r)
        for u in range(2):
            q = q_ref[r, u * block : (u + 1) * block]
            scores = []
            for side, first, last in spans(u):
                k = keys[side][first * block : last * block]
                s = lax.dot_general(q, k, (((1,), (1,)), ((), ())), preferred_element_type=jnp.float32)
                for v in range(last - first):
                    entry = len(scores)
                    shut = jnp.broadcast_to(bias[u][r : r + 1, entry : entry + 1], (block, block))
                    scores.append(s[:, v * block : (v + 1) * block] * inv_root + shut)
            top = jnp.max(functools.reduce(jnp.maximum, scores), axis=1, keepdims=True)
            powers = [jnp.exp(s - top) for s in scores]
            inverse = 1.0 / jnp.sum(functools.reduce(jnp.add, powers), axis=1, keepdims=True)
            for entry, p in enumerate(powers):
                here = slice(entry * block, (entry + 1) * block)
                out_ref[r, u * block : (u + 1) * block, here] = (p * inverse).astype(jnp.bfloat16)


def mix_kernel(r, weights, outer, own, middle, out_ref):
    block = weights.shape[1] // 2
    values = neighbours(outer, own, middle, V_ORDER.index(r) % 2)
    for u in range(2):
        w = weights[r, u * block : (u + 1) * block]
        v = [values[side][first * block : last * block] for side, first, last in spans(u)]
        result = jnp.dot(w, jnp.concatenate(v, axis=0), preferred_element_type=jnp.float32)
        out_ref[u * block : (u + 1) * block] = result.astype(jnp.bfloat16)


def pack_kernel(*refs):
    keep_ref, send_ref = refs[4:]
    _, core, _ = where_am_i()
    block = keep_ref.shape[1]
    for r, ref in enumerate(refs[:4]):
        for rel, out_ref in enumerate((keep_ref, send_ref)):
            out_ref[r] = ref[pl.ds(pl.multiple_of((core ^ rel) * block, block), block), :]


def gather_kernel(mine, other, out_ref):
    _, core, depth = where_am_i()
    for rel, ref in enumerate((mine, other)):
        for r in range(4):
            at = pl.multiple_of((2 * (depth ^ r) + (core ^ rel)) * HD, HD)
            out_ref[:, pl.ds(at, HD)] = ref[r]


def call(kernel, outs, places, scratch=(), macs=0, limit=32):
    spaces = {"s": SMEM, "v": VMEM, "a": pl.ANY}
    return pl.pallas_call(
        kernel,
        out_shape=outs,
        in_specs=[pl.BlockSpec(memory_space=spaces[place]) for place in places],
        out_specs=jax.tree.map(lambda _: pl.BlockSpec(memory_space=VMEM), outs),
        scratch_shapes=list(scratch),
        cost_estimate=pl.CostEstimate(flops=2 * macs, bytes_accessed=0, transcendentals=0),
        compiler_params=pltpu.CompilerParams(vmem_limit_bytes=limit * 2**20),
    )


def plane_device(raw, stream, conv_w, gain, w_qkv, mask):
    time_len, site_len, feat_len = raw.shape
    block, width = time_len * site_len, stream.shape[2]
    half, size = width // 2, w_qkv.shape[0]
    bf16, f32 = jnp.bfloat16, jnp.float32

    def array(*shape, kind=bf16):
        return jax.ShapeDtypeStruct(shape, kind)

    far_raw = swap_z(w_qkv, 2)

    raw, stream = raw.reshape(block, feat_len), stream.reshape(block, width)
    conv_w, gain = conv_w.reshape(3 * feat_len, width), gain.reshape(1, width)
    more = block // 2 + EXTRA
    *to, kept, own_flags = call(
        split_kernel,
        (array(size + more, PAIR), array(size + more, PAIR), array(block, PAIR), array(size, PAIR), array(EXTRA, HD)),
        "svv",
    )(mask.reshape(mask.shape[2]), w_qkv, raw)
    plane = [swap_depth(t, r) for t, r in zip(to, (1, 2, 3))]
    own = call(sort_kernel, array(size, 6 * HD), "vvv")(kept, *plane[:2])
    near = swap_z(own, 1)

    def embed(rs, *streams, finished=()):
        out = (array((len(rs) + len(finished)) * block, width),) + (array(block, half),) * (len(rs) - 1) * 2
        return call(
            functools.partial(embed_kernel, rs, len(finished)),
            out,
            "v" * (6 + len(streams) + len(finished)),
            scratch=[VMEM((block, width), f32)],
            macs=len(rs) * block * 3 * feat_len * width,
        )(raw, *plane, conv_w, gain, *streams, *finished)

    tied = after(stream, plane[2])
    beside, above = swap_depth(tied, 1), swap_depth(tied, 2)
    (normed,) = embed((0,), stream)
    far_raw = after(far_raw, normed)

    even = (lax.axis_index("depth") & 1) == 0
    low, to_x, high = (far_raw[:, k * PAIR : (k + 1) * PAIR] for k in range(3))
    kept, to_y = jnp.where(even, low, high), jnp.where(even, high, low)
    from_x, from_y = swap_depth(to_x, 1), swap_depth(to_y, 2)
    beside, above = after(beside, to_x), after(above, to_y)
    stack, *diagonal = embed((1, 2), beside, above, finished=(normed,))
    from_x, from_y, stack, near = lax.optimization_barrier((from_x, from_y, stack, near))
    keep, send, flags = call(
        sort_far_kernel,
        (array(size, 3 * HD), array(size, 3 * HD), array(EXTRA, 3 * HD)),
        "v" * 7,
    )(kept, from_x, from_y, *plane, own_flags)
    diagonal = swap_depth(diagonal[0], 2), swap_depth(diagonal[1], 1)
    far = jnp.concatenate([keep, swap_core(send)], axis=0)
    last = swap_z(far, 1)
    far, near, stack = lax.optimization_barrier((far, near, stack))
    received = swap_core(jnp.concatenate([own[:, 3 * HD :], near[:, 3 * HD :], flags], axis=0))
    weights = (own, near, received, far)
    piece = 5 * block // 8
    early = (stack, swap_core(stack))
    rows = 2 * size
    total = call(partial_kernel, array(6 * block, 3 * HD, kind=f32), "v" * 6, macs=6 * block * 3 * rows * 3 * HD)(
        *early, *weights
    )
    (diagonal,) = embed((3,), jnp.concatenate([after(t, total) for t in diagonal], axis=1))
    swapped = [swap_core(diagonal[:piece]), swap_core(diagonal[piece:])]
    total_diagonal, diagonal = call(
        diagonal_kernel,
        (array(2 * block, 3 * HD, kind=f32), array(2 * block, width)),
        "v" * 7,
        macs=2 * block * 3 * rows * 3 * HD,
    )(diagonal, *swapped, *weights)
    one_head, half_head = array(4, 2 * block, HD), array(2, 2 * block, HD)
    q, k, *v = call(
        finish_kernel, (one_head, one_head, half_head, half_head), "v" * 6, macs=8 * block * rows * 3 * HD
    )(*early, diagonal, last, total, total_diagonal)

    weights = call(weigh_kernel, array(4, 2 * block, 5 * block), "v" * 6, macs=8 * block * 5 * block * HD)(
        q, swap_z(k, 1), k, swap_middle(k), flags, received
    )
    values = [(swap_z(t, 1), t, swap_middle(t)) for t in v]
    pieces = {}
    for r in V_ORDER:
        mixed = call(functools.partial(mix_kernel, r), array(2 * block, HD), "vvvv", macs=2 * block * 5 * block * HD)(
            weights, *values[V_ORDER.index(r) // 2]
        )
        pieces[r] = swap_depth(mixed, r) if r else mixed
    kept, sent = call(pack_kernel, (array(4, block, HD),) * 2, "vvvv")(*[pieces[r] for r in range(4)])
    context = call(gather_kernel, array(block, HEADS * HD), "vv")(kept, swap_core(sent))
    return context.reshape(time_len, site_len, HEADS * HD)


def from_behind(value, axis, by):
    devices = lax.axis_size(axis)
    pairs = [(i, i + by) for i in range(devices) if 0 <= i + by < devices]
    return lax.ppermute(value, axis, pairs)


def head_attend(query_head, key_head, value_head, allowed):
    inv_root = 1.0 / math.sqrt(HD)
    scores = (
        jnp.einsum("qd,kd->qk", query_head, key_head, preferred_element_type=jnp.float32) * inv_root
    )
    scores = jnp.where(allowed, scores, -1e30)
    row_max = jnp.max(scores, axis=-1, keepdims=True)
    powers = jnp.exp(scores - row_max)
    weights = (powers / jnp.sum(powers, axis=-1, keepdims=True)).astype(jnp.bfloat16)
    return jnp.dot(weights, value_head, preferred_element_type=jnp.float32).astype(jnp.bfloat16)


def per_device(raw, stream, conv_w, gain, w_qkv, mask):
    time_len, site_len, _ = raw.shape
    tok_rows = time_len * site_len
    normed = normed_tokens(padded_2(raw, (("depth", 1),), 1), stream, conv_w, gain)
    columns = lax.all_gather(w_qkv, "depth", axis=1, tiled=True)
    projected = jnp.dot(
        normed,
        lax.all_gather(columns, "tm", axis=0, tiled=True),
        preferred_element_type=jnp.float32,
    ).astype(jnp.bfloat16)
    head_cols = projected.shape[1] // 3
    queries = projected[:, :head_cols]
    keyvals = projected[:, head_cols:]
    earlier = []
    later = []
    moving_back = keyvals
    moving_ahead = keyvals
    for hop_index in range(RD):
        moving_back = from_behind(moving_back, "tm", 1)
        moving_ahead = from_behind(moving_ahead, "tm", -1)
        earlier.insert(0, moving_back)
        later.append(moving_ahead)
    gathered = jnp.concatenate(earlier + [keyvals] + later, axis=0)
    block_rows = BT * PP
    own_blocks = tok_rows // block_rows
    span_blocks = gathered.shape[0] // block_rows
    local_mask = mask[0]
    query_ids = jnp.arange(own_blocks, dtype=jnp.int32)[:, None]
    key_ids = jnp.arange(span_blocks, dtype=jnp.int32)[None, :]
    entry_ids = key_ids - query_ids
    picks = entry_ids[:, :, None] == jnp.arange(local_mask.shape[1], dtype=jnp.int32)[None, None, :]
    block_allowed = jnp.sum(jnp.where(picks, local_mask[:, None, :], 0), axis=-1) > 0
    allowed = jnp.repeat(jnp.repeat(block_allowed, block_rows, axis=0), block_rows, axis=1)
    query_heads = queries.reshape(tok_rows, HEADS, HD).transpose(1, 0, 2)
    key_heads = gathered[:, :head_cols].reshape(gathered.shape[0], HEADS, HD).transpose(1, 0, 2)
    value_heads = gathered[:, head_cols:].reshape(gathered.shape[0], HEADS, HD).transpose(1, 0, 2)
    context = lax.map(
        lambda operands: head_attend(operands[0], operands[1], operands[2], allowed),
        (query_heads, key_heads, value_heads),
    )
    return context.transpose(1, 0, 2).reshape(time_len, site_len, head_cols)


def solution(mesh):
    in_specs = (
        P("tm", "depth", None),
        P("tm", "depth", None),
        P(),
        P(),
        P("tm", "depth"),
        P("depth", "tm", None),
    )
    out_specs = P("tm", "depth", None)
    fits = mesh.shape["depth"] == 4 and mesh.shape["tm"] == 8
    return jax.shard_map(
        plane_device if fits else per_device, mesh=mesh, in_specs=in_specs, out_specs=out_specs, check_vma=False
    )
```

```python
import functools
import math

import jax
import jax.numpy as jnp
from jax import lax
from jax.experimental import pallas as pl
from jax.experimental.pallas import tpu as pltpu
from jax.sharding import PartitionSpec as P

HEADS = 8
HD = 128
BT = 16
PP = 8
RD = 2
VMEM = pltpu.VMEM
SMEM = pltpu.SMEM


def padded_2(value, sides, width):
    for axis, dim in sides:
        devices, length = (lax.axis_size(axis), value.shape[dim])
        up = [(i, (i + 1) % devices) for i in range(devices - 1)]
        down = [(j, i) for i, j in up]
        last = lax.slice_in_dim(value, length - width, length, axis=dim)
        leading = lax.slice_in_dim(value, 0, width, axis=dim)
        before = lax.ppermute(last, axis, up)
        after = lax.ppermute(leading, axis, down)
        value = jnp.concatenate([before, value, after], axis=dim)
    return value


def normed_tokens(padded, stream, conv_w, gain):
    time_len, site_len, width = stream.shape
    tok_rows = time_len * site_len
    embedded = stream.reshape(tok_rows, width).astype(jnp.float32)
    for offset in range(3):
        window = padded[:, offset : offset + site_len].reshape(tok_rows, padded.shape[2])
        embedded = embedded + jnp.dot(window, conv_w[offset], preferred_element_type=jnp.float32)
    scale = lax.rsqrt(jnp.mean(embedded * embedded, axis=-1, keepdims=True) + 1e-05)
    return (embedded * scale * gain).astype(jnp.bfloat16)


PAIR = 2 * HD
V_ORDER = (3, 1, 2, 0)
EXTRA = 16


def hop(value, fn):
    pairs = []
    for z in range(4):
        for core in range(2):
            for depth in range(4):
                to = fn(z, core, depth)
                if to is not None:
                    pairs.append(((2 * z + core) * 4 + depth, (2 * to[0] + to[1]) * 4 + to[2]))
    return lax.ppermute(value, ("tm", "depth"), pairs)


def swap_core(value):
    return hop(value, lambda z, c, d: (z, 1 - c, d))


def swap_depth(value, bits):
    return hop(value, lambda z, c, d: (z, c, d ^ bits))


def swap_z(value, bits):
    return hop(value, lambda z, c, d: (z ^ bits, c, d))


def swap_middle(value):
    return hop(value, lambda z, c, d: (z ^ 3, c, d) if z in (1, 2) else None)


def after(value, *others):
    return lax.optimization_barrier((value, *others))[0]


def where_am_i():
    tm = lax.axis_index("tm")
    return tm >> 1, tm & 1, lax.axis_index("depth")


def split_kernel(w, raw, to_x, to_y, to_across, keep):
    _, _, depth = where_am_i()
    even = (depth & 1) == 0
    size, half = w.shape[0], (raw.shape[0] - EXTRA) // 2
    low, high = w[:, :PAIR], w[:, 2 * PAIR :]
    to_x[:size] = w[:, PAIR : 2 * PAIR]
    to_y[:size] = jnp.where(even, high, low)
    keep[...] = jnp.where(even, low, high)
    at = to_across.shape[0] - EXTRA - half
    for i in range(2):
        to_across[:at, i * HD : (i + 1) * HD] = raw[:at]
    for ref, at in ((to_x, size), (to_y, size), (to_across, at)):
        for i in range(2):
            here = slice(i * HD, (i + 1) * HD)
            ref[at : at + half, here] = raw[i * half : (i + 1) * half]
            ref[at + half :, here] = raw[2 * half :]


def sorted_groups(kept, from_x, from_y):
    _, core, depth = where_am_i()
    first, even = core == 0, (depth & 1) == 0
    size = kept.shape[0]
    low = jnp.where(even, kept[...], from_y[:size])
    high = jnp.where(even, from_y[:size], kept[...])
    groups = (low, from_x[:size], high)
    turn = jnp.where(depth == 3, 0, depth)
    for third in range(3):
        group = jnp.where(turn == 0, groups[third], jnp.where(turn == 1, groups[(third + 1) % 3], groups[(third + 2) % 3]))
        yield third, jnp.where(first, group[:, :HD], group[:, HD:]), jnp.where(first, group[:, HD:], group[:, :HD])


def sort_kernel(kept, from_x, from_y, out_ref):
    for third, mine, other in sorted_groups(kept, from_x, from_y):
        out_ref[:, third * HD : (third + 1) * HD] = mine
        out_ref[:, (3 + third) * HD : (4 + third) * HD] = other


def sort_far_kernel(kept, from_x, from_y, plane_x, plane_y, across, raw, keep_ref, send_ref, flags_ref):
    for third, mine, other in sorted_groups(kept, from_x, from_y):
        send_ref[:, third * HD : (third + 1) * HD] = other
        keep_ref[:, third * HD : (third + 1) * HD] = mine
    row = lax.broadcasted_iota(jnp.int32, (EXTRA, HD), 0)
    flags = raw[raw.shape[0] - EXTRA :].astype(jnp.float32)
    for r, ref in enumerate((plane_x, plane_y, across)):
        flags = jnp.where(row == r + 1, ref[ref.shape[0] - EXTRA :, :HD].astype(jnp.float32), flags)
    flags = flags.astype(jnp.bfloat16)
    for k in range(3):
        flags_ref[:, k * HD : (k + 1) * HD] = flags


def embed_kernel(rs, more, raw, plane_x, plane_y, across, conv_w, gain, *refs):
    count = len(rs)
    streams, finished, (out_ref, *onward, acc) = refs[:count], refs[count : count + more], refs[count + more :]
    for ref in finished:
        out_ref[: ref.shape[0]] = ref[...]
    for i, ref in enumerate(onward):
        half = ref.shape[1]
        ref[...] = streams[i][:, i * half : (i + 1) * half]
    _, _, depth = where_am_i()
    rows, width = raw.shape[0] - EXTRA, conv_w.shape[1]
    raws = [raw[:rows]]
    for ref in (plane_x, plane_y, across):
        at = ref.shape[0] - EXTRA - rows // 2
        raws.append(jnp.concatenate([ref[at : at + rows // 2, :HD], ref[at : at + rows // 2, HD:]], axis=0))
    raws = [value.astype(jnp.float32).reshape(rows // PP, PP, HD) for value in raws]
    done = out_ref.shape[0] - len(rs) * rows
    for i, r in enumerate(rs):
        place = depth ^ r
        even = (place & 1) == 0
        side, far = raws[r ^ 1], raws[r ^ 3]
        before = jnp.where(even, jnp.where(place == 2, far[:, PP - 1 :], 0.0), side[:, PP - 1 :])
        behind = jnp.where(even, side[:, :1], jnp.where(place == 1, far[:, :1], 0.0))
        padded = jnp.concatenate([before, raws[r], behind], axis=1)
        windows = [padded[:, j : j + PP].reshape(rows, HD).astype(jnp.bfloat16) for j in range(3)]
        windows = jnp.concatenate(windows, axis=1)
        total, step = jnp.zeros((rows, 1), jnp.float32), width // 4
        for at in range(0, width, step):
            here = slice(at, at + step)
            part = jnp.dot(windows, conv_w[:, here], preferred_element_type=jnp.float32)
            part += streams[i][:, here].astype(jnp.float32)
            acc[:, here] = part
            total += jnp.sum(part * part, axis=1, keepdims=True)
        scale = lax.rsqrt(total / width + 1e-05)
        out_ref[done + i * rows : done + (i + 1) * rows] = (acc[...] * scale * gain[...]).astype(jnp.bfloat16)


def take(refs, source, core, rows):
    half = rows // 2
    cuts = [pl.ds(pl.multiple_of(source * rows + c * half, half), half) for c in (core, 1 - core)]
    return jnp.concatenate([jnp.concatenate([ref[:, at] for at in cuts], axis=1) for ref in refs], axis=0)


def three_shards(x_refs, own, near, received, far):
    z, core, _ = where_am_i()
    size, width = own.shape[0], 3 * HD
    w = [own[:, :width], received[:size], far[...]]
    w = jnp.concatenate(w + [near[:, :width], received[size : 2 * size]], axis=0)
    x = [take(x_refs, source, core, 2 * size) for source in (z, z ^ 2, z ^ 1)]
    return jnp.dot(jnp.concatenate(x, axis=1), w, preferred_element_type=jnp.float32)


def partial_kernel(*refs):
    refs[-1][...] = three_shards(refs[:2], *refs[2:-1])


def diagonal_kernel(mine, top, bottom, *refs):
    weights, (acc_ref, x_ref) = refs[:-2], refs[-2:]
    at = 0
    for ref in (mine, top, bottom):
        x_ref[at : at + ref.shape[0]] = ref[...]
        at += ref.shape[0]
    acc_ref[...] = three_shards([x_ref], *weights)


ROW_ORDER = ((0, 1, 2, 6), (3, 4, 5, 7))


def finish_kernel(*refs):
    x_refs, (last, acc_in, acc_diagonal, q_ref, k_ref, v_first, v_second) = refs[:3], refs[3:]
    z, core, _ = where_am_i()
    block, early = q_ref.shape[1] // 2, acc_in.shape[0]
    value = jnp.dot(take(x_refs, z ^ 3, core, last.shape[0]), last[...], preferred_element_type=jnp.float32)
    value = [acc_in[...] + value[:early], acc_diagonal[...] + value[early:]]
    value = jnp.concatenate(value, axis=0).astype(jnp.bfloat16)
    for rel in range(2):
        at = pl.ds(pl.multiple_of((core ^ rel) * block, block), block)
        for r in range(4):
            row = ROW_ORDER[rel][r]
            mine = value[row * block : (row + 1) * block]
            v_at = V_ORDER.index(r)
            q_ref[r, at, :] = mine[:, :HD]
            k_ref[r, at, :] = mine[:, HD:PAIR]
            (v_first, v_second)[v_at // 3][v_at % 3, at, :] = mine[:, PAIR:]


def spans(u):
    return ((0, u, 2), (1, 0, 2), (2, 0, 1 + u))


def neighbours(outer, own, middle, index):
    z, _, _ = where_am_i()
    odd = (z & 1) == 1
    outer, middle = outer[index], middle[index]
    return jnp.where(odd, outer, middle), own[index], jnp.where(odd, middle, outer)


def weigh_kernel(q_ref, outer, own, middle, own_flags, received, out_ref):
    _, core, _ = where_am_i()
    block = q_ref.shape[1] // 2
    inv_root = 1.0 / math.sqrt(HD)
    flags = [own_flags[:, :HD].astype(jnp.float32), received[-EXTRA:, :HD].astype(jnp.float32)]
    flags = [jnp.where(core == u, flags[0], flags[1]) for u in range(2)]
    bias = [(f - 1.0) * 1e30 for f in flags]
    for r in range(4):
        keys = neighbours(outer, own, middle, r)
        for u in range(2):
            q = q_ref[r, u * block : (u + 1) * block]
            scores = []
            for side, first, last in spans(u):
                k = keys[side][first * block : last * block]
                s = lax.dot_general(q, k, (((1,), (1,)), ((), ())), preferred_element_type=jnp.float32)
                for v in range(last - first):
                    entry = len(scores)
                    shut = jnp.broadcast_to(bias[u][r : r + 1, entry : entry + 1], (block, block))
                    scores.append(s[:, v * block : (v + 1) * block] * inv_root + shut)
            top = jnp.max(functools.reduce(jnp.maximum, scores), axis=1, keepdims=True)
            powers = [jnp.exp(s - top) for s in scores]
            inverse = 1.0 / jnp.sum(functools.reduce(jnp.add, powers), axis=1, keepdims=True)
            for entry, p in enumerate(powers):
                here = slice(entry * block, (entry + 1) * block)
                out_ref[r, u * block : (u + 1) * block, here] = (p * inverse).astype(jnp.bfloat16)


def mix_kernel(r, weights, outer, own, middle, out_ref):
    block = weights.shape[1] // 2
    values = neighbours(outer, own, middle, V_ORDER.index(r) % 3)
    for u in range(2):
        w = weights[r, u * block : (u + 1) * block]
        v = [values[side][first * block : last * block] for side, first, last in spans(u)]
        result = jnp.dot(w, jnp.concatenate(v, axis=0), preferred_element_type=jnp.float32)
        out_ref[u * block : (u + 1) * block] = result.astype(jnp.bfloat16)


def pack_kernel(*refs):
    keep_ref, send_ref = refs[4:]
    _, core, _ = where_am_i()
    block = keep_ref.shape[1]
    for r, ref in enumerate(refs[:4]):
        for rel, out_ref in enumerate((keep_ref, send_ref)):
            out_ref[r] = ref[pl.ds(pl.multiple_of((core ^ rel) * block, block), block), :]


def gather_kernel(mine, other, out_ref):
    _, core, depth = where_am_i()
    for rel, ref in enumerate((mine, other)):
        for r in range(4):
            at = pl.multiple_of((2 * (depth ^ r) + (core ^ rel)) * HD, HD)
            out_ref[:, pl.ds(at, HD)] = ref[r]


def call(kernel, outs, places, scratch=(), macs=0, limit=32):
    spaces = {"v": VMEM}
    return pl.pallas_call(
        kernel,
        out_shape=outs,
        in_specs=[pl.BlockSpec(memory_space=spaces[place]) for place in places],
        out_specs=jax.tree.map(lambda _: pl.BlockSpec(memory_space=VMEM), outs),
        scratch_shapes=list(scratch),
        cost_estimate=pl.CostEstimate(flops=2 * macs, bytes_accessed=0, transcendentals=0),
        compiler_params=pltpu.CompilerParams(vmem_limit_bytes=limit * 2**20),
    )


def plane_device(raw, stream, conv_w, gain, w_qkv, mask):
    time_len, site_len, feat_len = raw.shape
    block, width = time_len * site_len, stream.shape[2]
    half, size = width // 2, w_qkv.shape[0]
    bf16, f32 = jnp.bfloat16, jnp.float32

    def array(*shape, kind=bf16):
        return jax.ShapeDtypeStruct(shape, kind)

    far_raw = swap_z(w_qkv, 2)

    mask_row = jnp.pad(mask.reshape(1, mask.shape[2]), ((0, 0), (0, feat_len - mask.shape[2]))).astype(bf16)
    raw = jnp.concatenate([raw.reshape(block, feat_len), jnp.broadcast_to(mask_row, (EXTRA, feat_len))], axis=0)
    stream = stream.reshape(block, width)
    conv_w, gain = conv_w.reshape(3 * feat_len, width), gain.reshape(1, width)
    more = block // 2 + EXTRA
    *to, kept = call(
        split_kernel,
        (array(size + more, PAIR), array(size + more, PAIR), array(block, PAIR), array(size, PAIR)),
        "vv",
    )(w_qkv, raw)
    plane = [swap_depth(t, r) for t, r in zip(to, (1, 2, 3))]
    own = call(sort_kernel, array(size, 6 * HD), "vvv")(kept, *plane[:2])
    near = swap_z(own, 1)

    def embed(rs, *streams, finished=()):
        out = (array((len(rs) + len(finished)) * block, width),) + (array(block, half),) * (len(rs) - 1) * 2
        return call(
            functools.partial(embed_kernel, rs, len(finished)),
            out,
            "v" * (6 + len(streams) + len(finished)),
            scratch=[VMEM((block, width), f32)],
            macs=len(rs) * block * 3 * feat_len * width,
        )(raw, *plane, conv_w, gain, *streams, *finished)

    tied = after(stream, plane[2])
    beside, above = swap_depth(tied, 1), swap_depth(tied, 2)
    (normed,) = embed((0,), stream)
    far_raw = after(far_raw, normed)

    even = (lax.axis_index("depth") & 1) == 0
    low, to_x, high = (far_raw[:, k * PAIR : (k + 1) * PAIR] for k in range(3))
    kept, to_y = jnp.where(even, low, high), jnp.where(even, high, low)
    from_x, from_y = swap_depth(to_x, 1), swap_depth(to_y, 2)
    beside, above = after(beside, to_x), after(above, to_y)
    stack, *diagonal = embed((1, 2), beside, above, finished=(normed,))
    from_x, from_y, stack, near = lax.optimization_barrier((from_x, from_y, stack, near))
    keep, send, flags = call(
        sort_far_kernel,
        (array(size, 3 * HD), array(size, 3 * HD), array(EXTRA, 3 * HD)),
        "v" * 7,
    )(kept, from_x, from_y, *plane, raw)
    diagonal = swap_depth(diagonal[0], 2), swap_depth(diagonal[1], 1)
    far = jnp.concatenate([keep, swap_core(send)], axis=0)
    last = swap_z(far, 1)
    far, near, stack = lax.optimization_barrier((far, near, stack))
    received = swap_core(jnp.concatenate([own[:, 3 * HD :], near[:, 3 * HD :], flags], axis=0))
    weights = (own, near, received, far)
    piece = 5 * block // 8
    early = (stack, swap_core(stack))
    rows = 2 * size
    total = call(partial_kernel, array(6 * block, 3 * HD, kind=f32), "v" * 6, macs=6 * block * 3 * rows * 3 * HD)(
        *early, *weights
    )
    (diagonal,) = embed((3,), jnp.concatenate([after(t, total) for t in diagonal], axis=1))
    swapped = [swap_core(diagonal[:piece]), swap_core(diagonal[piece:])]
    total_diagonal, diagonal = call(
        diagonal_kernel,
        (array(2 * block, 3 * HD, kind=f32), array(2 * block, width)),
        "v" * 7,
        macs=2 * block * 3 * rows * 3 * HD,
    )(diagonal, *swapped, *weights)
    one_head = array(4, 2 * block, HD)
    q, k, *v = call(
        finish_kernel, (one_head, one_head, array(3, 2 * block, HD), array(1, 2 * block, HD)), "v" * 6, macs=8 * block * rows * 3 * HD
    )(*early, diagonal, last, total, total_diagonal)

    weights = call(weigh_kernel, array(4, 2 * block, 5 * block), "v" * 6, macs=8 * block * 5 * block * HD)(
        q, swap_z(k, 1), k, swap_middle(k), flags, received
    )
    values = [(swap_z(t, 1), t, swap_middle(t)) for t in v]
    pieces = {}
    for i, r in enumerate(V_ORDER):
        mixed = call(functools.partial(mix_kernel, r), array(2 * block, HD), "vvvv", macs=2 * block * 5 * block * HD)(
            weights, *values[i // 3]
        )
        pieces[r] = swap_depth(mixed, r) if r else mixed
    kept, sent = call(pack_kernel, (array(4, block, HD),) * 2, "vvvv")(*[pieces[r] for r in range(4)])
    context = call(gather_kernel, array(block, HEADS * HD), "vv")(kept, swap_core(sent))
    return context.reshape(time_len, site_len, HEADS * HD)


def from_behind(value, axis, by):
    devices = lax.axis_size(axis)
    pairs = [(i, i + by) for i in range(devices) if 0 <= i + by < devices]
    return lax.ppermute(value, axis, pairs)


def head_attend(query_head, key_head, value_head, allowed):
    inv_root = 1.0 / math.sqrt(HD)
    scores = (
        jnp.einsum("qd,kd->qk", query_head, key_head, preferred_element_type=jnp.float32) * inv_root
    )
    scores = jnp.where(allowed, scores, -1e30)
    row_max = jnp.max(scores, axis=-1, keepdims=True)
    powers = jnp.exp(scores - row_max)
    weights = (powers / jnp.sum(powers, axis=-1, keepdims=True)).astype(jnp.bfloat16)
    return jnp.dot(weights, value_head, preferred_element_type=jnp.float32).astype(jnp.bfloat16)


def per_device(raw, stream, conv_w, gain, w_qkv, mask):
    time_len, site_len, _ = raw.shape
    tok_rows = time_len * site_len
    normed = normed_tokens(padded_2(raw, (("depth", 1),), 1), stream, conv_w, gain)
    columns = lax.all_gather(w_qkv, "depth", axis=1, tiled=True)
    projected = jnp.dot(
        normed,
        lax.all_gather(columns, "tm", axis=0, tiled=True),
        preferred_element_type=jnp.float32,
    ).astype(jnp.bfloat16)
    head_cols = projected.shape[1] // 3
    queries = projected[:, :head_cols]
    keyvals = projected[:, head_cols:]
    earlier = []
    later = []
    moving_back = keyvals
    moving_ahead = keyvals
    for hop_index in range(RD):
        moving_back = from_behind(moving_back, "tm", 1)
        moving_ahead = from_behind(moving_ahead, "tm", -1)
        earlier.insert(0, moving_back)
        later.append(moving_ahead)
    gathered = jnp.concatenate(earlier + [keyvals] + later, axis=0)
    block_rows = BT * PP
    own_blocks = tok_rows // block_rows
    span_blocks = gathered.shape[0] // block_rows
    local_mask = mask[0]
    query_ids = jnp.arange(own_blocks, dtype=jnp.int32)[:, None]
    key_ids = jnp.arange(span_blocks, dtype=jnp.int32)[None, :]
    entry_ids = key_ids - query_ids
    picks = entry_ids[:, :, None] == jnp.arange(local_mask.shape[1], dtype=jnp.int32)[None, None, :]
    block_allowed = jnp.sum(jnp.where(picks, local_mask[:, None, :], 0), axis=-1) > 0
    allowed = jnp.repeat(jnp.repeat(block_allowed, block_rows, axis=0), block_rows, axis=1)
    query_heads = queries.reshape(tok_rows, HEADS, HD).transpose(1, 0, 2)
    key_heads = gathered[:, :head_cols].reshape(gathered.shape[0], HEADS, HD).transpose(1, 0, 2)
    value_heads = gathered[:, head_cols:].reshape(gathered.shape[0], HEADS, HD).transpose(1, 0, 2)
    context = lax.map(
        lambda operands: head_attend(operands[0], operands[1], operands[2], allowed),
        (query_heads, key_heads, value_heads),
    )
    return context.transpose(1, 0, 2).reshape(time_len, site_len, head_cols)


def solution(mesh):
    in_specs = (
        P("tm", "depth", None),
        P("tm", "depth", None),
        P(),
        P(),
        P("tm", "depth"),
        P("depth", "tm", None),
    )
    out_specs = P("tm", "depth", None)
    fits = mesh.shape["depth"] == 4 and mesh.shape["tm"] == 8
    return jax.shard_map(
        plane_device if fits else per_device, mesh=mesh, in_specs=in_specs, out_specs=out_specs, check_vma=False
    )
```

```python
import functools
import math

import jax
import jax.numpy as jnp
from jax import lax
from jax.experimental import pallas as pl
from jax.experimental.pallas import tpu as pltpu
from jax.sharding import PartitionSpec as P

HEADS = 8
HD = 128
BT = 16
PP = 8
RD = 2
VMEM = pltpu.VMEM
SMEM = pltpu.SMEM


def padded_2(value, sides, width):
    for axis, dim in sides:
        devices, length = (lax.axis_size(axis), value.shape[dim])
        up = [(i, (i + 1) % devices) for i in range(devices - 1)]
        down = [(j, i) for i, j in up]
        last = lax.slice_in_dim(value, length - width, length, axis=dim)
        leading = lax.slice_in_dim(value, 0, width, axis=dim)
        before = lax.ppermute(last, axis, up)
        after = lax.ppermute(leading, axis, down)
        value = jnp.concatenate([before, value, after], axis=dim)
    return value


def normed_tokens(padded, stream, conv_w, gain):
    time_len, site_len, width = stream.shape
    tok_rows = time_len * site_len
    embedded = stream.reshape(tok_rows, width).astype(jnp.float32)
    for offset in range(3):
        window = padded[:, offset : offset + site_len].reshape(tok_rows, padded.shape[2])
        embedded = embedded + jnp.dot(window, conv_w[offset], preferred_element_type=jnp.float32)
    scale = lax.rsqrt(jnp.mean(embedded * embedded, axis=-1, keepdims=True) + 1e-05)
    return (embedded * scale * gain).astype(jnp.bfloat16)


PAIR = 2 * HD
V_ORDER = (3, 1, 2, 0)
EXTRA = 16


def hop(value, fn):
    pairs = []
    for z in range(4):
        for core in range(2):
            for depth in range(4):
                to = fn(z, core, depth)
                if to is not None:
                    pairs.append(((2 * z + core) * 4 + depth, (2 * to[0] + to[1]) * 4 + to[2]))
    return lax.ppermute(value, ("tm", "depth"), pairs)


def swap_core(value):
    return hop(value, lambda z, c, d: (z, 1 - c, d))


def swap_depth(value, bits):
    return hop(value, lambda z, c, d: (z, c, d ^ bits))


def swap_z(value, bits):
    return hop(value, lambda z, c, d: (z ^ bits, c, d))


def swap_middle(value):
    return hop(value, lambda z, c, d: (z ^ 3, c, d) if z in (1, 2) else None)


def after(value, *others):
    return lax.optimization_barrier((value, *others))[0]


def where_am_i():
    tm = lax.axis_index("tm")
    return tm >> 1, tm & 1, lax.axis_index("depth")


def split_kernel(w, raw, to_x, to_y, to_across, keep):
    _, _, depth = where_am_i()
    even = (depth & 1) == 0
    size, half = w.shape[0], (raw.shape[0] - EXTRA) // 2
    low, high = w[:, :PAIR], w[:, 2 * PAIR :]
    to_x[:size] = w[:, PAIR : 2 * PAIR]
    to_y[:size] = jnp.where(even, high, low)
    keep[...] = jnp.where(even, low, high)
    at = to_across.shape[0] - EXTRA - half
    for i in range(2):
        to_across[:at, i * HD : (i + 1) * HD] = raw[:at]
    for ref, at in ((to_x, size), (to_y, size), (to_across, at)):
        for i in range(2):
            here = slice(i * HD, (i + 1) * HD)
            ref[at : at + half, here] = raw[i * half : (i + 1) * half]
            ref[at + half :, here] = raw[2 * half :]


def sorted_groups(kept, from_x, from_y):
    _, core, depth = where_am_i()
    first, even = core == 0, (depth & 1) == 0
    size = kept.shape[0]
    low = jnp.where(even, kept[...], from_y[:size])
    high = jnp.where(even, from_y[:size], kept[...])
    groups = (low, from_x[:size], high)
    turn = jnp.where(depth == 3, 0, depth)
    for third in range(3):
        group = jnp.where(turn == 0, groups[third], jnp.where(turn == 1, groups[(third + 1) % 3], groups[(third + 2) % 3]))
        yield third, jnp.where(first, group[:, :HD], group[:, HD:]), jnp.where(first, group[:, HD:], group[:, :HD])


def sort_kernel(kept, from_x, from_y, out_ref):
    for third, mine, other in sorted_groups(kept, from_x, from_y):
        out_ref[:, third * HD : (third + 1) * HD] = mine
        out_ref[:, (3 + third) * HD : (4 + third) * HD] = other


def sort_far_kernel(kept, from_x, from_y, plane_x, plane_y, across, raw, keep_ref, send_ref, flags_ref):
    for third, mine, other in sorted_groups(kept, from_x, from_y):
        send_ref[:, third * HD : (third + 1) * HD] = other
        keep_ref[:, third * HD : (third + 1) * HD] = mine
    row = lax.broadcasted_iota(jnp.int32, (EXTRA, HD), 0)
    flags = raw[raw.shape[0] - EXTRA :].astype(jnp.float32)
    for r, ref in enumerate((plane_x, plane_y, across)):
        flags = jnp.where(row == r + 1, ref[ref.shape[0] - EXTRA :, :HD].astype(jnp.float32), flags)
    flags = flags.astype(jnp.bfloat16)
    for k in range(3):
        flags_ref[:, k * HD : (k + 1) * HD] = flags


def embed_kernel(rs, more, raw, plane_x, plane_y, across, conv_w, gain, *refs):
    count = len(rs)
    streams, finished, (out_ref, *onward, acc) = refs[:count], refs[count : count + more], refs[count + more :]
    for ref in finished:
        out_ref[: ref.shape[0]] = ref[...]
    for i, ref in enumerate(onward):
        half = ref.shape[1]
        ref[...] = streams[i][:, i * half : (i + 1) * half]
    _, _, depth = where_am_i()
    rows, width = raw.shape[0] - EXTRA, conv_w.shape[1]
    raws = [raw[:rows]]
    for ref in (plane_x, plane_y, across):
        at = ref.shape[0] - EXTRA - rows // 2
        raws.append(jnp.concatenate([ref[at : at + rows // 2, :HD], ref[at : at + rows // 2, HD:]], axis=0))
    raws = [value.astype(jnp.float32).reshape(rows // PP, PP, HD) for value in raws]
    done = out_ref.shape[0] - len(rs) * rows
    for i, r in enumerate(rs):
        place = depth ^ r
        even = (place & 1) == 0
        side, far = raws[r ^ 1], raws[r ^ 3]
        before = jnp.where(even, jnp.where(place == 2, far[:, PP - 1 :], 0.0), side[:, PP - 1 :])
        behind = jnp.where(even, side[:, :1], jnp.where(place == 1, far[:, :1], 0.0))
        padded = jnp.concatenate([before, raws[r], behind], axis=1)
        windows = [padded[:, j : j + PP].reshape(rows, HD).astype(jnp.bfloat16) for j in range(3)]
        windows = jnp.concatenate(windows, axis=1)
        total, step = jnp.zeros((rows, 1), jnp.float32), width // 4
        for at in range(0, width, step):
            here = slice(at, at + step)
            part = jnp.dot(windows, conv_w[:, here], preferred_element_type=jnp.float32)
            part += streams[i][:, here].astype(jnp.float32)
            acc[:, here] = part
            total += jnp.sum(part * part, axis=1, keepdims=True)
        scale = lax.rsqrt(total / width + 1e-05)
        out_ref[done + i * rows : done + (i + 1) * rows] = (acc[...] * scale * gain[...]).astype(jnp.bfloat16)


def take(refs, source, core, rows):
    half = rows // 2
    cuts = [pl.ds(pl.multiple_of(source * rows + c * half, half), half) for c in (core, 1 - core)]
    return jnp.concatenate([jnp.concatenate([ref[:, at] for at in cuts], axis=1) for ref in refs], axis=0)


def three_shards(x_refs, own, near, received, far):
    z, core, _ = where_am_i()
    size, width = own.shape[0], 3 * HD
    w = [own[:, :width], received[:size], far[...]]
    w = jnp.concatenate(w + [near[:, :width], received[size : 2 * size]], axis=0)
    x = [take(x_refs, source, core, 2 * size) for source in (z, z ^ 2, z ^ 1)]
    return jnp.dot(jnp.concatenate(x, axis=1), w, preferred_element_type=jnp.float32)


def partial_kernel(*refs):
    refs[-1][...] = three_shards(refs[:2], *refs[2:-1])


def diagonal_kernel(mine, top, bottom, *refs):
    weights, (acc_ref, x_ref) = refs[:-2], refs[-2:]
    at = 0
    for ref in (mine, top, bottom):
        x_ref[at : at + ref.shape[0]] = ref[...]
        at += ref.shape[0]
    acc_ref[...] = three_shards([x_ref], *weights)


ROW_ORDER = ((0, 1, 2, 6), (3, 4, 5, 7))


def finish_kernel(*refs):
    x_refs, (last, acc_in, acc_diagonal, q_ref, k_ref, v_first, v_second) = refs[:3], refs[3:]
    z, core, _ = where_am_i()
    block, early = q_ref.shape[1] // 2, acc_in.shape[0]
    value = jnp.dot(take(x_refs, z ^ 3, core, last.shape[0]), last[...], preferred_element_type=jnp.float32)
    value = [acc_in[...] + value[:early], acc_diagonal[...] + value[early:]]
    value = jnp.concatenate(value, axis=0).astype(jnp.bfloat16)
    for rel in range(2):
        at = pl.ds(pl.multiple_of((core ^ rel) * block, block), block)
        for r in range(4):
            row = ROW_ORDER[rel][r]
            mine = value[row * block : (row + 1) * block]
            v_at = V_ORDER.index(r)
            q_ref[r, at, :] = mine[:, :HD]
            k_ref[r, at, :] = mine[:, HD:PAIR]
            (v_first, v_second)[v_at // 3][v_at % 3, at, :] = mine[:, PAIR:]


def spans(u):
    return ((0, u, 2), (1, 0, 2), (2, 0, 1 + u))


def neighbours(outer, own, middle, index):
    z, _, _ = where_am_i()
    odd = (z & 1) == 1
    outer, middle = outer[index], middle[index]
    return jnp.where(odd, outer, middle), own[index], jnp.where(odd, middle, outer)


def weigh_kernel(q_ref, middle, own, outer, own_flags, received, out_ref):
    _, core, _ = where_am_i()
    block = q_ref.shape[1] // 2
    inv_root = 1.0 / math.sqrt(HD)
    flags = [own_flags[:, :HD].astype(jnp.float32), received[-EXTRA:, :HD].astype(jnp.float32)]
    flags = [jnp.where(core == u, flags[0], flags[1]) for u in range(2)]
    bias = [(f - 1.0) * 1e30 for f in flags]
    for r in range(4):
        keys = neighbours(outer, own, middle, r)
        for u in range(2):
            q = q_ref[r, u * block : (u + 1) * block]
            scores = []
            for side, first, last in spans(u):
                k = keys[side][first * block : last * block]
                s = lax.dot_general(q, k, (((1,), (1,)), ((), ())), preferred_element_type=jnp.float32)
                for v in range(last - first):
                    entry = len(scores)
                    shut = jnp.broadcast_to(bias[u][r : r + 1, entry : entry + 1], (block, block))
                    scores.append(s[:, v * block : (v + 1) * block] * inv_root + shut)
            top = jnp.max(functools.reduce(jnp.maximum, scores), axis=1, keepdims=True)
            powers = [jnp.exp(s - top) for s in scores]
            inverse = 1.0 / jnp.sum(functools.reduce(jnp.add, powers), axis=1, keepdims=True)
            for entry, p in enumerate(powers):
                here = slice(entry * block, (entry + 1) * block)
                out_ref[r, u * block : (u + 1) * block, here] = (p * inverse).astype(jnp.bfloat16)


def mix_kernel(r, weights, middle, own, outer, out_ref):
    block = weights.shape[1] // 2
    values = neighbours(outer, own, middle, V_ORDER.index(r) % 3)
    for u in range(2):
        w = weights[r, u * block : (u + 1) * block]
        v = [values[side][first * block : last * block] for side, first, last in spans(u)]
        result = jnp.dot(w, jnp.concatenate(v, axis=0), preferred_element_type=jnp.float32)
        out_ref[u * block : (u + 1) * block] = result.astype(jnp.bfloat16)


def pack_kernel(*refs):
    keep_ref, send_ref = refs[4:]
    _, core, _ = where_am_i()
    block = keep_ref.shape[1]
    for r, ref in enumerate(refs[:4]):
        for rel, out_ref in enumerate((keep_ref, send_ref)):
            out_ref[r] = ref[pl.ds(pl.multiple_of((core ^ rel) * block, block), block), :]


def gather_kernel(mine, other, out_ref):
    _, core, depth = where_am_i()
    for rel, ref in enumerate((mine, other)):
        for r in range(4):
            at = pl.multiple_of((2 * (depth ^ r) + (core ^ rel)) * HD, HD)
            out_ref[:, pl.ds(at, HD)] = ref[r]


def call(kernel, outs, places, scratch=(), macs=0, limit=32):
    spaces = {"v": VMEM}
    return pl.pallas_call(
        kernel,
        out_shape=outs,
        in_specs=[pl.BlockSpec(memory_space=spaces[place]) for place in places],
        out_specs=jax.tree.map(lambda _: pl.BlockSpec(memory_space=VMEM), outs),
        scratch_shapes=list(scratch),
        cost_estimate=pl.CostEstimate(flops=2 * macs, bytes_accessed=0, transcendentals=0),
        compiler_params=pltpu.CompilerParams(vmem_limit_bytes=limit * 2**20),
    )


def plane_device(raw, stream, conv_w, gain, w_qkv, mask):
    time_len, site_len, feat_len = raw.shape
    block, width = time_len * site_len, stream.shape[2]
    half, size = width // 2, w_qkv.shape[0]
    bf16, f32 = jnp.bfloat16, jnp.float32

    def array(*shape, kind=bf16):
        return jax.ShapeDtypeStruct(shape, kind)

    far_raw = swap_z(w_qkv, 2)

    mask_row = jnp.pad(mask.reshape(1, mask.shape[2]), ((0, 0), (0, feat_len - mask.shape[2]))).astype(bf16)
    raw = jnp.concatenate([raw.reshape(block, feat_len), jnp.broadcast_to(mask_row, (EXTRA, feat_len))], axis=0)
    stream = stream.reshape(block, width)
    conv_w, gain = conv_w.reshape(3 * feat_len, width), gain.reshape(1, width)
    more = block // 2 + EXTRA
    *to, kept = call(
        split_kernel,
        (array(size + more, PAIR), array(size + more, PAIR), array(block, PAIR), array(size, PAIR)),
        "vv",
    )(w_qkv, raw)
    plane = [swap_depth(t, r) for t, r in zip(to, (1, 2, 3))]
    own = call(sort_kernel, array(size, 6 * HD), "vvv")(kept, *plane[:2])
    near = swap_z(own, 1)

    def embed(rs, *streams, finished=()):
        out = (array((len(rs) + len(finished)) * block, width),) + (array(block, half),) * (len(rs) - 1) * 2
        return call(
            functools.partial(embed_kernel, rs, len(finished)),
            out,
            "v" * (6 + len(streams) + len(finished)),
            scratch=[VMEM((block, width), f32)],
            macs=len(rs) * block * 3 * feat_len * width,
        )(raw, *plane, conv_w, gain, *streams, *finished)

    tied = after(stream, plane[2])
    beside, above = swap_depth(tied, 1), swap_depth(tied, 2)
    (normed,) = embed((0,), stream)
    far_raw = after(far_raw, normed)

    even = (lax.axis_index("depth") & 1) == 0
    low, to_x, high = (far_raw[:, k * PAIR : (k + 1) * PAIR] for k in range(3))
    kept, to_y = jnp.where(even, low, high), jnp.where(even, high, low)
    from_x, from_y = swap_depth(to_x, 1), swap_depth(to_y, 2)
    beside, above = after(beside, to_x), after(above, to_y)
    stack, *diagonal = embed((1, 2), beside, above, finished=(normed,))
    from_x, from_y, stack, near = lax.optimization_barrier((from_x, from_y, stack, near))
    keep, send, flags = call(
        sort_far_kernel,
        (array(size, 3 * HD), array(size, 3 * HD), array(EXTRA, 3 * HD)),
        "v" * 7,
    )(kept, from_x, from_y, *plane, raw)
    diagonal = swap_depth(diagonal[0], 2), swap_depth(diagonal[1], 1)
    far = jnp.concatenate([keep, swap_core(send)], axis=0)
    last = swap_z(far, 1)
    far, near, stack = lax.optimization_barrier((far, near, stack))
    received = swap_core(jnp.concatenate([own[:, 3 * HD :], near[:, 3 * HD :], flags], axis=0))
    weights = (own, near, received, far)
    piece = 5 * block // 8
    early = (stack, swap_core(stack))
    rows = 2 * size
    total = call(partial_kernel, array(6 * block, 3 * HD, kind=f32), "v" * 6, macs=6 * block * 3 * rows * 3 * HD)(
        *early, *weights
    )
    (diagonal,) = embed((3,), jnp.concatenate([after(t, total) for t in diagonal], axis=1))
    swapped = [swap_core(diagonal[:piece]), swap_core(diagonal[piece:])]
    total_diagonal, diagonal = call(
        diagonal_kernel,
        (array(2 * block, 3 * HD, kind=f32), array(2 * block, width)),
        "v" * 7,
        macs=2 * block * 3 * rows * 3 * HD,
    )(diagonal, *swapped, *weights)
    one_head = array(4, 2 * block, HD)
    q, k, *v = call(
        finish_kernel, (one_head, one_head, array(3, 2 * block, HD), array(1, 2 * block, HD)), "v" * 6, macs=8 * block * rows * 3 * HD
    )(*early, diagonal, last, total, total_diagonal)

    middle = swap_middle(k)
    outer = swap_z(k, 1)
    weights = call(weigh_kernel, array(4, 2 * block, 5 * block), "v" * 6, macs=8 * block * 5 * block * HD)(
        q, middle, k, outer, flags, received
    )
    values = []
    for t in v:
        middle = swap_middle(t)
        values.append((middle, t, swap_z(t, 1)))
    pieces = {}
    for i, r in enumerate(V_ORDER):
        mixed = call(functools.partial(mix_kernel, r), array(2 * block, HD), "vvvv", macs=2 * block * 5 * block * HD)(
            weights, *values[i // 3]
        )
        pieces[r] = swap_depth(mixed, r) if r else mixed
    kept, sent = call(pack_kernel, (array(4, block, HD),) * 2, "vvvv")(*[pieces[r] for r in range(4)])
    context = call(gather_kernel, array(block, HEADS * HD), "vv")(kept, swap_core(sent))
    return context.reshape(time_len, site_len, HEADS * HD)


def from_behind(value, axis, by):
    devices = lax.axis_size(axis)
    pairs = [(i, i + by) for i in range(devices) if 0 <= i + by < devices]
    return lax.ppermute(value, axis, pairs)


def head_attend(query_head, key_head, value_head, allowed):
    inv_root = 1.0 / math.sqrt(HD)
    scores = (
        jnp.einsum("qd,kd->qk", query_head, key_head, preferred_element_type=jnp.float32) * inv_root
    )
    scores = jnp.where(allowed, scores, -1e30)
    row_max = jnp.max(scores, axis=-1, keepdims=True)
    powers = jnp.exp(scores - row_max)
    weights = (powers / jnp.sum(powers, axis=-1, keepdims=True)).astype(jnp.bfloat16)
    return jnp.dot(weights, value_head, preferred_element_type=jnp.float32).astype(jnp.bfloat16)


def per_device(raw, stream, conv_w, gain, w_qkv, mask):
    time_len, site_len, _ = raw.shape
    tok_rows = time_len * site_len
    normed = normed_tokens(padded_2(raw, (("depth", 1),), 1), stream, conv_w, gain)
    columns = lax.all_gather(w_qkv, "depth", axis=1, tiled=True)
    projected = jnp.dot(
        normed,
        lax.all_gather(columns, "tm", axis=0, tiled=True),
        preferred_element_type=jnp.float32,
    ).astype(jnp.bfloat16)
    head_cols = projected.shape[1] // 3
    queries = projected[:, :head_cols]
    keyvals = projected[:, head_cols:]
    earlier = []
    later = []
    moving_back = keyvals
    moving_ahead = keyvals
    for hop_index in range(RD):
        moving_back = from_behind(moving_back, "tm", 1)
        moving_ahead = from_behind(moving_ahead, "tm", -1)
        earlier.insert(0, moving_back)
        later.append(moving_ahead)
    gathered = jnp.concatenate(earlier + [keyvals] + later, axis=0)
    block_rows = BT * PP
    own_blocks = tok_rows // block_rows
    span_blocks = gathered.shape[0] // block_rows
    local_mask = mask[0]
    query_ids = jnp.arange(own_blocks, dtype=jnp.int32)[:, None]
    key_ids = jnp.arange(span_blocks, dtype=jnp.int32)[None, :]
    entry_ids = key_ids - query_ids
    picks = entry_ids[:, :, None] == jnp.arange(local_mask.shape[1], dtype=jnp.int32)[None, None, :]
    block_allowed = jnp.sum(jnp.where(picks, local_mask[:, None, :], 0), axis=-1) > 0
    allowed = jnp.repeat(jnp.repeat(block_allowed, block_rows, axis=0), block_rows, axis=1)
    query_heads = queries.reshape(tok_rows, HEADS, HD).transpose(1, 0, 2)
    key_heads = gathered[:, :head_cols].reshape(gathered.shape[0], HEADS, HD).transpose(1, 0, 2)
    value_heads = gathered[:, head_cols:].reshape(gathered.shape[0], HEADS, HD).transpose(1, 0, 2)
    context = lax.map(
        lambda operands: head_attend(operands[0], operands[1], operands[2], allowed),
        (query_heads, key_heads, value_heads),
    )
    return context.transpose(1, 0, 2).reshape(time_len, site_len, head_cols)


def solution(mesh):
    in_specs = (
        P("tm", "depth", None),
        P("tm", "depth", None),
        P(),
        P(),
        P("tm", "depth"),
        P("depth", "tm", None),
    )
    out_specs = P("tm", "depth", None)
    fits = mesh.shape["depth"] == 4 and mesh.shape["tm"] == 8
    return jax.shard_map(
        plane_device if fits else per_device, mesh=mesh, in_specs=in_specs, out_specs=out_specs, check_vma=False
    )
```

```python
import functools
import math

import jax
import jax.numpy as jnp
from jax import lax
from jax.experimental import pallas as pl
from jax.experimental.pallas import tpu as pltpu
from jax.sharding import PartitionSpec as P

HEADS = 8
HD = 128
BT = 16
PP = 8
RD = 2
VMEM = pltpu.VMEM
SMEM = pltpu.SMEM


def padded_2(value, sides, width):
    for axis, dim in sides:
        devices, length = (lax.axis_size(axis), value.shape[dim])
        up = [(i, (i + 1) % devices) for i in range(devices - 1)]
        down = [(j, i) for i, j in up]
        last = lax.slice_in_dim(value, length - width, length, axis=dim)
        leading = lax.slice_in_dim(value, 0, width, axis=dim)
        before = lax.ppermute(last, axis, up)
        after = lax.ppermute(leading, axis, down)
        value = jnp.concatenate([before, value, after], axis=dim)
    return value


def normed_tokens(padded, stream, conv_w, gain):
    time_len, site_len, width = stream.shape
    tok_rows = time_len * site_len
    embedded = stream.reshape(tok_rows, width).astype(jnp.float32)
    for offset in range(3):
        window = padded[:, offset : offset + site_len].reshape(tok_rows, padded.shape[2])
        embedded = embedded + jnp.dot(window, conv_w[offset], preferred_element_type=jnp.float32)
    scale = lax.rsqrt(jnp.mean(embedded * embedded, axis=-1, keepdims=True) + 1e-05)
    return (embedded * scale * gain).astype(jnp.bfloat16)


PAIR = 2 * HD
V_ORDER = (3, 1, 2, 0)
EXTRA = 16


def hop(value, fn):
    pairs = []
    for z in range(4):
        for core in range(2):
            for depth in range(4):
                to = fn(z, core, depth)
                if to is not None:
                    pairs.append(((2 * z + core) * 4 + depth, (2 * to[0] + to[1]) * 4 + to[2]))
    return lax.ppermute(value, ("tm", "depth"), pairs)


def swap_core(value):
    return hop(value, lambda z, c, d: (z, 1 - c, d))


def swap_depth(value, bits):
    return hop(value, lambda z, c, d: (z, c, d ^ bits))


def swap_z(value, bits):
    return hop(value, lambda z, c, d: (z ^ bits, c, d))


def swap_middle(value):
    return hop(value, lambda z, c, d: (z ^ 3, c, d) if z in (1, 2) else None)


def after(value, *others):
    return lax.optimization_barrier((value, *others))[0]


def where_am_i():
    tm = lax.axis_index("tm")
    return tm >> 1, tm & 1, lax.axis_index("depth")


def split_kernel(w, raw, to_x, to_y, to_across, keep):
    _, _, depth = where_am_i()
    even = (depth & 1) == 0
    size, half = w.shape[0], (raw.shape[0] - EXTRA) // 2
    low, high = w[:, :PAIR], w[:, 2 * PAIR :]
    to_x[:size] = w[:, PAIR : 2 * PAIR]
    to_y[:size] = jnp.where(even, high, low)
    keep[...] = jnp.where(even, low, high)
    at = to_across.shape[0] - EXTRA - half
    for i in range(2):
        to_across[:at, i * HD : (i + 1) * HD] = raw[:at]
    for ref, at in ((to_x, size), (to_y, size), (to_across, at)):
        for i in range(2):
            here = slice(i * HD, (i + 1) * HD)
            ref[at : at + half, here] = raw[i * half : (i + 1) * half]
            ref[at + half :, here] = raw[2 * half :]


def sorted_groups(kept, from_x, from_y):
    _, core, depth = where_am_i()
    first, even = core == 0, (depth & 1) == 0
    size = kept.shape[0]
    low = jnp.where(even, kept[...], from_y[:size])
    high = jnp.where(even, from_y[:size], kept[...])
    groups = (low, from_x[:size], high)
    turn = jnp.where(depth == 3, 0, depth)
    for third in range(3):
        group = jnp.where(turn == 0, groups[third], jnp.where(turn == 1, groups[(third + 1) % 3], groups[(third + 2) % 3]))
        yield third, jnp.where(first, group[:, :HD], group[:, HD:]), jnp.where(first, group[:, HD:], group[:, :HD])


def sort_kernel(kept, from_x, from_y, out_ref):
    for third, mine, other in sorted_groups(kept, from_x, from_y):
        out_ref[:, third * HD : (third + 1) * HD] = mine
        out_ref[:, (3 + third) * HD : (4 + third) * HD] = other


def sort_far_kernel(kept, from_x, from_y, plane_x, plane_y, across, raw, keep_ref, send_ref, flags_ref):
    for third, mine, other in sorted_groups(kept, from_x, from_y):
        send_ref[:, third * HD : (third + 1) * HD] = other
        keep_ref[:, third * HD : (third + 1) * HD] = mine
    row = lax.broadcasted_iota(jnp.int32, (EXTRA, HD), 0)
    flags = raw[raw.shape[0] - EXTRA :].astype(jnp.float32)
    for r, ref in enumerate((plane_x, plane_y, across)):
        flags = jnp.where(row == r + 1, ref[ref.shape[0] - EXTRA :, :HD].astype(jnp.float32), flags)
    flags = flags.astype(jnp.bfloat16)
    for k in range(3):
        flags_ref[:, k * HD : (k + 1) * HD] = flags


def embed_kernel(rs, more, raw, plane_x, plane_y, across, conv_w, gain, *refs):
    count = len(rs)
    streams, finished, (out_ref, *onward, acc) = refs[:count], refs[count : count + more], refs[count + more :]
    for ref in finished:
        out_ref[: ref.shape[0]] = ref[...]
    for i, ref in enumerate(onward):
        half = ref.shape[1]
        ref[...] = streams[i][:, i * half : (i + 1) * half]
    _, _, depth = where_am_i()
    rows, width = raw.shape[0] - EXTRA, conv_w.shape[1]
    raws = [raw[:rows]]
    for ref in (plane_x, plane_y, across):
        at = ref.shape[0] - EXTRA - rows // 2
        raws.append(jnp.concatenate([ref[at : at + rows // 2, :HD], ref[at : at + rows // 2, HD:]], axis=0))
    raws = [value.astype(jnp.float32).reshape(rows // PP, PP, HD) for value in raws]
    done = out_ref.shape[0] - len(rs) * rows
    for i, r in enumerate(rs):
        place = depth ^ r
        even = (place & 1) == 0
        side, far = raws[r ^ 1], raws[r ^ 3]
        before = jnp.where(even, jnp.where(place == 2, far[:, PP - 1 :], 0.0), side[:, PP - 1 :])
        behind = jnp.where(even, side[:, :1], jnp.where(place == 1, far[:, :1], 0.0))
        padded = jnp.concatenate([before, raws[r], behind], axis=1)
        windows = [padded[:, j : j + PP].reshape(rows, HD).astype(jnp.bfloat16) for j in range(3)]
        windows = jnp.concatenate(windows, axis=1)
        total, step = jnp.zeros((rows, 1), jnp.float32), width // 4
        for at in range(0, width, step):
            here = slice(at, at + step)
            part = jnp.dot(windows, conv_w[:, here], preferred_element_type=jnp.float32)
            part += streams[i][:, here].astype(jnp.float32)
            acc[:, here] = part
            total += jnp.sum(part * part, axis=1, keepdims=True)
        scale = lax.rsqrt(total / width + 1e-05)
        out_ref[done + i * rows : done + (i + 1) * rows] = (acc[...] * scale * gain[...]).astype(jnp.bfloat16)


def take(refs, source, core, rows):
    half = rows // 2
    cuts = [pl.ds(pl.multiple_of(source * rows + c * half, half), half) for c in (core, 1 - core)]
    return jnp.concatenate([jnp.concatenate([ref[:, at] for at in cuts], axis=1) for ref in refs], axis=0)


def three_shards(x_refs, own, near, received, far):
    z, core, _ = where_am_i()
    size, width = own.shape[0], 3 * HD
    w = [own[:, :width], received[:size], far[...]]
    w = jnp.concatenate(w + [near[:, :width], received[size : 2 * size]], axis=0)
    x = [take(x_refs, source, core, 2 * size) for source in (z, z ^ 2, z ^ 1)]
    return jnp.dot(jnp.concatenate(x, axis=1), w, preferred_element_type=jnp.float32)


def partial_kernel(*refs):
    refs[-1][...] = three_shards(refs[:2], *refs[2:-1])


def diagonal_kernel(mine, top, bottom, *refs):
    weights, (acc_ref, x_ref) = refs[:-2], refs[-2:]
    at = 0
    for ref in (mine, top, bottom):
        x_ref[at : at + ref.shape[0]] = ref[...]
        at += ref.shape[0]
    acc_ref[...] = three_shards([x_ref], *weights)


ROW_ORDER = ((0, 1, 2, 6), (3, 4, 5, 7))


def finish_kernel(*refs):
    x_refs, (last, acc_in, acc_diagonal, q_ref, k_ref, v_ref) = refs[:3], refs[3:]
    z, core, _ = where_am_i()
    block, early = q_ref.shape[1] // 2, acc_in.shape[0]
    value = jnp.dot(take(x_refs, z ^ 3, core, last.shape[0]), last[...], preferred_element_type=jnp.float32)
    value = [acc_in[...] + value[:early], acc_diagonal[...] + value[early:]]
    value = jnp.concatenate(value, axis=0).astype(jnp.bfloat16)
    for rel in range(2):
        at = pl.ds(pl.multiple_of((core ^ rel) * block, block), block)
        for r in range(4):
            row = ROW_ORDER[rel][r]
            mine = value[row * block : (row + 1) * block]
            for third, ref in enumerate((q_ref, k_ref, v_ref)):
                ref[r, at, :] = mine[:, third * HD : (third + 1) * HD]


def spans(u):
    return ((0, u, 2), (1, 0, 2), (2, 0, 1 + u))


def neighbours(outer, own, middle, index):
    z, _, _ = where_am_i()
    odd = (z & 1) == 1
    outer, middle = outer[index], middle[index]
    return jnp.where(odd, outer, middle), own[index], jnp.where(odd, middle, outer)


def weigh_kernel(q_ref, middle, own, outer, own_flags, received, out_ref):
    _, core, _ = where_am_i()
    block = q_ref.shape[1] // 2
    inv_root = 1.0 / math.sqrt(HD)
    flags = [own_flags[:, :HD].astype(jnp.float32), received[-EXTRA:, :HD].astype(jnp.float32)]
    flags = [jnp.where(core == u, flags[0], flags[1]) for u in range(2)]
    bias = [(f - 1.0) * 1e30 for f in flags]
    for r in range(4):
        keys = neighbours(outer, own, middle, r)
        for u in range(2):
            q = q_ref[r, u * block : (u + 1) * block]
            scores = []
            for side, first, last in spans(u):
                k = keys[side][first * block : last * block]
                s = lax.dot_general(q, k, (((1,), (1,)), ((), ())), preferred_element_type=jnp.float32)
                for v in range(last - first):
                    entry = len(scores)
                    shut = jnp.broadcast_to(bias[u][r : r + 1, entry : entry + 1], (block, block))
                    scores.append(s[:, v * block : (v + 1) * block] * inv_root + shut)
            top = jnp.max(functools.reduce(jnp.maximum, scores), axis=1, keepdims=True)
            powers = [jnp.exp(s - top) for s in scores]
            inverse = 1.0 / jnp.sum(functools.reduce(jnp.add, powers), axis=1, keepdims=True)
            for entry, p in enumerate(powers):
                here = slice(entry * block, (entry + 1) * block)
                out_ref[r, u * block : (u + 1) * block, here] = (p * inverse).astype(jnp.bfloat16)


def mix_kernel(r, weights, middle, own, outer, out_ref):
    block = weights.shape[1] // 2
    values = neighbours(outer, own, middle, r)
    for u in range(2):
        w = weights[r, u * block : (u + 1) * block]
        v = [values[side][first * block : last * block] for side, first, last in spans(u)]
        result = jnp.dot(w, jnp.concatenate(v, axis=0), preferred_element_type=jnp.float32)
        out_ref[u * block : (u + 1) * block] = result.astype(jnp.bfloat16)


def pack_kernel(*refs):
    keep_ref, send_ref = refs[4:]
    _, core, _ = where_am_i()
    block = keep_ref.shape[1]
    for r, ref in enumerate(refs[:4]):
        for rel, out_ref in enumerate((keep_ref, send_ref)):
            out_ref[r] = ref[pl.ds(pl.multiple_of((core ^ rel) * block, block), block), :]


def gather_kernel(mine, other, out_ref):
    _, core, depth = where_am_i()
    for rel, ref in enumerate((mine, other)):
        for r in range(4):
            at = pl.multiple_of((2 * (depth ^ r) + (core ^ rel)) * HD, HD)
            out_ref[:, pl.ds(at, HD)] = ref[r]


def call(kernel, outs, places, scratch=(), macs=0, limit=32):
    spaces = {"v": VMEM}
    return pl.pallas_call(
        kernel,
        out_shape=outs,
        in_specs=[pl.BlockSpec(memory_space=spaces[place]) for place in places],
        out_specs=jax.tree.map(lambda _: pl.BlockSpec(memory_space=VMEM), outs),
        scratch_shapes=list(scratch),
        cost_estimate=pl.CostEstimate(flops=2 * macs, bytes_accessed=0, transcendentals=0),
        compiler_params=pltpu.CompilerParams(vmem_limit_bytes=limit * 2**20),
    )


def plane_device(raw, stream, conv_w, gain, w_qkv, mask):
    time_len, site_len, feat_len = raw.shape
    block, width = time_len * site_len, stream.shape[2]
    half, size = width // 2, w_qkv.shape[0]
    bf16, f32 = jnp.bfloat16, jnp.float32

    def array(*shape, kind=bf16):
        return jax.ShapeDtypeStruct(shape, kind)

    far_raw = swap_z(w_qkv, 2)

    mask_row = jnp.pad(mask.reshape(1, mask.shape[2]), ((0, 0), (0, feat_len - mask.shape[2]))).astype(bf16)
    raw = jnp.concatenate([raw.reshape(block, feat_len), jnp.broadcast_to(mask_row, (EXTRA, feat_len))], axis=0)
    stream = stream.reshape(block, width)
    conv_w, gain = conv_w.reshape(3 * feat_len, width), gain.reshape(1, width)
    more = block // 2 + EXTRA
    *to, kept = call(
        split_kernel,
        (array(size + more, PAIR), array(size + more, PAIR), array(block, PAIR), array(size, PAIR)),
        "vv",
    )(w_qkv, raw)
    plane = [swap_depth(t, r) for t, r in zip(to, (1, 2, 3))]
    own = call(sort_kernel, array(size, 6 * HD), "vvv")(kept, *plane[:2])
    near = swap_z(own, 1)

    def embed(rs, *streams, finished=()):
        out = (array((len(rs) + len(finished)) * block, width),) + (array(block, half),) * (len(rs) - 1) * 2
        return call(
            functools.partial(embed_kernel, rs, len(finished)),
            out,
            "v" * (6 + len(streams) + len(finished)),
            scratch=[VMEM((block, width), f32)],
            macs=len(rs) * block * 3 * feat_len * width,
        )(raw, *plane, conv_w, gain, *streams, *finished)

    tied = after(stream, plane[2])
    beside, above = swap_depth(tied, 1), swap_depth(tied, 2)
    (normed,) = embed((0,), stream)
    far_raw = after(far_raw, normed)

    even = (lax.axis_index("depth") & 1) == 0
    low, to_x, high = (far_raw[:, k * PAIR : (k + 1) * PAIR] for k in range(3))
    kept, to_y = jnp.where(even, low, high), jnp.where(even, high, low)
    from_x, from_y = swap_depth(to_x, 1), swap_depth(to_y, 2)
    beside, above = after(beside, to_x), after(above, to_y)
    stack, *diagonal = embed((1, 2), beside, above, finished=(normed,))
    from_x, from_y, stack, near = lax.optimization_barrier((from_x, from_y, stack, near))
    keep, send, flags = call(
        sort_far_kernel,
        (array(size, 3 * HD), array(size, 3 * HD), array(EXTRA, 3 * HD)),
        "v" * 7,
    )(kept, from_x, from_y, *plane, raw)
    diagonal = swap_depth(diagonal[0], 2), swap_depth(diagonal[1], 1)
    far = jnp.concatenate([keep, swap_core(send)], axis=0)
    last = swap_z(far, 1)
    far, near, stack = lax.optimization_barrier((far, near, stack))
    received = swap_core(jnp.concatenate([own[:, 3 * HD :], near[:, 3 * HD :], flags], axis=0))
    weights = (own, near, received, far)
    piece = 5 * block // 8
    early = (stack, swap_core(stack))
    rows = 2 * size
    total = call(partial_kernel, array(6 * block, 3 * HD, kind=f32), "v" * 6, macs=6 * block * 3 * rows * 3 * HD)(
        *early, *weights
    )
    (diagonal,) = embed((3,), jnp.concatenate([after(t, total) for t in diagonal], axis=1))
    swapped = [swap_core(diagonal[:piece]), swap_core(diagonal[piece:])]
    total_diagonal, diagonal = call(
        diagonal_kernel,
        (array(2 * block, 3 * HD, kind=f32), array(2 * block, width)),
        "v" * 7,
        macs=2 * block * 3 * rows * 3 * HD,
    )(diagonal, *swapped, *weights)
    one_head = array(4, 2 * block, HD)
    q, k, v = call(
        finish_kernel, (one_head,) * 3, "v" * 6, macs=8 * block * rows * 3 * HD
    )(*early, diagonal, last, total, total_diagonal)

    middle = swap_middle(k)
    outer = swap_z(k, 1)
    weights = call(weigh_kernel, array(4, 2 * block, 5 * block), "v" * 6, macs=8 * block * 5 * block * HD)(
        q, middle, k, outer, flags, received
    )
    values = (swap_middle(v), v, swap_z(v, 1))
    pieces = {}
    for r in V_ORDER:
        mixed = call(functools.partial(mix_kernel, r), array(2 * block, HD), "vvvv", macs=2 * block * 5 * block * HD)(
            weights, *values
        )
        pieces[r] = swap_depth(mixed, r) if r else mixed
    kept, sent = call(pack_kernel, (array(4, block, HD),) * 2, "vvvv")(*[pieces[r] for r in range(4)])
    context = call(gather_kernel, array(block, HEADS * HD), "vv")(kept, swap_core(sent))
    return context.reshape(time_len, site_len, HEADS * HD)


def from_behind(value, axis, by):
    devices = lax.axis_size(axis)
    pairs = [(i, i + by) for i in range(devices) if 0 <= i + by < devices]
    return lax.ppermute(value, axis, pairs)


def head_attend(query_head, key_head, value_head, allowed):
    inv_root = 1.0 / math.sqrt(HD)
    scores = (
        jnp.einsum("qd,kd->qk", query_head, key_head, preferred_element_type=jnp.float32) * inv_root
    )
    scores = jnp.where(allowed, scores, -1e30)
    row_max = jnp.max(scores, axis=-1, keepdims=True)
    powers = jnp.exp(scores - row_max)
    weights = (powers / jnp.sum(powers, axis=-1, keepdims=True)).astype(jnp.bfloat16)
    return jnp.dot(weights, value_head, preferred_element_type=jnp.float32).astype(jnp.bfloat16)


def per_device(raw, stream, conv_w, gain, w_qkv, mask):
    time_len, site_len, _ = raw.shape
    tok_rows = time_len * site_len
    normed = normed_tokens(padded_2(raw, (("depth", 1),), 1), stream, conv_w, gain)
    columns = lax.all_gather(w_qkv, "depth", axis=1, tiled=True)
    projected = jnp.dot(
        normed,
        lax.all_gather(columns, "tm", axis=0, tiled=True),
        preferred_element_type=jnp.float32,
    ).astype(jnp.bfloat16)
    head_cols = projected.shape[1] // 3
    queries = projected[:, :head_cols]
    keyvals = projected[:, head_cols:]
    earlier = []
    later = []
    moving_back = keyvals
    moving_ahead = keyvals
    for hop_index in range(RD):
        moving_back = from_behind(moving_back, "tm", 1)
        moving_ahead = from_behind(moving_ahead, "tm", -1)
        earlier.insert(0, moving_back)
        later.append(moving_ahead)
    gathered = jnp.concatenate(earlier + [keyvals] + later, axis=0)
    block_rows = BT * PP
    own_blocks = tok_rows // block_rows
    span_blocks = gathered.shape[0] // block_rows
    local_mask = mask[0]
    query_ids = jnp.arange(own_blocks, dtype=jnp.int32)[:, None]
    key_ids = jnp.arange(span_blocks, dtype=jnp.int32)[None, :]
    entry_ids = key_ids - query_ids
    picks = entry_ids[:, :, None] == jnp.arange(local_mask.shape[1], dtype=jnp.int32)[None, None, :]
    block_allowed = jnp.sum(jnp.where(picks, local_mask[:, None, :], 0), axis=-1) > 0
    allowed = jnp.repeat(jnp.repeat(block_allowed, block_rows, axis=0), block_rows, axis=1)
    query_heads = queries.reshape(tok_rows, HEADS, HD).transpose(1, 0, 2)
    key_heads = gathered[:, :head_cols].reshape(gathered.shape[0], HEADS, HD).transpose(1, 0, 2)
    value_heads = gathered[:, head_cols:].reshape(gathered.shape[0], HEADS, HD).transpose(1, 0, 2)
    context = lax.map(
        lambda operands: head_attend(operands[0], operands[1], operands[2], allowed),
        (query_heads, key_heads, value_heads),
    )
    return context.transpose(1, 0, 2).reshape(time_len, site_len, head_cols)


def solution(mesh):
    in_specs = (
        P("tm", "depth", None),
        P("tm", "depth", None),
        P(),
        P(),
        P("tm", "depth"),
        P("depth", "tm", None),
    )
    out_specs = P("tm", "depth", None)
    fits = mesh.shape["depth"] == 4 and mesh.shape["tm"] == 8
    return jax.shard_map(
        plane_device if fits else per_device, mesh=mesh, in_specs=in_specs, out_specs=out_specs, check_vma=False
    )
```

```python
import functools
import math

import jax
import jax.numpy as jnp
from jax import lax
from jax.experimental import pallas as pl
from jax.experimental.pallas import tpu as pltpu
from jax.sharding import PartitionSpec as P

HEADS = 8
HD = 128
BT = 16
PP = 8
RD = 2
VMEM = pltpu.VMEM
SMEM = pltpu.SMEM


def padded_2(value, sides, width):
    for axis, dim in sides:
        devices, length = (lax.axis_size(axis), value.shape[dim])
        up = [(i, (i + 1) % devices) for i in range(devices - 1)]
        down = [(j, i) for i, j in up]
        last = lax.slice_in_dim(value, length - width, length, axis=dim)
        leading = lax.slice_in_dim(value, 0, width, axis=dim)
        before = lax.ppermute(last, axis, up)
        after = lax.ppermute(leading, axis, down)
        value = jnp.concatenate([before, value, after], axis=dim)
    return value


def normed_tokens(padded, stream, conv_w, gain):
    time_len, site_len, width = stream.shape
    tok_rows = time_len * site_len
    embedded = stream.reshape(tok_rows, width).astype(jnp.float32)
    for offset in range(3):
        window = padded[:, offset : offset + site_len].reshape(tok_rows, padded.shape[2])
        embedded = embedded + jnp.dot(window, conv_w[offset], preferred_element_type=jnp.float32)
    scale = lax.rsqrt(jnp.mean(embedded * embedded, axis=-1, keepdims=True) + 1e-05)
    return (embedded * scale * gain).astype(jnp.bfloat16)


PAIR = 2 * HD
EXTRA = 16


def hop(value, fn):
    pairs = []
    for z in range(4):
        for core in range(2):
            for depth in range(4):
                to = fn(z, core, depth)
                if to is not None:
                    pairs.append(((2 * z + core) * 4 + depth, (2 * to[0] + to[1]) * 4 + to[2]))
    return lax.ppermute(value, ("tm", "depth"), pairs)


def swap_core(value):
    return hop(value, lambda z, c, d: (z, 1 - c, d))


def swap_depth(value, bits):
    return hop(value, lambda z, c, d: (z, c, d ^ bits))


def swap_z(value, bits):
    return hop(value, lambda z, c, d: (z ^ bits, c, d))


def swap_middle(value):
    return hop(value, lambda z, c, d: (z ^ 3, c, d) if z in (1, 2) else None)


def after(value, *others):
    return lax.optimization_barrier((value, *others))[0]


def where_am_i():
    tm = lax.axis_index("tm")
    return tm >> 1, tm & 1, lax.axis_index("depth")


def split_kernel(w, raw, to_x, to_y, to_across, keep):
    _, _, depth = where_am_i()
    even = (depth & 1) == 0
    size, half = w.shape[0], (raw.shape[0] - EXTRA) // 2
    low, high = w[:, :PAIR], w[:, 2 * PAIR :]
    to_x[:size] = w[:, PAIR : 2 * PAIR]
    to_y[:size] = jnp.where(even, high, low)
    keep[...] = jnp.where(even, low, high)
    at = to_across.shape[0] - EXTRA - half
    for i in range(2):
        to_across[:at, i * HD : (i + 1) * HD] = raw[:at]
    for ref, at in ((to_x, size), (to_y, size), (to_across, at)):
        for i in range(2):
            here = slice(i * HD, (i + 1) * HD)
            ref[at : at + half, here] = raw[i * half : (i + 1) * half]
            ref[at + half :, here] = raw[2 * half :]


def sorted_groups(kept, from_x, from_y):
    _, core, depth = where_am_i()
    first, even = core == 0, (depth & 1) == 0
    size = kept.shape[0]
    low = jnp.where(even, kept[...], from_y[:size])
    high = jnp.where(even, from_y[:size], kept[...])
    groups = (low, from_x[:size], high)
    turn = jnp.where(depth == 3, 0, depth)
    for third in range(3):
        group = jnp.where(turn == 0, groups[third], jnp.where(turn == 1, groups[(third + 1) % 3], groups[(third + 2) % 3]))
        yield third, jnp.where(first, group[:, :HD], group[:, HD:]), jnp.where(first, group[:, HD:], group[:, :HD])


def sort_kernel(kept, from_x, from_y, out_ref):
    for third, mine, other in sorted_groups(kept, from_x, from_y):
        out_ref[:, third * HD : (third + 1) * HD] = mine
        out_ref[:, (3 + third) * HD : (4 + third) * HD] = other


def sort_far_kernel(kept, from_x, from_y, plane_x, plane_y, across, raw, keep_ref, send_ref, flags_ref):
    for third, mine, other in sorted_groups(kept, from_x, from_y):
        send_ref[:, third * HD : (third + 1) * HD] = other
        keep_ref[:, third * HD : (third + 1) * HD] = mine
    row = lax.broadcasted_iota(jnp.int32, (EXTRA, HD), 0)
    flags = raw[raw.shape[0] - EXTRA :].astype(jnp.float32)
    for r, ref in enumerate((plane_x, plane_y, across)):
        flags = jnp.where(row == r + 1, ref[ref.shape[0] - EXTRA :, :HD].astype(jnp.float32), flags)
    flags = flags.astype(jnp.bfloat16)
    for k in range(3):
        flags_ref[:, k * HD : (k + 1) * HD] = flags


def embed_kernel(rs, more, raw, plane_x, plane_y, across, conv_w, gain, *refs):
    count = len(rs)
    streams, finished, (out_ref, *onward, acc) = refs[:count], refs[count : count + more], refs[count + more :]
    for ref in finished:
        out_ref[: ref.shape[0]] = ref[...]
    for i, ref in enumerate(onward):
        half = ref.shape[1]
        ref[...] = streams[i][:, i * half : (i + 1) * half]
    _, _, depth = where_am_i()
    rows, width = raw.shape[0] - EXTRA, conv_w.shape[1]
    raws = [raw[:rows]]
    for ref in (plane_x, plane_y, across):
        at = ref.shape[0] - EXTRA - rows // 2
        raws.append(jnp.concatenate([ref[at : at + rows // 2, :HD], ref[at : at + rows // 2, HD:]], axis=0))
    raws = [value.astype(jnp.float32).reshape(rows // PP, PP, HD) for value in raws]
    done = out_ref.shape[0] - len(rs) * rows
    for i, r in enumerate(rs):
        place = depth ^ r
        even = (place & 1) == 0
        side, far = raws[r ^ 1], raws[r ^ 3]
        before = jnp.where(even, jnp.where(place == 2, far[:, PP - 1 :], 0.0), side[:, PP - 1 :])
        behind = jnp.where(even, side[:, :1], jnp.where(place == 1, far[:, :1], 0.0))
        padded = jnp.concatenate([before, raws[r], behind], axis=1)
        windows = [padded[:, j : j + PP].reshape(rows, HD).astype(jnp.bfloat16) for j in range(3)]
        windows = jnp.concatenate(windows, axis=1)
        total, step = jnp.zeros((rows, 1), jnp.float32), width // 4
        for at in range(0, width, step):
            here = slice(at, at + step)
            part = jnp.dot(windows, conv_w[:, here], preferred_element_type=jnp.float32)
            part += streams[i][:, here].astype(jnp.float32)
            acc[:, here] = part
            total += jnp.sum(part * part, axis=1, keepdims=True)
        scale = lax.rsqrt(total / width + 1e-05)
        out_ref[done + i * rows : done + (i + 1) * rows] = (acc[...] * scale * gain[...]).astype(jnp.bfloat16)


def take(refs, source, core, rows):
    half = rows // 2
    cuts = [pl.ds(pl.multiple_of(source * rows + c * half, half), half) for c in (core, 1 - core)]
    return jnp.concatenate([jnp.concatenate([ref[:, at] for at in cuts], axis=1) for ref in refs], axis=0)


def three_shards(x_refs, own, near, received, far):
    z, core, _ = where_am_i()
    size, width = own.shape[0], 3 * HD
    w = [own[:, :width], received[:size], far[...]]
    w = jnp.concatenate(w + [near[:, :width], received[size : 2 * size]], axis=0)
    x = [take(x_refs, source, core, 2 * size) for source in (z, z ^ 2, z ^ 1)]
    return jnp.dot(jnp.concatenate(x, axis=1), w, preferred_element_type=jnp.float32)


def partial_kernel(*refs):
    refs[-1][...] = three_shards(refs[:2], *refs[2:-1])


def diagonal_kernel(mine, top, bottom, *refs):
    weights, (acc_ref, x_ref) = refs[:-2], refs[-2:]
    at = 0
    for ref in (mine, top, bottom):
        x_ref[at : at + ref.shape[0]] = ref[...]
        at += ref.shape[0]
    acc_ref[...] = three_shards([x_ref], *weights)


ROW_ORDER = ((0, 1, 2, 6), (3, 4, 5, 7))


def finish_kernel(*refs):
    x_refs, (last, acc_in, acc_diagonal, q_ref, k_ref, v_ref) = refs[:3], refs[3:]
    z, core, _ = where_am_i()
    block, early = q_ref.shape[1] // 2, acc_in.shape[0]
    value = jnp.dot(take(x_refs, z ^ 3, core, last.shape[0]), last[...], preferred_element_type=jnp.float32)
    value = [acc_in[...] + value[:early], acc_diagonal[...] + value[early:]]
    value = jnp.concatenate(value, axis=0).astype(jnp.bfloat16)
    for rel in range(2):
        at = pl.ds(pl.multiple_of((core ^ rel) * block, block), block)
        for r in range(4):
            row = ROW_ORDER[rel][r]
            mine = value[row * block : (row + 1) * block]
            for third, ref in enumerate((q_ref, k_ref, v_ref)):
                ref[r, at, :] = mine[:, third * HD : (third + 1) * HD]


def spans(u):
    return ((0, u, 2), (1, 0, 2), (2, 0, 1 + u))


def neighbours(outer, own, middle, index):
    z, _, _ = where_am_i()
    odd = (z & 1) == 1
    outer, middle = outer[index], middle[index]
    return jnp.where(odd, outer, middle), own[index], jnp.where(odd, middle, outer)


def weigh_kernel(q_ref, middle, own, outer, own_flags, received, out_ref):
    _, core, _ = where_am_i()
    block = q_ref.shape[1] // 2
    inv_root = 1.0 / math.sqrt(HD)
    flags = [own_flags[:, :HD].astype(jnp.float32), received[-EXTRA:, :HD].astype(jnp.float32)]
    flags = [jnp.where(core == u, flags[0], flags[1]) for u in range(2)]
    bias = [(f - 1.0) * 1e30 for f in flags]
    for r in range(4):
        keys = neighbours(outer, own, middle, r)
        for u in range(2):
            q = q_ref[r, u * block : (u + 1) * block]
            scores = []
            for side, first, last in spans(u):
                k = keys[side][first * block : last * block]
                s = lax.dot_general(q, k, (((1,), (1,)), ((), ())), preferred_element_type=jnp.float32)
                for v in range(last - first):
                    entry = len(scores)
                    shut = jnp.broadcast_to(bias[u][r : r + 1, entry : entry + 1], (block, block))
                    scores.append(s[:, v * block : (v + 1) * block] * inv_root + shut)
            top = jnp.max(functools.reduce(jnp.maximum, scores), axis=1, keepdims=True)
            powers = [jnp.exp(s - top) for s in scores]
            inverse = 1.0 / jnp.sum(functools.reduce(jnp.add, powers), axis=1, keepdims=True)
            for entry, p in enumerate(powers):
                here = slice(entry * block, (entry + 1) * block)
                out_ref[r, u * block : (u + 1) * block, here] = (p * inverse).astype(jnp.bfloat16)


def mix_kernel(weights, middle, own, outer, keep_ref, send_ref):
    _, core, _ = where_am_i()
    block = weights.shape[1] // 2
    for r in range(4):
        values = neighbours(outer, own, middle, r)
        results = []
        for u in range(2):
            w = weights[r, u * block : (u + 1) * block]
            v = [values[side][first * block : last * block] for side, first, last in spans(u)]
            result = jnp.dot(w, jnp.concatenate(v, axis=0), preferred_element_type=jnp.float32)
            results.append(result.astype(jnp.bfloat16))
        keep_ref[r] = jnp.where(core == 0, results[0], results[1])
        send_ref[r] = jnp.where(core == 0, results[1], results[0])


def pair_kernel(mine, other, x_ref, y_ref, diagonal_ref):
    for r, ref in enumerate((x_ref, y_ref, diagonal_ref)):
        ref[:, :HD] = mine[r + 1]
        ref[:, HD:] = other[r + 1]


def gather_kernel(mine, other, x, y, diagonal, out_ref):
    _, core, depth = where_am_i()
    pairs = [(mine[0], other[0])] + [(ref[:, :HD], ref[:, HD:]) for ref in (x, y, diagonal)]
    for r, pair in enumerate(pairs):
        for rel in range(2):
            at = pl.multiple_of((2 * (depth ^ r) + (core ^ rel)) * HD, HD)
            out_ref[:, pl.ds(at, HD)] = pair[rel]


def call(kernel, outs, places, scratch=(), macs=0, limit=32):
    spaces = {"v": VMEM}
    return pl.pallas_call(
        kernel,
        out_shape=outs,
        in_specs=[pl.BlockSpec(memory_space=spaces[place]) for place in places],
        out_specs=jax.tree.map(lambda _: pl.BlockSpec(memory_space=VMEM), outs),
        scratch_shapes=list(scratch),
        cost_estimate=pl.CostEstimate(flops=2 * macs, bytes_accessed=0, transcendentals=0),
        compiler_params=pltpu.CompilerParams(vmem_limit_bytes=limit * 2**20),
    )


def plane_device(raw, stream, conv_w, gain, w_qkv, mask):
    time_len, site_len, feat_len = raw.shape
    block, width = time_len * site_len, stream.shape[2]
    half, size = width // 2, w_qkv.shape[0]
    bf16, f32 = jnp.bfloat16, jnp.float32

    def array(*shape, kind=bf16):
        return jax.ShapeDtypeStruct(shape, kind)

    far_raw = swap_z(w_qkv, 2)

    mask_row = jnp.pad(mask.reshape(1, mask.shape[2]), ((0, 0), (0, feat_len - mask.shape[2]))).astype(bf16)
    raw = jnp.concatenate([raw.reshape(block, feat_len), jnp.broadcast_to(mask_row, (EXTRA, feat_len))], axis=0)
    stream = stream.reshape(block, width)
    conv_w, gain = conv_w.reshape(3 * feat_len, width), gain.reshape(1, width)
    more = block // 2 + EXTRA
    *to, kept = call(
        split_kernel,
        (array(size + more, PAIR), array(size + more, PAIR), array(block, PAIR), array(size, PAIR)),
        "vv",
    )(w_qkv, raw)
    plane = [swap_depth(t, r) for t, r in zip(to, (1, 2, 3))]
    own = call(sort_kernel, array(size, 6 * HD), "vvv")(kept, *plane[:2])
    near = swap_z(own, 1)

    def embed(rs, *streams, finished=()):
        out = (array((len(rs) + len(finished)) * block, width),) + (array(block, half),) * (len(rs) - 1) * 2
        return call(
            functools.partial(embed_kernel, rs, len(finished)),
            out,
            "v" * (6 + len(streams) + len(finished)),
            scratch=[VMEM((block, width), f32)],
            macs=len(rs) * block * 3 * feat_len * width,
        )(raw, *plane, conv_w, gain, *streams, *finished)

    tied = after(stream, plane[2])
    beside, above = swap_depth(tied, 1), swap_depth(tied, 2)
    (normed,) = embed((0,), stream)
    far_raw = after(far_raw, normed)

    even = (lax.axis_index("depth") & 1) == 0
    low, to_x, high = (far_raw[:, k * PAIR : (k + 1) * PAIR] for k in range(3))
    kept, to_y = jnp.where(even, low, high), jnp.where(even, high, low)
    from_x, from_y = swap_depth(to_x, 1), swap_depth(to_y, 2)
    beside, above = after(beside, to_x), after(above, to_y)
    stack, *diagonal = embed((1, 2), beside, above, finished=(normed,))
    from_x, from_y, stack, near = lax.optimization_barrier((from_x, from_y, stack, near))
    keep, send, flags = call(
        sort_far_kernel,
        (array(size, 3 * HD), array(size, 3 * HD), array(EXTRA, 3 * HD)),
        "v" * 7,
    )(kept, from_x, from_y, *plane, raw)
    diagonal = swap_depth(diagonal[0], 2), swap_depth(diagonal[1], 1)
    far = jnp.concatenate([keep, swap_core(send)], axis=0)
    last = swap_z(far, 1)
    far, near, stack = lax.optimization_barrier((far, near, stack))
    received = swap_core(jnp.concatenate([own[:, 3 * HD :], near[:, 3 * HD :], flags], axis=0))
    weights = (own, near, received, far)
    piece = 5 * block // 8
    early = (stack, swap_core(stack))
    rows = 2 * size
    total = call(partial_kernel, array(6 * block, 3 * HD, kind=f32), "v" * 6, macs=6 * block * 3 * rows * 3 * HD)(
        *early, *weights
    )
    (diagonal,) = embed((3,), jnp.concatenate([after(t, total) for t in diagonal], axis=1))
    swapped = [swap_core(diagonal[:piece]), swap_core(diagonal[piece:])]
    total_diagonal, diagonal = call(
        diagonal_kernel,
        (array(2 * block, 3 * HD, kind=f32), array(2 * block, width)),
        "v" * 7,
        macs=2 * block * 3 * rows * 3 * HD,
    )(diagonal, *swapped, *weights)
    one_head = array(4, 2 * block, HD)
    q, k, v = call(
        finish_kernel, (one_head,) * 3, "v" * 6, macs=8 * block * rows * 3 * HD
    )(*early, diagonal, last, total, total_diagonal)

    middle = swap_middle(k)
    outer = swap_z(k, 1)
    weights = call(weigh_kernel, array(4, 2 * block, 5 * block), "v" * 6, macs=8 * block * 5 * block * HD)(
        q, middle, k, outer, flags, received
    )
    values = (swap_middle(v), v, swap_z(v, 1))
    kept, sent = call(mix_kernel, (array(4, block, HD),) * 2, "vvvv", macs=8 * block * 5 * block * HD)(weights, *values)
    received = swap_core(sent)
    x, y, across = call(pair_kernel, (array(block, PAIR),) * 3, "vv")(kept, received)
    across, x, y = swap_depth(across, 3), swap_depth(x, 1), swap_depth(y, 2)
    context = call(gather_kernel, array(block, HEADS * HD), "v" * 5)(kept, received, x, y, across)
    return context.reshape(time_len, site_len, HEADS * HD)


def from_behind(value, axis, by):
    devices = lax.axis_size(axis)
    pairs = [(i, i + by) for i in range(devices) if 0 <= i + by < devices]
    return lax.ppermute(value, axis, pairs)


def head_attend(query_head, key_head, value_head, allowed):
    inv_root = 1.0 / math.sqrt(HD)
    scores = (
        jnp.einsum("qd,kd->qk", query_head, key_head, preferred_element_type=jnp.float32) * inv_root
    )
    scores = jnp.where(allowed, scores, -1e30)
    row_max = jnp.max(scores, axis=-1, keepdims=True)
    powers = jnp.exp(scores - row_max)
    weights = (powers / jnp.sum(powers, axis=-1, keepdims=True)).astype(jnp.bfloat16)
    return jnp.dot(weights, value_head, preferred_element_type=jnp.float32).astype(jnp.bfloat16)


def per_device(raw, stream, conv_w, gain, w_qkv, mask):
    time_len, site_len, _ = raw.shape
    tok_rows = time_len * site_len
    normed = normed_tokens(padded_2(raw, (("depth", 1),), 1), stream, conv_w, gain)
    columns = lax.all_gather(w_qkv, "depth", axis=1, tiled=True)
    projected = jnp.dot(
        normed,
        lax.all_gather(columns, "tm", axis=0, tiled=True),
        preferred_element_type=jnp.float32,
    ).astype(jnp.bfloat16)
    head_cols = projected.shape[1] // 3
    queries = projected[:, :head_cols]
    keyvals = projected[:, head_cols:]
    earlier = []
    later = []
    moving_back = keyvals
    moving_ahead = keyvals
    for hop_index in range(RD):
        moving_back = from_behind(moving_back, "tm", 1)
        moving_ahead = from_behind(moving_ahead, "tm", -1)
        earlier.insert(0, moving_back)
        later.append(moving_ahead)
    gathered = jnp.concatenate(earlier + [keyvals] + later, axis=0)
    block_rows = BT * PP
    own_blocks = tok_rows // block_rows
    span_blocks = gathered.shape[0] // block_rows
    local_mask = mask[0]
    query_ids = jnp.arange(own_blocks, dtype=jnp.int32)[:, None]
    key_ids = jnp.arange(span_blocks, dtype=jnp.int32)[None, :]
    entry_ids = key_ids - query_ids
    picks = entry_ids[:, :, None] == jnp.arange(local_mask.shape[1], dtype=jnp.int32)[None, None, :]
    block_allowed = jnp.sum(jnp.where(picks, local_mask[:, None, :], 0), axis=-1) > 0
    allowed = jnp.repeat(jnp.repeat(block_allowed, block_rows, axis=0), block_rows, axis=1)
    query_heads = queries.reshape(tok_rows, HEADS, HD).transpose(1, 0, 2)
    key_heads = gathered[:, :head_cols].reshape(gathered.shape[0], HEADS, HD).transpose(1, 0, 2)
    value_heads = gathered[:, head_cols:].reshape(gathered.shape[0], HEADS, HD).transpose(1, 0, 2)
    context = lax.map(
        lambda operands: head_attend(operands[0], operands[1], operands[2], allowed),
        (query_heads, key_heads, value_heads),
    )
    return context.transpose(1, 0, 2).reshape(time_len, site_len, head_cols)


def solution(mesh):
    in_specs = (
        P("tm", "depth", None),
        P("tm", "depth", None),
        P(),
        P(),
        P("tm", "depth"),
        P("depth", "tm", None),
    )
    out_specs = P("tm", "depth", None)
    fits = mesh.shape["depth"] == 4 and mesh.shape["tm"] == 8
    return jax.shard_map(
        plane_device if fits else per_device, mesh=mesh, in_specs=in_specs, out_specs=out_specs, check_vma=False
    )
```

```python
import functools
import math

import jax
import jax.numpy as jnp
from jax import lax
from jax.experimental import pallas as pl
from jax.experimental.pallas import tpu as pltpu
from jax.sharding import PartitionSpec as P

HEADS = 8
HD = 128
BT = 16
PP = 8
RD = 2
VMEM = pltpu.VMEM
SMEM = pltpu.SMEM


def padded_2(value, sides, width):
    for axis, dim in sides:
        devices, length = (lax.axis_size(axis), value.shape[dim])
        up = [(i, (i + 1) % devices) for i in range(devices - 1)]
        down = [(j, i) for i, j in up]
        last = lax.slice_in_dim(value, length - width, length, axis=dim)
        leading = lax.slice_in_dim(value, 0, width, axis=dim)
        before = lax.ppermute(last, axis, up)
        after = lax.ppermute(leading, axis, down)
        value = jnp.concatenate([before, value, after], axis=dim)
    return value


def normed_tokens(padded, stream, conv_w, gain):
    time_len, site_len, width = stream.shape
    tok_rows = time_len * site_len
    embedded = stream.reshape(tok_rows, width).astype(jnp.float32)
    for offset in range(3):
        window = padded[:, offset : offset + site_len].reshape(tok_rows, padded.shape[2])
        embedded = embedded + jnp.dot(window, conv_w[offset], preferred_element_type=jnp.float32)
    scale = lax.rsqrt(jnp.mean(embedded * embedded, axis=-1, keepdims=True) + 1e-05)
    return (embedded * scale * gain).astype(jnp.bfloat16)


PAIR = 2 * HD
EXTRA = 16


def hop(value, fn):
    pairs = []
    for z in range(4):
        for core in range(2):
            for depth in range(4):
                to = fn(z, core, depth)
                if to is not None:
                    pairs.append(((2 * z + core) * 4 + depth, (2 * to[0] + to[1]) * 4 + to[2]))
    return lax.ppermute(value, ("tm", "depth"), pairs)


def swap_core(value):
    return hop(value, lambda z, c, d: (z, 1 - c, d))


def swap_depth(value, bits):
    return hop(value, lambda z, c, d: (z, c, d ^ bits))


def swap_z(value, bits):
    return hop(value, lambda z, c, d: (z ^ bits, c, d))


def swap_middle(value):
    return hop(value, lambda z, c, d: (z ^ 3, c, d) if z in (1, 2) else None)


def after(value, *others):
    return lax.optimization_barrier((value, *others))[0]


def where_am_i():
    tm = lax.axis_index("tm")
    return tm >> 1, tm & 1, lax.axis_index("depth")


def split_kernel(w, raw, to_x, to_y, to_across, keep):
    _, _, depth = where_am_i()
    even = (depth & 1) == 0
    size, half = w.shape[0], (raw.shape[0] - EXTRA) // 2
    low, high = w[:, :PAIR], w[:, 2 * PAIR :]
    to_x[:size] = w[:, PAIR : 2 * PAIR]
    to_y[:size] = jnp.where(even, high, low)
    keep[...] = jnp.where(even, low, high)
    at = to_across.shape[0] - EXTRA - half
    for i in range(2):
        to_across[:at, i * HD : (i + 1) * HD] = raw[:at]
    for ref, at in ((to_x, size), (to_y, size), (to_across, at)):
        for i in range(2):
            here = slice(i * HD, (i + 1) * HD)
            ref[at : at + half, here] = raw[i * half : (i + 1) * half]
            ref[at + half :, here] = raw[2 * half :]


def sorted_groups(kept, from_x, from_y):
    _, core, depth = where_am_i()
    first, even = core == 0, (depth & 1) == 0
    size = kept.shape[0]
    low = jnp.where(even, kept[...], from_y[:size])
    high = jnp.where(even, from_y[:size], kept[...])
    groups = (low, from_x[:size], high)
    turn = jnp.where(depth == 3, 0, depth)
    for third in range(3):
        group = jnp.where(turn == 0, groups[third], jnp.where(turn == 1, groups[(third + 1) % 3], groups[(third + 2) % 3]))
        yield third, jnp.where(first, group[:, :HD], group[:, HD:]), jnp.where(first, group[:, HD:], group[:, :HD])


def sort_kernel(kept, from_x, from_y, out_ref):
    for third, mine, other in sorted_groups(kept, from_x, from_y):
        out_ref[:, third * HD : (third + 1) * HD] = mine
        out_ref[:, (3 + third) * HD : (4 + third) * HD] = other


def sort_far_kernel(kept, from_x, from_y, plane_x, plane_y, across, raw, keep_ref, send_ref, flags_ref):
    for third, mine, other in sorted_groups(kept, from_x, from_y):
        send_ref[:, third * HD : (third + 1) * HD] = other
        keep_ref[:, third * HD : (third + 1) * HD] = mine
    row = lax.broadcasted_iota(jnp.int32, (EXTRA, HD), 0)
    flags = raw[raw.shape[0] - EXTRA :].astype(jnp.float32)
    for r, ref in enumerate((plane_x, plane_y, across)):
        flags = jnp.where(row == r + 1, ref[ref.shape[0] - EXTRA :, :HD].astype(jnp.float32), flags)
    flags = flags.astype(jnp.bfloat16)
    for k in range(3):
        flags_ref[:, k * HD : (k + 1) * HD] = flags


def embed_kernel(rs, more, raw, plane_x, plane_y, across, conv_w, gain, *refs):
    count = len(rs)
    streams, finished, (out_ref, *onward, acc) = refs[:count], refs[count : count + more], refs[count + more :]
    for ref in finished:
        out_ref[: ref.shape[0]] = ref[...]
    for i, ref in enumerate(onward):
        half = ref.shape[1]
        ref[...] = streams[i][:, i * half : (i + 1) * half]
    _, _, depth = where_am_i()
    rows, width = raw.shape[0] - EXTRA, conv_w.shape[1]
    raws = [raw[:rows]]
    for ref in (plane_x, plane_y, across):
        at = ref.shape[0] - EXTRA - rows // 2
        raws.append(jnp.concatenate([ref[at : at + rows // 2, :HD], ref[at : at + rows // 2, HD:]], axis=0))
    raws = [value.astype(jnp.float32).reshape(rows // PP, PP, HD) for value in raws]
    done = out_ref.shape[0] - len(rs) * rows
    for i, r in enumerate(rs):
        place = depth ^ r
        even = (place & 1) == 0
        side, far = raws[r ^ 1], raws[r ^ 3]
        before = jnp.where(even, jnp.where(place == 2, far[:, PP - 1 :], 0.0), side[:, PP - 1 :])
        behind = jnp.where(even, side[:, :1], jnp.where(place == 1, far[:, :1], 0.0))
        padded = jnp.concatenate([before, raws[r], behind], axis=1)
        windows = [padded[:, j : j + PP].reshape(rows, HD).astype(jnp.bfloat16) for j in range(3)]
        windows = jnp.concatenate(windows, axis=1)
        total, step = jnp.zeros((rows, 1), jnp.float32), width // 4
        for at in range(0, width, step):
            here = slice(at, at + step)
            part = jnp.dot(windows, conv_w[:, here], preferred_element_type=jnp.float32)
            part += streams[i][:, here].astype(jnp.float32)
            acc[:, here] = part
            total += jnp.sum(part * part, axis=1, keepdims=True)
        scale = lax.rsqrt(total / width + 1e-05)
        out_ref[done + i * rows : done + (i + 1) * rows] = (acc[...] * scale * gain[...]).astype(jnp.bfloat16)


def take(refs, source, core, rows):
    half = rows // 2
    cuts = [pl.ds(pl.multiple_of(source * rows + c * half, half), half) for c in (core, 1 - core)]
    return jnp.concatenate([jnp.concatenate([ref[:, at] for at in cuts], axis=1) for ref in refs], axis=0)


def three_shards(x_refs, own, near, received, far):
    z, core, _ = where_am_i()
    size, width = own.shape[0], 3 * HD
    w = [own[:, :width], received[:size], far[...]]
    w = jnp.concatenate(w + [near[:, :width], received[size : 2 * size]], axis=0)
    x = [take(x_refs, source, core, 2 * size) for source in (z, z ^ 2, z ^ 1)]
    return jnp.dot(jnp.concatenate(x, axis=1), w, preferred_element_type=jnp.float32)


def partial_kernel(*refs):
    refs[-1][...] = three_shards(refs[:2], *refs[2:-1])


def diagonal_kernel(mine, top, bottom, *refs):
    weights, (acc_ref, x_ref) = refs[:-2], refs[-2:]
    at = 0
    for ref in (mine, top, bottom):
        x_ref[at : at + ref.shape[0]] = ref[...]
        at += ref.shape[0]
    acc_ref[...] = three_shards([x_ref], *weights)


ROW_ORDER = ((0, 1, 2, 6), (3, 4, 5, 7))


def finish_kernel(*refs):
    x_refs, (last, acc_in, acc_diagonal, q_ref, k_ref, v_ref) = refs[:3], refs[3:]
    z, core, _ = where_am_i()
    block, early = q_ref.shape[1] // 2, acc_in.shape[0]
    value = jnp.dot(take(x_refs, z ^ 3, core, last.shape[0]), last[...], preferred_element_type=jnp.float32)
    value = [acc_in[...] + value[:early], acc_diagonal[...] + value[early:]]
    value = jnp.concatenate(value, axis=0).astype(jnp.bfloat16)
    for rel in range(2):
        at = pl.ds(pl.multiple_of((core ^ rel) * block, block), block)
        for r in range(4):
            row = ROW_ORDER[rel][r]
            mine = value[row * block : (row + 1) * block]
            for third, ref in enumerate((q_ref, k_ref, v_ref)):
                ref[r, at, :] = mine[:, third * HD : (third + 1) * HD]


def spans(u):
    return ((0, u, 2), (1, 0, 2), (2, 0, 1 + u))


def neighbours(outer, own, middle, index):
    z, _, _ = where_am_i()
    odd = (z & 1) == 1
    outer, middle = outer[index], middle[index]
    return jnp.where(odd, outer, middle), own[index], jnp.where(odd, middle, outer)


def weigh_kernel(q_ref, middle, own, outer, own_flags, received, out_ref):
    _, core, _ = where_am_i()
    block = q_ref.shape[1] // 2
    inv_root = 1.0 / math.sqrt(HD)
    flags = [own_flags[:, :HD].astype(jnp.float32), received[-EXTRA:, :HD].astype(jnp.float32)]
    flags = [jnp.where(core == u, flags[0], flags[1]) for u in range(2)]
    bias = [(f - 1.0) * 1e30 for f in flags]
    for r in range(4):
        keys = neighbours(outer, own, middle, r)
        for u in range(2):
            q = q_ref[r, u * block : (u + 1) * block]
            scores = []
            for side, first, last in spans(u):
                k = keys[side][first * block : last * block]
                s = lax.dot_general(q, k, (((1,), (1,)), ((), ())), preferred_element_type=jnp.float32)
                for v in range(last - first):
                    entry = len(scores)
                    shut = jnp.broadcast_to(bias[u][r : r + 1, entry : entry + 1], (block, block))
                    scores.append(s[:, v * block : (v + 1) * block] * inv_root + shut)
            top = jnp.max(functools.reduce(jnp.maximum, scores), axis=1, keepdims=True)
            powers = [jnp.exp(s - top) for s in scores]
            inverse = 1.0 / jnp.sum(functools.reduce(jnp.add, powers), axis=1, keepdims=True)
            for entry, p in enumerate(powers):
                here = slice(entry * block, (entry + 1) * block)
                out_ref[r, u * block : (u + 1) * block, here] = (p * inverse).astype(jnp.bfloat16)


def mix_kernel(weights, middle, own, outer, keep_ref, send_ref):
    _, core, _ = where_am_i()
    block = weights.shape[1] // 2
    for r in range(4):
        values = neighbours(outer, own, middle, r)
        results = []
        for u in range(2):
            w = weights[r, u * block : (u + 1) * block]
            v = [values[side][first * block : last * block] for side, first, last in spans(u)]
            result = jnp.dot(w, jnp.concatenate(v, axis=0), preferred_element_type=jnp.float32)
            results.append(result.astype(jnp.bfloat16))
        keep_ref[r] = jnp.where(core == 0, results[0], results[1])
        send_ref[r] = jnp.where(core == 0, results[1], results[0])


def pair_kernel(mine, other, x_ref, y_ref, diagonal_ref):
    for r, ref in enumerate((x_ref, y_ref, diagonal_ref)):
        ref[:, :HD] = mine[r + 1]
        ref[:, HD:] = other[r + 1]


def gather_kernel(mine, other, diagonal, x, y, out_ref):
    _, core, depth = where_am_i()
    pairs = [(mine[0], other[0])] + [(ref[:, :HD], ref[:, HD:]) for ref in (x, y, diagonal)]
    for r, pair in enumerate(pairs):
        for rel in range(2):
            at = pl.multiple_of((2 * (depth ^ r) + (core ^ rel)) * HD, HD)
            out_ref[:, pl.ds(at, HD)] = pair[rel]


def call(kernel, outs, places, scratch=(), macs=0, limit=32):
    spaces = {"v": VMEM}
    return pl.pallas_call(
        kernel,
        out_shape=outs,
        in_specs=[pl.BlockSpec(memory_space=spaces[place]) for place in places],
        out_specs=jax.tree.map(lambda _: pl.BlockSpec(memory_space=VMEM), outs),
        scratch_shapes=list(scratch),
        cost_estimate=pl.CostEstimate(flops=2 * macs, bytes_accessed=0, transcendentals=0),
        compiler_params=pltpu.CompilerParams(vmem_limit_bytes=limit * 2**20),
    )


def plane_device(raw, stream, conv_w, gain, w_qkv, mask):
    time_len, site_len, feat_len = raw.shape
    block, width = time_len * site_len, stream.shape[2]
    half, size = width // 2, w_qkv.shape[0]
    bf16, f32 = jnp.bfloat16, jnp.float32

    def array(*shape, kind=bf16):
        return jax.ShapeDtypeStruct(shape, kind)

    far_raw = swap_z(w_qkv, 2)

    mask_row = jnp.pad(mask.reshape(1, mask.shape[2]), ((0, 0), (0, feat_len - mask.shape[2]))).astype(bf16)
    raw = jnp.concatenate([raw.reshape(block, feat_len), jnp.broadcast_to(mask_row, (EXTRA, feat_len))], axis=0)
    stream = stream.reshape(block, width)
    conv_w, gain = conv_w.reshape(3 * feat_len, width), gain.reshape(1, width)
    more = block // 2 + EXTRA
    *to, kept = call(
        split_kernel,
        (array(size + more, PAIR), array(size + more, PAIR), array(block, PAIR), array(size, PAIR)),
        "vv",
    )(w_qkv, raw)
    plane = [swap_depth(t, r) for t, r in zip(to, (1, 2, 3))]
    own = call(sort_kernel, array(size, 6 * HD), "vvv")(kept, *plane[:2])
    near = swap_z(own, 1)

    def embed(rs, *streams, finished=()):
        out = (array((len(rs) + len(finished)) * block, width),) + (array(block, half),) * (len(rs) - 1) * 2
        return call(
            functools.partial(embed_kernel, rs, len(finished)),
            out,
            "v" * (6 + len(streams) + len(finished)),
            scratch=[VMEM((block, width), f32)],
            macs=len(rs) * block * 3 * feat_len * width,
        )(raw, *plane, conv_w, gain, *streams, *finished)

    tied = after(stream, plane[2])
    beside, above = swap_depth(tied, 1), swap_depth(tied, 2)
    (normed,) = embed((0,), stream)
    far_raw = after(far_raw, normed)

    even = (lax.axis_index("depth") & 1) == 0
    low, to_x, high = (far_raw[:, k * PAIR : (k + 1) * PAIR] for k in range(3))
    kept, to_y = jnp.where(even, low, high), jnp.where(even, high, low)
    from_x, from_y = swap_depth(to_x, 1), swap_depth(to_y, 2)
    beside, above = after(beside, to_x), after(above, to_y)
    stack, *diagonal = embed((1, 2), beside, above, finished=(normed,))
    from_x, from_y, stack, near = lax.optimization_barrier((from_x, from_y, stack, near))
    keep, send, flags = call(
        sort_far_kernel,
        (array(size, 3 * HD), array(size, 3 * HD), array(EXTRA, 3 * HD)),
        "v" * 7,
    )(kept, from_x, from_y, *plane, raw)
    diagonal = swap_depth(diagonal[0], 2), swap_depth(diagonal[1], 1)
    far = jnp.concatenate([keep, swap_core(send)], axis=0)
    last = swap_z(far, 1)
    far, near, stack = lax.optimization_barrier((far, near, stack))
    received = swap_core(jnp.concatenate([own[:, 3 * HD :], near[:, 3 * HD :], flags], axis=0))
    weights = (own, near, received, far)
    piece = 5 * block // 8
    early = (stack, swap_core(stack))
    rows = 2 * size
    total = call(partial_kernel, array(6 * block, 3 * HD, kind=f32), "v" * 6, macs=6 * block * 3 * rows * 3 * HD)(
        *early, *weights
    )
    (diagonal,) = embed((3,), jnp.concatenate([after(t, total) for t in diagonal], axis=1))
    swapped = [swap_core(diagonal[:piece]), swap_core(diagonal[piece:])]
    total_diagonal, diagonal = call(
        diagonal_kernel,
        (array(2 * block, 3 * HD, kind=f32), array(2 * block, width)),
        "v" * 7,
        macs=2 * block * 3 * rows * 3 * HD,
    )(diagonal, *swapped, *weights)
    one_head = array(4, 2 * block, HD)
    q, k, v = call(
        finish_kernel, (one_head,) * 3, "v" * 6, macs=8 * block * rows * 3 * HD
    )(*early, diagonal, last, total, total_diagonal)

    middle = swap_middle(k)
    outer = swap_z(k, 1)
    weights = call(weigh_kernel, array(4, 2 * block, 5 * block), "v" * 6, macs=8 * block * 5 * block * HD)(
        q, middle, k, outer, flags, received
    )
    values = (swap_middle(v), v, swap_z(v, 1))
    kept, sent = call(mix_kernel, (array(4, block, HD),) * 2, "vvvv", macs=8 * block * 5 * block * HD)(weights, *values)
    received = swap_core(sent)
    x, y, across = call(pair_kernel, (array(block, PAIR),) * 3, "vv")(kept, received)
    across, x, y = swap_depth(across, 3), swap_depth(x, 1), swap_depth(y, 2)
    context = call(gather_kernel, array(block, HEADS * HD), "v" * 5)(kept, received, across, x, y)
    return context.reshape(time_len, site_len, HEADS * HD)


def from_behind(value, axis, by):
    devices = lax.axis_size(axis)
    pairs = [(i, i + by) for i in range(devices) if 0 <= i + by < devices]
    return lax.ppermute(value, axis, pairs)


def head_attend(query_head, key_head, value_head, allowed):
    inv_root = 1.0 / math.sqrt(HD)
    scores = (
        jnp.einsum("qd,kd->qk", query_head, key_head, preferred_element_type=jnp.float32) * inv_root
    )
    scores = jnp.where(allowed, scores, -1e30)
    row_max = jnp.max(scores, axis=-1, keepdims=True)
    powers = jnp.exp(scores - row_max)
    weights = (powers / jnp.sum(powers, axis=-1, keepdims=True)).astype(jnp.bfloat16)
    return jnp.dot(weights, value_head, preferred_element_type=jnp.float32).astype(jnp.bfloat16)


def per_device(raw, stream, conv_w, gain, w_qkv, mask):
    time_len, site_len, _ = raw.shape
    tok_rows = time_len * site_len
    normed = normed_tokens(padded_2(raw, (("depth", 1),), 1), stream, conv_w, gain)
    columns = lax.all_gather(w_qkv, "depth", axis=1, tiled=True)
    projected = jnp.dot(
        normed,
        lax.all_gather(columns, "tm", axis=0, tiled=True),
        preferred_element_type=jnp.float32,
    ).astype(jnp.bfloat16)
    head_cols = projected.shape[1] // 3
    queries = projected[:, :head_cols]
    keyvals = projected[:, head_cols:]
    earlier = []
    later = []
    moving_back = keyvals
    moving_ahead = keyvals
    for hop_index in range(RD):
        moving_back = from_behind(moving_back, "tm", 1)
        moving_ahead = from_behind(moving_ahead, "tm", -1)
        earlier.insert(0, moving_back)
        later.append(moving_ahead)
    gathered = jnp.concatenate(earlier + [keyvals] + later, axis=0)
    block_rows = BT * PP
    own_blocks = tok_rows // block_rows
    span_blocks = gathered.shape[0] // block_rows
    local_mask = mask[0]
    query_ids = jnp.arange(own_blocks, dtype=jnp.int32)[:, None]
    key_ids = jnp.arange(span_blocks, dtype=jnp.int32)[None, :]
    entry_ids = key_ids - query_ids
    picks = entry_ids[:, :, None] == jnp.arange(local_mask.shape[1], dtype=jnp.int32)[None, None, :]
    block_allowed = jnp.sum(jnp.where(picks, local_mask[:, None, :], 0), axis=-1) > 0
    allowed = jnp.repeat(jnp.repeat(block_allowed, block_rows, axis=0), block_rows, axis=1)
    query_heads = queries.reshape(tok_rows, HEADS, HD).transpose(1, 0, 2)
    key_heads = gathered[:, :head_cols].reshape(gathered.shape[0], HEADS, HD).transpose(1, 0, 2)
    value_heads = gathered[:, head_cols:].reshape(gathered.shape[0], HEADS, HD).transpose(1, 0, 2)
    context = lax.map(
        lambda operands: head_attend(operands[0], operands[1], operands[2], allowed),
        (query_heads, key_heads, value_heads),
    )
    return context.transpose(1, 0, 2).reshape(time_len, site_len, head_cols)


def solution(mesh):
    in_specs = (
        P("tm", "depth", None),
        P("tm", "depth", None),
        P(),
        P(),
        P("tm", "depth"),
        P("depth", "tm", None),
    )
    out_specs = P("tm", "depth", None)
    fits = mesh.shape["depth"] == 4 and mesh.shape["tm"] == 8
    return jax.shard_map(
        plane_device if fits else per_device, mesh=mesh, in_specs=in_specs, out_specs=out_specs, check_vma=False
    )
```

```python
import functools
import math

import jax
import jax.numpy as jnp
from jax import lax
from jax.experimental import pallas as pl
from jax.experimental.pallas import tpu as pltpu
from jax.sharding import PartitionSpec as P

HEADS = 8
HD = 128
BT = 16
PP = 8
RD = 2
VMEM = pltpu.VMEM
SMEM = pltpu.SMEM


def padded_2(value, sides, width):
    for axis, dim in sides:
        devices, length = (lax.axis_size(axis), value.shape[dim])
        up = [(i, (i + 1) % devices) for i in range(devices - 1)]
        down = [(j, i) for i, j in up]
        last = lax.slice_in_dim(value, length - width, length, axis=dim)
        leading = lax.slice_in_dim(value, 0, width, axis=dim)
        before = lax.ppermute(last, axis, up)
        after = lax.ppermute(leading, axis, down)
        value = jnp.concatenate([before, value, after], axis=dim)
    return value


def normed_tokens(padded, stream, conv_w, gain):
    time_len, site_len, width = stream.shape
    tok_rows = time_len * site_len
    embedded = stream.reshape(tok_rows, width).astype(jnp.float32)
    for offset in range(3):
        window = padded[:, offset : offset + site_len].reshape(tok_rows, padded.shape[2])
        embedded = embedded + jnp.dot(window, conv_w[offset], preferred_element_type=jnp.float32)
    scale = lax.rsqrt(jnp.mean(embedded * embedded, axis=-1, keepdims=True) + 1e-05)
    return (embedded * scale * gain).astype(jnp.bfloat16)


PAIR = 2 * HD
V_ORDER = (3, 1, 2, 0)
EXTRA = 16


def hop(value, fn):
    pairs = []
    for z in range(4):
        for core in range(2):
            for depth in range(4):
                to = fn(z, core, depth)
                if to is not None:
                    pairs.append(((2 * z + core) * 4 + depth, (2 * to[0] + to[1]) * 4 + to[2]))
    return lax.ppermute(value, ("tm", "depth"), pairs)


def swap_core(value):
    return hop(value, lambda z, c, d: (z, 1 - c, d))


def swap_depth(value, bits):
    return hop(value, lambda z, c, d: (z, c, d ^ bits))


def swap_z(value, bits):
    return hop(value, lambda z, c, d: (z ^ bits, c, d))


def swap_middle(value):
    return hop(value, lambda z, c, d: (z ^ 3, c, d) if z in (1, 2) else None)


def after(value, *others):
    return lax.optimization_barrier((value, *others))[0]


def where_am_i():
    tm = lax.axis_index("tm")
    return tm >> 1, tm & 1, lax.axis_index("depth")


def split_kernel(mask, w, raw, to_x, to_y, to_across, keep, flags_ref):
    _, _, depth = where_am_i()
    even = (depth & 1) == 0
    size, half = w.shape[0], raw.shape[0] // 2
    low, high = w[:, :PAIR], w[:, 2 * PAIR :]
    to_x[:size] = w[:, PAIR : 2 * PAIR]
    to_y[:size] = jnp.where(even, high, low)
    keep[...] = jnp.where(even, low, high)
    lane = lax.broadcasted_iota(jnp.int32, (EXTRA, HD), 1)
    flags = jnp.zeros((EXTRA, HD), jnp.int32)
    for entry in range(mask.shape[0]):
        flags = jnp.where(lane == entry, mask[entry], flags)
    flags = flags.astype(jnp.float32).astype(jnp.bfloat16)
    flags_ref[...] = flags
    at = to_across.shape[0] - EXTRA - half
    for i in range(2):
        to_across[:at, i * HD : (i + 1) * HD] = raw[:at]
    for ref, at in ((to_x, size), (to_y, size), (to_across, at)):
        for i in range(2):
            here = slice(i * HD, (i + 1) * HD)
            ref[at : at + half, here] = raw[i * half : (i + 1) * half]
            ref[at + half :, here] = flags


def sorted_groups(kept, from_x, from_y):
    _, core, depth = where_am_i()
    first, even = core == 0, (depth & 1) == 0
    size = kept.shape[0]
    low = jnp.where(even, kept[...], from_y[:size])
    high = jnp.where(even, from_y[:size], kept[...])
    groups = (low, from_x[:size], high)
    turn = jnp.where(depth == 3, 0, depth)
    for third in range(3):
        group = jnp.where(turn == 0, groups[third], jnp.where(turn == 1, groups[(third + 1) % 3], groups[(third + 2) % 3]))
        yield third, jnp.where(first, group[:, :HD], group[:, HD:]), jnp.where(first, group[:, HD:], group[:, :HD])


def sort_kernel(kept, from_x, from_y, out_ref):
    for third, mine, other in sorted_groups(kept, from_x, from_y):
        out_ref[:, third * HD : (third + 1) * HD] = mine
        out_ref[:, (3 + third) * HD : (4 + third) * HD] = other


def sort_far_kernel(kept, from_x, from_y, plane_x, plane_y, across, own_flags, keep_ref, send_ref, flags_ref):
    for third, mine, other in sorted_groups(kept, from_x, from_y):
        send_ref[:, third * HD : (third + 1) * HD] = other
        keep_ref[:, third * HD : (third + 1) * HD] = mine
    row = lax.broadcasted_iota(jnp.int32, (EXTRA, HD), 0)
    flags = own_flags[...].astype(jnp.float32)
    for r, ref in enumerate((plane_x, plane_y, across)):
        flags = jnp.where(row == r + 1, ref[ref.shape[0] - EXTRA :, :HD].astype(jnp.float32), flags)
    flags = flags.astype(jnp.bfloat16)
    for k in range(3):
        flags_ref[:, k * HD : (k + 1) * HD] = flags


def embed_kernel(rs, more, raw, plane_x, plane_y, across, conv_w, gain, *refs):
    count = len(rs)
    streams, finished, (out_ref, *onward, acc) = refs[:count], refs[count : count + more], refs[count + more :]
    for ref in finished:
        out_ref[: ref.shape[0]] = ref[...]
    for i, ref in enumerate(onward):
        half = ref.shape[1]
        ref[...] = streams[i][:, i * half : (i + 1) * half]
    _, _, depth = where_am_i()
    rows, width = raw.shape[0], conv_w.shape[1]
    raws = [raw[...]]
    for ref in (plane_x, plane_y, across):
        at = ref.shape[0] - EXTRA - rows // 2
        raws.append(jnp.concatenate([ref[at : at + rows // 2, :HD], ref[at : at + rows // 2, HD:]], axis=0))
    raws = [value.astype(jnp.float32).reshape(rows // PP, PP, HD) for value in raws]
    done = out_ref.shape[0] - len(rs) * rows
    for i, r in enumerate(rs):
        place = depth ^ r
        even = (place & 1) == 0
        side, far = raws[r ^ 1], raws[r ^ 3]
        before = jnp.where(even, jnp.where(place == 2, far[:, PP - 1 :], 0.0), side[:, PP - 1 :])
        behind = jnp.where(even, side[:, :1], jnp.where(place == 1, far[:, :1], 0.0))
        padded = jnp.concatenate([before, raws[r], behind], axis=1)
        windows = [padded[:, j : j + PP].reshape(rows, HD).astype(jnp.bfloat16) for j in range(3)]
        windows = jnp.concatenate(windows, axis=1)
        total, step = jnp.zeros((rows, 1), jnp.float32), width // 4
        for at in range(0, width, step):
            here = slice(at, at + step)
            part = jnp.dot(windows, conv_w[:, here], preferred_element_type=jnp.float32)
            part += streams[i][:, here].astype(jnp.float32)
            acc[:, here] = part
            total += jnp.sum(part * part, axis=1, keepdims=True)
        scale = lax.rsqrt(total / width + 1e-05)
        out_ref[done + i * rows : done + (i + 1) * rows] = (acc[...] * scale * gain[...]).astype(jnp.bfloat16)


def take(refs, source, core, rows):
    half = rows // 2
    cuts = [pl.ds(pl.multiple_of(source * rows + c * half, half), half) for c in (core, 1 - core)]
    return jnp.concatenate([jnp.concatenate([ref[:, at] for at in cuts], axis=1) for ref in refs], axis=0)


def three_shards(x_refs, own, near, received, far):
    z, core, _ = where_am_i()
    size, width = own.shape[0], 3 * HD
    w = [own[:, :width], received[:size], far[...]]
    w = jnp.concatenate(w + [near[:, :width], received[size : 2 * size]], axis=0)
    x = [take(x_refs, source, core, 2 * size) for source in (z, z ^ 2, z ^ 1)]
    return jnp.dot(jnp.concatenate(x, axis=1), w, preferred_element_type=jnp.float32)


def partial_kernel(*refs):
    refs[-1][...] = three_shards(refs[:2], *refs[2:-1])


def diagonal_kernel(mine, top, bottom, *refs):
    weights, (acc_ref, x_ref) = refs[:-2], refs[-2:]
    at = 0
    for ref in (mine, top, bottom):
        x_ref[at : at + ref.shape[0]] = ref[...]
        at += ref.shape[0]
    acc_ref[...] = three_shards([x_ref], *weights)


ROW_ORDER = ((0, 1, 2, 6), (3, 4, 5, 7))


def finish_kernel(*refs):
    x_refs, (last, acc_in, acc_diagonal, q_ref, k_ref, v_first, v_second) = refs[:3], refs[3:]
    z, core, _ = where_am_i()
    block, early = q_ref.shape[1] // 2, acc_in.shape[0]
    value = jnp.dot(take(x_refs, z ^ 3, core, last.shape[0]), last[...], preferred_element_type=jnp.float32)
    value = [acc_in[...] + value[:early], acc_diagonal[...] + value[early:]]
    value = jnp.concatenate(value, axis=0).astype(jnp.bfloat16)
    for rel in range(2):
        at = pl.ds(pl.multiple_of((core ^ rel) * block, block), block)
        for r in range(4):
            row = ROW_ORDER[rel][r]
            mine = value[row * block : (row + 1) * block]
            v_at = V_ORDER.index(r)
            q_ref[r, at, :] = mine[:, :HD]
            k_ref[r, at, :] = mine[:, HD:PAIR]
            (v_first, v_second)[v_at // 2][v_at % 2, at, :] = mine[:, PAIR:]


def spans(u):
    return ((0, u, 2), (1, 0, 2), (2, 0, 1 + u))


def neighbours(outer, own, middle, index):
    z, _, _ = where_am_i()
    odd = (z & 1) == 1
    outer, middle = outer[index], middle[index]
    return jnp.where(odd, outer, middle), own[index], jnp.where(odd, middle, outer)


def weigh_kernel(q_ref, middle, own, outer, own_flags, received, out_ref):
    _, core, _ = where_am_i()
    block = q_ref.shape[1] // 2
    inv_root = 1.0 / math.sqrt(HD)
    flags = [own_flags[:, :HD].astype(jnp.float32), received[-EXTRA:, :HD].astype(jnp.float32)]
    flags = [jnp.where(core == u, flags[0], flags[1]) for u in range(2)]
    bias = [(f - 1.0) * 1e30 for f in flags]
    for r in range(4):
        keys = neighbours(outer, own, middle, r)
        for u in range(2):
            q = q_ref[r, u * block : (u + 1) * block]
            scores = []
            for side, first, last in spans(u):
                k = keys[side][first * block : last * block]
                s = lax.dot_general(q, k, (((1,), (1,)), ((), ())), preferred_element_type=jnp.float32)
                for v in range(last - first):
                    entry = len(scores)
                    shut = jnp.broadcast_to(bias[u][r : r + 1, entry : entry + 1], (block, block))
                    scores.append(s[:, v * block : (v + 1) * block] * inv_root + shut)
            top = jnp.max(functools.reduce(jnp.maximum, scores), axis=1, keepdims=True)
            powers = [jnp.exp(s - top) for s in scores]
            inverse = 1.0 / jnp.sum(functools.reduce(jnp.add, powers), axis=1, keepdims=True)
            for entry, p in enumerate(powers):
                here = slice(entry * block, (entry + 1) * block)
                out_ref[r, u * block : (u + 1) * block, here] = (p * inverse).astype(jnp.bfloat16)


def mix_kernel(r, weights, middle, own, outer, out_ref):
    block = weights.shape[1] // 2
    values = neighbours(outer, own, middle, V_ORDER.index(r) % 2)
    for u in range(2):
        w = weights[r, u * block : (u + 1) * block]
        v = [values[side][first * block : last * block] for side, first, last in spans(u)]
        result = jnp.dot(w, jnp.concatenate(v, axis=0), preferred_element_type=jnp.float32)
        out_ref[u * block : (u + 1) * block] = result.astype(jnp.bfloat16)


def pack_kernel(*refs):
    keep_ref, send_ref = refs[4:]
    _, core, _ = where_am_i()
    block = keep_ref.shape[1]
    for r, ref in enumerate(refs[:4]):
        for rel, out_ref in enumerate((keep_ref, send_ref)):
            out_ref[r] = ref[pl.ds(pl.multiple_of((core ^ rel) * block, block), block), :]


def gather_kernel(mine, other, out_ref):
    _, core, depth = where_am_i()
    for rel, ref in enumerate((mine, other)):
        for r in range(4):
            at = pl.multiple_of((2 * (depth ^ r) + (core ^ rel)) * HD, HD)
            out_ref[:, pl.ds(at, HD)] = ref[r]


def call(kernel, outs, places, scratch=(), macs=0, limit=32):
    spaces = {"s": SMEM, "v": VMEM, "a": pl.ANY}
    return pl.pallas_call(
        kernel,
        out_shape=outs,
        in_specs=[pl.BlockSpec(memory_space=spaces[place]) for place in places],
        out_specs=jax.tree.map(lambda _: pl.BlockSpec(memory_space=VMEM), outs),
        scratch_shapes=list(scratch),
        cost_estimate=pl.CostEstimate(flops=2 * macs, bytes_accessed=0, transcendentals=0),
        compiler_params=pltpu.CompilerParams(vmem_limit_bytes=limit * 2**20),
    )


def plane_device(raw, stream, conv_w, gain, w_qkv, mask):
    time_len, site_len, feat_len = raw.shape
    block, width = time_len * site_len, stream.shape[2]
    half, size = width // 2, w_qkv.shape[0]
    bf16, f32 = jnp.bfloat16, jnp.float32

    def array(*shape, kind=bf16):
        return jax.ShapeDtypeStruct(shape, kind)

    far_raw = swap_z(w_qkv, 2)

    raw, stream = raw.reshape(block, feat_len), stream.reshape(block, width)
    conv_w, gain = conv_w.reshape(3 * feat_len, width), gain.reshape(1, width)
    more = block // 2 + EXTRA
    *to, kept, own_flags = call(
        split_kernel,
        (array(size + more, PAIR), array(size + more, PAIR), array(block, PAIR), array(size, PAIR), array(EXTRA, HD)),
        "svv",
    )(mask.reshape(mask.shape[2]), w_qkv, raw)
    plane = [swap_depth(t, r) for t, r in zip(to, (1, 2, 3))]
    own = call(sort_kernel, array(size, 6 * HD), "vvv")(kept, *plane[:2])
    near = swap_z(own, 1)

    def embed(rs, *streams, finished=()):
        out = (array((len(rs) + len(finished)) * block, width),) + (array(block, half),) * (len(rs) - 1) * 2
        return call(
            functools.partial(embed_kernel, rs, len(finished)),
            out,
            "v" * (6 + len(streams) + len(finished)),
            scratch=[VMEM((block, width), f32)],
            macs=len(rs) * block * 3 * feat_len * width,
        )(raw, *plane, conv_w, gain, *streams, *finished)

    tied = after(stream, plane[2])
    beside, above = swap_depth(tied, 1), swap_depth(tied, 2)
    (normed,) = embed((0,), stream)
    far_raw = after(far_raw, normed)

    even = (lax.axis_index("depth") & 1) == 0
    low, to_x, high = (far_raw[:, k * PAIR : (k + 1) * PAIR] for k in range(3))
    kept, to_y = jnp.where(even, low, high), jnp.where(even, high, low)
    from_x, from_y = swap_depth(to_x, 1), swap_depth(to_y, 2)
    beside, above = after(beside, to_x), after(above, to_y)
    stack, *diagonal = embed((1, 2), beside, above, finished=(normed,))
    from_x, from_y, stack, near = lax.optimization_barrier((from_x, from_y, stack, near))
    keep, send, flags = call(
        sort_far_kernel,
        (array(size, 3 * HD), array(size, 3 * HD), array(EXTRA, 3 * HD)),
        "v" * 7,
    )(kept, from_x, from_y, *plane, own_flags)
    diagonal = swap_depth(diagonal[0], 2), swap_depth(diagonal[1], 1)
    far = jnp.concatenate([keep, swap_core(send)], axis=0)
    last = swap_z(far, 1)
    far, near, stack = lax.optimization_barrier((far, near, stack))
    received = swap_core(jnp.concatenate([own[:, 3 * HD :], near[:, 3 * HD :], flags], axis=0))
    weights = (own, near, received, far)
    piece = 5 * block // 8
    early = (stack, swap_core(stack))
    rows = 2 * size
    total = call(partial_kernel, array(6 * block, 3 * HD, kind=f32), "v" * 6, macs=6 * block * 3 * rows * 3 * HD)(
        *early, *weights
    )
    (diagonal,) = embed((3,), jnp.concatenate([after(t, total) for t in diagonal], axis=1))
    swapped = [swap_core(diagonal[:piece]), swap_core(diagonal[piece:])]
    total_diagonal, diagonal = call(
        diagonal_kernel,
        (array(2 * block, 3 * HD, kind=f32), array(2 * block, width)),
        "v" * 7,
        macs=2 * block * 3 * rows * 3 * HD,
    )(diagonal, *swapped, *weights)
    one_head, half_head = array(4, 2 * block, HD), array(2, 2 * block, HD)
    q, k, *v = call(
        finish_kernel, (one_head, one_head, half_head, half_head), "v" * 6, macs=8 * block * rows * 3 * HD
    )(*early, diagonal, last, total, total_diagonal)

    weights = call(weigh_kernel, array(4, 2 * block, 5 * block), "v" * 6, macs=8 * block * 5 * block * HD)(
        q, swap_middle(k), k, swap_z(k, 1), flags, received
    )
    values = [(swap_middle(t), t, swap_z(t, 1)) for t in v]
    pieces = {}
    for r in V_ORDER:
        mixed = call(functools.partial(mix_kernel, r), array(2 * block, HD), "vvvv", macs=2 * block * 5 * block * HD)(
            weights, *values[V_ORDER.index(r) // 2]
        )
        pieces[r] = swap_depth(mixed, r) if r else mixed
    kept, sent = call(pack_kernel, (array(4, block, HD),) * 2, "vvvv")(*[pieces[r] for r in range(4)])
    context = call(gather_kernel, array(block, HEADS * HD), "vv")(kept, swap_core(sent))
    return context.reshape(time_len, site_len, HEADS * HD)


def from_behind(value, axis, by):
    devices = lax.axis_size(axis)
    pairs = [(i, i + by) for i in range(devices) if 0 <= i + by < devices]
    return lax.ppermute(value, axis, pairs)


def head_attend(query_head, key_head, value_head, allowed):
    inv_root = 1.0 / math.sqrt(HD)
    scores = (
        jnp.einsum("qd,kd->qk", query_head, key_head, preferred_element_type=jnp.float32) * inv_root
    )
    scores = jnp.where(allowed, scores, -1e30)
    row_max = jnp.max(scores, axis=-1, keepdims=True)
    powers = jnp.exp(scores - row_max)
    weights = (powers / jnp.sum(powers, axis=-1, keepdims=True)).astype(jnp.bfloat16)
    return jnp.dot(weights, value_head, preferred_element_type=jnp.float32).astype(jnp.bfloat16)


def per_device(raw, stream, conv_w, gain, w_qkv, mask):
    time_len, site_len, _ = raw.shape
    tok_rows = time_len * site_len
    normed = normed_tokens(padded_2(raw, (("depth", 1),), 1), stream, conv_w, gain)
    columns = lax.all_gather(w_qkv, "depth", axis=1, tiled=True)
    projected = jnp.dot(
        normed,
        lax.all_gather(columns, "tm", axis=0, tiled=True),
        preferred_element_type=jnp.float32,
    ).astype(jnp.bfloat16)
    head_cols = projected.shape[1] // 3
    queries = projected[:, :head_cols]
    keyvals = projected[:, head_cols:]
    earlier = []
    later = []
    moving_back = keyvals
    moving_ahead = keyvals
    for hop_index in range(RD):
        moving_back = from_behind(moving_back, "tm", 1)
        moving_ahead = from_behind(moving_ahead, "tm", -1)
        earlier.insert(0, moving_back)
        later.append(moving_ahead)
    gathered = jnp.concatenate(earlier + [keyvals] + later, axis=0)
    block_rows = BT * PP
    own_blocks = tok_rows // block_rows
    span_blocks = gathered.shape[0] // block_rows
    local_mask = mask[0]
    query_ids = jnp.arange(own_blocks, dtype=jnp.int32)[:, None]
    key_ids = jnp.arange(span_blocks, dtype=jnp.int32)[None, :]
    entry_ids = key_ids - query_ids
    picks = entry_ids[:, :, None] == jnp.arange(local_mask.shape[1], dtype=jnp.int32)[None, None, :]
    block_allowed = jnp.sum(jnp.where(picks, local_mask[:, None, :], 0), axis=-1) > 0
    allowed = jnp.repeat(jnp.repeat(block_allowed, block_rows, axis=0), block_rows, axis=1)
    query_heads = queries.reshape(tok_rows, HEADS, HD).transpose(1, 0, 2)
    key_heads = gathered[:, :head_cols].reshape(gathered.shape[0], HEADS, HD).transpose(1, 0, 2)
    value_heads = gathered[:, head_cols:].reshape(gathered.shape[0], HEADS, HD).transpose(1, 0, 2)
    context = lax.map(
        lambda operands: head_attend(operands[0], operands[1], operands[2], allowed),
        (query_heads, key_heads, value_heads),
    )
    return context.transpose(1, 0, 2).reshape(time_len, site_len, head_cols)


def solution(mesh):
    in_specs = (
        P("tm", "depth", None),
        P("tm", "depth", None),
        P(),
        P(),
        P("tm", "depth"),
        P("depth", "tm", None),
    )
    out_specs = P("tm", "depth", None)
    fits = mesh.shape["depth"] == 4 and mesh.shape["tm"] == 8
    return jax.shard_map(
        plane_device if fits else per_device, mesh=mesh, in_specs=in_specs, out_specs=out_specs, check_vma=False
    )
```

```python
import functools
import math

import jax
import jax.numpy as jnp
from jax import lax
from jax.experimental import pallas as pl
from jax.experimental.pallas import tpu as pltpu
from jax.sharding import PartitionSpec as P

HEADS = 8
HD = 128
BT = 16
PP = 8
RD = 2
VMEM = pltpu.VMEM
SMEM = pltpu.SMEM


def padded_2(value, sides, width):
    for axis, dim in sides:
        devices, length = (lax.axis_size(axis), value.shape[dim])
        up = [(i, (i + 1) % devices) for i in range(devices - 1)]
        down = [(j, i) for i, j in up]
        last = lax.slice_in_dim(value, length - width, length, axis=dim)
        leading = lax.slice_in_dim(value, 0, width, axis=dim)
        before = lax.ppermute(last, axis, up)
        after = lax.ppermute(leading, axis, down)
        value = jnp.concatenate([before, value, after], axis=dim)
    return value


def normed_tokens(padded, stream, conv_w, gain):
    time_len, site_len, width = stream.shape
    tok_rows = time_len * site_len
    embedded = stream.reshape(tok_rows, width).astype(jnp.float32)
    for offset in range(3):
        window = padded[:, offset : offset + site_len].reshape(tok_rows, padded.shape[2])
        embedded = embedded + jnp.dot(window, conv_w[offset], preferred_element_type=jnp.float32)
    scale = lax.rsqrt(jnp.mean(embedded * embedded, axis=-1, keepdims=True) + 1e-05)
    return (embedded * scale * gain).astype(jnp.bfloat16)


PAIR = 2 * HD
V_ORDER = (3, 1, 2, 0)
EXTRA = 16


def hop(value, fn):
    pairs = []
    for z in range(4):
        for core in range(2):
            for depth in range(4):
                to = fn(z, core, depth)
                if to is not None:
                    pairs.append(((2 * z + core) * 4 + depth, (2 * to[0] + to[1]) * 4 + to[2]))
    return lax.ppermute(value, ("tm", "depth"), pairs)


def swap_core(value):
    return hop(value, lambda z, c, d: (z, 1 - c, d))


def swap_depth(value, bits):
    return hop(value, lambda z, c, d: (z, c, d ^ bits))


def swap_z(value, bits):
    return hop(value, lambda z, c, d: (z ^ bits, c, d))


def swap_middle(value):
    return hop(value, lambda z, c, d: (z ^ 3, c, d) if z in (1, 2) else None)


def after(value, *others):
    return lax.optimization_barrier((value, *others))[0]


def where_am_i():
    tm = lax.axis_index("tm")
    return tm >> 1, tm & 1, lax.axis_index("depth")


def split_kernel(w, raw, to_x, to_y, to_across, keep):
    _, _, depth = where_am_i()
    even = (depth & 1) == 0
    size, half = w.shape[0], (raw.shape[0] - EXTRA) // 2
    low, high = w[:, :PAIR], w[:, 2 * PAIR :]
    to_x[:size] = w[:, PAIR : 2 * PAIR]
    to_y[:size] = jnp.where(even, high, low)
    keep[...] = jnp.where(even, low, high)
    at = to_across.shape[0] - EXTRA - half
    for i in range(2):
        to_across[:at, i * HD : (i + 1) * HD] = raw[:at]
    for ref, at in ((to_x, size), (to_y, size), (to_across, at)):
        for i in range(2):
            here = slice(i * HD, (i + 1) * HD)
            ref[at : at + half, here] = raw[i * half : (i + 1) * half]
            ref[at + half :, here] = raw[2 * half :]


def sorted_groups(kept, from_x, from_y):
    _, core, depth = where_am_i()
    first, even = core == 0, (depth & 1) == 0
    size = kept.shape[0]
    low = jnp.where(even, kept[...], from_y[:size])
    high = jnp.where(even, from_y[:size], kept[...])
    groups = (low, from_x[:size], high)
    turn = jnp.where(depth == 3, 0, depth)
    for third in range(3):
        group = jnp.where(turn == 0, groups[third], jnp.where(turn == 1, groups[(third + 1) % 3], groups[(third + 2) % 3]))
        yield third, jnp.where(first, group[:, :HD], group[:, HD:]), jnp.where(first, group[:, HD:], group[:, :HD])


def sort_kernel(kept, from_x, from_y, out_ref):
    for third, mine, other in sorted_groups(kept, from_x, from_y):
        out_ref[:, third * HD : (third + 1) * HD] = mine
        out_ref[:, (3 + third) * HD : (4 + third) * HD] = other


def sort_far_kernel(kept, from_x, from_y, plane_x, plane_y, across, raw, keep_ref, send_ref, flags_ref):
    for third, mine, other in sorted_groups(kept, from_x, from_y):
        send_ref[:, third * HD : (third + 1) * HD] = other
        keep_ref[:, third * HD : (third + 1) * HD] = mine
    row = lax.broadcasted_iota(jnp.int32, (EXTRA, HD), 0)
    flags = raw[raw.shape[0] - EXTRA :].astype(jnp.float32)
    for r, ref in enumerate((plane_x, plane_y, across)):
        flags = jnp.where(row == r + 1, ref[ref.shape[0] - EXTRA :, :HD].astype(jnp.float32), flags)
    flags = flags.astype(jnp.bfloat16)
    for k in range(3):
        flags_ref[:, k * HD : (k + 1) * HD] = flags


def embed_kernel(rs, more, raw, plane_x, plane_y, across, conv_w, gain, *refs):
    count = len(rs)
    streams, finished, (out_ref, *onward, acc) = refs[:count], refs[count : count + more], refs[count + more :]
    for ref in finished:
        out_ref[: ref.shape[0]] = ref[...]
    for i, ref in enumerate(onward):
        half = ref.shape[1]
        ref[...] = streams[i][:, i * half : (i + 1) * half]
    _, _, depth = where_am_i()
    rows, width = raw.shape[0] - EXTRA, conv_w.shape[1]
    raws = [raw[:rows]]
    for ref in (plane_x, plane_y, across):
        at = ref.shape[0] - EXTRA - rows // 2
        raws.append(jnp.concatenate([ref[at : at + rows // 2, :HD], ref[at : at + rows // 2, HD:]], axis=0))
    raws = [value.astype(jnp.float32).reshape(rows // PP, PP, HD) for value in raws]
    done = out_ref.shape[0] - len(rs) * rows
    for i, r in enumerate(rs):
        place = depth ^ r
        even = (place & 1) == 0
        side, far = raws[r ^ 1], raws[r ^ 3]
        before = jnp.where(even, jnp.where(place == 2, far[:, PP - 1 :], 0.0), side[:, PP - 1 :])
        behind = jnp.where(even, side[:, :1], jnp.where(place == 1, far[:, :1], 0.0))
        padded = jnp.concatenate([before, raws[r], behind], axis=1)
        windows = [padded[:, j : j + PP].reshape(rows, HD).astype(jnp.bfloat16) for j in range(3)]
        windows = jnp.concatenate(windows, axis=1)
        total, step = jnp.zeros((rows, 1), jnp.float32), width // 4
        for at in range(0, width, step):
            here = slice(at, at + step)
            part = jnp.dot(windows, conv_w[:, here], preferred_element_type=jnp.float32)
            part += streams[i][:, here].astype(jnp.float32)
            acc[:, here] = part
            total += jnp.sum(part * part, axis=1, keepdims=True)
        scale = lax.rsqrt(total / width + 1e-05)
        out_ref[done + i * rows : done + (i + 1) * rows] = (acc[...] * scale * gain[...]).astype(jnp.bfloat16)


def take(refs, source, core, rows):
    half = rows // 2
    cuts = [pl.ds(pl.multiple_of(source * rows + c * half, half), half) for c in (core, 1 - core)]
    return jnp.concatenate([jnp.concatenate([ref[:, at] for at in cuts], axis=1) for ref in refs], axis=0)


def three_shards(x_refs, own, near, received, far):
    z, core, _ = where_am_i()
    size, width = own.shape[0], 3 * HD
    w = [own[:, :width], received[:size], far[...]]
    w = jnp.concatenate(w + [near[:, :width], received[size : 2 * size]], axis=0)
    x = [take(x_refs, source, core, 2 * size) for source in (z, z ^ 2, z ^ 1)]
    return jnp.dot(jnp.concatenate(x, axis=1), w, preferred_element_type=jnp.float32)


def partial_kernel(*refs):
    refs[-1][...] = three_shards(refs[:2], *refs[2:-1])


def diagonal_kernel(mine, top, bottom, *refs):
    weights, (acc_ref, x_ref) = refs[:-2], refs[-2:]
    at = 0
    for ref in (mine, top, bottom):
        x_ref[at : at + ref.shape[0]] = ref[...]
        at += ref.shape[0]
    acc_ref[...] = three_shards([x_ref], *weights)


ROW_ORDER = ((0, 1, 2, 6), (3, 4, 5, 7))


def finish_kernel(*refs):
    x_refs, (last, acc_in, acc_diagonal, q_ref, k_ref, v_first, v_second) = refs[:3], refs[3:]
    z, core, _ = where_am_i()
    block, early = q_ref.shape[1] // 2, acc_in.shape[0]
    value = jnp.dot(take(x_refs, z ^ 3, core, last.shape[0]), last[...], preferred_element_type=jnp.float32)
    value = [acc_in[...] + value[:early], acc_diagonal[...] + value[early:]]
    value = jnp.concatenate(value, axis=0).astype(jnp.bfloat16)
    for rel in range(2):
        at = pl.ds(pl.multiple_of((core ^ rel) * block, block), block)
        for r in range(4):
            row = ROW_ORDER[rel][r]
            mine = value[row * block : (row + 1) * block]
            v_at = V_ORDER.index(r)
            q_ref[r, at, :] = mine[:, :HD]
            k_ref[r, at, :] = mine[:, HD:PAIR]
            (v_first, v_second)[v_at // 2][v_at % 2, at, :] = mine[:, PAIR:]


def spans(u):
    return ((0, u, 2), (1, 0, 2), (2, 0, 1 + u))


def neighbours(outer, own, middle, index):
    z, _, _ = where_am_i()
    odd = (z & 1) == 1
    outer, middle = outer[index], middle[index]
    return jnp.where(odd, outer, middle), own[index], jnp.where(odd, middle, outer)


def weigh_kernel(q_ref, outer, own, middle, own_flags, received, out_ref):
    _, core, _ = where_am_i()
    block = q_ref.shape[1] // 2
    inv_root = 1.0 / math.sqrt(HD)
    flags = [own_flags[:, :HD].astype(jnp.float32), received[-EXTRA:, :HD].astype(jnp.float32)]
    flags = [jnp.where(core == u, flags[0], flags[1]) for u in range(2)]
    bias = [(f - 1.0) * 1e30 for f in flags]
    for r in range(4):
        keys = neighbours(outer, own, middle, r)
        for u in range(2):
            q = q_ref[r, u * block : (u + 1) * block]
            scores = []
            for side, first, last in spans(u):
                k = keys[side][first * block : last * block]
                s = lax.dot_general(q, k, (((1,), (1,)), ((), ())), preferred_element_type=jnp.float32)
                for v in range(last - first):
                    entry = len(scores)
                    shut = jnp.broadcast_to(bias[u][r : r + 1, entry : entry + 1], (block, block))
                    scores.append(s[:, v * block : (v + 1) * block] * inv_root + shut)
            top = jnp.max(functools.reduce(jnp.maximum, scores), axis=1, keepdims=True)
            powers = [jnp.exp(s - top) for s in scores]
            inverse = 1.0 / jnp.sum(functools.reduce(jnp.add, powers), axis=1, keepdims=True)
            for entry, p in enumerate(powers):
                here = slice(entry * block, (entry + 1) * block)
                out_ref[r, u * block : (u + 1) * block, here] = (p * inverse).astype(jnp.bfloat16)


def mix_kernel(r, weights, outer, own, middle, out_ref):
    block = weights.shape[1] // 2
    values = neighbours(outer, own, middle, V_ORDER.index(r) % 2)
    for u in range(2):
        w = weights[r, u * block : (u + 1) * block]
        v = [values[side][first * block : last * block] for side, first, last in spans(u)]
        result = jnp.dot(w, jnp.concatenate(v, axis=0), preferred_element_type=jnp.float32)
        out_ref[u * block : (u + 1) * block] = result.astype(jnp.bfloat16)


def pack_kernel(*refs):
    keep_ref, send_ref = refs[4:]
    _, core, _ = where_am_i()
    block = keep_ref.shape[1]
    for r, ref in enumerate(refs[:4]):
        for rel, out_ref in enumerate((keep_ref, send_ref)):
            out_ref[r] = ref[pl.ds(pl.multiple_of((core ^ rel) * block, block), block), :]


def gather_kernel(mine, other, out_ref):
    _, core, depth = where_am_i()
    for rel, ref in enumerate((mine, other)):
        for r in range(4):
            at = pl.multiple_of((2 * (depth ^ r) + (core ^ rel)) * HD, HD)
            out_ref[:, pl.ds(at, HD)] = ref[r]


def call(kernel, outs, places, scratch=(), macs=0, limit=32):
    spaces = {"v": VMEM}
    return pl.pallas_call(
        kernel,
        out_shape=outs,
        in_specs=[pl.BlockSpec(memory_space=spaces[place]) for place in places],
        out_specs=jax.tree.map(lambda _: pl.BlockSpec(memory_space=VMEM), outs),
        scratch_shapes=list(scratch),
        cost_estimate=pl.CostEstimate(flops=2 * macs, bytes_accessed=0, transcendentals=0),
        compiler_params=pltpu.CompilerParams(vmem_limit_bytes=limit * 2**20),
    )


def plane_device(raw, stream, conv_w, gain, w_qkv, mask):
    time_len, site_len, feat_len = raw.shape
    block, width = time_len * site_len, stream.shape[2]
    half, size = width // 2, w_qkv.shape[0]
    bf16, f32 = jnp.bfloat16, jnp.float32

    def array(*shape, kind=bf16):
        return jax.ShapeDtypeStruct(shape, kind)

    far_raw = swap_z(w_qkv, 2)

    mask_row = jnp.pad(mask.reshape(1, mask.shape[2]), ((0, 0), (0, feat_len - mask.shape[2]))).astype(bf16)
    raw = jnp.concatenate([raw.reshape(block, feat_len), jnp.broadcast_to(mask_row, (EXTRA, feat_len))], axis=0)
    stream = stream.reshape(block, width)
    conv_w, gain = conv_w.reshape(3 * feat_len, width), gain.reshape(1, width)
    more = block // 2 + EXTRA
    *to, kept = call(
        split_kernel,
        (array(size + more, PAIR), array(size + more, PAIR), array(block, PAIR), array(size, PAIR)),
        "vv",
    )(w_qkv, raw)
    plane = [swap_depth(t, r) for t, r in zip(to, (1, 2, 3))]
    own = call(sort_kernel, array(size, 6 * HD), "vvv")(kept, *plane[:2])
    near = swap_z(own, 1)

    def embed(rs, *streams, finished=()):
        out = (array((len(rs) + len(finished)) * block, width),) + (array(block, half),) * (len(rs) - 1) * 2
        return call(
            functools.partial(embed_kernel, rs, len(finished)),
            out,
            "v" * (6 + len(streams) + len(finished)),
            scratch=[VMEM((block, width), f32)],
            macs=len(rs) * block * 3 * feat_len * width,
        )(raw, *plane, conv_w, gain, *streams, *finished)

    tied = after(stream, plane[2])
    beside, above = swap_depth(tied, 1), swap_depth(tied, 2)
    (normed,) = embed((0,), stream)
    far_raw = after(far_raw, normed)

    even = (lax.axis_index("depth") & 1) == 0
    low, to_x, high = (far_raw[:, k * PAIR : (k + 1) * PAIR] for k in range(3))
    kept, to_y = jnp.where(even, low, high), jnp.where(even, high, low)
    from_x, from_y = swap_depth(to_x, 1), swap_depth(to_y, 2)
    beside, above = after(beside, to_x), after(above, to_y)
    stack, *diagonal = embed((1, 2), beside, above, finished=(normed,))
    from_x, from_y, stack, near = lax.optimization_barrier((from_x, from_y, stack, near))
    keep, send, flags = call(
        sort_far_kernel,
        (array(size, 3 * HD), array(size, 3 * HD), array(EXTRA, 3 * HD)),
        "v" * 7,
    )(kept, from_x, from_y, *plane, raw)
    diagonal = swap_depth(diagonal[0], 2), swap_depth(diagonal[1], 1)
    far = jnp.concatenate([keep, swap_core(send)], axis=0)
    last = swap_z(far, 1)
    far, near, stack = lax.optimization_barrier((far, near, stack))
    received = swap_core(jnp.concatenate([own[:, 3 * HD :], near[:, 3 * HD :], flags], axis=0))
    weights = (own, near, received, far)
    piece = 5 * block // 8
    early = (stack, swap_core(stack))
    rows = 2 * size
    total = call(partial_kernel, array(6 * block, 3 * HD, kind=f32), "v" * 6, macs=6 * block * 3 * rows * 3 * HD)(
        *early, *weights
    )
    (diagonal,) = embed((3,), jnp.concatenate([after(t, total) for t in diagonal], axis=1))
    swapped = [swap_core(diagonal[:piece]), swap_core(diagonal[piece:])]
    total_diagonal, diagonal = call(
        diagonal_kernel,
        (array(2 * block, 3 * HD, kind=f32), array(2 * block, width)),
        "v" * 7,
        macs=2 * block * 3 * rows * 3 * HD,
    )(diagonal, *swapped, *weights)
    one_head, half_head = array(4, 2 * block, HD), array(2, 2 * block, HD)
    q, k, *v = call(
        finish_kernel, (one_head, one_head, half_head, half_head), "v" * 6, macs=8 * block * rows * 3 * HD
    )(*early, diagonal, last, total, total_diagonal)

    weights = call(weigh_kernel, array(4, 2 * block, 5 * block), "v" * 6, macs=8 * block * 5 * block * HD)(
        q, swap_z(k, 1), k, swap_middle(k), flags, received
    )
    values = [(swap_z(t, 1), t, swap_middle(t)) for t in v]
    pieces = {}
    for i, r in enumerate(V_ORDER):
        mixed = call(functools.partial(mix_kernel, r), array(2 * block, HD), "vvvv", macs=2 * block * 5 * block * HD)(
            weights, *values[i // 2]
        )
        pieces[r] = swap_depth(mixed, r) if r else mixed
    kept, sent = call(pack_kernel, (array(4, block, HD),) * 2, "vvvv")(*[pieces[r] for r in range(4)])
    context = call(gather_kernel, array(block, HEADS * HD), "vv")(kept, swap_core(sent))
    return context.reshape(time_len, site_len, HEADS * HD)


def from_behind(value, axis, by):
    devices = lax.axis_size(axis)
    pairs = [(i, i + by) for i in range(devices) if 0 <= i + by < devices]
    return lax.ppermute(value, axis, pairs)


def head_attend(query_head, key_head, value_head, allowed):
    inv_root = 1.0 / math.sqrt(HD)
    scores = (
        jnp.einsum("qd,kd->qk", query_head, key_head, preferred_element_type=jnp.float32) * inv_root
    )
    scores = jnp.where(allowed, scores, -1e30)
    row_max = jnp.max(scores, axis=-1, keepdims=True)
    powers = jnp.exp(scores - row_max)
    weights = (powers / jnp.sum(powers, axis=-1, keepdims=True)).astype(jnp.bfloat16)
    return jnp.dot(weights, value_head, preferred_element_type=jnp.float32).astype(jnp.bfloat16)


def per_device(raw, stream, conv_w, gain, w_qkv, mask):
    time_len, site_len, _ = raw.shape
    tok_rows = time_len * site_len
    normed = normed_tokens(padded_2(raw, (("depth", 1),), 1), stream, conv_w, gain)
    columns = lax.all_gather(w_qkv, "depth", axis=1, tiled=True)
    projected = jnp.dot(
        normed,
        lax.all_gather(columns, "tm", axis=0, tiled=True),
        preferred_element_type=jnp.float32,
    ).astype(jnp.bfloat16)
    head_cols = projected.shape[1] // 3
    queries = projected[:, :head_cols]
    keyvals = projected[:, head_cols:]
    earlier = []
    later = []
    moving_back = keyvals
    moving_ahead = keyvals
    for hop_index in range(RD):
        moving_back = from_behind(moving_back, "tm", 1)
        moving_ahead = from_behind(moving_ahead, "tm", -1)
        earlier.insert(0, moving_back)
        later.append(moving_ahead)
    gathered = jnp.concatenate(earlier + [keyvals] + later, axis=0)
    block_rows = BT * PP
    own_blocks = tok_rows // block_rows
    span_blocks = gathered.shape[0] // block_rows
    local_mask = mask[0]
    query_ids = jnp.arange(own_blocks, dtype=jnp.int32)[:, None]
    key_ids = jnp.arange(span_blocks, dtype=jnp.int32)[None, :]
    entry_ids = key_ids - query_ids
    picks = entry_ids[:, :, None] == jnp.arange(local_mask.shape[1], dtype=jnp.int32)[None, None, :]
    block_allowed = jnp.sum(jnp.where(picks, local_mask[:, None, :], 0), axis=-1) > 0
    allowed = jnp.repeat(jnp.repeat(block_allowed, block_rows, axis=0), block_rows, axis=1)
    query_heads = queries.reshape(tok_rows, HEADS, HD).transpose(1, 0, 2)
    key_heads = gathered[:, :head_cols].reshape(gathered.shape[0], HEADS, HD).transpose(1, 0, 2)
    value_heads = gathered[:, head_cols:].reshape(gathered.shape[0], HEADS, HD).transpose(1, 0, 2)
    context = lax.map(
        lambda operands: head_attend(operands[0], operands[1], operands[2], allowed),
        (query_heads, key_heads, value_heads),
    )
    return context.transpose(1, 0, 2).reshape(time_len, site_len, head_cols)


def solution(mesh):
    in_specs = (
        P("tm", "depth", None),
        P("tm", "depth", None),
        P(),
        P(),
        P("tm", "depth"),
        P("depth", "tm", None),
    )
    out_specs = P("tm", "depth", None)
    fits = mesh.shape["depth"] == 4 and mesh.shape["tm"] == 8
    return jax.shard_map(
        plane_device if fits else per_device, mesh=mesh, in_specs=in_specs, out_specs=out_specs, check_vma=False
    )
```

```python
import functools
import math

import jax
import jax.numpy as jnp
from jax import lax
from jax.experimental import pallas as pl
from jax.experimental.pallas import tpu as pltpu
from jax.sharding import PartitionSpec as P

HEADS = 8
HD = 128
BT = 16
PP = 8
RD = 2
VMEM = pltpu.VMEM
SMEM = pltpu.SMEM


def padded_2(value, sides, width):
    for axis, dim in sides:
        devices, length = (lax.axis_size(axis), value.shape[dim])
        up = [(i, (i + 1) % devices) for i in range(devices - 1)]
        down = [(j, i) for i, j in up]
        last = lax.slice_in_dim(value, length - width, length, axis=dim)
        leading = lax.slice_in_dim(value, 0, width, axis=dim)
        before = lax.ppermute(last, axis, up)
        after = lax.ppermute(leading, axis, down)
        value = jnp.concatenate([before, value, after], axis=dim)
    return value


def normed_tokens(padded, stream, conv_w, gain):
    time_len, site_len, width = stream.shape
    tok_rows = time_len * site_len
    embedded = stream.reshape(tok_rows, width).astype(jnp.float32)
    for offset in range(3):
        window = padded[:, offset : offset + site_len].reshape(tok_rows, padded.shape[2])
        embedded = embedded + jnp.dot(window, conv_w[offset], preferred_element_type=jnp.float32)
    scale = lax.rsqrt(jnp.mean(embedded * embedded, axis=-1, keepdims=True) + 1e-05)
    return (embedded * scale * gain).astype(jnp.bfloat16)


PAIR = 2 * HD
V_ORDER = (3, 1, 2, 0)
EXTRA = 16


def hop(value, fn):
    pairs = []
    for z in range(4):
        for core in range(2):
            for depth in range(4):
                to = fn(z, core, depth)
                if to is not None:
                    pairs.append(((2 * z + core) * 4 + depth, (2 * to[0] + to[1]) * 4 + to[2]))
    return lax.ppermute(value, ("tm", "depth"), pairs)


def swap_core(value):
    return hop(value, lambda z, c, d: (z, 1 - c, d))


def swap_depth(value, bits):
    return hop(value, lambda z, c, d: (z, c, d ^ bits))


def swap_z(value, bits):
    return hop(value, lambda z, c, d: (z ^ bits, c, d))


def swap_middle(value):
    return hop(value, lambda z, c, d: (z ^ 3, c, d) if z in (1, 2) else None)


def after(value, *others):
    return lax.optimization_barrier((value, *others))[0]


def where_am_i():
    tm = lax.axis_index("tm")
    return tm >> 1, tm & 1, lax.axis_index("depth")


def split_kernel(w, raw, to_x, to_y, to_across, keep):
    _, _, depth = where_am_i()
    even = (depth & 1) == 0
    size, half = w.shape[0], (raw.shape[0] - EXTRA) // 2
    low, high = w[:, :PAIR], w[:, 2 * PAIR :]
    to_x[:size] = w[:, PAIR : 2 * PAIR]
    to_y[:size] = jnp.where(even, high, low)
    keep[...] = jnp.where(even, low, high)
    at = to_across.shape[0] - EXTRA - half
    for i in range(2):
        to_across[:at, i * HD : (i + 1) * HD] = raw[:at]
    for ref, at in ((to_x, size), (to_y, size), (to_across, at)):
        for i in range(2):
            here = slice(i * HD, (i + 1) * HD)
            ref[at : at + half, here] = raw[i * half : (i + 1) * half]
            ref[at + half :, here] = raw[2 * half :]


def sorted_groups(kept, from_x, from_y):
    _, core, depth = where_am_i()
    first, even = core == 0, (depth & 1) == 0
    size = kept.shape[0]
    low = jnp.where(even, kept[...], from_y[:size])
    high = jnp.where(even, from_y[:size], kept[...])
    groups = (low, from_x[:size], high)
    turn = jnp.where(depth == 3, 0, depth)
    for third in range(3):
        group = jnp.where(turn == 0, groups[third], jnp.where(turn == 1, groups[(third + 1) % 3], groups[(third + 2) % 3]))
        yield third, jnp.where(first, group[:, :HD], group[:, HD:]), jnp.where(first, group[:, HD:], group[:, :HD])


def sort_kernel(kept, from_x, from_y, out_ref):
    for third, mine, other in sorted_groups(kept, from_x, from_y):
        out_ref[:, third * HD : (third + 1) * HD] = mine
        out_ref[:, (3 + third) * HD : (4 + third) * HD] = other


def sort_far_kernel(kept, from_x, from_y, plane_x, plane_y, across, raw, keep_ref, send_ref, flags_ref):
    for third, mine, other in sorted_groups(kept, from_x, from_y):
        send_ref[:, third * HD : (third + 1) * HD] = other
        keep_ref[:, third * HD : (third + 1) * HD] = mine
    row = lax.broadcasted_iota(jnp.int32, (EXTRA, HD), 0)
    flags = raw[raw.shape[0] - EXTRA :].astype(jnp.float32)
    for r, ref in enumerate((plane_x, plane_y, across)):
        flags = jnp.where(row == r + 1, ref[ref.shape[0] - EXTRA :, :HD].astype(jnp.float32), flags)
    flags = flags.astype(jnp.bfloat16)
    for k in range(3):
        flags_ref[:, k * HD : (k + 1) * HD] = flags


def other_kernel(own, near, flags, out_ref):
    size, width = own.shape[0], 3 * HD
    out_ref[:size] = own[:, width:]
    out_ref[size : 2 * size] = near[:, width:]
    out_ref[2 * size :] = flags[...]


def embed_kernel(rs, more, raw, plane_x, plane_y, across, conv_w, gain, *refs):
    count = len(rs)
    halves = 2 if rs == (3,) else 1
    count *= halves
    streams, finished, (out_ref, *onward, acc) = refs[:count], refs[count : count + more], refs[count + more :]
    for ref in finished:
        out_ref[: ref.shape[0]] = ref[...]
    if len(rs) > 1:
        for i, ref in enumerate(onward):
            half = ref.shape[1]
            ref[...] = streams[i][:, i * half : (i + 1) * half]
    _, _, depth = where_am_i()
    rows, width = raw.shape[0] - EXTRA, conv_w.shape[1]
    raws = [raw[:rows]]
    for ref in (plane_x, plane_y, across):
        at = ref.shape[0] - EXTRA - rows // 2
        raws.append(jnp.concatenate([ref[at : at + rows // 2, :HD], ref[at : at + rows // 2, HD:]], axis=0))
    raws = [value.astype(jnp.float32).reshape(rows // PP, PP, HD) for value in raws]
    done = out_ref.shape[0] - len(rs) * rows
    for i, r in enumerate(rs):
        place = depth ^ r
        even = (place & 1) == 0
        side, far = raws[r ^ 1], raws[r ^ 3]
        before = jnp.where(even, jnp.where(place == 2, far[:, PP - 1 :], 0.0), side[:, PP - 1 :])
        behind = jnp.where(even, side[:, :1], jnp.where(place == 1, far[:, :1], 0.0))
        padded = jnp.concatenate([before, raws[r], behind], axis=1)
        windows = [padded[:, j : j + PP].reshape(rows, HD).astype(jnp.bfloat16) for j in range(3)]
        windows = jnp.concatenate(windows, axis=1)
        total, step = jnp.zeros((rows, 1), jnp.float32), width // 4
        for at in range(0, width, step):
            here = slice(at, at + step)
            part = jnp.dot(windows, conv_w[:, here], preferred_element_type=jnp.float32)
            each = width // halves
            part += streams[i + at // each][:, at % each : at % each + step].astype(jnp.float32)
            acc[:, here] = part
            total += jnp.sum(part * part, axis=1, keepdims=True)
        scale = lax.rsqrt(total / width + 1e-05)
        normed = (acc[...] * scale * gain[...]).astype(jnp.bfloat16)
        out_ref[done + i * rows : done + (i + 1) * rows] = normed
        if halves > 1:
            cut = onward[0].shape[0]
            onward[0][...], onward[1][...] = normed[:cut], normed[cut:]


def take(refs, source, core, rows):
    half = rows // 2
    cuts = [pl.ds(pl.multiple_of(source * rows + c * half, half), half) for c in (core, 1 - core)]
    return jnp.concatenate([jnp.concatenate([ref[:, at] for at in cuts], axis=1) for ref in refs], axis=0)


def three_shards(x_refs, own, near, received, far):
    z, core, _ = where_am_i()
    size, width = own.shape[0], 3 * HD
    w = [own[:, :width], received[:size], far[...]]
    w = jnp.concatenate(w + [near[:, :width], received[size : 2 * size]], axis=0)
    x = [take(x_refs, source, core, 2 * size) for source in (z, z ^ 2, z ^ 1)]
    return jnp.dot(jnp.concatenate(x, axis=1), w, preferred_element_type=jnp.float32)


def partial_kernel(*refs):
    refs[-1][...] = three_shards(refs[:2], *refs[2:-1])


def diagonal_kernel(mine, top, bottom, *refs):
    weights, (acc_ref, x_ref) = refs[:-2], refs[-2:]
    at = 0
    for ref in (mine, top, bottom):
        x_ref[at : at + ref.shape[0]] = ref[...]
        at += ref.shape[0]
    acc_ref[...] = three_shards([x_ref], *weights)


ROW_ORDER = ((0, 1, 2, 6), (3, 4, 5, 7))


def finish_kernel(*refs):
    x_refs, (last, acc_in, acc_diagonal, q_ref, k_ref, v_first, v_second) = refs[:3], refs[3:]
    z, core, _ = where_am_i()
    block, early = q_ref.shape[1] // 2, acc_in.shape[0]
    value = jnp.dot(take(x_refs, z ^ 3, core, last.shape[0]), last[...], preferred_element_type=jnp.float32)
    value = [acc_in[...] + value[:early], acc_diagonal[...] + value[early:]]
    value = jnp.concatenate(value, axis=0).astype(jnp.bfloat16)
    for rel in range(2):
        at = pl.ds(pl.multiple_of((core ^ rel) * block, block), block)
        for r in range(4):
            row = ROW_ORDER[rel][r]
            mine = value[row * block : (row + 1) * block]
            v_at = V_ORDER.index(r)
            q_ref[r, at, :] = mine[:, :HD]
            k_ref[r, at, :] = mine[:, HD:PAIR]
            (v_first, v_second)[v_at // 2][v_at % 2, at, :] = mine[:, PAIR:]


def spans(u):
    return ((0, u, 2), (1, 0, 2), (2, 0, 1 + u))


def neighbours(outer, own, middle, index):
    z, _, _ = where_am_i()
    odd = (z & 1) == 1
    outer, middle = outer[index], middle[index]
    return jnp.where(odd, outer, middle), own[index], jnp.where(odd, middle, outer)


def weigh_kernel(q_ref, outer, own, middle, own_flags, received, out_ref):
    _, core, _ = where_am_i()
    block = q_ref.shape[1] // 2
    inv_root = 1.0 / math.sqrt(HD)
    flags = [own_flags[:, :HD].astype(jnp.float32), received[-EXTRA:, :HD].astype(jnp.float32)]
    flags = [jnp.where(core == u, flags[0], flags[1]) for u in range(2)]
    bias = [(f - 1.0) * 1e30 for f in flags]
    for r in range(4):
        keys = neighbours(outer, own, middle, r)
        for u in range(2):
            q = q_ref[r, u * block : (u + 1) * block]
            scores = []
            for side, first, last in spans(u):
                k = keys[side][first * block : last * block]
                s = lax.dot_general(q, k, (((1,), (1,)), ((), ())), preferred_element_type=jnp.float32)
                for v in range(last - first):
                    entry = len(scores)
                    shut = jnp.broadcast_to(bias[u][r : r + 1, entry : entry + 1], (block, block))
                    scores.append(s[:, v * block : (v + 1) * block] * inv_root + shut)
            top = jnp.max(functools.reduce(jnp.maximum, scores), axis=1, keepdims=True)
            powers = [jnp.exp(s - top) for s in scores]
            inverse = 1.0 / jnp.sum(functools.reduce(jnp.add, powers), axis=1, keepdims=True)
            for entry, p in enumerate(powers):
                here = slice(entry * block, (entry + 1) * block)
                out_ref[r, u * block : (u + 1) * block, here] = (p * inverse).astype(jnp.bfloat16)


def mix_kernel(r, weights, outer, own, middle, out_ref):
    block = weights.shape[1] // 2
    values = neighbours(outer, own, middle, V_ORDER.index(r) % 2)
    for u in range(2):
        w = weights[r, u * block : (u + 1) * block]
        v = [values[side][first * block : last * block] for side, first, last in spans(u)]
        result = jnp.dot(w, jnp.concatenate(v, axis=0), preferred_element_type=jnp.float32)
        out_ref[u * block : (u + 1) * block] = result.astype(jnp.bfloat16)


def pack_kernel(*refs):
    keep_ref, send_ref = refs[4:]
    _, core, _ = where_am_i()
    block = keep_ref.shape[1]
    for r, ref in enumerate(refs[:4]):
        for rel, out_ref in enumerate((keep_ref, send_ref)):
            out_ref[r] = ref[pl.ds(pl.multiple_of((core ^ rel) * block, block), block), :]


def gather_kernel(mine, other, out_ref):
    _, core, depth = where_am_i()
    for rel, ref in enumerate((mine, other)):
        for r in range(4):
            at = pl.multiple_of((2 * (depth ^ r) + (core ^ rel)) * HD, HD)
            out_ref[:, pl.ds(at, HD)] = ref[r]


def call(kernel, outs, places, scratch=(), macs=0, limit=32):
    spaces = {"v": VMEM}
    return pl.pallas_call(
        kernel,
        out_shape=outs,
        in_specs=[pl.BlockSpec(memory_space=spaces[place]) for place in places],
        out_specs=jax.tree.map(lambda _: pl.BlockSpec(memory_space=VMEM), outs),
        scratch_shapes=list(scratch),
        cost_estimate=pl.CostEstimate(flops=2 * macs, bytes_accessed=0, transcendentals=0),
        compiler_params=pltpu.CompilerParams(vmem_limit_bytes=limit * 2**20),
    )


def plane_device(raw, stream, conv_w, gain, w_qkv, mask):
    time_len, site_len, feat_len = raw.shape
    block, width = time_len * site_len, stream.shape[2]
    half, size = width // 2, w_qkv.shape[0]
    bf16, f32 = jnp.bfloat16, jnp.float32

    def array(*shape, kind=bf16):
        return jax.ShapeDtypeStruct(shape, kind)

    far_raw = swap_z(w_qkv, 2)

    mask_row = jnp.pad(mask.reshape(1, mask.shape[2]), ((0, 0), (0, feat_len - mask.shape[2]))).astype(bf16)
    raw = jnp.concatenate([raw.reshape(block, feat_len), jnp.broadcast_to(mask_row, (EXTRA, feat_len))], axis=0)
    stream = stream.reshape(block, width)
    conv_w, gain = conv_w.reshape(3 * feat_len, width), gain.reshape(1, width)
    more = block // 2 + EXTRA
    *to, kept = call(
        split_kernel,
        (array(size + more, PAIR), array(size + more, PAIR), array(block, PAIR), array(size, PAIR)),
        "vv",
    )(w_qkv, raw)
    plane = [swap_depth(t, r) for t, r in zip(to, (1, 2, 3))]
    own = call(sort_kernel, array(size, 6 * HD), "vvv")(kept, *plane[:2])
    near = swap_z(own, 1)

    piece = 5 * block // 8
    def embed(rs, *streams, finished=()):
        onward = {1: (), 2: (array(block, half),) * 2}[len(rs)]
        if rs == (3,):
            onward = (array(piece, width), array(block - piece, width))
        out = (array((len(rs) + len(finished)) * block, width), *onward)
        return call(
            functools.partial(embed_kernel, rs, len(finished)),
            out,
            "v" * (6 + len(streams) + len(finished)),
            scratch=[VMEM((block, width), f32)],
            macs=len(rs) * block * 3 * feat_len * width,
        )(raw, *plane, conv_w, gain, *streams, *finished)

    tied = after(stream, plane[2])
    beside, above = swap_depth(tied, 1), swap_depth(tied, 2)
    (normed,) = embed((0,), stream)
    far_raw = after(far_raw, normed)

    even = (lax.axis_index("depth") & 1) == 0
    low, to_x, high = (far_raw[:, k * PAIR : (k + 1) * PAIR] for k in range(3))
    kept, to_y = jnp.where(even, low, high), jnp.where(even, high, low)
    from_x, from_y = swap_depth(to_x, 1), swap_depth(to_y, 2)
    beside, above = after(beside, to_x), after(above, to_y)
    stack, *diagonal = embed((1, 2), beside, above, finished=(normed,))
    from_x, from_y, stack, near = lax.optimization_barrier((from_x, from_y, stack, near))
    keep, send, flags = call(
        sort_far_kernel,
        (array(size, 3 * HD), array(size, 3 * HD), array(EXTRA, 3 * HD)),
        "v" * 7,
    )(kept, from_x, from_y, *plane, raw)
    diagonal = swap_depth(diagonal[0], 2), swap_depth(diagonal[1], 1)
    far = jnp.concatenate([keep, swap_core(send)], axis=0)
    last = swap_z(far, 1)
    far, near, stack = lax.optimization_barrier((far, near, stack))
    to_other = call(other_kernel, array(2 * size + EXTRA, 3 * HD), "vvv")(own, near, flags)
    received = swap_core(to_other)
    weights = (own, near, received, far)
    early = (stack, swap_core(stack))
    rows = 2 * size
    total = call(partial_kernel, array(6 * block, 3 * HD, kind=f32), "v" * 6, macs=6 * block * 3 * rows * 3 * HD)(
        *early, *weights
    )
    diagonal, *parts = embed((3,), *[after(t, total) for t in diagonal])
    swapped = [swap_core(t) for t in parts]
    total_diagonal, diagonal = call(
        diagonal_kernel,
        (array(2 * block, 3 * HD, kind=f32), array(2 * block, width)),
        "v" * 7,
        macs=2 * block * 3 * rows * 3 * HD,
    )(diagonal, *swapped, *weights)
    one_head, half_head = array(4, 2 * block, HD), array(2, 2 * block, HD)
    q, k, *v = call(
        finish_kernel, (one_head, one_head, half_head, half_head), "v" * 6, macs=8 * block * rows * 3 * HD
    )(*early, diagonal, last, total, total_diagonal)

    weights = call(weigh_kernel, array(4, 2 * block, 5 * block), "v" * 6, macs=8 * block * 5 * block * HD)(
        q, swap_z(k, 1), k, swap_middle(k), flags, received
    )
    values = [(swap_z(t, 1), t, swap_middle(t)) for t in v]
    pieces = {}
    for i, r in enumerate(V_ORDER):
        mixed = call(functools.partial(mix_kernel, r), array(2 * block, HD), "vvvv", macs=2 * block * 5 * block * HD)(
            weights, *values[i // 2]
        )
        pieces[r] = swap_depth(mixed, r) if r else mixed
    kept, sent = call(pack_kernel, (array(4, block, HD),) * 2, "vvvv")(*[pieces[r] for r in range(4)])
    context = call(gather_kernel, array(block, HEADS * HD), "vv")(kept, swap_core(sent))
    return context.reshape(time_len, site_len, HEADS * HD)


def from_behind(value, axis, by):
    devices = lax.axis_size(axis)
    pairs = [(i, i + by) for i in range(devices) if 0 <= i + by < devices]
    return lax.ppermute(value, axis, pairs)


def head_attend(query_head, key_head, value_head, allowed):
    inv_root = 1.0 / math.sqrt(HD)
    scores = (
        jnp.einsum("qd,kd->qk", query_head, key_head, preferred_element_type=jnp.float32) * inv_root
    )
    scores = jnp.where(allowed, scores, -1e30)
    row_max = jnp.max(scores, axis=-1, keepdims=True)
    powers = jnp.exp(scores - row_max)
    weights = (powers / jnp.sum(powers, axis=-1, keepdims=True)).astype(jnp.bfloat16)
    return jnp.dot(weights, value_head, preferred_element_type=jnp.float32).astype(jnp.bfloat16)


def per_device(raw, stream, conv_w, gain, w_qkv, mask):
    time_len, site_len, _ = raw.shape
    tok_rows = time_len * site_len
    normed = normed_tokens(padded_2(raw, (("depth", 1),), 1), stream, conv_w, gain)
    columns = lax.all_gather(w_qkv, "depth", axis=1, tiled=True)
    projected = jnp.dot(
        normed,
        lax.all_gather(columns, "tm", axis=0, tiled=True),
        preferred_element_type=jnp.float32,
    ).astype(jnp.bfloat16)
    head_cols = projected.shape[1] // 3
    queries = projected[:, :head_cols]
    keyvals = projected[:, head_cols:]
    earlier = []
    later = []
    moving_back = keyvals
    moving_ahead = keyvals
    for hop_index in range(RD):
        moving_back = from_behind(moving_back, "tm", 1)
        moving_ahead = from_behind(moving_ahead, "tm", -1)
        earlier.insert(0, moving_back)
        later.append(moving_ahead)
    gathered = jnp.concatenate(earlier + [keyvals] + later, axis=0)
    block_rows = BT * PP
    own_blocks = tok_rows // block_rows
    span_blocks = gathered.shape[0] // block_rows
    local_mask = mask[0]
    query_ids = jnp.arange(own_blocks, dtype=jnp.int32)[:, None]
    key_ids = jnp.arange(span_blocks, dtype=jnp.int32)[None, :]
    entry_ids = key_ids - query_ids
    picks = entry_ids[:, :, None] == jnp.arange(local_mask.shape[1], dtype=jnp.int32)[None, None, :]
    block_allowed = jnp.sum(jnp.where(picks, local_mask[:, None, :], 0), axis=-1) > 0
    allowed = jnp.repeat(jnp.repeat(block_allowed, block_rows, axis=0), block_rows, axis=1)
    query_heads = queries.reshape(tok_rows, HEADS, HD).transpose(1, 0, 2)
    key_heads = gathered[:, :head_cols].reshape(gathered.shape[0], HEADS, HD).transpose(1, 0, 2)
    value_heads = gathered[:, head_cols:].reshape(gathered.shape[0], HEADS, HD).transpose(1, 0, 2)
    context = lax.map(
        lambda operands: head_attend(operands[0], operands[1], operands[2], allowed),
        (query_heads, key_heads, value_heads),
    )
    return context.transpose(1, 0, 2).reshape(time_len, site_len, head_cols)


def solution(mesh):
    in_specs = (
        P("tm", "depth", None),
        P("tm", "depth", None),
        P(),
        P(),
        P("tm", "depth"),
        P("depth", "tm", None),
    )
    out_specs = P("tm", "depth", None)
    fits = mesh.shape["depth"] == 4 and mesh.shape["tm"] == 8
    return jax.shard_map(
        plane_device if fits else per_device, mesh=mesh, in_specs=in_specs, out_specs=out_specs, check_vma=False
    )
```

```python
import functools
import math

import jax
import jax.numpy as jnp
from jax import lax
from jax.experimental import pallas as pl
from jax.experimental.pallas import tpu as pltpu
from jax.sharding import PartitionSpec as P

HEADS = 8
HD = 128
BT = 16
PP = 8
RD = 2
VMEM = pltpu.VMEM
SMEM = pltpu.SMEM


def padded_2(value, sides, width):
    for axis, dim in sides:
        devices, length = (lax.axis_size(axis), value.shape[dim])
        up = [(i, (i + 1) % devices) for i in range(devices - 1)]
        down = [(j, i) for i, j in up]
        last = lax.slice_in_dim(value, length - width, length, axis=dim)
        leading = lax.slice_in_dim(value, 0, width, axis=dim)
        before = lax.ppermute(last, axis, up)
        after = lax.ppermute(leading, axis, down)
        value = jnp.concatenate([before, value, after], axis=dim)
    return value


def normed_tokens(padded, stream, conv_w, gain):
    time_len, site_len, width = stream.shape
    tok_rows = time_len * site_len
    embedded = stream.reshape(tok_rows, width).astype(jnp.float32)
    for offset in range(3):
        window = padded[:, offset : offset + site_len].reshape(tok_rows, padded.shape[2])
        embedded = embedded + jnp.dot(window, conv_w[offset], preferred_element_type=jnp.float32)
    scale = lax.rsqrt(jnp.mean(embedded * embedded, axis=-1, keepdims=True) + 1e-05)
    return (embedded * scale * gain).astype(jnp.bfloat16)


PAIR = 2 * HD
V_ORDER = (3, 1, 2, 0)
EXTRA = 16


def hop(value, fn):
    pairs = []
    for z in range(4):
        for core in range(2):
            for depth in range(4):
                to = fn(z, core, depth)
                if to is not None:
                    pairs.append(((2 * z + core) * 4 + depth, (2 * to[0] + to[1]) * 4 + to[2]))
    return lax.ppermute(value, ("tm", "depth"), pairs)


def swap_core(value):
    return hop(value, lambda z, c, d: (z, 1 - c, d))


def swap_depth(value, bits):
    return hop(value, lambda z, c, d: (z, c, d ^ bits))


def swap_z(value, bits):
    return hop(value, lambda z, c, d: (z ^ bits, c, d))


def swap_middle(value):
    return hop(value, lambda z, c, d: (z ^ 3, c, d) if z in (1, 2) else None)


def after(value, *others):
    return lax.optimization_barrier((value, *others))[0]


def where_am_i():
    tm = lax.axis_index("tm")
    return tm >> 1, tm & 1, lax.axis_index("depth")


def split_kernel(w, raw, to_x, to_y, to_across, keep):
    _, _, depth = where_am_i()
    even = (depth & 1) == 0
    size, half = w.shape[0], (raw.shape[0] - EXTRA) // 2
    low, high = w[:, :PAIR], w[:, 2 * PAIR :]
    to_x[:size] = w[:, PAIR : 2 * PAIR]
    to_y[:size] = jnp.where(even, high, low)
    keep[...] = jnp.where(even, low, high)
    at = to_across.shape[0] - EXTRA - half
    for i in range(2):
        to_across[:at, i * HD : (i + 1) * HD] = raw[:at]
    for ref, at in ((to_x, size), (to_y, size), (to_across, at)):
        for i in range(2):
            here = slice(i * HD, (i + 1) * HD)
            ref[at : at + half, here] = raw[i * half : (i + 1) * half]
            ref[at + half :, here] = raw[2 * half :]


def sorted_groups(kept, from_x, from_y):
    _, core, depth = where_am_i()
    first, even = core == 0, (depth & 1) == 0
    size = kept.shape[0]
    low = jnp.where(even, kept[...], from_y[:size])
    high = jnp.where(even, from_y[:size], kept[...])
    groups = (low, from_x[:size], high)
    turn = jnp.where(depth == 3, 0, depth)
    for third in range(3):
        group = jnp.where(turn == 0, groups[third], jnp.where(turn == 1, groups[(third + 1) % 3], groups[(third + 2) % 3]))
        yield third, jnp.where(first, group[:, :HD], group[:, HD:]), jnp.where(first, group[:, HD:], group[:, :HD])


def sort_kernel(kept, from_x, from_y, out_ref):
    for third, mine, other in sorted_groups(kept, from_x, from_y):
        out_ref[:, third * HD : (third + 1) * HD] = mine
        out_ref[:, (3 + third) * HD : (4 + third) * HD] = other


def sort_far_kernel(kept, from_x, from_y, plane_x, plane_y, across, raw, keep_ref, send_ref, flags_ref):
    for third, mine, other in sorted_groups(kept, from_x, from_y):
        send_ref[:, third * HD : (third + 1) * HD] = other
        keep_ref[:, third * HD : (third + 1) * HD] = mine
    row = lax.broadcasted_iota(jnp.int32, (EXTRA, HD), 0)
    flags = raw[raw.shape[0] - EXTRA :].astype(jnp.float32)
    for r, ref in enumerate((plane_x, plane_y, across)):
        flags = jnp.where(row == r + 1, ref[ref.shape[0] - EXTRA :, :HD].astype(jnp.float32), flags)
    flags = flags.astype(jnp.bfloat16)
    for k in range(3):
        flags_ref[:, k * HD : (k + 1) * HD] = flags


def other_kernel(own, near, flags, out_ref):
    size, width = own.shape[0], 3 * HD
    out_ref[:size] = own[:, width:]
    out_ref[size : 2 * size] = near[:, width:]
    out_ref[2 * size :] = flags[...]


def embed_kernel(rs, more, raw, plane_x, plane_y, across, conv_w, gain, *refs):
    count = len(rs)
    halves = 2 if rs == (3,) else 1
    count *= halves
    streams, finished, (out_ref, *onward, acc) = refs[:count], refs[count : count + more], refs[count + more :]
    for ref in finished:
        out_ref[: ref.shape[0]] = ref[...]
    if len(rs) > 1:
        for i, ref in enumerate(onward):
            half = ref.shape[1]
            ref[...] = streams[i][:, i * half : (i + 1) * half]
    _, _, depth = where_am_i()
    rows, width = raw.shape[0] - EXTRA, conv_w.shape[1]
    raws = [raw[:rows]]
    for ref in (plane_x, plane_y, across):
        at = ref.shape[0] - EXTRA - rows // 2
        raws.append(jnp.concatenate([ref[at : at + rows // 2, :HD], ref[at : at + rows // 2, HD:]], axis=0))
    raws = [value.astype(jnp.float32).reshape(rows // PP, PP, HD) for value in raws]
    done = out_ref.shape[0] - len(rs) * rows
    for i, r in enumerate(rs):
        place = depth ^ r
        even = (place & 1) == 0
        side, far = raws[r ^ 1], raws[r ^ 3]
        before = jnp.where(even, jnp.where(place == 2, far[:, PP - 1 :], 0.0), side[:, PP - 1 :])
        behind = jnp.where(even, side[:, :1], jnp.where(place == 1, far[:, :1], 0.0))
        padded = jnp.concatenate([before, raws[r], behind], axis=1)
        windows = [padded[:, j : j + PP].reshape(rows, HD).astype(jnp.bfloat16) for j in range(3)]
        windows = jnp.concatenate(windows, axis=1)
        total, step = jnp.zeros((rows, 1), jnp.float32), width // 4
        for at in range(0, width, step):
            here = slice(at, at + step)
            part = jnp.dot(windows, conv_w[:, here], preferred_element_type=jnp.float32)
            each = width // halves
            part += streams[i + at // each][:, at % each : at % each + step].astype(jnp.float32)
            acc[:, here] = part
            total += jnp.sum(part * part, axis=1, keepdims=True)
        scale = lax.rsqrt(total / width + 1e-05)
        normed = (acc[...] * scale * gain[...]).astype(jnp.bfloat16)
        out_ref[done + i * rows : done + (i + 1) * rows] = normed
        if halves > 1:
            cut = onward[0].shape[0]
            onward[0][...], onward[1][...] = normed[:cut], normed[cut:]


def take(refs, source, core, rows):
    half = rows // 2
    cuts = [pl.ds(pl.multiple_of(source * rows + c * half, half), half) for c in (core, 1 - core)]
    return jnp.concatenate([jnp.concatenate([ref[:, at] for at in cuts], axis=1) for ref in refs], axis=0)


def three_shards(x_refs, own, near, received, far):
    z, core, _ = where_am_i()
    size, width = own.shape[0], 3 * HD
    w = [own[:, :width], received[:size], far[...]]
    w = jnp.concatenate(w + [near[:, :width], received[size : 2 * size]], axis=0)
    x = [take(x_refs, source, core, 2 * size) for source in (z, z ^ 2, z ^ 1)]
    return jnp.dot(jnp.concatenate(x, axis=1), w, preferred_element_type=jnp.float32)


def partial_kernel(*refs):
    refs[-1][...] = three_shards(refs[:2], *refs[2:-1])


def diagonal_kernel(mine, top, bottom, *refs):
    weights, (acc_ref, x_ref) = refs[:-2], refs[-2:]
    at = 0
    for ref in (mine, top, bottom):
        x_ref[at : at + ref.shape[0]] = ref[...]
        at += ref.shape[0]
    acc_ref[...] = three_shards([x_ref], *weights)


ROW_ORDER = ((0, 1, 2, 6), (3, 4, 5, 7))


def finish_kernel(thirds, *refs):
    x_refs, (last, acc_in, acc_diagonal), out_refs = refs[:3], refs[3:6], refs[6:]
    z, core, _ = where_am_i()
    early = acc_in.shape[0]
    block = early // 6
    x = take(x_refs, z ^ 3, core, last.shape[0])
    for third in thirds:
        columns = slice(third * HD, (third + 1) * HD)
        value = jnp.dot(x, last[:, columns], preferred_element_type=jnp.float32)
        value = [acc_in[:, columns] + value[:early], acc_diagonal[:, columns] + value[early:]]
        value = jnp.concatenate(value, axis=0).astype(jnp.bfloat16)
        for rel in range(2):
            at = pl.ds(pl.multiple_of((core ^ rel) * block, block), block)
            for r in range(4):
                mine = value[ROW_ORDER[rel][r] * block : (ROW_ORDER[rel][r] + 1) * block]
                v_at = V_ORDER.index(r)
                if third == 2:
                    out_refs[1 + v_at // 2][v_at % 2, at, :] = mine
                else:
                    out_refs[0][r, at, :] = mine


def spans(u):
    return ((0, u, 2), (1, 0, 2), (2, 0, 1 + u))


def neighbours(outer, own, middle, index):
    z, _, _ = where_am_i()
    odd = (z & 1) == 1
    outer, middle = outer[index], middle[index]
    return jnp.where(odd, outer, middle), own[index], jnp.where(odd, middle, outer)


def weigh_kernel(q_ref, outer, own, middle, own_flags, received, out_ref):
    _, core, _ = where_am_i()
    block = q_ref.shape[1] // 2
    inv_root = 1.0 / math.sqrt(HD)
    flags = [own_flags[:, :HD].astype(jnp.float32), received[-EXTRA:, :HD].astype(jnp.float32)]
    flags = [jnp.where(core == u, flags[0], flags[1]) for u in range(2)]
    bias = [(f - 1.0) * 1e30 for f in flags]
    for r in range(4):
        keys = neighbours(outer, own, middle, r)
        for u in range(2):
            q = q_ref[r, u * block : (u + 1) * block]
            scores = []
            for side, first, last in spans(u):
                k = keys[side][first * block : last * block]
                s = lax.dot_general(q, k, (((1,), (1,)), ((), ())), preferred_element_type=jnp.float32)
                for v in range(last - first):
                    entry = len(scores)
                    shut = jnp.broadcast_to(bias[u][r : r + 1, entry : entry + 1], (block, block))
                    scores.append(s[:, v * block : (v + 1) * block] * inv_root + shut)
            top = jnp.max(functools.reduce(jnp.maximum, scores), axis=1, keepdims=True)
            powers = [jnp.exp(s - top) for s in scores]
            inverse = 1.0 / jnp.sum(functools.reduce(jnp.add, powers), axis=1, keepdims=True)
            for entry, p in enumerate(powers):
                here = slice(entry * block, (entry + 1) * block)
                out_ref[r, u * block : (u + 1) * block, here] = (p * inverse).astype(jnp.bfloat16)


def mix_kernel(r, weights, outer, own, middle, out_ref):
    block = weights.shape[1] // 2
    values = neighbours(outer, own, middle, V_ORDER.index(r) % 2)
    for u in range(2):
        w = weights[r, u * block : (u + 1) * block]
        v = [values[side][first * block : last * block] for side, first, last in spans(u)]
        result = jnp.dot(w, jnp.concatenate(v, axis=0), preferred_element_type=jnp.float32)
        out_ref[u * block : (u + 1) * block] = result.astype(jnp.bfloat16)


def pack_kernel(*refs):
    keep_ref, send_ref = refs[4:]
    _, core, _ = where_am_i()
    block = keep_ref.shape[1]
    for r, ref in enumerate(refs[:4]):
        for rel, out_ref in enumerate((keep_ref, send_ref)):
            out_ref[r] = ref[pl.ds(pl.multiple_of((core ^ rel) * block, block), block), :]


def gather_kernel(mine, other, out_ref):
    _, core, depth = where_am_i()
    for rel, ref in enumerate((mine, other)):
        for r in range(4):
            at = pl.multiple_of((2 * (depth ^ r) + (core ^ rel)) * HD, HD)
            out_ref[:, pl.ds(at, HD)] = ref[r]


def call(kernel, outs, places, scratch=(), macs=0, limit=32):
    spaces = {"v": VMEM}
    return pl.pallas_call(
        kernel,
        out_shape=outs,
        in_specs=[pl.BlockSpec(memory_space=spaces[place]) for place in places],
        out_specs=jax.tree.map(lambda _: pl.BlockSpec(memory_space=VMEM), outs),
        scratch_shapes=list(scratch),
        cost_estimate=pl.CostEstimate(flops=2 * macs, bytes_accessed=0, transcendentals=0),
        compiler_params=pltpu.CompilerParams(vmem_limit_bytes=limit * 2**20),
    )


def plane_device(raw, stream, conv_w, gain, w_qkv, mask):
    time_len, site_len, feat_len = raw.shape
    block, width = time_len * site_len, stream.shape[2]
    half, size = width // 2, w_qkv.shape[0]
    bf16, f32 = jnp.bfloat16, jnp.float32

    def array(*shape, kind=bf16):
        return jax.ShapeDtypeStruct(shape, kind)

    far_raw = swap_z(w_qkv, 2)

    mask_row = jnp.pad(mask.reshape(1, mask.shape[2]), ((0, 0), (0, feat_len - mask.shape[2]))).astype(bf16)
    raw = jnp.concatenate([raw.reshape(block, feat_len), jnp.broadcast_to(mask_row, (EXTRA, feat_len))], axis=0)
    stream = stream.reshape(block, width)
    conv_w, gain = conv_w.reshape(3 * feat_len, width), gain.reshape(1, width)
    more = block // 2 + EXTRA
    *to, kept = call(
        split_kernel,
        (array(size + more, PAIR), array(size + more, PAIR), array(block, PAIR), array(size, PAIR)),
        "vv",
    )(w_qkv, raw)
    plane = [swap_depth(t, r) for t, r in zip(to, (1, 2, 3))]
    own = call(sort_kernel, array(size, 6 * HD), "vvv")(kept, *plane[:2])
    near = swap_z(own, 1)

    piece = 5 * block // 8
    def embed(rs, *streams, finished=()):
        onward = {1: (), 2: (array(block, half),) * 2}[len(rs)]
        if rs == (3,):
            onward = (array(piece, width), array(block - piece, width))
        out = (array((len(rs) + len(finished)) * block, width), *onward)
        return call(
            functools.partial(embed_kernel, rs, len(finished)),
            out,
            "v" * (6 + len(streams) + len(finished)),
            scratch=[VMEM((block, width), f32)],
            macs=len(rs) * block * 3 * feat_len * width,
        )(raw, *plane, conv_w, gain, *streams, *finished)

    tied = after(stream, plane[2])
    beside, above = swap_depth(tied, 1), swap_depth(tied, 2)
    (normed,) = embed((0,), stream)
    far_raw = after(far_raw, normed)

    even = (lax.axis_index("depth") & 1) == 0
    low, to_x, high = (far_raw[:, k * PAIR : (k + 1) * PAIR] for k in range(3))
    kept, to_y = jnp.where(even, low, high), jnp.where(even, high, low)
    from_x, from_y = swap_depth(to_x, 1), swap_depth(to_y, 2)
    beside, above = after(beside, to_x), after(above, to_y)
    stack, *diagonal = embed((1, 2), beside, above, finished=(normed,))
    from_x, from_y, stack, near = lax.optimization_barrier((from_x, from_y, stack, near))
    keep, send, flags = call(
        sort_far_kernel,
        (array(size, 3 * HD), array(size, 3 * HD), array(EXTRA, 3 * HD)),
        "v" * 7,
    )(kept, from_x, from_y, *plane, raw)
    diagonal = swap_depth(diagonal[0], 2), swap_depth(diagonal[1], 1)
    far = jnp.concatenate([keep, swap_core(send)], axis=0)
    last = swap_z(far, 1)
    far, near, stack = lax.optimization_barrier((far, near, stack))
    to_other = call(other_kernel, array(2 * size + EXTRA, 3 * HD), "vvv")(own, near, flags)
    received = swap_core(to_other)
    weights = (own, near, received, far)
    early = (stack, swap_core(stack))
    rows = 2 * size
    total = call(partial_kernel, array(6 * block, 3 * HD, kind=f32), "v" * 6, macs=6 * block * 3 * rows * 3 * HD)(
        *early, *weights
    )
    diagonal, *parts = embed((3,), *[after(t, total) for t in diagonal])
    swapped = [swap_core(t) for t in parts]
    total_diagonal, diagonal = call(
        diagonal_kernel,
        (array(2 * block, 3 * HD, kind=f32), array(2 * block, width)),
        "v" * 7,
        macs=2 * block * 3 * rows * 3 * HD,
    )(diagonal, *swapped, *weights)
    one_head, half_head = array(4, 2 * block, HD), array(2, 2 * block, HD)
    sums = (*early, diagonal, last, total, total_diagonal)
    macs = 8 * block * rows * HD
    (k,) = call(functools.partial(finish_kernel, (1,)), (one_head,), "v" * 6, macs=macs)(*sums)
    q, *v = call(functools.partial(finish_kernel, (0, 2)), (one_head, half_head, half_head), "v" * 6, macs=2 * macs)(*sums)

    weights = call(weigh_kernel, array(4, 2 * block, 5 * block), "v" * 6, macs=8 * block * 5 * block * HD)(
        q, swap_z(k, 1), k, swap_middle(k), flags, received
    )
    values = [(swap_z(t, 1), t, swap_middle(t)) for t in v]
    pieces = {}
    for i, r in enumerate(V_ORDER):
        mixed = call(functools.partial(mix_kernel, r), array(2 * block, HD), "vvvv", macs=2 * block * 5 * block * HD)(
            weights, *values[i // 2]
        )
        pieces[r] = swap_depth(mixed, r) if r else mixed
    kept, sent = call(pack_kernel, (array(4, block, HD),) * 2, "vvvv")(*[pieces[r] for r in range(4)])
    context = call(gather_kernel, array(block, HEADS * HD), "vv")(kept, swap_core(sent))
    return context.reshape(time_len, site_len, HEADS * HD)


def from_behind(value, axis, by):
    devices = lax.axis_size(axis)
    pairs = [(i, i + by) for i in range(devices) if 0 <= i + by < devices]
    return lax.ppermute(value, axis, pairs)


def head_attend(query_head, key_head, value_head, allowed):
    inv_root = 1.0 / math.sqrt(HD)
    scores = (
        jnp.einsum("qd,kd->qk", query_head, key_head, preferred_element_type=jnp.float32) * inv_root
    )
    scores = jnp.where(allowed, scores, -1e30)
    row_max = jnp.max(scores, axis=-1, keepdims=True)
    powers = jnp.exp(scores - row_max)
    weights = (powers / jnp.sum(powers, axis=-1, keepdims=True)).astype(jnp.bfloat16)
    return jnp.dot(weights, value_head, preferred_element_type=jnp.float32).astype(jnp.bfloat16)


def per_device(raw, stream, conv_w, gain, w_qkv, mask):
    time_len, site_len, _ = raw.shape
    tok_rows = time_len * site_len
    normed = normed_tokens(padded_2(raw, (("depth", 1),), 1), stream, conv_w, gain)
    columns = lax.all_gather(w_qkv, "depth", axis=1, tiled=True)
    projected = jnp.dot(
        normed,
        lax.all_gather(columns, "tm", axis=0, tiled=True),
        preferred_element_type=jnp.float32,
    ).astype(jnp.bfloat16)
    head_cols = projected.shape[1] // 3
    queries = projected[:, :head_cols]
    keyvals = projected[:, head_cols:]
    earlier = []
    later = []
    moving_back = keyvals
    moving_ahead = keyvals
    for hop_index in range(RD):
        moving_back = from_behind(moving_back, "tm", 1)
        moving_ahead = from_behind(moving_ahead, "tm", -1)
        earlier.insert(0, moving_back)
        later.append(moving_ahead)
    gathered = jnp.concatenate(earlier + [keyvals] + later, axis=0)
    block_rows = BT * PP
    own_blocks = tok_rows // block_rows
    span_blocks = gathered.shape[0] // block_rows
    local_mask = mask[0]
    query_ids = jnp.arange(own_blocks, dtype=jnp.int32)[:, None]
    key_ids = jnp.arange(span_blocks, dtype=jnp.int32)[None, :]
    entry_ids = key_ids - query_ids
    picks = entry_ids[:, :, None] == jnp.arange(local_mask.shape[1], dtype=jnp.int32)[None, None, :]
    block_allowed = jnp.sum(jnp.where(picks, local_mask[:, None, :], 0), axis=-1) > 0
    allowed = jnp.repeat(jnp.repeat(block_allowed, block_rows, axis=0), block_rows, axis=1)
    query_heads = queries.reshape(tok_rows, HEADS, HD).transpose(1, 0, 2)
    key_heads = gathered[:, :head_cols].reshape(gathered.shape[0], HEADS, HD).transpose(1, 0, 2)
    value_heads = gathered[:, head_cols:].reshape(gathered.shape[0], HEADS, HD).transpose(1, 0, 2)
    context = lax.map(
        lambda operands: head_attend(operands[0], operands[1], operands[2], allowed),
        (query_heads, key_heads, value_heads),
    )
    return context.transpose(1, 0, 2).reshape(time_len, site_len, head_cols)


def solution(mesh):
    in_specs = (
        P("tm", "depth", None),
        P("tm", "depth", None),
        P(),
        P(),
        P("tm", "depth"),
        P("depth", "tm", None),
    )
    out_specs = P("tm", "depth", None)
    fits = mesh.shape["depth"] == 4 and mesh.shape["tm"] == 8
    return jax.shard_map(
        plane_device if fits else per_device, mesh=mesh, in_specs=in_specs, out_specs=out_specs, check_vma=False
    )
```

```python
import functools
import math

import jax
import jax.numpy as jnp
from jax import lax
from jax.experimental import pallas as pl
from jax.experimental.pallas import tpu as pltpu
from jax.sharding import PartitionSpec as P

HEADS = 8
HD = 128
BT = 16
PP = 8
RD = 2
VMEM = pltpu.VMEM
SMEM = pltpu.SMEM


def padded_2(value, sides, width):
    for axis, dim in sides:
        devices, length = (lax.axis_size(axis), value.shape[dim])
        up = [(i, (i + 1) % devices) for i in range(devices - 1)]
        down = [(j, i) for i, j in up]
        last = lax.slice_in_dim(value, length - width, length, axis=dim)
        leading = lax.slice_in_dim(value, 0, width, axis=dim)
        before = lax.ppermute(last, axis, up)
        after = lax.ppermute(leading, axis, down)
        value = jnp.concatenate([before, value, after], axis=dim)
    return value


def normed_tokens(padded, stream, conv_w, gain):
    time_len, site_len, width = stream.shape
    tok_rows = time_len * site_len
    embedded = stream.reshape(tok_rows, width).astype(jnp.float32)
    for offset in range(3):
        window = padded[:, offset : offset + site_len].reshape(tok_rows, padded.shape[2])
        embedded = embedded + jnp.dot(window, conv_w[offset], preferred_element_type=jnp.float32)
    scale = lax.rsqrt(jnp.mean(embedded * embedded, axis=-1, keepdims=True) + 1e-05)
    return (embedded * scale * gain).astype(jnp.bfloat16)


PAIR = 2 * HD
V_ORDER = (3, 1, 2, 0)
EXTRA = 16


def hop(value, fn):
    pairs = []
    for z in range(4):
        for core in range(2):
            for depth in range(4):
                to = fn(z, core, depth)
                if to is not None:
                    pairs.append(((2 * z + core) * 4 + depth, (2 * to[0] + to[1]) * 4 + to[2]))
    return lax.ppermute(value, ("tm", "depth"), pairs)


def swap_core(value):
    return hop(value, lambda z, c, d: (z, 1 - c, d))


def swap_depth(value, bits):
    return hop(value, lambda z, c, d: (z, c, d ^ bits))


def swap_z(value, bits):
    return hop(value, lambda z, c, d: (z ^ bits, c, d))


def swap_middle(value):
    return hop(value, lambda z, c, d: (z ^ 3, c, d) if z in (1, 2) else None)


def after(value, *others):
    return lax.optimization_barrier((value, *others))[0]


def where_am_i():
    tm = lax.axis_index("tm")
    return tm >> 1, tm & 1, lax.axis_index("depth")


def split_kernel(w, raw, to_x, to_y, to_across, keep):
    _, _, depth = where_am_i()
    even = (depth & 1) == 0
    size, half = w.shape[0], (raw.shape[0] - EXTRA) // 2
    low, high = w[:, :PAIR], w[:, 2 * PAIR :]
    to_x[:size] = w[:, PAIR : 2 * PAIR]
    to_y[:size] = jnp.where(even, high, low)
    keep[...] = jnp.where(even, low, high)
    at = to_across.shape[0] - EXTRA - half
    for i in range(2):
        to_across[:at, i * HD : (i + 1) * HD] = raw[:at]
    for ref, at in ((to_x, size), (to_y, size), (to_across, at)):
        for i in range(2):
            here = slice(i * HD, (i + 1) * HD)
            ref[at : at + half, here] = raw[i * half : (i + 1) * half]
            ref[at + half :, here] = raw[2 * half :]


def sorted_groups(kept, from_x, from_y):
    _, core, depth = where_am_i()
    first, even = core == 0, (depth & 1) == 0
    size = kept.shape[0]
    low = jnp.where(even, kept[...], from_y[:size])
    high = jnp.where(even, from_y[:size], kept[...])
    groups = (low, from_x[:size], high)
    turn = jnp.where(depth == 3, 0, depth)
    for third in range(3):
        group = jnp.where(turn == 0, groups[third], jnp.where(turn == 1, groups[(third + 1) % 3], groups[(third + 2) % 3]))
        yield third, jnp.where(first, group[:, :HD], group[:, HD:]), jnp.where(first, group[:, HD:], group[:, :HD])


def sort_kernel(kept, from_x, from_y, out_ref):
    for third, mine, other in sorted_groups(kept, from_x, from_y):
        out_ref[:, third * HD : (third + 1) * HD] = mine
        out_ref[:, (3 + third) * HD : (4 + third) * HD] = other


def sort_far_kernel(kept, from_x, from_y, plane_x, plane_y, across, raw, keep_ref, send_ref, flags_ref):
    for third, mine, other in sorted_groups(kept, from_x, from_y):
        send_ref[:, third * HD : (third + 1) * HD] = other
        keep_ref[:, third * HD : (third + 1) * HD] = mine
    row = lax.broadcasted_iota(jnp.int32, (EXTRA, HD), 0)
    flags = raw[raw.shape[0] - EXTRA :].astype(jnp.float32)
    for r, ref in enumerate((plane_x, plane_y, across)):
        flags = jnp.where(row == r + 1, ref[ref.shape[0] - EXTRA :, :HD].astype(jnp.float32), flags)
    flags = flags.astype(jnp.bfloat16)
    for k in range(3):
        flags_ref[:, k * HD : (k + 1) * HD] = flags


def other_kernel(own, near, flags, out_ref):
    size, width = own.shape[0], 3 * HD
    out_ref[:size] = own[:, width:]
    out_ref[size : 2 * size] = near[:, width:]
    out_ref[2 * size :] = flags[...]


def embed_kernel(rs, more, raw, plane_x, plane_y, across, conv_w, gain, *refs):
    count = len(rs)
    halves = 2 if rs == (3,) else 1
    count *= halves
    streams, finished, (out_ref, *onward, acc) = refs[:count], refs[count : count + more], refs[count + more :]
    for ref in finished:
        out_ref[: ref.shape[0]] = ref[...]
    if len(rs) > 1:
        for i, ref in enumerate(onward):
            half = ref.shape[1]
            ref[...] = streams[i][:, i * half : (i + 1) * half]
    _, _, depth = where_am_i()
    rows, width = raw.shape[0] - EXTRA, conv_w.shape[1]
    raws = [raw[:rows]]
    for ref in (plane_x, plane_y, across):
        at = ref.shape[0] - EXTRA - rows // 2
        raws.append(jnp.concatenate([ref[at : at + rows // 2, :HD], ref[at : at + rows // 2, HD:]], axis=0))
    raws = [value.astype(jnp.float32).reshape(rows // PP, PP, HD) for value in raws]
    done = out_ref.shape[0] - len(rs) * rows
    for i, r in enumerate(rs):
        place = depth ^ r
        even = (place & 1) == 0
        side, far = raws[r ^ 1], raws[r ^ 3]
        before = jnp.where(even, jnp.where(place == 2, far[:, PP - 1 :], 0.0), side[:, PP - 1 :])
        behind = jnp.where(even, side[:, :1], jnp.where(place == 1, far[:, :1], 0.0))
        padded = jnp.concatenate([before, raws[r], behind], axis=1)
        windows = [padded[:, j : j + PP].reshape(rows, HD).astype(jnp.bfloat16) for j in range(3)]
        windows = jnp.concatenate(windows, axis=1)
        total, step = jnp.zeros((rows, 1), jnp.float32), width // 4
        for at in range(0, width, step):
            here = slice(at, at + step)
            part = jnp.dot(windows, conv_w[:, here], preferred_element_type=jnp.float32)
            each = width // halves
            part += streams[i + at // each][:, at % each : at % each + step].astype(jnp.float32)
            acc[:, here] = part
            total += jnp.sum(part * part, axis=1, keepdims=True)
        scale = lax.rsqrt(total / width + 1e-05)
        normed = (acc[...] * scale * gain[...]).astype(jnp.bfloat16)
        out_ref[done + i * rows : done + (i + 1) * rows] = normed
        if halves > 1:
            cut = onward[0].shape[0]
            onward[0][...], onward[1][...] = normed[:cut], normed[cut:]


def take(refs, source, core, rows):
    half = rows // 2
    cuts = [pl.ds(pl.multiple_of(source * rows + c * half, half), half) for c in (core, 1 - core)]
    return jnp.concatenate([jnp.concatenate([ref[:, at] for at in cuts], axis=1) for ref in refs], axis=0)


def three_shards(x_refs, own, near, received, far):
    z, core, _ = where_am_i()
    size, width = own.shape[0], 3 * HD
    w = [own[:, :width], received[:size], far[...]]
    w = jnp.concatenate(w + [near[:, :width], received[size : 2 * size]], axis=0)
    x = [take(x_refs, source, core, 2 * size) for source in (z, z ^ 2, z ^ 1)]
    return jnp.dot(jnp.concatenate(x, axis=1), w, preferred_element_type=jnp.float32)


def partial_kernel(*refs):
    refs[-1][...] = three_shards(refs[:2], *refs[2:-1])


def diagonal_kernel(mine, top, bottom, *refs):
    weights, (acc_ref, x_ref) = refs[:-2], refs[-2:]
    at = 0
    for ref in (mine, top, bottom):
        x_ref[at : at + ref.shape[0]] = ref[...]
        at += ref.shape[0]
    acc_ref[...] = three_shards([x_ref], *weights)


ROW_ORDER = ((0, 1, 2, 6), (3, 4, 5, 7))


def finish_kernel(thirds, *refs):
    x_refs, (last, acc_in, acc_diagonal), out_refs = refs[:3], refs[3:6], refs[6:]
    z, core, _ = where_am_i()
    early = acc_in.shape[0]
    block = early // 6
    x = take(x_refs, z ^ 3, core, last.shape[0])
    for third in thirds:
        columns = slice(third * HD, (third + 1) * HD)
        value = jnp.dot(x, last[:, columns], preferred_element_type=jnp.float32)
        value = [acc_in[:, columns] + value[:early], acc_diagonal[:, columns] + value[early:]]
        value = jnp.concatenate(value, axis=0).astype(jnp.bfloat16)
        for rel in range(2):
            at = pl.ds(pl.multiple_of((core ^ rel) * block, block), block)
            for r in range(4):
                mine = value[ROW_ORDER[rel][r] * block : (ROW_ORDER[rel][r] + 1) * block]
                v_at = V_ORDER.index(r)
                if third == 2:
                    out_refs[1 + v_at // 2][v_at % 2, at, :] = mine
                else:
                    out_refs[0][r, at, :] = mine


def spans(u):
    return ((0, u, 2), (1, 0, 2), (2, 0, 1 + u))


def neighbours(outer, own, middle, index):
    z, _, _ = where_am_i()
    odd = (z & 1) == 1
    outer, middle = outer[index], middle[index]
    return jnp.where(odd, outer, middle), own[index], jnp.where(odd, middle, outer)


def weigh_kernel(q_ref, outer, own, middle, own_flags, received, out_ref):
    _, core, _ = where_am_i()
    block = q_ref.shape[1] // 2
    inv_root = 1.0 / math.sqrt(HD)
    flags = [own_flags[:, :HD].astype(jnp.float32), received[-EXTRA:, :HD].astype(jnp.float32)]
    flags = [jnp.where(core == u, flags[0], flags[1]) for u in range(2)]
    bias = [(f - 1.0) * 1e30 for f in flags]
    for r in range(4):
        keys = neighbours(outer, own, middle, r)
        for u in range(2):
            q = q_ref[r, u * block : (u + 1) * block]
            scores = []
            for side, first, last in spans(u):
                k = keys[side][first * block : last * block]
                s = lax.dot_general(q, k, (((1,), (1,)), ((), ())), preferred_element_type=jnp.float32)
                for v in range(last - first):
                    entry = len(scores)
                    shut = jnp.broadcast_to(bias[u][r : r + 1, entry : entry + 1], (block, block))
                    scores.append(s[:, v * block : (v + 1) * block] * inv_root + shut)
            top = jnp.max(functools.reduce(jnp.maximum, scores), axis=1, keepdims=True)
            powers = [jnp.exp(s - top) for s in scores]
            inverse = 1.0 / jnp.sum(functools.reduce(jnp.add, powers), axis=1, keepdims=True)
            for entry, p in enumerate(powers):
                here = slice(entry * block, (entry + 1) * block)
                out_ref[r, u * block : (u + 1) * block, here] = (p * inverse).astype(jnp.bfloat16)


def mix_kernel(r, weights, outer, own, middle, out_ref):
    block = weights.shape[1] // 2
    values = neighbours(outer, own, middle, V_ORDER.index(r) % 2)
    for u in range(2):
        w = weights[r, u * block : (u + 1) * block]
        v = [values[side][first * block : last * block] for side, first, last in spans(u)]
        result = jnp.dot(w, jnp.concatenate(v, axis=0), preferred_element_type=jnp.float32)
        out_ref[u * block : (u + 1) * block] = result.astype(jnp.bfloat16)


def pack_kernel(*refs):
    keep_ref, send_ref = refs[4:]
    _, core, _ = where_am_i()
    block = keep_ref.shape[1]
    for r, ref in enumerate(refs[:4]):
        for rel, out_ref in enumerate((keep_ref, send_ref)):
            out_ref[r] = ref[pl.ds(pl.multiple_of((core ^ rel) * block, block), block), :]


def gather_kernel(mine, other, out_ref):
    _, core, depth = where_am_i()
    for rel, ref in enumerate((mine, other)):
        for r in range(4):
            at = pl.multiple_of((2 * (depth ^ r) + (core ^ rel)) * HD, HD)
            out_ref[:, pl.ds(at, HD)] = ref[r]


def call(kernel, outs, places, scratch=(), macs=0, limit=32):
    spaces = {"v": VMEM}
    return pl.pallas_call(
        kernel,
        out_shape=outs,
        in_specs=[pl.BlockSpec(memory_space=spaces[place]) for place in places],
        out_specs=jax.tree.map(lambda _: pl.BlockSpec(memory_space=VMEM), outs),
        scratch_shapes=list(scratch),
        cost_estimate=pl.CostEstimate(flops=2 * macs, bytes_accessed=0, transcendentals=0),
        compiler_params=pltpu.CompilerParams(vmem_limit_bytes=limit * 2**20),
    )


def plane_device(raw, stream, conv_w, gain, w_qkv, mask):
    time_len, site_len, feat_len = raw.shape
    block, width = time_len * site_len, stream.shape[2]
    half, size = width // 2, w_qkv.shape[0]
    bf16, f32 = jnp.bfloat16, jnp.float32

    def array(*shape, kind=bf16):
        return jax.ShapeDtypeStruct(shape, kind)


    mask_row = jnp.pad(mask.reshape(1, mask.shape[2]), ((0, 0), (0, feat_len - mask.shape[2]))).astype(bf16)
    raw = jnp.concatenate([raw.reshape(block, feat_len), jnp.broadcast_to(mask_row, (EXTRA, feat_len))], axis=0)
    stream = stream.reshape(block, width)
    conv_w, gain = conv_w.reshape(3 * feat_len, width), gain.reshape(1, width)
    more = block // 2 + EXTRA
    *to, kept = call(
        split_kernel,
        (array(size + more, PAIR), array(size + more, PAIR), array(block, PAIR), array(size, PAIR)),
        "vv",
    )(w_qkv, raw)
    far_raw = swap_z(after(w_qkv, kept), 2)
    plane = [swap_depth(t, r) for t, r in zip(to, (1, 2, 3))]
    own = call(sort_kernel, array(size, 6 * HD), "vvv")(kept, *plane[:2])
    near = swap_z(own, 1)

    piece = 5 * block // 8
    def embed(rs, *streams, finished=()):
        onward = {1: (), 2: (array(block, half),) * 2}[len(rs)]
        if rs == (3,):
            onward = (array(piece, width), array(block - piece, width))
        out = (array((len(rs) + len(finished)) * block, width), *onward)
        return call(
            functools.partial(embed_kernel, rs, len(finished)),
            out,
            "v" * (6 + len(streams) + len(finished)),
            scratch=[VMEM((block, width), f32)],
            macs=len(rs) * block * 3 * feat_len * width,
        )(raw, *plane, conv_w, gain, *streams, *finished)

    tied = after(stream, plane[2])
    beside, above = swap_depth(tied, 1), swap_depth(tied, 2)
    (normed,) = embed((0,), stream)
    far_raw = after(far_raw, normed)

    even = (lax.axis_index("depth") & 1) == 0
    low, to_x, high = (far_raw[:, k * PAIR : (k + 1) * PAIR] for k in range(3))
    kept, to_y = jnp.where(even, low, high), jnp.where(even, high, low)
    from_x, from_y = swap_depth(to_x, 1), swap_depth(to_y, 2)
    beside, above = after(beside, to_x), after(above, to_y)
    stack, *diagonal = embed((1, 2), beside, above, finished=(normed,))
    from_x, from_y, stack, near = lax.optimization_barrier((from_x, from_y, stack, near))
    keep, send, flags = call(
        sort_far_kernel,
        (array(size, 3 * HD), array(size, 3 * HD), array(EXTRA, 3 * HD)),
        "v" * 7,
    )(kept, from_x, from_y, *plane, raw)
    diagonal = swap_depth(diagonal[0], 2), swap_depth(diagonal[1], 1)
    far = jnp.concatenate([keep, swap_core(send)], axis=0)
    last = swap_z(far, 1)
    far, near, stack = lax.optimization_barrier((far, near, stack))
    to_other = call(other_kernel, array(2 * size + EXTRA, 3 * HD), "vvv")(own, near, flags)
    received = swap_core(to_other)
    weights = (own, near, received, far)
    early = (stack, swap_core(stack))
    rows = 2 * size
    total = call(partial_kernel, array(6 * block, 3 * HD, kind=f32), "v" * 6, macs=6 * block * 3 * rows * 3 * HD)(
        *early, *weights
    )
    diagonal, *parts = embed((3,), *[after(t, total) for t in diagonal])
    swapped = [swap_core(t) for t in parts]
    total_diagonal, diagonal = call(
        diagonal_kernel,
        (array(2 * block, 3 * HD, kind=f32), array(2 * block, width)),
        "v" * 7,
        macs=2 * block * 3 * rows * 3 * HD,
    )(diagonal, *swapped, *weights)
    one_head, half_head = array(4, 2 * block, HD), array(2, 2 * block, HD)
    sums = (*early, diagonal, last, total, total_diagonal)
    macs = 8 * block * rows * HD
    (k,) = call(functools.partial(finish_kernel, (1,)), (one_head,), "v" * 6, macs=macs)(*sums)
    q, *v = call(functools.partial(finish_kernel, (0, 2)), (one_head, half_head, half_head), "v" * 6, macs=2 * macs)(*sums)

    weights = call(weigh_kernel, array(4, 2 * block, 5 * block), "v" * 6, macs=8 * block * 5 * block * HD)(
        q, swap_z(k, 1), k, swap_middle(k), flags, received
    )
    values = [(swap_z(t, 1), t, swap_middle(t)) for t in v]
    pieces = {}
    for i, r in enumerate(V_ORDER):
        mixed = call(functools.partial(mix_kernel, r), array(2 * block, HD), "vvvv", macs=2 * block * 5 * block * HD)(
            weights, *values[i // 2]
        )
        pieces[r] = swap_depth(mixed, r) if r else mixed
    kept, sent = call(pack_kernel, (array(4, block, HD),) * 2, "vvvv")(*[pieces[r] for r in range(4)])
    context = call(gather_kernel, array(block, HEADS * HD), "vv")(kept, swap_core(sent))
    return context.reshape(time_len, site_len, HEADS * HD)


def from_behind(value, axis, by):
    devices = lax.axis_size(axis)
    pairs = [(i, i + by) for i in range(devices) if 0 <= i + by < devices]
    return lax.ppermute(value, axis, pairs)


def head_attend(query_head, key_head, value_head, allowed):
    inv_root = 1.0 / math.sqrt(HD)
    scores = (
        jnp.einsum("qd,kd->qk", query_head, key_head, preferred_element_type=jnp.float32) * inv_root
    )
    scores = jnp.where(allowed, scores, -1e30)
    row_max = jnp.max(scores, axis=-1, keepdims=True)
    powers = jnp.exp(scores - row_max)
    weights = (powers / jnp.sum(powers, axis=-1, keepdims=True)).astype(jnp.bfloat16)
    return jnp.dot(weights, value_head, preferred_element_type=jnp.float32).astype(jnp.bfloat16)


def per_device(raw, stream, conv_w, gain, w_qkv, mask):
    time_len, site_len, _ = raw.shape
    tok_rows = time_len * site_len
    normed = normed_tokens(padded_2(raw, (("depth", 1),), 1), stream, conv_w, gain)
    columns = lax.all_gather(w_qkv, "depth", axis=1, tiled=True)
    projected = jnp.dot(
        normed,
        lax.all_gather(columns, "tm", axis=0, tiled=True),
        preferred_element_type=jnp.float32,
    ).astype(jnp.bfloat16)
    head_cols = projected.shape[1] // 3
    queries = projected[:, :head_cols]
    keyvals = projected[:, head_cols:]
    earlier = []
    later = []
    moving_back = keyvals
    moving_ahead = keyvals
    for hop_index in range(RD):
        moving_back = from_behind(moving_back, "tm", 1)
        moving_ahead = from_behind(moving_ahead, "tm", -1)
        earlier.insert(0, moving_back)
        later.append(moving_ahead)
    gathered = jnp.concatenate(earlier + [keyvals] + later, axis=0)
    block_rows = BT * PP
    own_blocks = tok_rows // block_rows
    span_blocks = gathered.shape[0] // block_rows
    local_mask = mask[0]
    query_ids = jnp.arange(own_blocks, dtype=jnp.int32)[:, None]
    key_ids = jnp.arange(span_blocks, dtype=jnp.int32)[None, :]
    entry_ids = key_ids - query_ids
    picks = entry_ids[:, :, None] == jnp.arange(local_mask.shape[1], dtype=jnp.int32)[None, None, :]
    block_allowed = jnp.sum(jnp.where(picks, local_mask[:, None, :], 0), axis=-1) > 0
    allowed = jnp.repeat(jnp.repeat(block_allowed, block_rows, axis=0), block_rows, axis=1)
    query_heads = queries.reshape(tok_rows, HEADS, HD).transpose(1, 0, 2)
    key_heads = gathered[:, :head_cols].reshape(gathered.shape[0], HEADS, HD).transpose(1, 0, 2)
    value_heads = gathered[:, head_cols:].reshape(gathered.shape[0], HEADS, HD).transpose(1, 0, 2)
    context = lax.map(
        lambda operands: head_attend(operands[0], operands[1], operands[2], allowed),
        (query_heads, key_heads, value_heads),
    )
    return context.transpose(1, 0, 2).reshape(time_len, site_len, head_cols)


def solution(mesh):
    in_specs = (
        P("tm", "depth", None),
        P("tm", "depth", None),
        P(),
        P(),
        P("tm", "depth"),
        P("depth", "tm", None),
    )
    out_specs = P("tm", "depth", None)
    fits = mesh.shape["depth"] == 4 and mesh.shape["tm"] == 8
    return jax.shard_map(
        plane_device if fits else per_device, mesh=mesh, in_specs=in_specs, out_specs=out_specs, check_vma=False
    )
```

```python
import functools
import math

import jax
import jax.numpy as jnp
from jax import lax
from jax.experimental import pallas as pl
from jax.experimental.pallas import tpu as pltpu
from jax.sharding import PartitionSpec as P

HEADS = 8
HD = 128
BT = 16
PP = 8
RD = 2
VMEM = pltpu.VMEM
SMEM = pltpu.SMEM


def padded_2(value, sides, width):
    for axis, dim in sides:
        devices, length = (lax.axis_size(axis), value.shape[dim])
        up = [(i, (i + 1) % devices) for i in range(devices - 1)]
        down = [(j, i) for i, j in up]
        last = lax.slice_in_dim(value, length - width, length, axis=dim)
        leading = lax.slice_in_dim(value, 0, width, axis=dim)
        before = lax.ppermute(last, axis, up)
        after = lax.ppermute(leading, axis, down)
        value = jnp.concatenate([before, value, after], axis=dim)
    return value


def normed_tokens(padded, stream, conv_w, gain):
    time_len, site_len, width = stream.shape
    tok_rows = time_len * site_len
    embedded = stream.reshape(tok_rows, width).astype(jnp.float32)
    for offset in range(3):
        window = padded[:, offset : offset + site_len].reshape(tok_rows, padded.shape[2])
        embedded = embedded + jnp.dot(window, conv_w[offset], preferred_element_type=jnp.float32)
    scale = lax.rsqrt(jnp.mean(embedded * embedded, axis=-1, keepdims=True) + 1e-05)
    return (embedded * scale * gain).astype(jnp.bfloat16)


PAIR = 2 * HD
V_ORDER = (3, 1, 2, 0)
EXTRA = 16


def hop(value, fn):
    pairs = []
    for z in range(4):
        for core in range(2):
            for depth in range(4):
                to = fn(z, core, depth)
                if to is not None:
                    pairs.append(((2 * z + core) * 4 + depth, (2 * to[0] + to[1]) * 4 + to[2]))
    return lax.ppermute(value, ("tm", "depth"), pairs)


def swap_core(value):
    return hop(value, lambda z, c, d: (z, 1 - c, d))


def swap_depth(value, bits):
    return hop(value, lambda z, c, d: (z, c, d ^ bits))


def swap_z(value, bits):
    return hop(value, lambda z, c, d: (z ^ bits, c, d))


def swap_middle(value):
    return hop(value, lambda z, c, d: (z ^ 3, c, d) if z in (1, 2) else None)


def after(value, *others):
    return lax.optimization_barrier((value, *others))[0]


def where_am_i():
    tm = lax.axis_index("tm")
    return tm >> 1, tm & 1, lax.axis_index("depth")


def split_kernel(w, raw, to_x, to_y, to_across, keep):
    _, _, depth = where_am_i()
    even = (depth & 1) == 0
    size, half = w.shape[0], (raw.shape[0] - EXTRA) // 2
    low, high = w[:, :PAIR], w[:, 2 * PAIR :]
    to_x[:size] = w[:, PAIR : 2 * PAIR]
    to_y[:size] = jnp.where(even, high, low)
    keep[...] = jnp.where(even, low, high)
    at = to_across.shape[0] - EXTRA - half
    for i in range(2):
        to_across[:at, i * HD : (i + 1) * HD] = raw[:at]
    for ref, at in ((to_x, size), (to_y, size), (to_across, at)):
        for i in range(2):
            here = slice(i * HD, (i + 1) * HD)
            ref[at : at + half, here] = raw[i * half : (i + 1) * half]
            ref[at + half :, here] = raw[2 * half :]


def sorted_groups(kept, from_x, from_y):
    _, core, depth = where_am_i()
    first, even = core == 0, (depth & 1) == 0
    size = kept.shape[0]
    low = jnp.where(even, kept[...], from_y[:size])
    high = jnp.where(even, from_y[:size], kept[...])
    groups = (low, from_x[:size], high)
    turn = jnp.where(depth == 3, 0, depth)
    for third in range(3):
        group = jnp.where(turn == 0, groups[third], jnp.where(turn == 1, groups[(third + 1) % 3], groups[(third + 2) % 3]))
        yield third, jnp.where(first, group[:, :HD], group[:, HD:]), jnp.where(first, group[:, HD:], group[:, :HD])


def sort_kernel(kept, from_x, from_y, out_ref):
    for third, mine, other in sorted_groups(kept, from_x, from_y):
        out_ref[:, third * HD : (third + 1) * HD] = mine
        out_ref[:, (3 + third) * HD : (4 + third) * HD] = other


def sort_far_kernel(kept, from_x, from_y, plane_x, plane_y, across, raw, keep_ref, send_ref, flags_ref):
    for third, mine, other in sorted_groups(kept, from_x, from_y):
        send_ref[:, third * HD : (third + 1) * HD] = other
        keep_ref[:, third * HD : (third + 1) * HD] = mine
    row = lax.broadcasted_iota(jnp.int32, (EXTRA, HD), 0)
    flags = raw[raw.shape[0] - EXTRA :].astype(jnp.float32)
    for r, ref in enumerate((plane_x, plane_y, across)):
        flags = jnp.where(row == r + 1, ref[ref.shape[0] - EXTRA :, :HD].astype(jnp.float32), flags)
    flags = flags.astype(jnp.bfloat16)
    for k in range(3):
        flags_ref[:, k * HD : (k + 1) * HD] = flags


def other_kernel(own, near, flags, out_ref):
    size, width = own.shape[0], 3 * HD
    out_ref[:size] = own[:, width:]
    out_ref[size : 2 * size] = near[:, width:]
    out_ref[2 * size :] = flags[...]


def embed_kernel(rs, more, raw, plane_x, plane_y, across, conv_w, gain, *refs):
    count = len(rs)
    halves = 2 if rs == (3,) else 1
    count *= halves
    streams, finished, (out_ref, *onward, acc) = refs[:count], refs[count : count + more], refs[count + more :]
    for ref in finished:
        out_ref[: ref.shape[0]] = ref[...]
    if len(rs) > 1:
        for i, ref in enumerate(onward):
            half = ref.shape[1]
            ref[...] = streams[i][:, i * half : (i + 1) * half]
    _, _, depth = where_am_i()
    rows, width = raw.shape[0] - EXTRA, conv_w.shape[1]
    raws = [raw[:rows]]
    for ref in (plane_x, plane_y, across):
        at = ref.shape[0] - EXTRA - rows // 2
        raws.append(jnp.concatenate([ref[at : at + rows // 2, :HD], ref[at : at + rows // 2, HD:]], axis=0))
    raws = [value.astype(jnp.float32).reshape(rows // PP, PP, HD) for value in raws]
    done = out_ref.shape[0] - len(rs) * rows
    for i, r in enumerate(rs):
        place = depth ^ r
        even = (place & 1) == 0
        side, far = raws[r ^ 1], raws[r ^ 3]
        before = jnp.where(even, jnp.where(place == 2, far[:, PP - 1 :], 0.0), side[:, PP - 1 :])
        behind = jnp.where(even, side[:, :1], jnp.where(place == 1, far[:, :1], 0.0))
        padded = jnp.concatenate([before, raws[r], behind], axis=1)
        windows = [padded[:, j : j + PP].reshape(rows, HD).astype(jnp.bfloat16) for j in range(3)]
        windows = jnp.concatenate(windows, axis=1)
        total, step = jnp.zeros((rows, 1), jnp.float32), width // 4
        for at in range(0, width, step):
            here = slice(at, at + step)
            part = jnp.dot(windows, conv_w[:, here], preferred_element_type=jnp.float32)
            each = width // halves
            part += streams[i + at // each][:, at % each : at % each + step].astype(jnp.float32)
            acc[:, here] = part
            total += jnp.sum(part * part, axis=1, keepdims=True)
        scale = lax.rsqrt(total / width + 1e-05)
        normed = (acc[...] * scale * gain[...]).astype(jnp.bfloat16)
        out_ref[done + i * rows : done + (i + 1) * rows] = normed
        if halves > 1:
            cut = onward[0].shape[0]
            onward[0][...], onward[1][...] = normed[:cut], normed[cut:]


def take(refs, source, core, rows):
    half = rows // 2
    cuts = [pl.ds(pl.multiple_of(source * rows + c * half, half), half) for c in (core, 1 - core)]
    return jnp.concatenate([jnp.concatenate([ref[:, at] for at in cuts], axis=1) for ref in refs], axis=0)


def three_shards(x_refs, own, near, received, far):
    z, core, _ = where_am_i()
    size, width = own.shape[0], 3 * HD
    w = [own[:, :width], received[:size], far[...]]
    w = jnp.concatenate(w + [near[:, :width], received[size : 2 * size]], axis=0)
    x = [take(x_refs, source, core, 2 * size) for source in (z, z ^ 2, z ^ 1)]
    return jnp.dot(jnp.concatenate(x, axis=1), w, preferred_element_type=jnp.float32)


def partial_kernel(*refs):
    refs[-1][...] = three_shards(refs[:2], *refs[2:-1])


def diagonal_kernel(mine, top, bottom, *refs):
    weights, (acc_ref, x_ref) = refs[:-2], refs[-2:]
    at = 0
    for ref in (mine, top, bottom):
        x_ref[at : at + ref.shape[0]] = ref[...]
        at += ref.shape[0]
    acc_ref[...] = three_shards([x_ref], *weights)


ROW_ORDER = ((0, 1, 2, 6), (3, 4, 5, 7))


def finish_kernel(thirds, *refs):
    x_refs, (last, acc_in, acc_diagonal), out_refs = refs[:3], refs[3:6], refs[6:]
    z, core, _ = where_am_i()
    early = acc_in.shape[0]
    block = early // 6
    x = take(x_refs, z ^ 3, core, last.shape[0])
    for third in thirds:
        columns = slice(third * HD, (third + 1) * HD)
        value = jnp.dot(x, last[:, columns], preferred_element_type=jnp.float32)
        value = [acc_in[:, columns] + value[:early], acc_diagonal[:, columns] + value[early:]]
        value = jnp.concatenate(value, axis=0).astype(jnp.bfloat16)
        for rel in range(2):
            at = pl.ds(pl.multiple_of((core ^ rel) * block, block), block)
            for r in range(4):
                mine = value[ROW_ORDER[rel][r] * block : (ROW_ORDER[rel][r] + 1) * block]
                v_at = V_ORDER.index(r)
                if third == 2:
                    out_refs[1 + v_at // 2][v_at % 2, at, :] = mine
                else:
                    out_refs[0][r, at, :] = mine


def spans(u):
    return ((0, u, 2), (1, 0, 2), (2, 0, 1 + u))


def neighbours(outer, own, middle, index):
    z, _, _ = where_am_i()
    odd = (z & 1) == 1
    outer, middle = outer[index], middle[index]
    return jnp.where(odd, outer, middle), own[index], jnp.where(odd, middle, outer)


def weigh_kernel(q_ref, outer, own, middle, own_flags, received, out_ref):
    _, core, _ = where_am_i()
    block = q_ref.shape[1] // 2
    inv_root = 1.0 / math.sqrt(HD)
    flags = [own_flags[:, :HD].astype(jnp.float32), received[-EXTRA:, :HD].astype(jnp.float32)]
    flags = [jnp.where(core == u, flags[0], flags[1]) for u in range(2)]
    bias = [(f - 1.0) * 1e30 for f in flags]
    for r in range(4):
        keys = neighbours(outer, own, middle, r)
        for u in range(2):
            q = q_ref[r, u * block : (u + 1) * block]
            scores = []
            for side, first, last in spans(u):
                k = keys[side][first * block : last * block]
                s = lax.dot_general(q, k, (((1,), (1,)), ((), ())), preferred_element_type=jnp.float32)
                for v in range(last - first):
                    entry = len(scores)
                    shut = jnp.broadcast_to(bias[u][r : r + 1, entry : entry + 1], (block, block))
                    scores.append(s[:, v * block : (v + 1) * block] * inv_root + shut)
            top = jnp.max(functools.reduce(jnp.maximum, scores), axis=1, keepdims=True)
            powers = [jnp.exp(s - top) for s in scores]
            inverse = 1.0 / jnp.sum(functools.reduce(jnp.add, powers), axis=1, keepdims=True)
            for entry, p in enumerate(powers):
                here = slice(entry * block, (entry + 1) * block)
                out_ref[r, u * block : (u + 1) * block, here] = (p * inverse).astype(jnp.bfloat16)


def mix_kernel(r, weights, middle, own, outer, out_ref):
    block = weights.shape[1] // 2
    values = neighbours(outer, own, middle, V_ORDER.index(r) % 2)
    for u in range(2):
        w = weights[r, u * block : (u + 1) * block]
        v = [values[side][first * block : last * block] for side, first, last in spans(u)]
        result = jnp.dot(w, jnp.concatenate(v, axis=0), preferred_element_type=jnp.float32)
        out_ref[u * block : (u + 1) * block] = result.astype(jnp.bfloat16)


def pack_kernel(*refs):
    keep_ref, send_ref = refs[4:]
    _, core, _ = where_am_i()
    block = keep_ref.shape[1]
    for r, ref in enumerate(refs[:4]):
        for rel, out_ref in enumerate((keep_ref, send_ref)):
            out_ref[r] = ref[pl.ds(pl.multiple_of((core ^ rel) * block, block), block), :]


def gather_kernel(mine, other, out_ref):
    _, core, depth = where_am_i()
    for rel, ref in enumerate((mine, other)):
        for r in range(4):
            at = pl.multiple_of((2 * (depth ^ r) + (core ^ rel)) * HD, HD)
            out_ref[:, pl.ds(at, HD)] = ref[r]


def call(kernel, outs, places, scratch=(), macs=0, limit=32):
    spaces = {"v": VMEM}
    return pl.pallas_call(
        kernel,
        out_shape=outs,
        in_specs=[pl.BlockSpec(memory_space=spaces[place]) for place in places],
        out_specs=jax.tree.map(lambda _: pl.BlockSpec(memory_space=VMEM), outs),
        scratch_shapes=list(scratch),
        cost_estimate=pl.CostEstimate(flops=2 * macs, bytes_accessed=0, transcendentals=0),
        compiler_params=pltpu.CompilerParams(vmem_limit_bytes=limit * 2**20),
    )


def plane_device(raw, stream, conv_w, gain, w_qkv, mask):
    time_len, site_len, feat_len = raw.shape
    block, width = time_len * site_len, stream.shape[2]
    half, size = width // 2, w_qkv.shape[0]
    bf16, f32 = jnp.bfloat16, jnp.float32

    def array(*shape, kind=bf16):
        return jax.ShapeDtypeStruct(shape, kind)

    far_raw = swap_z(w_qkv, 2)

    mask_row = jnp.pad(mask.reshape(1, mask.shape[2]), ((0, 0), (0, feat_len - mask.shape[2]))).astype(bf16)
    raw = jnp.concatenate([raw.reshape(block, feat_len), jnp.broadcast_to(mask_row, (EXTRA, feat_len))], axis=0)
    stream = stream.reshape(block, width)
    conv_w, gain = conv_w.reshape(3 * feat_len, width), gain.reshape(1, width)
    more = block // 2 + EXTRA
    *to, kept = call(
        split_kernel,
        (array(size + more, PAIR), array(size + more, PAIR), array(block, PAIR), array(size, PAIR)),
        "vv",
    )(w_qkv, raw)
    plane = [swap_depth(t, r) for t, r in zip(to, (1, 2, 3))]
    own = call(sort_kernel, array(size, 6 * HD), "vvv")(kept, *plane[:2])
    near = swap_z(own, 1)

    piece = 5 * block // 8
    def embed(rs, *streams, finished=()):
        onward = {1: (), 2: (array(block, half),) * 2}[len(rs)]
        if rs == (3,):
            onward = (array(piece, width), array(block - piece, width))
        out = (array((len(rs) + len(finished)) * block, width), *onward)
        return call(
            functools.partial(embed_kernel, rs, len(finished)),
            out,
            "v" * (6 + len(streams) + len(finished)),
            scratch=[VMEM((block, width), f32)],
            macs=len(rs) * block * 3 * feat_len * width,
        )(raw, *plane, conv_w, gain, *streams, *finished)

    tied = after(stream, plane[2])
    beside, above = swap_depth(tied, 1), swap_depth(tied, 2)
    (normed,) = embed((0,), stream)
    far_raw = after(far_raw, normed)

    even = (lax.axis_index("depth") & 1) == 0
    low, to_x, high = (far_raw[:, k * PAIR : (k + 1) * PAIR] for k in range(3))
    kept, to_y = jnp.where(even, low, high), jnp.where(even, high, low)
    from_x, from_y = swap_depth(to_x, 1), swap_depth(to_y, 2)
    beside, above = after(beside, to_x), after(above, to_y)
    stack, *diagonal = embed((1, 2), beside, above, finished=(normed,))
    from_x, from_y, stack, near = lax.optimization_barrier((from_x, from_y, stack, near))
    keep, send, flags = call(
        sort_far_kernel,
        (array(size, 3 * HD), array(size, 3 * HD), array(EXTRA, 3 * HD)),
        "v" * 7,
    )(kept, from_x, from_y, *plane, raw)
    diagonal = swap_depth(diagonal[0], 2), swap_depth(diagonal[1], 1)
    far = jnp.concatenate([keep, swap_core(send)], axis=0)
    last = swap_z(far, 1)
    far, near, stack = lax.optimization_barrier((far, near, stack))
    to_other = call(other_kernel, array(2 * size + EXTRA, 3 * HD), "vvv")(own, near, flags)
    received = swap_core(to_other)
    weights = (own, near, received, far)
    early = (stack, swap_core(stack))
    rows = 2 * size
    total = call(partial_kernel, array(6 * block, 3 * HD, kind=f32), "v" * 6, macs=6 * block * 3 * rows * 3 * HD)(
        *early, *weights
    )
    diagonal, *parts = embed((3,), *[after(t, total) for t in diagonal])
    swapped = [swap_core(t) for t in parts]
    total_diagonal, diagonal = call(
        diagonal_kernel,
        (array(2 * block, 3 * HD, kind=f32), array(2 * block, width)),
        "v" * 7,
        macs=2 * block * 3 * rows * 3 * HD,
    )(diagonal, *swapped, *weights)
    one_head, half_head = array(4, 2 * block, HD), array(2, 2 * block, HD)
    sums = (*early, diagonal, last, total, total_diagonal)
    macs = 8 * block * rows * HD
    (k,) = call(functools.partial(finish_kernel, (1,)), (one_head,), "v" * 6, macs=macs)(*sums)
    q, *v = call(functools.partial(finish_kernel, (0, 2)), (one_head, half_head, half_head), "v" * 6, macs=2 * macs)(*sums)

    weights = call(weigh_kernel, array(4, 2 * block, 5 * block), "v" * 6, macs=8 * block * 5 * block * HD)(
        q, swap_z(k, 1), k, swap_middle(k), flags, received
    )
    values = [(swap_middle(t), t, swap_z(t, 1)) for t in v]
    pieces = {}
    for i, r in enumerate(V_ORDER):
        mixed = call(functools.partial(mix_kernel, r), array(2 * block, HD), "vvvv", macs=2 * block * 5 * block * HD)(
            weights, *values[i // 2]
        )
        pieces[r] = swap_depth(mixed, r) if r else mixed
    kept, sent = call(pack_kernel, (array(4, block, HD),) * 2, "vvvv")(*[pieces[r] for r in range(4)])
    context = call(gather_kernel, array(block, HEADS * HD), "vv")(kept, swap_core(sent))
    return context.reshape(time_len, site_len, HEADS * HD)


def from_behind(value, axis, by):
    devices = lax.axis_size(axis)
    pairs = [(i, i + by) for i in range(devices) if 0 <= i + by < devices]
    return lax.ppermute(value, axis, pairs)


def head_attend(query_head, key_head, value_head, allowed):
    inv_root = 1.0 / math.sqrt(HD)
    scores = (
        jnp.einsum("qd,kd->qk", query_head, key_head, preferred_element_type=jnp.float32) * inv_root
    )
    scores = jnp.where(allowed, scores, -1e30)
    row_max = jnp.max(scores, axis=-1, keepdims=True)
    powers = jnp.exp(scores - row_max)
    weights = (powers / jnp.sum(powers, axis=-1, keepdims=True)).astype(jnp.bfloat16)
    return jnp.dot(weights, value_head, preferred_element_type=jnp.float32).astype(jnp.bfloat16)


def per_device(raw, stream, conv_w, gain, w_qkv, mask):
    time_len, site_len, _ = raw.shape
    tok_rows = time_len * site_len
    normed = normed_tokens(padded_2(raw, (("depth", 1),), 1), stream, conv_w, gain)
    columns = lax.all_gather(w_qkv, "depth", axis=1, tiled=True)
    projected = jnp.dot(
        normed,
        lax.all_gather(columns, "tm", axis=0, tiled=True),
        preferred_element_type=jnp.float32,
    ).astype(jnp.bfloat16)
    head_cols = projected.shape[1] // 3
    queries = projected[:, :head_cols]
    keyvals = projected[:, head_cols:]
    earlier = []
    later = []
    moving_back = keyvals
    moving_ahead = keyvals
    for hop_index in range(RD):
        moving_back = from_behind(moving_back, "tm", 1)
        moving_ahead = from_behind(moving_ahead, "tm", -1)
        earlier.insert(0, moving_back)
        later.append(moving_ahead)
    gathered = jnp.concatenate(earlier + [keyvals] + later, axis=0)
    block_rows = BT * PP
    own_blocks = tok_rows // block_rows
    span_blocks = gathered.shape[0] // block_rows
    local_mask = mask[0]
    query_ids = jnp.arange(own_blocks, dtype=jnp.int32)[:, None]
    key_ids = jnp.arange(span_blocks, dtype=jnp.int32)[None, :]
    entry_ids = key_ids - query_ids
    picks = entry_ids[:, :, None] == jnp.arange(local_mask.shape[1], dtype=jnp.int32)[None, None, :]
    block_allowed = jnp.sum(jnp.where(picks, local_mask[:, None, :], 0), axis=-1) > 0
    allowed = jnp.repeat(jnp.repeat(block_allowed, block_rows, axis=0), block_rows, axis=1)
    query_heads = queries.reshape(tok_rows, HEADS, HD).transpose(1, 0, 2)
    key_heads = gathered[:, :head_cols].reshape(gathered.shape[0], HEADS, HD).transpose(1, 0, 2)
    value_heads = gathered[:, head_cols:].reshape(gathered.shape[0], HEADS, HD).transpose(1, 0, 2)
    context = lax.map(
        lambda operands: head_attend(operands[0], operands[1], operands[2], allowed),
        (query_heads, key_heads, value_heads),
    )
    return context.transpose(1, 0, 2).reshape(time_len, site_len, head_cols)


def solution(mesh):
    in_specs = (
        P("tm", "depth", None),
        P("tm", "depth", None),
        P(),
        P(),
        P("tm", "depth"),
        P("depth", "tm", None),
    )
    out_specs = P("tm", "depth", None)
    fits = mesh.shape["depth"] == 4 and mesh.shape["tm"] == 8
    return jax.shard_map(
        plane_device if fits else per_device, mesh=mesh, in_specs=in_specs, out_specs=out_specs, check_vma=False
    )
```

```python
import functools
import math

import jax
import jax.numpy as jnp
from jax import lax
from jax.experimental import pallas as pl
from jax.experimental.pallas import tpu as pltpu
from jax.sharding import PartitionSpec as P

HEADS = 8
HD = 128
BT = 16
PP = 8
RD = 2
VMEM = pltpu.VMEM
SMEM = pltpu.SMEM


def padded_2(value, sides, width):
    for axis, dim in sides:
        devices, length = (lax.axis_size(axis), value.shape[dim])
        up = [(i, (i + 1) % devices) for i in range(devices - 1)]
        down = [(j, i) for i, j in up]
        last = lax.slice_in_dim(value, length - width, length, axis=dim)
        leading = lax.slice_in_dim(value, 0, width, axis=dim)
        before = lax.ppermute(last, axis, up)
        after = lax.ppermute(leading, axis, down)
        value = jnp.concatenate([before, value, after], axis=dim)
    return value


def normed_tokens(padded, stream, conv_w, gain):
    time_len, site_len, width = stream.shape
    tok_rows = time_len * site_len
    embedded = stream.reshape(tok_rows, width).astype(jnp.float32)
    for offset in range(3):
        window = padded[:, offset : offset + site_len].reshape(tok_rows, padded.shape[2])
        embedded = embedded + jnp.dot(window, conv_w[offset], preferred_element_type=jnp.float32)
    scale = lax.rsqrt(jnp.mean(embedded * embedded, axis=-1, keepdims=True) + 1e-05)
    return (embedded * scale * gain).astype(jnp.bfloat16)


PAIR = 2 * HD
V_ORDER = (3, 1, 2, 0)
EXTRA = 16


def hop(value, fn):
    pairs = []
    for z in range(4):
        for core in range(2):
            for depth in range(4):
                to = fn(z, core, depth)
                if to is not None:
                    pairs.append(((2 * z + core) * 4 + depth, (2 * to[0] + to[1]) * 4 + to[2]))
    return lax.ppermute(value, ("tm", "depth"), pairs)


def swap_core(value):
    return hop(value, lambda z, c, d: (z, 1 - c, d))


def swap_depth(value, bits):
    return hop(value, lambda z, c, d: (z, c, d ^ bits))


def swap_z(value, bits):
    return hop(value, lambda z, c, d: (z ^ bits, c, d))


def swap_middle(value):
    return hop(value, lambda z, c, d: (z ^ 3, c, d) if z in (1, 2) else None)


def after(value, *others):
    return lax.optimization_barrier((value, *others))[0]


def where_am_i():
    tm = lax.axis_index("tm")
    return tm >> 1, tm & 1, lax.axis_index("depth")


def split_kernel(w, raw, to_x, to_y, to_across, keep):
    _, _, depth = where_am_i()
    even = (depth & 1) == 0
    size, half = w.shape[0], (raw.shape[0] - EXTRA) // 2
    low, high = w[:, :PAIR], w[:, 2 * PAIR :]
    to_x[:size] = w[:, PAIR : 2 * PAIR]
    to_y[:size] = jnp.where(even, high, low)
    keep[...] = jnp.where(even, low, high)
    for ref, at in ((to_x, size), (to_y, size), (to_across, 0)):
        for i in range(2):
            here = slice(i * HD, (i + 1) * HD)
            ref[at : at + half, here] = raw[i * half : (i + 1) * half]
            ref[at + half :, here] = raw[2 * half :]


def sorted_groups(kept, from_x, from_y):
    _, core, depth = where_am_i()
    first, even = core == 0, (depth & 1) == 0
    size = kept.shape[0]
    low = jnp.where(even, kept[...], from_y[:size])
    high = jnp.where(even, from_y[:size], kept[...])
    groups = (low, from_x[:size], high)
    turn = jnp.where(depth == 3, 0, depth)
    for third in range(3):
        group = jnp.where(turn == 0, groups[third], jnp.where(turn == 1, groups[(third + 1) % 3], groups[(third + 2) % 3]))
        yield third, jnp.where(first, group[:, :HD], group[:, HD:]), jnp.where(first, group[:, HD:], group[:, :HD])


def sort_kernel(kept, from_x, from_y, out_ref):
    for third, mine, other in sorted_groups(kept, from_x, from_y):
        out_ref[:, third * HD : (third + 1) * HD] = mine
        out_ref[:, (3 + third) * HD : (4 + third) * HD] = other


def sort_far_kernel(kept, from_x, from_y, plane_x, plane_y, across, raw, keep_ref, send_ref, flags_ref):
    for third, mine, other in sorted_groups(kept, from_x, from_y):
        send_ref[:, third * HD : (third + 1) * HD] = other
        keep_ref[:, third * HD : (third + 1) * HD] = mine
    row = lax.broadcasted_iota(jnp.int32, (EXTRA, HD), 0)
    flags = raw[raw.shape[0] - EXTRA :].astype(jnp.float32)
    for r, ref in enumerate((plane_x, plane_y, across)):
        flags = jnp.where(row == r + 1, ref[ref.shape[0] - EXTRA :, :HD].astype(jnp.float32), flags)
    flags = flags.astype(jnp.bfloat16)
    for k in range(3):
        flags_ref[:, k * HD : (k + 1) * HD] = flags


def other_kernel(own, near, flags, out_ref):
    size, width = own.shape[0], 3 * HD
    out_ref[:size] = own[:, width:]
    out_ref[size : 2 * size] = near[:, width:]
    out_ref[2 * size :] = flags[...]


def embed_kernel(rs, more, raw, plane_x, plane_y, across, conv_w, gain, *refs):
    count = len(rs)
    halves = 2 if rs == (3,) else 1
    count *= halves
    streams, finished, (out_ref, *onward, acc) = refs[:count], refs[count : count + more], refs[count + more :]
    for ref in finished:
        out_ref[: ref.shape[0]] = ref[...]
    if len(rs) > 1:
        for i, ref in enumerate(onward):
            half = ref.shape[1]
            ref[...] = streams[i][:, i * half : (i + 1) * half]
    _, _, depth = where_am_i()
    rows, width = raw.shape[0] - EXTRA, conv_w.shape[1]
    raws = [raw[:rows]]
    for ref in (plane_x, plane_y, across):
        at = ref.shape[0] - EXTRA - rows // 2
        raws.append(jnp.concatenate([ref[at : at + rows // 2, :HD], ref[at : at + rows // 2, HD:]], axis=0))
    raws = [value.astype(jnp.float32).reshape(rows // PP, PP, HD) for value in raws]
    done = out_ref.shape[0] - len(rs) * rows
    for i, r in enumerate(rs):
        place = depth ^ r
        even = (place & 1) == 0
        side, far = raws[r ^ 1], raws[r ^ 3]
        before = jnp.where(even, jnp.where(place == 2, far[:, PP - 1 :], 0.0), side[:, PP - 1 :])
        behind = jnp.where(even, side[:, :1], jnp.where(place == 1, far[:, :1], 0.0))
        padded = jnp.concatenate([before, raws[r], behind], axis=1)
        windows = [padded[:, j : j + PP].reshape(rows, HD).astype(jnp.bfloat16) for j in range(3)]
        windows = jnp.concatenate(windows, axis=1)
        total, step = jnp.zeros((rows, 1), jnp.float32), width // 4
        for at in range(0, width, step):
            here = slice(at, at + step)
            part = jnp.dot(windows, conv_w[:, here], preferred_element_type=jnp.float32)
            each = width // halves
            part += streams[i + at // each][:, at % each : at % each + step].astype(jnp.float32)
            acc[:, here] = part
            total += jnp.sum(part * part, axis=1, keepdims=True)
        scale = lax.rsqrt(total / width + 1e-05)
        normed = (acc[...] * scale * gain[...]).astype(jnp.bfloat16)
        out_ref[done + i * rows : done + (i + 1) * rows] = normed
        if halves > 1:
            cut = onward[0].shape[0]
            onward[0][...], onward[1][...] = normed[:cut], normed[cut:]


def take(refs, source, core, rows):
    half = rows // 2
    cuts = [pl.ds(pl.multiple_of(source * rows + c * half, half), half) for c in (core, 1 - core)]
    return jnp.concatenate([jnp.concatenate([ref[:, at] for at in cuts], axis=1) for ref in refs], axis=0)


def three_shards(x_refs, own, near, received, far):
    z, core, _ = where_am_i()
    size, width = own.shape[0], 3 * HD
    w = [own[:, :width], received[:size], far[...]]
    w = jnp.concatenate(w + [near[:, :width], received[size : 2 * size]], axis=0)
    x = [take(x_refs, source, core, 2 * size) for source in (z, z ^ 2, z ^ 1)]
    return jnp.dot(jnp.concatenate(x, axis=1), w, preferred_element_type=jnp.float32)


def partial_kernel(*refs):
    refs[-1][...] = three_shards(refs[:2], *refs[2:-1])


def diagonal_kernel(mine, top, bottom, *refs):
    weights, (acc_ref, x_ref) = refs[:-2], refs[-2:]
    at = 0
    for ref in (mine, top, bottom):
        x_ref[at : at + ref.shape[0]] = ref[...]
        at += ref.shape[0]
    acc_ref[...] = three_shards([x_ref], *weights)


ROW_ORDER = ((0, 1, 2, 6), (3, 4, 5, 7))


def finish_kernel(thirds, *refs):
    x_refs, (last, acc_in, acc_diagonal), out_refs = refs[:3], refs[3:6], refs[6:]
    z, core, _ = where_am_i()
    early = acc_in.shape[0]
    block = early // 6
    x = take(x_refs, z ^ 3, core, last.shape[0])
    for third in thirds:
        columns = slice(third * HD, (third + 1) * HD)
        value = jnp.dot(x, last[:, columns], preferred_element_type=jnp.float32)
        value = [acc_in[:, columns] + value[:early], acc_diagonal[:, columns] + value[early:]]
        value = jnp.concatenate(value, axis=0).astype(jnp.bfloat16)
        for rel in range(2):
            at = pl.ds(pl.multiple_of((core ^ rel) * block, block), block)
            for r in range(4):
                mine = value[ROW_ORDER[rel][r] * block : (ROW_ORDER[rel][r] + 1) * block]
                v_at = V_ORDER.index(r)
                if third == 2:
                    out_refs[1 + v_at // 2][v_at % 2, at, :] = mine
                else:
                    out_refs[0][r, at, :] = mine


def spans(u):
    return ((0, u, 2), (1, 0, 2), (2, 0, 1 + u))


def neighbours(outer, own, middle, index):
    z, _, _ = where_am_i()
    odd = (z & 1) == 1
    outer, middle = outer[index], middle[index]
    return jnp.where(odd, outer, middle), own[index], jnp.where(odd, middle, outer)


def weigh_kernel(q_ref, outer, own, middle, own_flags, received, out_ref):
    _, core, _ = where_am_i()
    block = q_ref.shape[1] // 2
    inv_root = 1.0 / math.sqrt(HD)
    flags = [own_flags[:, :HD].astype(jnp.float32), received[-EXTRA:, :HD].astype(jnp.float32)]
    flags = [jnp.where(core == u, flags[0], flags[1]) for u in range(2)]
    bias = [(f - 1.0) * 1e30 for f in flags]
    for r in range(4):
        keys = neighbours(outer, own, middle, r)
        for u in range(2):
            q = q_ref[r, u * block : (u + 1) * block]
            scores = []
            for side, first, last in spans(u):
                k = keys[side][first * block : last * block]
                s = lax.dot_general(q, k, (((1,), (1,)), ((), ())), preferred_element_type=jnp.float32)
                for v in range(last - first):
                    entry = len(scores)
                    shut = jnp.broadcast_to(bias[u][r : r + 1, entry : entry + 1], (block, block))
                    scores.append(s[:, v * block : (v + 1) * block] * inv_root + shut)
            top = jnp.max(functools.reduce(jnp.maximum, scores), axis=1, keepdims=True)
            powers = [jnp.exp(s - top) for s in scores]
            inverse = 1.0 / jnp.sum(functools.reduce(jnp.add, powers), axis=1, keepdims=True)
            for entry, p in enumerate(powers):
                here = slice(entry * block, (entry + 1) * block)
                out_ref[r, u * block : (u + 1) * block, here] = (p * inverse).astype(jnp.bfloat16)


def mix_kernel(r, weights, outer, own, middle, out_ref):
    block = weights.shape[1] // 2
    values = neighbours(outer, own, middle, V_ORDER.index(r) % 2)
    for u in range(2):
        w = weights[r, u * block : (u + 1) * block]
        v = [values[side][first * block : last * block] for side, first, last in spans(u)]
        result = jnp.dot(w, jnp.concatenate(v, axis=0), preferred_element_type=jnp.float32)
        out_ref[u * block : (u + 1) * block] = result.astype(jnp.bfloat16)


def pack_kernel(*refs):
    keep_ref, send_ref = refs[4:]
    _, core, _ = where_am_i()
    block = keep_ref.shape[1]
    for r, ref in enumerate(refs[:4]):
        for rel, out_ref in enumerate((keep_ref, send_ref)):
            out_ref[r] = ref[pl.ds(pl.multiple_of((core ^ rel) * block, block), block), :]


def gather_kernel(mine, other, out_ref):
    _, core, depth = where_am_i()
    for rel, ref in enumerate((mine, other)):
        for r in range(4):
            at = pl.multiple_of((2 * (depth ^ r) + (core ^ rel)) * HD, HD)
            out_ref[:, pl.ds(at, HD)] = ref[r]


def call(kernel, outs, places, scratch=(), macs=0, limit=32):
    spaces = {"v": VMEM}
    return pl.pallas_call(
        kernel,
        out_shape=outs,
        in_specs=[pl.BlockSpec(memory_space=spaces[place]) for place in places],
        out_specs=jax.tree.map(lambda _: pl.BlockSpec(memory_space=VMEM), outs),
        scratch_shapes=list(scratch),
        cost_estimate=pl.CostEstimate(flops=2 * macs, bytes_accessed=0, transcendentals=0),
        compiler_params=pltpu.CompilerParams(vmem_limit_bytes=limit * 2**20),
    )


def plane_device(raw, stream, conv_w, gain, w_qkv, mask):
    time_len, site_len, feat_len = raw.shape
    block, width = time_len * site_len, stream.shape[2]
    half, size = width // 2, w_qkv.shape[0]
    bf16, f32 = jnp.bfloat16, jnp.float32

    def array(*shape, kind=bf16):
        return jax.ShapeDtypeStruct(shape, kind)

    far_raw = swap_z(w_qkv, 2)

    mask_row = jnp.pad(mask.reshape(1, mask.shape[2]), ((0, 0), (0, feat_len - mask.shape[2]))).astype(bf16)
    raw = jnp.concatenate([raw.reshape(block, feat_len), jnp.broadcast_to(mask_row, (EXTRA, feat_len))], axis=0)
    stream = stream.reshape(block, width)
    conv_w, gain = conv_w.reshape(3 * feat_len, width), gain.reshape(1, width)
    more = block // 2 + EXTRA
    *to, kept = call(
        split_kernel,
        (array(size + more, PAIR), array(size + more, PAIR), array(more, PAIR), array(size, PAIR)),
        "vv",
    )(w_qkv, raw)
    plane = [swap_depth(t, r) for t, r in zip(to, (1, 2, 3))]
    own = call(sort_kernel, array(size, 6 * HD), "vvv")(kept, *plane[:2])
    near = swap_z(own, 1)

    piece = 5 * block // 8
    def embed(rs, *streams, finished=()):
        onward = {1: (), 2: (array(block, half),) * 2}[len(rs)]
        if rs == (3,):
            onward = (array(piece, width), array(block - piece, width))
        out = (array((len(rs) + len(finished)) * block, width), *onward)
        return call(
            functools.partial(embed_kernel, rs, len(finished)),
            out,
            "v" * (6 + len(streams) + len(finished)),
            scratch=[VMEM((block, width), f32)],
            macs=len(rs) * block * 3 * feat_len * width,
        )(raw, *plane, conv_w, gain, *streams, *finished)

    tied = after(stream, to[0])
    beside, above = swap_depth(tied, 1), swap_depth(tied, 2)
    (normed,) = embed((0,), stream)

    even = (lax.axis_index("depth") & 1) == 0
    low, to_x, high = (far_raw[:, k * PAIR : (k + 1) * PAIR] for k in range(3))
    kept, to_y = jnp.where(even, low, high), jnp.where(even, high, low)
    from_x, from_y = swap_depth(to_x, 1), swap_depth(to_y, 2)
    beside, above = after(beside, to_x), after(above, to_y)
    stack, *diagonal = embed((1, 2), beside, above, finished=(normed,))
    from_x, from_y, stack, near = lax.optimization_barrier((from_x, from_y, stack, near))
    keep, send, flags = call(
        sort_far_kernel,
        (array(size, 3 * HD), array(size, 3 * HD), array(EXTRA, 3 * HD)),
        "v" * 7,
    )(kept, from_x, from_y, *plane, raw)
    diagonal = swap_depth(diagonal[0], 2), swap_depth(diagonal[1], 1)
    far = jnp.concatenate([keep, swap_core(send)], axis=0)
    last = swap_z(far, 1)
    far, near, stack = lax.optimization_barrier((far, near, stack))
    to_other = call(other_kernel, array(2 * size + EXTRA, 3 * HD), "vvv")(own, near, flags)
    received = swap_core(to_other)
    weights = (own, near, received, far)
    early = (stack, swap_core(stack))
    rows = 2 * size
    total = call(partial_kernel, array(6 * block, 3 * HD, kind=f32), "v" * 6, macs=6 * block * 3 * rows * 3 * HD)(
        *early, *weights
    )
    diagonal, *parts = embed((3,), *[after(t, total) for t in diagonal])
    swapped = [swap_core(t) for t in parts]
    total_diagonal, diagonal = call(
        diagonal_kernel,
        (array(2 * block, 3 * HD, kind=f32), array(2 * block, width)),
        "v" * 7,
        macs=2 * block * 3 * rows * 3 * HD,
    )(diagonal, *swapped, *weights)
    one_head, half_head = array(4, 2 * block, HD), array(2, 2 * block, HD)
    sums = (*early, diagonal, last, total, total_diagonal)
    macs = 8 * block * rows * HD
    (k,) = call(functools.partial(finish_kernel, (1,)), (one_head,), "v" * 6, macs=macs)(*sums)
    q, *v = call(functools.partial(finish_kernel, (0, 2)), (one_head, half_head, half_head), "v" * 6, macs=2 * macs)(*sums)

    weights = call(weigh_kernel, array(4, 2 * block, 5 * block), "v" * 6, macs=8 * block * 5 * block * HD)(
        q, swap_z(k, 1), k, swap_middle(k), flags, received
    )
    values = [(swap_z(t, 1), t, swap_middle(t)) for t in v]
    pieces = {}
    for i, r in enumerate(V_ORDER):
        mixed = call(functools.partial(mix_kernel, r), array(2 * block, HD), "vvvv", macs=2 * block * 5 * block * HD)(
            weights, *values[i // 2]
        )
        pieces[r] = swap_depth(mixed, r) if r else mixed
    kept, sent = call(pack_kernel, (array(4, block, HD),) * 2, "vvvv")(*[pieces[r] for r in range(4)])
    context = call(gather_kernel, array(block, HEADS * HD), "vv")(kept, swap_core(sent))
    return context.reshape(time_len, site_len, HEADS * HD)


def from_behind(value, axis, by):
    devices = lax.axis_size(axis)
    pairs = [(i, i + by) for i in range(devices) if 0 <= i + by < devices]
    return lax.ppermute(value, axis, pairs)


def head_attend(query_head, key_head, value_head, allowed):
    inv_root = 1.0 / math.sqrt(HD)
    scores = (
        jnp.einsum("qd,kd->qk", query_head, key_head, preferred_element_type=jnp.float32) * inv_root
    )
    scores = jnp.where(allowed, scores, -1e30)
    row_max = jnp.max(scores, axis=-1, keepdims=True)
    powers = jnp.exp(scores - row_max)
    weights = (powers / jnp.sum(powers, axis=-1, keepdims=True)).astype(jnp.bfloat16)
    return jnp.dot(weights, value_head, preferred_element_type=jnp.float32).astype(jnp.bfloat16)


def per_device(raw, stream, conv_w, gain, w_qkv, mask):
    time_len, site_len, _ = raw.shape
    tok_rows = time_len * site_len
    normed = normed_tokens(padded_2(raw, (("depth", 1),), 1), stream, conv_w, gain)
    columns = lax.all_gather(w_qkv, "depth", axis=1, tiled=True)
    projected = jnp.dot(
        normed,
        lax.all_gather(columns, "tm", axis=0, tiled=True),
        preferred_element_type=jnp.float32,
    ).astype(jnp.bfloat16)
    head_cols = projected.shape[1] // 3
    queries = projected[:, :head_cols]
    keyvals = projected[:, head_cols:]
    earlier = []
    later = []
    moving_back = keyvals
    moving_ahead = keyvals
    for hop_index in range(RD):
        moving_back = from_behind(moving_back, "tm", 1)
        moving_ahead = from_behind(moving_ahead, "tm", -1)
        earlier.insert(0, moving_back)
        later.append(moving_ahead)
    gathered = jnp.concatenate(earlier + [keyvals] + later, axis=0)
    block_rows = BT * PP
    own_blocks = tok_rows // block_rows
    span_blocks = gathered.shape[0] // block_rows
    local_mask = mask[0]
    query_ids = jnp.arange(own_blocks, dtype=jnp.int32)[:, None]
    key_ids = jnp.arange(span_blocks, dtype=jnp.int32)[None, :]
    entry_ids = key_ids - query_ids
    picks = entry_ids[:, :, None] == jnp.arange(local_mask.shape[1], dtype=jnp.int32)[None, None, :]
    block_allowed = jnp.sum(jnp.where(picks, local_mask[:, None, :], 0), axis=-1) > 0
    allowed = jnp.repeat(jnp.repeat(block_allowed, block_rows, axis=0), block_rows, axis=1)
    query_heads = queries.reshape(tok_rows, HEADS, HD).transpose(1, 0, 2)
    key_heads = gathered[:, :head_cols].reshape(gathered.shape[0], HEADS, HD).transpose(1, 0, 2)
    value_heads = gathered[:, head_cols:].reshape(gathered.shape[0], HEADS, HD).transpose(1, 0, 2)
    context = lax.map(
        lambda operands: head_attend(operands[0], operands[1], operands[2], allowed),
        (query_heads, key_heads, value_heads),
    )
    return context.transpose(1, 0, 2).reshape(time_len, site_len, head_cols)


def solution(mesh):
    in_specs = (
        P("tm", "depth", None),
        P("tm", "depth", None),
        P(),
        P(),
        P("tm", "depth"),
        P("depth", "tm", None),
    )
    out_specs = P("tm", "depth", None)
    fits = mesh.shape["depth"] == 4 and mesh.shape["tm"] == 8
    return jax.shard_map(
        plane_device if fits else per_device, mesh=mesh, in_specs=in_specs, out_specs=out_specs, check_vma=False
    )
```

```python
import functools
import math

import jax
import jax.numpy as jnp
from jax import lax
from jax.experimental import pallas as pl
from jax.experimental.pallas import tpu as pltpu
from jax.sharding import PartitionSpec as P

HEADS = 8
HD = 128
BT = 16
PP = 8
RD = 2
VMEM = pltpu.VMEM
SMEM = pltpu.SMEM


def padded_2(value, sides, width):
    for axis, dim in sides:
        devices, length = (lax.axis_size(axis), value.shape[dim])
        up = [(i, (i + 1) % devices) for i in range(devices - 1)]
        down = [(j, i) for i, j in up]
        last = lax.slice_in_dim(value, length - width, length, axis=dim)
        leading = lax.slice_in_dim(value, 0, width, axis=dim)
        before = lax.ppermute(last, axis, up)
        after = lax.ppermute(leading, axis, down)
        value = jnp.concatenate([before, value, after], axis=dim)
    return value


def normed_tokens(padded, stream, conv_w, gain):
    time_len, site_len, width = stream.shape
    tok_rows = time_len * site_len
    embedded = stream.reshape(tok_rows, width).astype(jnp.float32)
    for offset in range(3):
        window = padded[:, offset : offset + site_len].reshape(tok_rows, padded.shape[2])
        embedded = embedded + jnp.dot(window, conv_w[offset], preferred_element_type=jnp.float32)
    scale = lax.rsqrt(jnp.mean(embedded * embedded, axis=-1, keepdims=True) + 1e-05)
    return (embedded * scale * gain).astype(jnp.bfloat16)


PAIR = 2 * HD
V_ORDER = (3, 1, 2, 0)
EXTRA = 16


def hop(value, fn):
    pairs = []
    for z in range(4):
        for core in range(2):
            for depth in range(4):
                to = fn(z, core, depth)
                if to is not None:
                    pairs.append(((2 * z + core) * 4 + depth, (2 * to[0] + to[1]) * 4 + to[2]))
    return lax.ppermute(value, ("tm", "depth"), pairs)


def swap_core(value):
    return hop(value, lambda z, c, d: (z, 1 - c, d))


def swap_depth(value, bits):
    return hop(value, lambda z, c, d: (z, c, d ^ bits))


def swap_z(value, bits):
    return hop(value, lambda z, c, d: (z ^ bits, c, d))


def swap_middle(value):
    return hop(value, lambda z, c, d: (z ^ 3, c, d) if z in (1, 2) else None)


def after(value, *others):
    return lax.optimization_barrier((value, *others))[0]


def where_am_i():
    tm = lax.axis_index("tm")
    return tm >> 1, tm & 1, lax.axis_index("depth")


def split_kernel(w, raw, to_x, to_y, to_across, keep):
    _, _, depth = where_am_i()
    even = (depth & 1) == 0
    size, half = w.shape[0], (raw.shape[0] - EXTRA) // 2
    low, high = w[:, :PAIR], w[:, 2 * PAIR :]
    to_x[:size] = w[:, PAIR : 2 * PAIR]
    to_y[:size] = jnp.where(even, high, low)
    keep[...] = jnp.where(even, low, high)
    for ref, at in ((to_x, size), (to_y, size), (to_across, 0)):
        for i in range(2):
            here = slice(i * HD, (i + 1) * HD)
            ref[at : at + half, here] = raw[i * half : (i + 1) * half]
            ref[at + half :, here] = raw[2 * half :]


def sorted_groups(kept, from_x, from_y):
    _, core, depth = where_am_i()
    first, even = core == 0, (depth & 1) == 0
    size = kept.shape[0]
    low = jnp.where(even, kept[...], from_y[:size])
    high = jnp.where(even, from_y[:size], kept[...])
    groups = (low, from_x[:size], high)
    turn = jnp.where(depth == 3, 0, depth)
    for third in range(3):
        group = jnp.where(turn == 0, groups[third], jnp.where(turn == 1, groups[(third + 1) % 3], groups[(third + 2) % 3]))
        yield third, jnp.where(first, group[:, :HD], group[:, HD:]), jnp.where(first, group[:, HD:], group[:, :HD])


def sort_kernel(kept, from_x, from_y, out_ref):
    for third, mine, other in sorted_groups(kept, from_x, from_y):
        out_ref[:, third * HD : (third + 1) * HD] = mine
        out_ref[:, (3 + third) * HD : (4 + third) * HD] = other


def sort_far_kernel(kept, from_x, from_y, plane_x, plane_y, across, raw, keep_ref, send_ref, flags_ref):
    for third, mine, other in sorted_groups(kept, from_x, from_y):
        send_ref[:, third * HD : (third + 1) * HD] = other
        keep_ref[:, third * HD : (third + 1) * HD] = mine
    row = lax.broadcasted_iota(jnp.int32, (EXTRA, HD), 0)
    flags = raw[raw.shape[0] - EXTRA :].astype(jnp.float32)
    for r, ref in enumerate((plane_x, plane_y, across)):
        flags = jnp.where(row == r + 1, ref[ref.shape[0] - EXTRA :, :HD].astype(jnp.float32), flags)
    flags = flags.astype(jnp.bfloat16)
    for k in range(3):
        flags_ref[:, k * HD : (k + 1) * HD] = flags


def other_kernel(own, near, flags, out_ref):
    size, width = own.shape[0], 3 * HD
    out_ref[:size] = own[:, width:]
    out_ref[size : 2 * size] = near[:, width:]
    out_ref[2 * size :] = flags[...]


def embed_kernel(rs, more, raw, plane_x, plane_y, across, conv_w, gain, *refs):
    count = len(rs)
    halves = 2 if rs == (3,) else 1
    count *= halves
    streams, finished, (out_ref, *onward, acc) = refs[:count], refs[count : count + more], refs[count + more :]
    for ref in finished:
        out_ref[: ref.shape[0]] = ref[...]
    if len(rs) > 1:
        for i, ref in enumerate(onward):
            half = ref.shape[1]
            ref[...] = streams[i][:, i * half : (i + 1) * half]
    _, _, depth = where_am_i()
    rows, width = raw.shape[0] - EXTRA, conv_w.shape[1]
    raws = [raw[:rows]]
    for ref in (plane_x, plane_y, across):
        at = ref.shape[0] - EXTRA - rows // 2
        raws.append(jnp.concatenate([ref[at : at + rows // 2, :HD], ref[at : at + rows // 2, HD:]], axis=0))
    raws = [value.astype(jnp.float32).reshape(rows // PP, PP, HD) for value in raws]
    done = out_ref.shape[0] - len(rs) * rows
    for i, r in enumerate(rs):
        place = depth ^ r
        even = (place & 1) == 0
        side, far = raws[r ^ 1], raws[r ^ 3]
        before = jnp.where(even, jnp.where(place == 2, far[:, PP - 1 :], 0.0), side[:, PP - 1 :])
        behind = jnp.where(even, side[:, :1], jnp.where(place == 1, far[:, :1], 0.0))
        padded = jnp.concatenate([before, raws[r], behind], axis=1)
        windows = [padded[:, j : j + PP].reshape(rows, HD).astype(jnp.bfloat16) for j in range(3)]
        windows = jnp.concatenate(windows, axis=1)
        total, step = jnp.zeros((rows, 1), jnp.float32), width // 4
        for at in range(0, width, step):
            here = slice(at, at + step)
            part = jnp.dot(windows, conv_w[:, here], preferred_element_type=jnp.float32)
            each = width // halves
            part += streams[i + at // each][:, at % each : at % each + step].astype(jnp.float32)
            acc[:, here] = part
            total += jnp.sum(part * part, axis=1, keepdims=True)
        scale = lax.rsqrt(total / width + 1e-05)
        normed = (acc[...] * scale * gain[...]).astype(jnp.bfloat16)
        out_ref[done + i * rows : done + (i + 1) * rows] = normed
        if halves > 1:
            cut = onward[0].shape[0]
            onward[0][...], onward[1][...] = normed[:cut], normed[cut:]


def take(refs, source, core, rows):
    half = rows // 2
    cuts = [pl.ds(pl.multiple_of(source * rows + c * half, half), half) for c in (core, 1 - core)]
    return jnp.concatenate([jnp.concatenate([ref[:, at] for at in cuts], axis=1) for ref in refs], axis=0)


def three_shards(x_refs, own, near, received, far):
    z, core, _ = where_am_i()
    size, width = own.shape[0], 3 * HD
    w = [own[:, :width], received[:size], far[...]]
    w = jnp.concatenate(w + [near[:, :width], received[size : 2 * size]], axis=0)
    x = [take(x_refs, source, core, 2 * size) for source in (z, z ^ 2, z ^ 1)]
    return jnp.dot(jnp.concatenate(x, axis=1), w, preferred_element_type=jnp.float32)


def partial_kernel(*refs):
    refs[-1][...] = three_shards(refs[:2], *refs[2:-1])


def diagonal_kernel(mine, top, bottom, *refs):
    weights, (acc_ref, x_ref) = refs[:-2], refs[-2:]
    at = 0
    for ref in (mine, top, bottom):
        x_ref[at : at + ref.shape[0]] = ref[...]
        at += ref.shape[0]
    acc_ref[...] = three_shards([x_ref], *weights)


ROW_ORDER = ((0, 1, 2, 6), (3, 4, 5, 7))


def finish_kernel(thirds, *refs):
    x_refs, (last, acc_in, acc_diagonal), out_refs = refs[:3], refs[3:6], refs[6:]
    z, core, _ = where_am_i()
    early = acc_in.shape[0]
    block = early // 6
    x = take(x_refs, z ^ 3, core, last.shape[0])
    for third in thirds:
        columns = slice(third * HD, (third + 1) * HD)
        value = jnp.dot(x, last[:, columns], preferred_element_type=jnp.float32)
        value = [acc_in[:, columns] + value[:early], acc_diagonal[:, columns] + value[early:]]
        value = jnp.concatenate(value, axis=0).astype(jnp.bfloat16)
        for rel in range(2):
            at = pl.ds(pl.multiple_of((core ^ rel) * block, block), block)
            for r in range(4):
                mine = value[ROW_ORDER[rel][r] * block : (ROW_ORDER[rel][r] + 1) * block]
                v_at = V_ORDER.index(r)
                if third == 2:
                    out_refs[1 + v_at // 2][v_at % 2, at, :] = mine
                else:
                    out_refs[0][r, at, :] = mine


def spans(u):
    return ((0, u, 2), (1, 0, 2), (2, 0, 1 + u))


def neighbours(outer, own, middle, index):
    z, _, _ = where_am_i()
    odd = (z & 1) == 1
    outer, middle = outer[index], middle[index]
    return jnp.where(odd, outer, middle), own[index], jnp.where(odd, middle, outer)


def weigh_kernel(q_ref, outer, own, middle, own_flags, received, out_ref):
    _, core, _ = where_am_i()
    block = q_ref.shape[1] // 2
    inv_root = 1.0 / math.sqrt(HD)
    flags = [own_flags[:, :HD].astype(jnp.float32), received[-EXTRA:, :HD].astype(jnp.float32)]
    flags = [jnp.where(core == u, flags[0], flags[1]) for u in range(2)]
    bias = [(f - 1.0) * 1e30 for f in flags]
    for r in range(4):
        keys = neighbours(outer, own, middle, r)
        for u in range(2):
            q = q_ref[r, u * block : (u + 1) * block]
            scores = []
            for side, first, last in spans(u):
                k = keys[side][first * block : last * block]
                s = lax.dot_general(q, k, (((1,), (1,)), ((), ())), preferred_element_type=jnp.float32)
                for v in range(last - first):
                    entry = len(scores)
                    shut = jnp.broadcast_to(bias[u][r : r + 1, entry : entry + 1], (block, block))
                    scores.append(s[:, v * block : (v + 1) * block] * inv_root + shut)
            top = jnp.max(functools.reduce(jnp.maximum, scores), axis=1, keepdims=True)
            powers = [jnp.exp(s - top) for s in scores]
            inverse = 1.0 / jnp.sum(functools.reduce(jnp.add, powers), axis=1, keepdims=True)
            for entry, p in enumerate(powers):
                here = slice(entry * block, (entry + 1) * block)
                out_ref[r, u * block : (u + 1) * block, here] = (p * inverse).astype(jnp.bfloat16)


def mix_kernel(r, weights, outer, own, middle, out_ref):
    block = weights.shape[1] // 2
    values = neighbours(outer, own, middle, V_ORDER.index(r) % 2)
    for u in range(2):
        w = weights[r, u * block : (u + 1) * block]
        v = [values[side][first * block : last * block] for side, first, last in spans(u)]
        result = jnp.dot(w, jnp.concatenate(v, axis=0), preferred_element_type=jnp.float32)
        out_ref[u * block : (u + 1) * block] = result.astype(jnp.bfloat16)


def pack_kernel(*refs):
    keep_ref, send_ref = refs[4:]
    _, core, _ = where_am_i()
    block = keep_ref.shape[1]
    for r, ref in enumerate(refs[:4]):
        for rel, out_ref in enumerate((keep_ref, send_ref)):
            out_ref[r] = ref[pl.ds(pl.multiple_of((core ^ rel) * block, block), block), :]


def gather_kernel(mine, other, out_ref):
    _, core, depth = where_am_i()
    for rel, ref in enumerate((mine, other)):
        for r in range(4):
            at = pl.multiple_of((2 * (depth ^ r) + (core ^ rel)) * HD, HD)
            out_ref[:, pl.ds(at, HD)] = ref[r]


def call(kernel, outs, places, scratch=(), macs=0, limit=32):
    spaces = {"v": VMEM}
    return pl.pallas_call(
        kernel,
        out_shape=outs,
        in_specs=[pl.BlockSpec(memory_space=spaces[place]) for place in places],
        out_specs=jax.tree.map(lambda _: pl.BlockSpec(memory_space=VMEM), outs),
        scratch_shapes=list(scratch),
        cost_estimate=pl.CostEstimate(flops=2 * macs, bytes_accessed=0, transcendentals=0),
        compiler_params=pltpu.CompilerParams(vmem_limit_bytes=limit * 2**20),
    )


def plane_device(raw, stream, conv_w, gain, w_qkv, mask):
    time_len, site_len, feat_len = raw.shape
    block, width = time_len * site_len, stream.shape[2]
    half, size = width // 2, w_qkv.shape[0]
    bf16, f32 = jnp.bfloat16, jnp.float32

    def array(*shape, kind=bf16):
        return jax.ShapeDtypeStruct(shape, kind)

    far_raw = swap_z(w_qkv, 2)

    mask_row = jnp.pad(mask.reshape(1, mask.shape[2]), ((0, 0), (0, feat_len - mask.shape[2]))).astype(bf16)
    raw = jnp.concatenate([raw.reshape(block, feat_len), jnp.broadcast_to(mask_row, (EXTRA, feat_len))], axis=0)
    stream = stream.reshape(block, width)
    conv_w, gain = conv_w.reshape(3 * feat_len, width), gain.reshape(1, width)
    more = block // 2 + EXTRA
    *to, kept = call(
        split_kernel,
        (array(size + more, PAIR), array(size + more, PAIR), array(more, PAIR), array(size, PAIR)),
        "vv",
    )(w_qkv, raw)
    plane = [swap_depth(t, r) for t, r in zip(to, (1, 2, 3))]
    own = call(sort_kernel, array(size, 6 * HD), "vvv")(kept, *plane[:2])
    near = swap_z(own, 1)
    far_raw = after(far_raw, own)

    piece = 5 * block // 8
    def embed(rs, *streams, finished=()):
        onward = {1: (), 2: (array(block, half),) * 2}[len(rs)]
        if rs == (3,):
            onward = (array(piece, width), array(block - piece, width))
        out = (array((len(rs) + len(finished)) * block, width), *onward)
        return call(
            functools.partial(embed_kernel, rs, len(finished)),
            out,
            "v" * (6 + len(streams) + len(finished)),
            scratch=[VMEM((block, width), f32)],
            macs=len(rs) * block * 3 * feat_len * width,
        )(raw, *plane, conv_w, gain, *streams, *finished)

    tied = after(stream, to[0])
    beside, above = swap_depth(tied, 1), swap_depth(tied, 2)
    (normed,) = embed((0,), stream)

    even = (lax.axis_index("depth") & 1) == 0
    low, to_x, high = (far_raw[:, k * PAIR : (k + 1) * PAIR] for k in range(3))
    kept, to_y = jnp.where(even, low, high), jnp.where(even, high, low)
    from_x, from_y = swap_depth(to_x, 1), swap_depth(to_y, 2)
    beside, above = after(beside, to_x), after(above, to_y)
    stack, *diagonal = embed((1, 2), beside, above, finished=(normed,))
    from_x, from_y, stack, near = lax.optimization_barrier((from_x, from_y, stack, near))
    keep, send, flags = call(
        sort_far_kernel,
        (array(size, 3 * HD), array(size, 3 * HD), array(EXTRA, 3 * HD)),
        "v" * 7,
    )(kept, from_x, from_y, *plane, raw)
    diagonal = swap_depth(diagonal[0], 2), swap_depth(diagonal[1], 1)
    far = jnp.concatenate([keep, swap_core(send)], axis=0)
    last = swap_z(far, 1)
    far, near, stack = lax.optimization_barrier((far, near, stack))
    to_other = call(other_kernel, array(2 * size + EXTRA, 3 * HD), "vvv")(own, near, flags)
    received = swap_core(to_other)
    weights = (own, near, received, far)
    early = (stack, swap_core(stack))
    rows = 2 * size
    total = call(partial_kernel, array(6 * block, 3 * HD, kind=f32), "v" * 6, macs=6 * block * 3 * rows * 3 * HD)(
        *early, *weights
    )
    diagonal, *parts = embed((3,), *[after(t, total) for t in diagonal])
    swapped = [swap_core(t) for t in parts]
    total_diagonal, diagonal = call(
        diagonal_kernel,
        (array(2 * block, 3 * HD, kind=f32), array(2 * block, width)),
        "v" * 7,
        macs=2 * block * 3 * rows * 3 * HD,
    )(diagonal, *swapped, *weights)
    one_head, half_head = array(4, 2 * block, HD), array(2, 2 * block, HD)
    sums = (*early, diagonal, last, total, total_diagonal)
    macs = 8 * block * rows * HD
    (k,) = call(functools.partial(finish_kernel, (1,)), (one_head,), "v" * 6, macs=macs)(*sums)
    q, *v = call(functools.partial(finish_kernel, (0, 2)), (one_head, half_head, half_head), "v" * 6, macs=2 * macs)(*sums)

    weights = call(weigh_kernel, array(4, 2 * block, 5 * block), "v" * 6, macs=8 * block * 5 * block * HD)(
        q, swap_z(k, 1), k, swap_middle(k), flags, received
    )
    values = [(swap_z(t, 1), t, swap_middle(t)) for t in v]
    pieces = {}
    for i, r in enumerate(V_ORDER):
        mixed = call(functools.partial(mix_kernel, r), array(2 * block, HD), "vvvv", macs=2 * block * 5 * block * HD)(
            weights, *values[i // 2]
        )
        pieces[r] = swap_depth(mixed, r) if r else mixed
    kept, sent = call(pack_kernel, (array(4, block, HD),) * 2, "vvvv")(*[pieces[r] for r in range(4)])
    context = call(gather_kernel, array(block, HEADS * HD), "vv")(kept, swap_core(sent))
    return context.reshape(time_len, site_len, HEADS * HD)


def from_behind(value, axis, by):
    devices = lax.axis_size(axis)
    pairs = [(i, i + by) for i in range(devices) if 0 <= i + by < devices]
    return lax.ppermute(value, axis, pairs)


def head_attend(query_head, key_head, value_head, allowed):
    inv_root = 1.0 / math.sqrt(HD)
    scores = (
        jnp.einsum("qd,kd->qk", query_head, key_head, preferred_element_type=jnp.float32) * inv_root
    )
    scores = jnp.where(allowed, scores, -1e30)
    row_max = jnp.max(scores, axis=-1, keepdims=True)
    powers = jnp.exp(scores - row_max)
    weights = (powers / jnp.sum(powers, axis=-1, keepdims=True)).astype(jnp.bfloat16)
    return jnp.dot(weights, value_head, preferred_element_type=jnp.float32).astype(jnp.bfloat16)


def per_device(raw, stream, conv_w, gain, w_qkv, mask):
    time_len, site_len, _ = raw.shape
    tok_rows = time_len * site_len
    normed = normed_tokens(padded_2(raw, (("depth", 1),), 1), stream, conv_w, gain)
    columns = lax.all_gather(w_qkv, "depth", axis=1, tiled=True)
    projected = jnp.dot(
        normed,
        lax.all_gather(columns, "tm", axis=0, tiled=True),
        preferred_element_type=jnp.float32,
    ).astype(jnp.bfloat16)
    head_cols = projected.shape[1] // 3
    queries = projected[:, :head_cols]
    keyvals = projected[:, head_cols:]
    earlier = []
    later = []
    moving_back = keyvals
    moving_ahead = keyvals
    for hop_index in range(RD):
        moving_back = from_behind(moving_back, "tm", 1)
        moving_ahead = from_behind(moving_ahead, "tm", -1)
        earlier.insert(0, moving_back)
        later.append(moving_ahead)
    gathered = jnp.concatenate(earlier + [keyvals] + later, axis=0)
    block_rows = BT * PP
    own_blocks = tok_rows // block_rows
    span_blocks = gathered.shape[0] // block_rows
    local_mask = mask[0]
    query_ids = jnp.arange(own_blocks, dtype=jnp.int32)[:, None]
    key_ids = jnp.arange(span_blocks, dtype=jnp.int32)[None, :]
    entry_ids = key_ids - query_ids
    picks = entry_ids[:, :, None] == jnp.arange(local_mask.shape[1], dtype=jnp.int32)[None, None, :]
    block_allowed = jnp.sum(jnp.where(picks, local_mask[:, None, :], 0), axis=-1) > 0
    allowed = jnp.repeat(jnp.repeat(block_allowed, block_rows, axis=0), block_rows, axis=1)
    query_heads = queries.reshape(tok_rows, HEADS, HD).transpose(1, 0, 2)
    key_heads = gathered[:, :head_cols].reshape(gathered.shape[0], HEADS, HD).transpose(1, 0, 2)
    value_heads = gathered[:, head_cols:].reshape(gathered.shape[0], HEADS, HD).transpose(1, 0, 2)
    context = lax.map(
        lambda operands: head_attend(operands[0], operands[1], operands[2], allowed),
        (query_heads, key_heads, value_heads),
    )
    return context.transpose(1, 0, 2).reshape(time_len, site_len, head_cols)


def solution(mesh):
    in_specs = (
        P("tm", "depth", None),
        P("tm", "depth", None),
        P(),
        P(),
        P("tm", "depth"),
        P("depth", "tm", None),
    )
    out_specs = P("tm", "depth", None)
    fits = mesh.shape["depth"] == 4 and mesh.shape["tm"] == 8
    return jax.shard_map(
        plane_device if fits else per_device, mesh=mesh, in_specs=in_specs, out_specs=out_specs, check_vma=False
    )
```

```python
import functools
import math

import jax
import jax.numpy as jnp
from jax import lax
from jax.experimental import pallas as pl
from jax.experimental.pallas import tpu as pltpu
from jax.sharding import PartitionSpec as P

HEADS = 8
HD = 128
BT = 16
PP = 8
RD = 2
VMEM = pltpu.VMEM
SMEM = pltpu.SMEM


def padded_2(value, sides, width):
    for axis, dim in sides:
        devices, length = (lax.axis_size(axis), value.shape[dim])
        up = [(i, (i + 1) % devices) for i in range(devices - 1)]
        down = [(j, i) for i, j in up]
        last = lax.slice_in_dim(value, length - width, length, axis=dim)
        leading = lax.slice_in_dim(value, 0, width, axis=dim)
        before = lax.ppermute(last, axis, up)
        after = lax.ppermute(leading, axis, down)
        value = jnp.concatenate([before, value, after], axis=dim)
    return value


def normed_tokens(padded, stream, conv_w, gain):
    time_len, site_len, width = stream.shape
    tok_rows = time_len * site_len
    embedded = stream.reshape(tok_rows, width).astype(jnp.float32)
    for offset in range(3):
        window = padded[:, offset : offset + site_len].reshape(tok_rows, padded.shape[2])
        embedded = embedded + jnp.dot(window, conv_w[offset], preferred_element_type=jnp.float32)
    scale = lax.rsqrt(jnp.mean(embedded * embedded, axis=-1, keepdims=True) + 1e-05)
    return (embedded * scale * gain).astype(jnp.bfloat16)


PAIR = 2 * HD
V_ORDER = (3, 1, 2, 0)
EXTRA = 16


def hop(value, fn):
    pairs = []
    for z in range(4):
        for core in range(2):
            for depth in range(4):
                to = fn(z, core, depth)
                if to is not None:
                    pairs.append(((2 * z + core) * 4 + depth, (2 * to[0] + to[1]) * 4 + to[2]))
    return lax.ppermute(value, ("tm", "depth"), pairs)


def swap_core(value):
    return hop(value, lambda z, c, d: (z, 1 - c, d))


def swap_depth(value, bits):
    return hop(value, lambda z, c, d: (z, c, d ^ bits))


def swap_z(value, bits):
    return hop(value, lambda z, c, d: (z ^ bits, c, d))


def swap_middle(value):
    return hop(value, lambda z, c, d: (z ^ 3, c, d) if z in (1, 2) else None)


def after(value, *others):
    return lax.optimization_barrier((value, *others))[0]


def where_am_i():
    tm = lax.axis_index("tm")
    return tm >> 1, tm & 1, lax.axis_index("depth")


def split_kernel(w, raw, to_x, to_y, to_across, keep):
    _, _, depth = where_am_i()
    even = (depth & 1) == 0
    size, half = w.shape[0], (raw.shape[0] - EXTRA) // 2
    low, high = w[:, :PAIR], w[:, 2 * PAIR :]
    to_x[:size] = w[:, PAIR : 2 * PAIR]
    to_y[:size] = jnp.where(even, high, low)
    keep[...] = jnp.where(even, low, high)
    for ref, at in ((to_x, size), (to_y, size), (to_across, 0)):
        for i in range(2):
            here = slice(i * HD, (i + 1) * HD)
            ref[at : at + half, here] = raw[i * half : (i + 1) * half]
            ref[at + half :, here] = raw[2 * half :]


def sorted_groups(kept, from_x, from_y):
    _, core, depth = where_am_i()
    first, even = core == 0, (depth & 1) == 0
    size = kept.shape[0]
    low = jnp.where(even, kept[...], from_y[:size])
    high = jnp.where(even, from_y[:size], kept[...])
    groups = (low, from_x[:size], high)
    turn = jnp.where(depth == 3, 0, depth)
    for third in range(3):
        group = jnp.where(turn == 0, groups[third], jnp.where(turn == 1, groups[(third + 1) % 3], groups[(third + 2) % 3]))
        yield third, jnp.where(first, group[:, :HD], group[:, HD:]), jnp.where(first, group[:, HD:], group[:, :HD])


def sort_kernel(kept, from_x, from_y, out_ref):
    for third, mine, other in sorted_groups(kept, from_x, from_y):
        out_ref[:, third * HD : (third + 1) * HD] = mine
        out_ref[:, (3 + third) * HD : (4 + third) * HD] = other


def sort_far_kernel(kept, from_x, from_y, plane_x, plane_y, across, raw, keep_ref, send_ref, flags_ref):
    for third, mine, other in sorted_groups(kept, from_x, from_y):
        send_ref[:, third * HD : (third + 1) * HD] = other
        keep_ref[:, third * HD : (third + 1) * HD] = mine
    row = lax.broadcasted_iota(jnp.int32, (EXTRA, HD), 0)
    flags = raw[raw.shape[0] - EXTRA :].astype(jnp.float32)
    for r, ref in enumerate((plane_x, plane_y, across)):
        flags = jnp.where(row == r + 1, ref[ref.shape[0] - EXTRA :, :HD].astype(jnp.float32), flags)
    flags = flags.astype(jnp.bfloat16)
    for k in range(3):
        flags_ref[:, k * HD : (k + 1) * HD] = flags


def other_kernel(own, near, flags, out_ref):
    size, width = own.shape[0], 3 * HD
    out_ref[:size] = own[:, width:]
    out_ref[size : 2 * size] = near[:, width:]
    out_ref[2 * size :] = flags[...]


def embed_kernel(rs, more, raw, plane_x, plane_y, across, conv_w, gain, *refs):
    count = len(rs)
    halves = 2 if rs == (3,) else 1
    count *= halves
    streams, finished, (out_ref, *onward, acc) = refs[:count], refs[count : count + more], refs[count + more :]
    for ref in finished:
        out_ref[: ref.shape[0]] = ref[...]
    if len(rs) > 1:
        for i, ref in enumerate(onward):
            half = ref.shape[1]
            ref[...] = streams[i][:, i * half : (i + 1) * half]
    _, _, depth = where_am_i()
    rows, width = raw.shape[0] - EXTRA, conv_w.shape[1]
    raws = [raw[:rows]]
    for ref in (plane_x, plane_y, across):
        at = ref.shape[0] - EXTRA - rows // 2
        raws.append(jnp.concatenate([ref[at : at + rows // 2, :HD], ref[at : at + rows // 2, HD:]], axis=0))
    raws = [value.astype(jnp.float32).reshape(rows // PP, PP, HD) for value in raws]
    done = out_ref.shape[0] - len(rs) * rows
    for i, r in enumerate(rs):
        place = depth ^ r
        even = (place & 1) == 0
        side, far = raws[r ^ 1], raws[r ^ 3]
        before = jnp.where(even, jnp.where(place == 2, far[:, PP - 1 :], 0.0), side[:, PP - 1 :])
        behind = jnp.where(even, side[:, :1], jnp.where(place == 1, far[:, :1], 0.0))
        padded = jnp.concatenate([before, raws[r], behind], axis=1)
        windows = [padded[:, j : j + PP].reshape(rows, HD).astype(jnp.bfloat16) for j in range(3)]
        windows = jnp.concatenate(windows, axis=1)
        total, step = jnp.zeros((rows, 1), jnp.float32), width // 4
        for at in range(0, width, step):
            here = slice(at, at + step)
            part = jnp.dot(windows, conv_w[:, here], preferred_element_type=jnp.float32)
            each = width // halves
            part += streams[i + at // each][:, at % each : at % each + step].astype(jnp.float32)
            acc[:, here] = part
            total += jnp.sum(part * part, axis=1, keepdims=True)
        scale = lax.rsqrt(total / width + 1e-05)
        normed = (acc[...] * scale * gain[...]).astype(jnp.bfloat16)
        out_ref[done + i * rows : done + (i + 1) * rows] = normed
        if halves > 1:
            cut = onward[0].shape[0]
            onward[0][...], onward[1][...] = normed[:cut], normed[cut:]


def take(refs, source, core, rows):
    half = rows // 2
    cuts = [pl.ds(pl.multiple_of(source * rows + c * half, half), half) for c in (core, 1 - core)]
    return jnp.concatenate([jnp.concatenate([ref[:, at] for at in cuts], axis=1) for ref in refs], axis=0)


def three_shards(x_refs, own, near, received, far):
    z, core, _ = where_am_i()
    size, width = own.shape[0], 3 * HD
    w = [own[:, :width], received[:size], far[...]]
    w = jnp.concatenate(w + [near[:, :width], received[size : 2 * size]], axis=0)
    x = [take(x_refs, source, core, 2 * size) for source in (z, z ^ 2, z ^ 1)]
    return jnp.dot(jnp.concatenate(x, axis=1), w, preferred_element_type=jnp.float32)


def partial_kernel(*refs):
    refs[-1][...] = three_shards(refs[:2], *refs[2:-1])


def diagonal_kernel(mine, top, bottom, *refs):
    weights, (acc_ref, x_ref) = refs[:-2], refs[-2:]
    at = 0
    for ref in (mine, top, bottom):
        x_ref[at : at + ref.shape[0]] = ref[...]
        at += ref.shape[0]
    acc_ref[...] = three_shards([x_ref], *weights)


ROW_ORDER = ((0, 1, 2, 6), (3, 4, 5, 7))


def finish_kernel(thirds, *refs):
    x_refs, (last, acc_in, acc_diagonal), out_refs = refs[:3], refs[3:6], refs[6:]
    z, core, _ = where_am_i()
    early = acc_in.shape[0]
    block = early // 6
    x = take(x_refs, z ^ 3, core, last.shape[0])
    for third in thirds:
        columns = slice(third * HD, (third + 1) * HD)
        value = jnp.dot(x, last[:, columns], preferred_element_type=jnp.float32)
        value = [acc_in[:, columns] + value[:early], acc_diagonal[:, columns] + value[early:]]
        value = jnp.concatenate(value, axis=0).astype(jnp.bfloat16)
        for rel in range(2):
            at = pl.ds(pl.multiple_of((core ^ rel) * block, block), block)
            for r in range(4):
                mine = value[ROW_ORDER[rel][r] * block : (ROW_ORDER[rel][r] + 1) * block]
                v_at = V_ORDER.index(r)
                if third == 2:
                    out_refs[1 + v_at // 2][v_at % 2, at, :] = mine
                else:
                    out_refs[0][r, at, :] = mine


def spans(u):
    return ((0, u, 2), (1, 0, 2), (2, 0, 1 + u))


def neighbours(outer, own, middle, index):
    z, _, _ = where_am_i()
    odd = (z & 1) == 1
    outer, middle = outer[index], middle[index]
    return jnp.where(odd, outer, middle), own[index], jnp.where(odd, middle, outer)


def weigh_kernel(q_ref, outer, own, middle, own_flags, received, out_ref):
    _, core, _ = where_am_i()
    block = q_ref.shape[1] // 2
    inv_root = 1.0 / math.sqrt(HD)
    flags = [own_flags[:, :HD].astype(jnp.float32), received[-EXTRA:, :HD].astype(jnp.float32)]
    flags = [jnp.where(core == u, flags[0], flags[1]) for u in range(2)]
    bias = [(f - 1.0) * 1e30 for f in flags]
    for r in range(4):
        keys = neighbours(outer, own, middle, r)
        for u in range(2):
            q = q_ref[r, u * block : (u + 1) * block]
            scores = []
            for side, first, last in spans(u):
                k = keys[side][first * block : last * block]
                s = lax.dot_general(q, k, (((1,), (1,)), ((), ())), preferred_element_type=jnp.float32)
                for v in range(last - first):
                    entry = len(scores)
                    shut = jnp.broadcast_to(bias[u][r : r + 1, entry : entry + 1], (block, block))
                    scores.append(s[:, v * block : (v + 1) * block] * inv_root + shut)
            top = jnp.max(functools.reduce(jnp.maximum, scores), axis=1, keepdims=True)
            powers = [jnp.exp(s - top) for s in scores]
            inverse = 1.0 / jnp.sum(functools.reduce(jnp.add, powers), axis=1, keepdims=True)
            for entry, p in enumerate(powers):
                here = slice(entry * block, (entry + 1) * block)
                out_ref[r, u * block : (u + 1) * block, here] = (p * inverse).astype(jnp.bfloat16)


def mix_kernel(r, weights, outer, own, middle, out_ref):
    block = weights.shape[1] // 2
    values = neighbours(outer, own, middle, V_ORDER.index(r) % 2)
    for u in range(2):
        w = weights[r, u * block : (u + 1) * block]
        v = [values[side][first * block : last * block] for side, first, last in spans(u)]
        result = jnp.dot(w, jnp.concatenate(v, axis=0), preferred_element_type=jnp.float32)
        out_ref[u * block : (u + 1) * block] = result.astype(jnp.bfloat16)


def pack_kernel(*refs):
    keep_ref, send_ref = refs[4:]
    _, core, _ = where_am_i()
    block = keep_ref.shape[1]
    for r, ref in enumerate(refs[:4]):
        for rel, out_ref in enumerate((keep_ref, send_ref)):
            out_ref[r] = ref[pl.ds(pl.multiple_of((core ^ rel) * block, block), block), :]


def gather_kernel(mine, other, out_ref):
    _, core, depth = where_am_i()
    for rel, ref in enumerate((mine, other)):
        for r in range(4):
            at = pl.multiple_of((2 * (depth ^ r) + (core ^ rel)) * HD, HD)
            out_ref[:, pl.ds(at, HD)] = ref[r]


def call(kernel, outs, places, scratch=(), macs=0, limit=32):
    spaces = {"v": VMEM}
    return pl.pallas_call(
        kernel,
        out_shape=outs,
        in_specs=[pl.BlockSpec(memory_space=spaces[place]) for place in places],
        out_specs=jax.tree.map(lambda _: pl.BlockSpec(memory_space=VMEM), outs),
        scratch_shapes=list(scratch),
        cost_estimate=pl.CostEstimate(flops=2 * macs, bytes_accessed=0, transcendentals=0),
        compiler_params=pltpu.CompilerParams(vmem_limit_bytes=limit * 2**20),
    )


def plane_device(raw, stream, conv_w, gain, w_qkv, mask):
    time_len, site_len, feat_len = raw.shape
    block, width = time_len * site_len, stream.shape[2]
    half, size = width // 2, w_qkv.shape[0]
    bf16, f32 = jnp.bfloat16, jnp.float32

    def array(*shape, kind=bf16):
        return jax.ShapeDtypeStruct(shape, kind)

    far_raw = swap_z(w_qkv, 2)

    mask_row = jnp.pad(mask.reshape(1, mask.shape[2]), ((0, 0), (0, feat_len - mask.shape[2]))).astype(bf16)
    raw = jnp.concatenate([raw.reshape(block, feat_len), jnp.broadcast_to(mask_row, (EXTRA, feat_len))], axis=0)
    stream = stream.reshape(block, width)
    conv_w, gain = conv_w.reshape(3 * feat_len, width), gain.reshape(1, width)
    more = block // 2 + EXTRA
    *to, kept = call(
        split_kernel,
        (array(size + more, PAIR), array(size + more, PAIR), array(more, PAIR), array(size, PAIR)),
        "vv",
    )(w_qkv, raw)
    plane = [swap_depth(t, r) for t, r in zip(to, (1, 2, 3))]
    own = call(sort_kernel, array(size, 6 * HD), "vvv")(kept, *plane[:2])
    near = swap_z(own, 1)
    far_raw = after(far_raw, own)

    piece = 5 * block // 8
    def embed(rs, *streams, finished=()):
        onward = {1: (), 2: (array(block, half),) * 2}[len(rs)]
        if rs == (3,):
            onward = (array(piece, width), array(block - piece, width))
        out = (array((len(rs) + len(finished)) * block, width), *onward)
        return call(
            functools.partial(embed_kernel, rs, len(finished)),
            out,
            "v" * (6 + len(streams) + len(finished)),
            scratch=[VMEM((block, width), f32)],
            macs=len(rs) * block * 3 * feat_len * width,
        )(raw, *plane, conv_w, gain, *streams, *finished)

    tied = after(stream, to[0])
    beside, above = swap_depth(tied, 1), swap_depth(tied, 2)

    even = (lax.axis_index("depth") & 1) == 0
    low, to_x, high = (far_raw[:, k * PAIR : (k + 1) * PAIR] for k in range(3))
    kept, to_y = jnp.where(even, low, high), jnp.where(even, high, low)
    from_x, from_y = swap_depth(to_x, 1), swap_depth(to_y, 2)
    beside, above = after(beside, to_x), after(above, to_y)
    (normed,) = embed((0,), after(stream, to_x))
    stack, *diagonal = embed((1, 2), beside, above, finished=(normed,))
    from_x, from_y, stack, near = lax.optimization_barrier((from_x, from_y, stack, near))
    keep, send, flags = call(
        sort_far_kernel,
        (array(size, 3 * HD), array(size, 3 * HD), array(EXTRA, 3 * HD)),
        "v" * 7,
    )(kept, from_x, from_y, *plane, raw)
    diagonal = swap_depth(diagonal[0], 2), swap_depth(diagonal[1], 1)
    far = jnp.concatenate([keep, swap_core(send)], axis=0)
    last = swap_z(far, 1)
    far, near, stack = lax.optimization_barrier((far, near, stack))
    to_other = call(other_kernel, array(2 * size + EXTRA, 3 * HD), "vvv")(own, near, flags)
    received = swap_core(to_other)
    weights = (own, near, received, far)
    early = (stack, swap_core(stack))
    rows = 2 * size
    total = call(partial_kernel, array(6 * block, 3 * HD, kind=f32), "v" * 6, macs=6 * block * 3 * rows * 3 * HD)(
        *early, *weights
    )
    diagonal, *parts = embed((3,), *[after(t, total) for t in diagonal])
    swapped = [swap_core(t) for t in parts]
    total_diagonal, diagonal = call(
        diagonal_kernel,
        (array(2 * block, 3 * HD, kind=f32), array(2 * block, width)),
        "v" * 7,
        macs=2 * block * 3 * rows * 3 * HD,
    )(diagonal, *swapped, *weights)
    one_head, half_head = array(4, 2 * block, HD), array(2, 2 * block, HD)
    sums = (*early, diagonal, last, total, total_diagonal)
    macs = 8 * block * rows * HD
    (k,) = call(functools.partial(finish_kernel, (1,)), (one_head,), "v" * 6, macs=macs)(*sums)
    q, *v = call(functools.partial(finish_kernel, (0, 2)), (one_head, half_head, half_head), "v" * 6, macs=2 * macs)(*sums)

    weights = call(weigh_kernel, array(4, 2 * block, 5 * block), "v" * 6, macs=8 * block * 5 * block * HD)(
        q, swap_z(k, 1), k, swap_middle(k), flags, received
    )
    values = [(swap_z(t, 1), t, swap_middle(t)) for t in v]
    pieces = {}
    for i, r in enumerate(V_ORDER):
        mixed = call(functools.partial(mix_kernel, r), array(2 * block, HD), "vvvv", macs=2 * block * 5 * block * HD)(
            weights, *values[i // 2]
        )
        pieces[r] = swap_depth(mixed, r) if r else mixed
    kept, sent = call(pack_kernel, (array(4, block, HD),) * 2, "vvvv")(*[pieces[r] for r in range(4)])
    context = call(gather_kernel, array(block, HEADS * HD), "vv")(kept, swap_core(sent))
    return context.reshape(time_len, site_len, HEADS * HD)


def from_behind(value, axis, by):
    devices = lax.axis_size(axis)
    pairs = [(i, i + by) for i in range(devices) if 0 <= i + by < devices]
    return lax.ppermute(value, axis, pairs)


def head_attend(query_head, key_head, value_head, allowed):
    inv_root = 1.0 / math.sqrt(HD)
    scores = (
        jnp.einsum("qd,kd->qk", query_head, key_head, preferred_element_type=jnp.float32) * inv_root
    )
    scores = jnp.where(allowed, scores, -1e30)
    row_max = jnp.max(scores, axis=-1, keepdims=True)
    powers = jnp.exp(scores - row_max)
    weights = (powers / jnp.sum(powers, axis=-1, keepdims=True)).astype(jnp.bfloat16)
    return jnp.dot(weights, value_head, preferred_element_type=jnp.float32).astype(jnp.bfloat16)


def per_device(raw, stream, conv_w, gain, w_qkv, mask):
    time_len, site_len, _ = raw.shape
    tok_rows = time_len * site_len
    normed = normed_tokens(padded_2(raw, (("depth", 1),), 1), stream, conv_w, gain)
    columns = lax.all_gather(w_qkv, "depth", axis=1, tiled=True)
    projected = jnp.dot(
        normed,
        lax.all_gather(columns, "tm", axis=0, tiled=True),
        preferred_element_type=jnp.float32,
    ).astype(jnp.bfloat16)
    head_cols = projected.shape[1] // 3
    queries = projected[:, :head_cols]
    keyvals = projected[:, head_cols:]
    earlier = []
    later = []
    moving_back = keyvals
    moving_ahead = keyvals
    for hop_index in range(RD):
        moving_back = from_behind(moving_back, "tm", 1)
        moving_ahead = from_behind(moving_ahead, "tm", -1)
        earlier.insert(0, moving_back)
        later.append(moving_ahead)
    gathered = jnp.concatenate(earlier + [keyvals] + later, axis=0)
    block_rows = BT * PP
    own_blocks = tok_rows // block_rows
    span_blocks = gathered.shape[0] // block_rows
    local_mask = mask[0]
    query_ids = jnp.arange(own_blocks, dtype=jnp.int32)[:, None]
    key_ids = jnp.arange(span_blocks, dtype=jnp.int32)[None, :]
    entry_ids = key_ids - query_ids
    picks = entry_ids[:, :, None] == jnp.arange(local_mask.shape[1], dtype=jnp.int32)[None, None, :]
    block_allowed = jnp.sum(jnp.where(picks, local_mask[:, None, :], 0), axis=-1) > 0
    allowed = jnp.repeat(jnp.repeat(block_allowed, block_rows, axis=0), block_rows, axis=1)
    query_heads = queries.reshape(tok_rows, HEADS, HD).transpose(1, 0, 2)
    key_heads = gathered[:, :head_cols].reshape(gathered.shape[0], HEADS, HD).transpose(1, 0, 2)
    value_heads = gathered[:, head_cols:].reshape(gathered.shape[0], HEADS, HD).transpose(1, 0, 2)
    context = lax.map(
        lambda operands: head_attend(operands[0], operands[1], operands[2], allowed),
        (query_heads, key_heads, value_heads),
    )
    return context.transpose(1, 0, 2).reshape(time_len, site_len, head_cols)


def solution(mesh):
    in_specs = (
        P("tm", "depth", None),
        P("tm", "depth", None),
        P(),
        P(),
        P("tm", "depth"),
        P("depth", "tm", None),
    )
    out_specs = P("tm", "depth", None)
    fits = mesh.shape["depth"] == 4 and mesh.shape["tm"] == 8
    return jax.shard_map(
        plane_device if fits else per_device, mesh=mesh, in_specs=in_specs, out_specs=out_specs, check_vma=False
    )
```

```python
import functools
import math

import jax
import jax.numpy as jnp
from jax import lax
from jax.experimental import pallas as pl
from jax.experimental.pallas import tpu as pltpu
from jax.sharding import PartitionSpec as P

HEADS = 8
HD = 128
BT = 16
PP = 8
RD = 2
VMEM = pltpu.VMEM
SMEM = pltpu.SMEM


def padded_2(value, sides, width):
    for axis, dim in sides:
        devices, length = (lax.axis_size(axis), value.shape[dim])
        up = [(i, (i + 1) % devices) for i in range(devices - 1)]
        down = [(j, i) for i, j in up]
        last = lax.slice_in_dim(value, length - width, length, axis=dim)
        leading = lax.slice_in_dim(value, 0, width, axis=dim)
        before = lax.ppermute(last, axis, up)
        after = lax.ppermute(leading, axis, down)
        value = jnp.concatenate([before, value, after], axis=dim)
    return value


def normed_tokens(padded, stream, conv_w, gain):
    time_len, site_len, width = stream.shape
    tok_rows = time_len * site_len
    embedded = stream.reshape(tok_rows, width).astype(jnp.float32)
    for offset in range(3):
        window = padded[:, offset : offset + site_len].reshape(tok_rows, padded.shape[2])
        embedded = embedded + jnp.dot(window, conv_w[offset], preferred_element_type=jnp.float32)
    scale = lax.rsqrt(jnp.mean(embedded * embedded, axis=-1, keepdims=True) + 1e-05)
    return (embedded * scale * gain).astype(jnp.bfloat16)


PAIR = 2 * HD
V_ORDER = (3, 1, 2, 0)
EXTRA = 16


def hop(value, fn):
    pairs = []
    for z in range(4):
        for core in range(2):
            for depth in range(4):
                to = fn(z, core, depth)
                if to is not None:
                    pairs.append(((2 * z + core) * 4 + depth, (2 * to[0] + to[1]) * 4 + to[2]))
    return lax.ppermute(value, ("tm", "depth"), pairs)


def swap_core(value):
    return hop(value, lambda z, c, d: (z, 1 - c, d))


def swap_depth(value, bits):
    return hop(value, lambda z, c, d: (z, c, d ^ bits))


def swap_z(value, bits):
    return hop(value, lambda z, c, d: (z ^ bits, c, d))


def swap_middle(value):
    return hop(value, lambda z, c, d: (z ^ 3, c, d) if z in (1, 2) else None)


def after(value, *others):
    return lax.optimization_barrier((value, *others))[0]


def where_am_i():
    tm = lax.axis_index("tm")
    return tm >> 1, tm & 1, lax.axis_index("depth")


def split_kernel(w, raw, to_x, to_y, to_across, keep):
    _, _, depth = where_am_i()
    even = (depth & 1) == 0
    size, half = w.shape[0], (raw.shape[0] - EXTRA) // 2
    low, high = w[:, :PAIR], w[:, 2 * PAIR :]
    to_x[:size] = w[:, PAIR : 2 * PAIR]
    to_y[:size] = jnp.where(even, high, low)
    keep[...] = jnp.where(even, low, high)
    for ref, at in ((to_x, size), (to_y, size), (to_across, 0)):
        for i in range(2):
            here = slice(i * HD, (i + 1) * HD)
            ref[at : at + half, here] = raw[i * half : (i + 1) * half]
            ref[at + half :, here] = raw[2 * half :]


def sorted_groups(kept, from_x, from_y):
    _, core, depth = where_am_i()
    first, even = core == 0, (depth & 1) == 0
    size = kept.shape[0]
    low = jnp.where(even, kept[...], from_y[:size])
    high = jnp.where(even, from_y[:size], kept[...])
    groups = (low, from_x[:size], high)
    turn = jnp.where(depth == 3, 0, depth)
    for third in range(3):
        group = jnp.where(turn == 0, groups[third], jnp.where(turn == 1, groups[(third + 1) % 3], groups[(third + 2) % 3]))
        yield third, jnp.where(first, group[:, :HD], group[:, HD:]), jnp.where(first, group[:, HD:], group[:, :HD])


def sort_kernel(kept, from_x, from_y, out_ref):
    for third, mine, other in sorted_groups(kept, from_x, from_y):
        out_ref[:, third * HD : (third + 1) * HD] = mine
        out_ref[:, (3 + third) * HD : (4 + third) * HD] = other


def sort_far_kernel(kept, from_x, from_y, plane_x, plane_y, across, raw, keep_ref, send_ref, flags_ref):
    for third, mine, other in sorted_groups(kept, from_x, from_y):
        send_ref[:, third * HD : (third + 1) * HD] = other
        keep_ref[:, third * HD : (third + 1) * HD] = mine
    row = lax.broadcasted_iota(jnp.int32, (EXTRA, HD), 0)
    flags = raw[raw.shape[0] - EXTRA :].astype(jnp.float32)
    for r, ref in enumerate((plane_x, plane_y, across)):
        flags = jnp.where(row == r + 1, ref[ref.shape[0] - EXTRA :, :HD].astype(jnp.float32), flags)
    flags = flags.astype(jnp.bfloat16)
    for k in range(3):
        flags_ref[:, k * HD : (k + 1) * HD] = flags


def other_kernel(own, near, flags, out_ref):
    size, width = own.shape[0], 3 * HD
    out_ref[:size] = own[:, width:]
    out_ref[size : 2 * size] = near[:, width:]
    out_ref[2 * size :] = flags[...]


def embed_kernel(rs, more, raw, plane_x, plane_y, across, conv_w, gain, *refs):
    count = len(rs)
    halves = 2 if rs == (3,) else 1
    count *= halves
    streams, finished, (out_ref, *onward, acc) = refs[:count], refs[count : count + more], refs[count + more :]
    for ref in finished:
        out_ref[: ref.shape[0]] = ref[...]
    if len(rs) > 1:
        for i, ref in enumerate(onward):
            half = ref.shape[1]
            ref[...] = streams[i][:, i * half : (i + 1) * half]
    _, _, depth = where_am_i()
    rows, width = raw.shape[0] - EXTRA, conv_w.shape[1]
    raws = [raw[:rows]]
    for ref in (plane_x, plane_y, across):
        at = ref.shape[0] - EXTRA - rows // 2
        raws.append(jnp.concatenate([ref[at : at + rows // 2, :HD], ref[at : at + rows // 2, HD:]], axis=0))
    raws = [value.astype(jnp.float32).reshape(rows // PP, PP, HD) for value in raws]
    done = out_ref.shape[0] - len(rs) * rows
    for i, r in enumerate(rs):
        place = depth ^ r
        even = (place & 1) == 0
        side, far = raws[r ^ 1], raws[r ^ 3]
        before = jnp.where(even, jnp.where(place == 2, far[:, PP - 1 :], 0.0), side[:, PP - 1 :])
        behind = jnp.where(even, side[:, :1], jnp.where(place == 1, far[:, :1], 0.0))
        padded = jnp.concatenate([before, raws[r], behind], axis=1)
        windows = [padded[:, j : j + PP].reshape(rows, HD).astype(jnp.bfloat16) for j in range(3)]
        windows = jnp.concatenate(windows, axis=1)
        total, step = jnp.zeros((rows, 1), jnp.float32), width // 4
        for at in range(0, width, step):
            here = slice(at, at + step)
            part = jnp.dot(windows, conv_w[:, here], preferred_element_type=jnp.float32)
            each = width // halves
            part += streams[i + at // each][:, at % each : at % each + step].astype(jnp.float32)
            acc[:, here] = part
            total += jnp.sum(part * part, axis=1, keepdims=True)
        scale = lax.rsqrt(total / width + 1e-05)
        normed = (acc[...] * scale * gain[...]).astype(jnp.bfloat16)
        out_ref[done + i * rows : done + (i + 1) * rows] = normed
        if halves > 1:
            cut = onward[0].shape[0]
            onward[0][...], onward[1][...] = normed[:cut], normed[cut:]


def take(refs, source, core, rows):
    half = rows // 2
    cuts = [pl.ds(pl.multiple_of(source * rows + c * half, half), half) for c in (core, 1 - core)]
    return jnp.concatenate([jnp.concatenate([ref[:, at] for at in cuts], axis=1) for ref in refs], axis=0)


def three_shards(x_refs, own, near, received, far):
    z, core, _ = where_am_i()
    size, width = own.shape[0], 3 * HD
    w = [own[:, :width], received[:size], far[...]]
    w = jnp.concatenate(w + [near[:, :width], received[size : 2 * size]], axis=0)
    x = [take(x_refs, source, core, 2 * size) for source in (z, z ^ 2, z ^ 1)]
    return jnp.dot(jnp.concatenate(x, axis=1), w, preferred_element_type=jnp.float32)


def partial_kernel(*refs):
    refs[-1][...] = three_shards(refs[:2], *refs[2:-1])


def diagonal_kernel(mine, top, bottom, *refs):
    weights, (acc_ref, x_ref) = refs[:-2], refs[-2:]
    at = 0
    for ref in (mine, top, bottom):
        x_ref[at : at + ref.shape[0]] = ref[...]
        at += ref.shape[0]
    acc_ref[...] = three_shards([x_ref], *weights)


ROW_ORDER = ((0, 1, 2, 6), (3, 4, 5, 7))


def finish_kernel(thirds, *refs):
    x_refs, (last, acc_in, acc_diagonal), out_refs = refs[:3], refs[3:6], refs[6:]
    z, core, _ = where_am_i()
    early = acc_in.shape[0]
    block = early // 6
    x = take(x_refs, z ^ 3, core, last.shape[0])
    for third in thirds:
        columns = slice(third * HD, (third + 1) * HD)
        value = jnp.dot(x, last[:, columns], preferred_element_type=jnp.float32)
        value = [acc_in[:, columns] + value[:early], acc_diagonal[:, columns] + value[early:]]
        value = jnp.concatenate(value, axis=0).astype(jnp.bfloat16)
        for rel in range(2):
            at = pl.ds(pl.multiple_of((core ^ rel) * block, block), block)
            for r in range(4):
                mine = value[ROW_ORDER[rel][r] * block : (ROW_ORDER[rel][r] + 1) * block]
                v_at = V_ORDER.index(r)
                if third == 2:
                    out_refs[1 + v_at // 2][v_at % 2, at, :] = mine
                else:
                    out_refs[0][r, at, :] = mine


def spans(u):
    return ((0, u, 2), (1, 0, 2), (2, 0, 1 + u))


def neighbours(outer, own, middle, index):
    z, _, _ = where_am_i()
    odd = (z & 1) == 1
    outer, middle = outer[index], middle[index]
    return jnp.where(odd, outer, middle), own[index], jnp.where(odd, middle, outer)


def weigh_kernel(q_ref, outer, own, middle, own_flags, received, out_ref):
    _, core, _ = where_am_i()
    block = q_ref.shape[1] // 2
    inv_root = 1.0 / math.sqrt(HD)
    flags = [own_flags[:, :HD].astype(jnp.float32), received[-EXTRA:, :HD].astype(jnp.float32)]
    flags = [jnp.where(core == u, flags[0], flags[1]) for u in range(2)]
    bias = [(f - 1.0) * 1e30 for f in flags]
    for r in range(4):
        keys = neighbours(outer, own, middle, r)
        for u in range(2):
            q = q_ref[r, u * block : (u + 1) * block]
            scores = []
            for side, first, last in spans(u):
                k = keys[side][first * block : last * block]
                s = lax.dot_general(q, k, (((1,), (1,)), ((), ())), preferred_element_type=jnp.float32)
                for v in range(last - first):
                    entry = len(scores)
                    shut = jnp.broadcast_to(bias[u][r : r + 1, entry : entry + 1], (block, block))
                    scores.append(s[:, v * block : (v + 1) * block] * inv_root + shut)
            top = jnp.max(functools.reduce(jnp.maximum, scores), axis=1, keepdims=True)
            powers = [jnp.exp(s - top) for s in scores]
            inverse = 1.0 / jnp.sum(functools.reduce(jnp.add, powers), axis=1, keepdims=True)
            for entry, p in enumerate(powers):
                here = slice(entry * block, (entry + 1) * block)
                out_ref[r, u * block : (u + 1) * block, here] = (p * inverse).astype(jnp.bfloat16)


def mix_kernel(r, weights, outer, own, middle, out_ref):
    block = weights.shape[1] // 2
    values = neighbours(outer, own, middle, V_ORDER.index(r) % 2)
    for u in range(2):
        w = weights[r, u * block : (u + 1) * block]
        v = [values[side][first * block : last * block] for side, first, last in spans(u)]
        result = jnp.dot(w, jnp.concatenate(v, axis=0), preferred_element_type=jnp.float32)
        out_ref[u * block : (u + 1) * block] = result.astype(jnp.bfloat16)


def pack_kernel(*refs):
    keep_ref, send_ref = refs[4:]
    _, core, _ = where_am_i()
    block = keep_ref.shape[1]
    for r, ref in enumerate(refs[:4]):
        for rel, out_ref in enumerate((keep_ref, send_ref)):
            out_ref[r] = ref[pl.ds(pl.multiple_of((core ^ rel) * block, block), block), :]


def gather_kernel(mine, other, out_ref):
    _, core, depth = where_am_i()
    for rel, ref in enumerate((mine, other)):
        for r in range(4):
            at = pl.multiple_of((2 * (depth ^ r) + (core ^ rel)) * HD, HD)
            out_ref[:, pl.ds(at, HD)] = ref[r]


def call(kernel, outs, places, scratch=(), macs=0, limit=32):
    spaces = {"v": VMEM}
    return pl.pallas_call(
        kernel,
        out_shape=outs,
        in_specs=[pl.BlockSpec(memory_space=spaces[place]) for place in places],
        out_specs=jax.tree.map(lambda _: pl.BlockSpec(memory_space=VMEM), outs),
        scratch_shapes=list(scratch),
        cost_estimate=pl.CostEstimate(flops=2 * macs, bytes_accessed=0, transcendentals=0),
        compiler_params=pltpu.CompilerParams(vmem_limit_bytes=limit * 2**20),
    )


def plane_device(raw, stream, conv_w, gain, w_qkv, mask):
    time_len, site_len, feat_len = raw.shape
    block, width = time_len * site_len, stream.shape[2]
    half, size = width // 2, w_qkv.shape[0]
    bf16, f32 = jnp.bfloat16, jnp.float32

    def array(*shape, kind=bf16):
        return jax.ShapeDtypeStruct(shape, kind)

    far_raw = swap_z(w_qkv, 2)

    mask_row = jnp.pad(mask.reshape(1, mask.shape[2]), ((0, 0), (0, feat_len - mask.shape[2]))).astype(bf16)
    raw = jnp.concatenate([raw.reshape(block, feat_len), jnp.broadcast_to(mask_row, (EXTRA, feat_len))], axis=0)
    stream = stream.reshape(block, width)
    conv_w, gain = conv_w.reshape(3 * feat_len, width), gain.reshape(1, width)
    more = block // 2 + EXTRA
    *to, kept = call(
        split_kernel,
        (array(size + more, PAIR), array(size + more, PAIR), array(more, PAIR), array(size, PAIR)),
        "vv",
    )(w_qkv, raw)
    plane = [swap_depth(t, r) for t, r in zip(to, (1, 2, 3))]
    own = call(sort_kernel, array(size, 6 * HD), "vvv")(after(kept, plane[2]), *plane[:2])
    near = swap_z(own, 1)
    far_raw = after(far_raw, own)

    piece = 5 * block // 8
    def embed(rs, *streams, finished=()):
        onward = {1: (), 2: (array(block, half),) * 2}[len(rs)]
        if rs == (3,):
            onward = (array(piece, width), array(block - piece, width))
        out = (array((len(rs) + len(finished)) * block, width), *onward)
        return call(
            functools.partial(embed_kernel, rs, len(finished)),
            out,
            "v" * (6 + len(streams) + len(finished)),
            scratch=[VMEM((block, width), f32)],
            macs=len(rs) * block * 3 * feat_len * width,
        )(raw, *plane, conv_w, gain, *streams, *finished)

    tied = after(stream, to[0])
    beside, above = swap_depth(tied, 1), swap_depth(tied, 2)
    (normed,) = embed((0,), stream)

    even = (lax.axis_index("depth") & 1) == 0
    low, to_x, high = (far_raw[:, k * PAIR : (k + 1) * PAIR] for k in range(3))
    kept, to_y = jnp.where(even, low, high), jnp.where(even, high, low)
    from_x, from_y = swap_depth(to_x, 1), swap_depth(to_y, 2)
    beside, above = after(beside, to_x), after(above, to_y)
    stack, *diagonal = embed((1, 2), beside, above, finished=(normed,))
    from_x, from_y, stack, near = lax.optimization_barrier((from_x, from_y, stack, near))
    keep, send, flags = call(
        sort_far_kernel,
        (array(size, 3 * HD), array(size, 3 * HD), array(EXTRA, 3 * HD)),
        "v" * 7,
    )(kept, from_x, from_y, *plane, raw)
    diagonal = swap_depth(diagonal[0], 2), swap_depth(diagonal[1], 1)
    far = jnp.concatenate([keep, swap_core(send)], axis=0)
    last = swap_z(far, 1)
    far, near, stack = lax.optimization_barrier((far, near, stack))
    to_other = call(other_kernel, array(2 * size + EXTRA, 3 * HD), "vvv")(own, near, flags)
    received = swap_core(to_other)
    weights = (own, near, received, far)
    early = (stack, swap_core(stack))
    rows = 2 * size
    total = call(partial_kernel, array(6 * block, 3 * HD, kind=f32), "v" * 6, macs=6 * block * 3 * rows * 3 * HD)(
        *early, *weights
    )
    diagonal, *parts = embed((3,), *[after(t, total) for t in diagonal])
    swapped = [swap_core(t) for t in parts]
    total_diagonal, diagonal = call(
        diagonal_kernel,
        (array(2 * block, 3 * HD, kind=f32), array(2 * block, width)),
        "v" * 7,
        macs=2 * block * 3 * rows * 3 * HD,
    )(diagonal, *swapped, *weights)
    one_head, half_head = array(4, 2 * block, HD), array(2, 2 * block, HD)
    sums = (*early, diagonal, last, total, total_diagonal)
    macs = 8 * block * rows * HD
    (k,) = call(functools.partial(finish_kernel, (1,)), (one_head,), "v" * 6, macs=macs)(*sums)
    q, *v = call(functools.partial(finish_kernel, (0, 2)), (one_head, half_head, half_head), "v" * 6, macs=2 * macs)(*sums)

    weights = call(weigh_kernel, array(4, 2 * block, 5 * block), "v" * 6, macs=8 * block * 5 * block * HD)(
        q, swap_z(k, 1), k, swap_middle(k), flags, received
    )
    values = [(swap_z(t, 1), t, swap_middle(t)) for t in v]
    pieces = {}
    for i, r in enumerate(V_ORDER):
        mixed = call(functools.partial(mix_kernel, r), array(2 * block, HD), "vvvv", macs=2 * block * 5 * block * HD)(
            weights, *values[i // 2]
        )
        pieces[r] = swap_depth(mixed, r) if r else mixed
    kept, sent = call(pack_kernel, (array(4, block, HD),) * 2, "vvvv")(*[pieces[r] for r in range(4)])
    context = call(gather_kernel, array(block, HEADS * HD), "vv")(kept, swap_core(sent))
    return context.reshape(time_len, site_len, HEADS * HD)


def from_behind(value, axis, by):
    devices = lax.axis_size(axis)
    pairs = [(i, i + by) for i in range(devices) if 0 <= i + by < devices]
    return lax.ppermute(value, axis, pairs)


def head_attend(query_head, key_head, value_head, allowed):
    inv_root = 1.0 / math.sqrt(HD)
    scores = (
        jnp.einsum("qd,kd->qk", query_head, key_head, preferred_element_type=jnp.float32) * inv_root
    )
    scores = jnp.where(allowed, scores, -1e30)
    row_max = jnp.max(scores, axis=-1, keepdims=True)
    powers = jnp.exp(scores - row_max)
    weights = (powers / jnp.sum(powers, axis=-1, keepdims=True)).astype(jnp.bfloat16)
    return jnp.dot(weights, value_head, preferred_element_type=jnp.float32).astype(jnp.bfloat16)


def per_device(raw, stream, conv_w, gain, w_qkv, mask):
    time_len, site_len, _ = raw.shape
    tok_rows = time_len * site_len
    normed = normed_tokens(padded_2(raw, (("depth", 1),), 1), stream, conv_w, gain)
    columns = lax.all_gather(w_qkv, "depth", axis=1, tiled=True)
    projected = jnp.dot(
        normed,
        lax.all_gather(columns, "tm", axis=0, tiled=True),
        preferred_element_type=jnp.float32,
    ).astype(jnp.bfloat16)
    head_cols = projected.shape[1] // 3
    queries = projected[:, :head_cols]
    keyvals = projected[:, head_cols:]
    earlier = []
    later = []
    moving_back = keyvals
    moving_ahead = keyvals
    for hop_index in range(RD):
        moving_back = from_behind(moving_back, "tm", 1)
        moving_ahead = from_behind(moving_ahead, "tm", -1)
        earlier.insert(0, moving_back)
        later.append(moving_ahead)
    gathered = jnp.concatenate(earlier + [keyvals] + later, axis=0)
    block_rows = BT * PP
    own_blocks = tok_rows // block_rows
    span_blocks = gathered.shape[0] // block_rows
    local_mask = mask[0]
    query_ids = jnp.arange(own_blocks, dtype=jnp.int32)[:, None]
    key_ids = jnp.arange(span_blocks, dtype=jnp.int32)[None, :]
    entry_ids = key_ids - query_ids
    picks = entry_ids[:, :, None] == jnp.arange(local_mask.shape[1], dtype=jnp.int32)[None, None, :]
    block_allowed = jnp.sum(jnp.where(picks, local_mask[:, None, :], 0), axis=-1) > 0
    allowed = jnp.repeat(jnp.repeat(block_allowed, block_rows, axis=0), block_rows, axis=1)
    query_heads = queries.reshape(tok_rows, HEADS, HD).transpose(1, 0, 2)
    key_heads = gathered[:, :head_cols].reshape(gathered.shape[0], HEADS, HD).transpose(1, 0, 2)
    value_heads = gathered[:, head_cols:].reshape(gathered.shape[0], HEADS, HD).transpose(1, 0, 2)
    context = lax.map(
        lambda operands: head_attend(operands[0], operands[1], operands[2], allowed),
        (query_heads, key_heads, value_heads),
    )
    return context.transpose(1, 0, 2).reshape(time_len, site_len, head_cols)


def solution(mesh):
    in_specs = (
        P("tm", "depth", None),
        P("tm", "depth", None),
        P(),
        P(),
        P("tm", "depth"),
        P("depth", "tm", None),
    )
    out_specs = P("tm", "depth", None)
    fits = mesh.shape["depth"] == 4 and mesh.shape["tm"] == 8
    return jax.shard_map(
        plane_device if fits else per_device, mesh=mesh, in_specs=in_specs, out_specs=out_specs, check_vma=False
    )
```

```python
import functools
import math

import jax
import jax.numpy as jnp
from jax import lax
from jax.experimental import pallas as pl
from jax.experimental.pallas import tpu as pltpu
from jax.sharding import PartitionSpec as P

HEADS = 8
HD = 128
BT = 16
PP = 8
RD = 2
VMEM = pltpu.VMEM
SMEM = pltpu.SMEM


def padded_2(value, sides, width):
    for axis, dim in sides:
        devices, length = (lax.axis_size(axis), value.shape[dim])
        up = [(i, (i + 1) % devices) for i in range(devices - 1)]
        down = [(j, i) for i, j in up]
        last = lax.slice_in_dim(value, length - width, length, axis=dim)
        leading = lax.slice_in_dim(value, 0, width, axis=dim)
        before = lax.ppermute(last, axis, up)
        after = lax.ppermute(leading, axis, down)
        value = jnp.concatenate([before, value, after], axis=dim)
    return value


def normed_tokens(padded, stream, conv_w, gain):
    time_len, site_len, width = stream.shape
    tok_rows = time_len * site_len
    embedded = stream.reshape(tok_rows, width).astype(jnp.float32)
    for offset in range(3):
        window = padded[:, offset : offset + site_len].reshape(tok_rows, padded.shape[2])
        embedded = embedded + jnp.dot(window, conv_w[offset], preferred_element_type=jnp.float32)
    scale = lax.rsqrt(jnp.mean(embedded * embedded, axis=-1, keepdims=True) + 1e-05)
    return (embedded * scale * gain).astype(jnp.bfloat16)


PAIR = 2 * HD
V_ORDER = (3, 1, 2, 0)
EXTRA = 16


def hop(value, fn):
    pairs = []
    for z in range(4):
        for core in range(2):
            for depth in range(4):
                to = fn(z, core, depth)
                if to is not None:
                    pairs.append(((2 * z + core) * 4 + depth, (2 * to[0] + to[1]) * 4 + to[2]))
    return lax.ppermute(value, ("tm", "depth"), pairs)


def swap_core(value):
    return hop(value, lambda z, c, d: (z, 1 - c, d))


def swap_depth(value, bits):
    return hop(value, lambda z, c, d: (z, c, d ^ bits))


def swap_z(value, bits):
    return hop(value, lambda z, c, d: (z ^ bits, c, d))


def swap_middle(value):
    return hop(value, lambda z, c, d: (z ^ 3, c, d) if z in (1, 2) else None)


def after(value, *others):
    return lax.optimization_barrier((value, *others))[0]


def where_am_i():
    tm = lax.axis_index("tm")
    return tm >> 1, tm & 1, lax.axis_index("depth")


def split_kernel(w, raw, to_x, to_y, to_across, keep):
    _, _, depth = where_am_i()
    even = (depth & 1) == 0
    size, half = w.shape[0], (raw.shape[0] - EXTRA) // 2
    low, high = w[:, :PAIR], w[:, 2 * PAIR :]
    to_x[:size] = w[:, PAIR : 2 * PAIR]
    to_y[:size] = jnp.where(even, high, low)
    keep[...] = jnp.where(even, low, high)
    for ref, at in ((to_x, size), (to_y, size), (to_across, 0)):
        for i in range(2):
            here = slice(i * HD, (i + 1) * HD)
            ref[at : at + half, here] = raw[i * half : (i + 1) * half]
            ref[at + half :, here] = raw[2 * half :]


def sorted_groups(kept, from_x, from_y):
    _, core, depth = where_am_i()
    first, even = core == 0, (depth & 1) == 0
    size = kept.shape[0]
    low = jnp.where(even, kept[...], from_y[:size])
    high = jnp.where(even, from_y[:size], kept[...])
    groups = (low, from_x[:size], high)
    turn = jnp.where(depth == 3, 0, depth)
    for third in range(3):
        group = jnp.where(turn == 0, groups[third], jnp.where(turn == 1, groups[(third + 1) % 3], groups[(third + 2) % 3]))
        yield third, jnp.where(first, group[:, :HD], group[:, HD:]), jnp.where(first, group[:, HD:], group[:, :HD])


def sort_kernel(kept, from_x, from_y, out_ref):
    for third, mine, other in sorted_groups(kept, from_x, from_y):
        out_ref[:, third * HD : (third + 1) * HD] = mine
        out_ref[:, (3 + third) * HD : (4 + third) * HD] = other


def sort_far_kernel(kept, from_x, from_y, plane_x, plane_y, across, raw, keep_ref, send_ref, flags_ref):
    for third, mine, other in sorted_groups(kept, from_x, from_y):
        send_ref[:, third * HD : (third + 1) * HD] = other
        keep_ref[:, third * HD : (third + 1) * HD] = mine
    row = lax.broadcasted_iota(jnp.int32, (EXTRA, HD), 0)
    flags = raw[raw.shape[0] - EXTRA :].astype(jnp.float32)
    for r, ref in enumerate((plane_x, plane_y, across)):
        flags = jnp.where(row == r + 1, ref[ref.shape[0] - EXTRA :, :HD].astype(jnp.float32), flags)
    flags = flags.astype(jnp.bfloat16)
    for k in range(3):
        flags_ref[:, k * HD : (k + 1) * HD] = flags


def other_kernel(own, near, flags, out_ref):
    size, width = own.shape[0], 3 * HD
    out_ref[:size] = own[:, width:]
    out_ref[size : 2 * size] = near[:, width:]
    out_ref[2 * size :] = flags[...]


def embed_kernel(rs, more, raw, plane_x, plane_y, across, conv_w, gain, *refs):
    count = len(rs)
    streamed = count > 1
    if streamed:
        refs, (tokens, sems) = refs[:-2], refs[-2:]
    halves = 2 if rs == (3,) else 1
    count *= halves
    streams, finished, (out_ref, *onward, acc) = refs[:count], refs[count : count + more], refs[count + more :]
    for ref in finished:
        out_ref[: ref.shape[0]] = ref[...]
    copies = {}
    if streamed:
        part = conv_w.shape[1] // 4
        for i in range(count):
            for at in range(0, conv_w.shape[1], part):
                here = pl.ds(at, part)
                copies[i, at] = pltpu.make_async_copy(
                    streams[i].at[:, here], tokens.at[i, :, here], sems.at[4 * i + at // part]
                )
                copies[i, at].start()
    _, _, depth = where_am_i()
    rows, width = raw.shape[0] - EXTRA, conv_w.shape[1]
    raws = [raw[:rows]]
    for ref in (plane_x, plane_y, across):
        at = ref.shape[0] - EXTRA - rows // 2
        raws.append(jnp.concatenate([ref[at : at + rows // 2, :HD], ref[at : at + rows // 2, HD:]], axis=0))
    raws = [value.astype(jnp.float32).reshape(rows // PP, PP, HD) for value in raws]
    done = out_ref.shape[0] - len(rs) * rows
    for i, r in enumerate(rs):
        place = depth ^ r
        even = (place & 1) == 0
        side, far = raws[r ^ 1], raws[r ^ 3]
        before = jnp.where(even, jnp.where(place == 2, far[:, PP - 1 :], 0.0), side[:, PP - 1 :])
        behind = jnp.where(even, side[:, :1], jnp.where(place == 1, far[:, :1], 0.0))
        padded = jnp.concatenate([before, raws[r], behind], axis=1)
        windows = [padded[:, j : j + PP].reshape(rows, HD).astype(jnp.bfloat16) for j in range(3)]
        windows = jnp.concatenate(windows, axis=1)
        total, step = jnp.zeros((rows, 1), jnp.float32), width // 4
        for at in range(0, width, step):
            here = slice(at, at + step)
            part = jnp.dot(windows, conv_w[:, here], preferred_element_type=jnp.float32)
            if streamed:
                copies[i, at].wait()
                part += tokens[i, :, here].astype(jnp.float32)
            else:
                each = width // halves
                part += streams[i + at // each][:, at % each : at % each + step].astype(jnp.float32)
            acc[:, here] = part
            total += jnp.sum(part * part, axis=1, keepdims=True)
        scale = lax.rsqrt(total / width + 1e-05)
        normed = (acc[...] * scale * gain[...]).astype(jnp.bfloat16)
        out_ref[done + i * rows : done + (i + 1) * rows] = normed
        if streamed:
            half = onward[i].shape[1]
            onward[i][...] = tokens[i, :, i * half : (i + 1) * half]
        if halves > 1:
            cut = onward[0].shape[0]
            onward[0][...], onward[1][...] = normed[:cut], normed[cut:]


def take(refs, source, core, rows):
    half = rows // 2
    cuts = [pl.ds(pl.multiple_of(source * rows + c * half, half), half) for c in (core, 1 - core)]
    return jnp.concatenate([jnp.concatenate([ref[:, at] for at in cuts], axis=1) for ref in refs], axis=0)


def three_shards(x_refs, own, near, received, far):
    z, core, _ = where_am_i()
    size, width = own.shape[0], 3 * HD
    w = [own[:, :width], received[:size], far[...]]
    w = jnp.concatenate(w + [near[:, :width], received[size : 2 * size]], axis=0)
    x = [take(x_refs, source, core, 2 * size) for source in (z, z ^ 2, z ^ 1)]
    return jnp.dot(jnp.concatenate(x, axis=1), w, preferred_element_type=jnp.float32)


def partial_kernel(*refs):
    refs[-1][...] = three_shards(refs[:2], *refs[2:-1])


def diagonal_kernel(mine, top, bottom, *refs):
    weights, (acc_ref, x_ref) = refs[:-2], refs[-2:]
    at = 0
    for ref in (mine, top, bottom):
        x_ref[at : at + ref.shape[0]] = ref[...]
        at += ref.shape[0]
    acc_ref[...] = three_shards([x_ref], *weights)


ROW_ORDER = ((0, 1, 2, 6), (3, 4, 5, 7))


def finish_kernel(thirds, *refs):
    x_refs, (last, acc_in, acc_diagonal), out_refs = refs[:3], refs[3:6], refs[6:]
    z, core, _ = where_am_i()
    early = acc_in.shape[0]
    block = early // 6
    x = take(x_refs, z ^ 3, core, last.shape[0])
    for third in thirds:
        columns = slice(third * HD, (third + 1) * HD)
        value = jnp.dot(x, last[:, columns], preferred_element_type=jnp.float32)
        value = [acc_in[:, columns] + value[:early], acc_diagonal[:, columns] + value[early:]]
        value = jnp.concatenate(value, axis=0).astype(jnp.bfloat16)
        for rel in range(2):
            at = pl.ds(pl.multiple_of((core ^ rel) * block, block), block)
            for r in range(4):
                mine = value[ROW_ORDER[rel][r] * block : (ROW_ORDER[rel][r] + 1) * block]
                v_at = V_ORDER.index(r)
                if third == 2:
                    out_refs[1 + v_at // 2][v_at % 2, at, :] = mine
                else:
                    out_refs[0][r, at, :] = mine


def spans(u):
    return ((0, u, 2), (1, 0, 2), (2, 0, 1 + u))


def neighbours(outer, own, middle, index):
    z, _, _ = where_am_i()
    odd = (z & 1) == 1
    outer, middle = outer[index], middle[index]
    return jnp.where(odd, outer, middle), own[index], jnp.where(odd, middle, outer)


def weigh_kernel(q_ref, outer, own, middle, own_flags, received, out_ref):
    _, core, _ = where_am_i()
    block = q_ref.shape[1] // 2
    inv_root = 1.0 / math.sqrt(HD)
    flags = [own_flags[:, :HD].astype(jnp.float32), received[-EXTRA:, :HD].astype(jnp.float32)]
    flags = [jnp.where(core == u, flags[0], flags[1]) for u in range(2)]
    bias = [(f - 1.0) * 1e30 for f in flags]
    for r in range(4):
        keys = neighbours(outer, own, middle, r)
        for u in range(2):
            q = q_ref[r, u * block : (u + 1) * block]
            scores = []
            for side, first, last in spans(u):
                k = keys[side][first * block : last * block]
                s = lax.dot_general(q, k, (((1,), (1,)), ((), ())), preferred_element_type=jnp.float32)
                for v in range(last - first):
                    entry = len(scores)
                    shut = jnp.broadcast_to(bias[u][r : r + 1, entry : entry + 1], (block, block))
                    scores.append(s[:, v * block : (v + 1) * block] * inv_root + shut)
            top = jnp.max(functools.reduce(jnp.maximum, scores), axis=1, keepdims=True)
            powers = [jnp.exp(s - top) for s in scores]
            inverse = 1.0 / jnp.sum(functools.reduce(jnp.add, powers), axis=1, keepdims=True)
            for entry, p in enumerate(powers):
                here = slice(entry * block, (entry + 1) * block)
                out_ref[r, u * block : (u + 1) * block, here] = (p * inverse).astype(jnp.bfloat16)


def mix_kernel(r, weights, outer, own, middle, out_ref):
    block = weights.shape[1] // 2
    values = neighbours(outer, own, middle, V_ORDER.index(r) % 2)
    for u in range(2):
        w = weights[r, u * block : (u + 1) * block]
        v = [values[side][first * block : last * block] for side, first, last in spans(u)]
        result = jnp.dot(w, jnp.concatenate(v, axis=0), preferred_element_type=jnp.float32)
        out_ref[u * block : (u + 1) * block] = result.astype(jnp.bfloat16)


def pack_kernel(*refs):
    keep_ref, send_ref = refs[4:]
    _, core, _ = where_am_i()
    block = keep_ref.shape[1]
    for r, ref in enumerate(refs[:4]):
        for rel, out_ref in enumerate((keep_ref, send_ref)):
            out_ref[r] = ref[pl.ds(pl.multiple_of((core ^ rel) * block, block), block), :]


def gather_kernel(mine, other, out_ref):
    _, core, depth = where_am_i()
    for rel, ref in enumerate((mine, other)):
        for r in range(4):
            at = pl.multiple_of((2 * (depth ^ r) + (core ^ rel)) * HD, HD)
            out_ref[:, pl.ds(at, HD)] = ref[r]


def call(kernel, outs, places, scratch=(), macs=0, limit=32):
    spaces = {"v": VMEM, "a": pl.ANY}
    return pl.pallas_call(
        kernel,
        out_shape=outs,
        in_specs=[pl.BlockSpec(memory_space=spaces[place]) for place in places],
        out_specs=jax.tree.map(lambda _: pl.BlockSpec(memory_space=VMEM), outs),
        scratch_shapes=list(scratch),
        cost_estimate=pl.CostEstimate(flops=2 * macs, bytes_accessed=0, transcendentals=0),
        compiler_params=pltpu.CompilerParams(vmem_limit_bytes=limit * 2**20),
    )


def plane_device(raw, stream, conv_w, gain, w_qkv, mask):
    time_len, site_len, feat_len = raw.shape
    block, width = time_len * site_len, stream.shape[2]
    half, size = width // 2, w_qkv.shape[0]
    bf16, f32 = jnp.bfloat16, jnp.float32

    def array(*shape, kind=bf16):
        return jax.ShapeDtypeStruct(shape, kind)

    far_raw = swap_z(w_qkv, 2)

    mask_row = jnp.pad(mask.reshape(1, mask.shape[2]), ((0, 0), (0, feat_len - mask.shape[2]))).astype(bf16)
    raw = jnp.concatenate([raw.reshape(block, feat_len), jnp.broadcast_to(mask_row, (EXTRA, feat_len))], axis=0)
    stream = stream.reshape(block, width)
    conv_w, gain = conv_w.reshape(3 * feat_len, width), gain.reshape(1, width)
    more = block // 2 + EXTRA
    *to, kept = call(
        split_kernel,
        (array(size + more, PAIR), array(size + more, PAIR), array(more, PAIR), array(size, PAIR)),
        "vv",
    )(w_qkv, raw)
    plane = [swap_depth(t, r) for t, r in zip(to, (1, 2, 3))]
    own = call(sort_kernel, array(size, 6 * HD), "vvv")(kept, *plane[:2])
    near = swap_z(own, 1)
    far_raw = after(far_raw, own)

    piece = 5 * block // 8
    def embed(rs, *streams, finished=()):
        onward = {1: (), 2: (array(block, half),) * 2}[len(rs)]
        if rs == (3,):
            onward = (array(piece, width), array(block - piece, width))
        out = (array((len(rs) + len(finished)) * block, width), *onward)
        return call(
            functools.partial(embed_kernel, rs, len(finished)),
            out,
            "v" * 6 + ("a" if len(rs) > 1 else "v") * len(streams) + "v" * len(finished),
            scratch=[VMEM((block, width), f32)]
            + [VMEM((2, block, width), bf16), pltpu.SemaphoreType.DMA((8,))] * (len(rs) > 1),
            macs=len(rs) * block * 3 * feat_len * width,
        )(raw, *plane, conv_w, gain, *streams, *finished)

    tied = after(stream, to[0])
    beside, above = swap_depth(tied, 1), swap_depth(tied, 2)
    (normed,) = embed((0,), stream)

    even = (lax.axis_index("depth") & 1) == 0
    low, to_x, high = (far_raw[:, k * PAIR : (k + 1) * PAIR] for k in range(3))
    kept, to_y = jnp.where(even, low, high), jnp.where(even, high, low)
    from_x, from_y = swap_depth(to_x, 1), swap_depth(to_y, 2)
    beside, above = after(beside, to_x), after(above, to_y)
    stack, *diagonal = embed((1, 2), beside, above, finished=(normed,))
    from_x, from_y, stack, near = lax.optimization_barrier((from_x, from_y, stack, near))
    keep, send, flags = call(
        sort_far_kernel,
        (array(size, 3 * HD), array(size, 3 * HD), array(EXTRA, 3 * HD)),
        "v" * 7,
    )(kept, from_x, from_y, *plane, raw)
    diagonal = swap_depth(diagonal[0], 2), swap_depth(diagonal[1], 1)
    far = jnp.concatenate([keep, swap_core(send)], axis=0)
    last = swap_z(far, 1)
    far, near, stack = lax.optimization_barrier((far, near, stack))
    to_other = call(other_kernel, array(2 * size + EXTRA, 3 * HD), "vvv")(own, near, flags)
    received = swap_core(to_other)
    weights = (own, near, received, far)
    early = (stack, swap_core(stack))
    rows = 2 * size
    total = call(partial_kernel, array(6 * block, 3 * HD, kind=f32), "v" * 6, macs=6 * block * 3 * rows * 3 * HD)(
        *early, *weights
    )
    diagonal, *parts = embed((3,), *[after(t, total) for t in diagonal])
    swapped = [swap_core(t) for t in parts]
    total_diagonal, diagonal = call(
        diagonal_kernel,
        (array(2 * block, 3 * HD, kind=f32), array(2 * block, width)),
        "v" * 7,
        macs=2 * block * 3 * rows * 3 * HD,
    )(diagonal, *swapped, *weights)
    one_head, half_head = array(4, 2 * block, HD), array(2, 2 * block, HD)
    sums = (*early, diagonal, last, total, total_diagonal)
    macs = 8 * block * rows * HD
    (k,) = call(functools.partial(finish_kernel, (1,)), (one_head,), "v" * 6, macs=macs)(*sums)
    q, *v = call(functools.partial(finish_kernel, (0, 2)), (one_head, half_head, half_head), "v" * 6, macs=2 * macs)(*sums)

    weights = call(weigh_kernel, array(4, 2 * block, 5 * block), "v" * 6, macs=8 * block * 5 * block * HD)(
        q, swap_z(k, 1), k, swap_middle(k), flags, received
    )
    values = [(swap_z(t, 1), t, swap_middle(t)) for t in v]
    pieces = {}
    for i, r in enumerate(V_ORDER):
        mixed = call(functools.partial(mix_kernel, r), array(2 * block, HD), "vvvv", macs=2 * block * 5 * block * HD)(
            weights, *values[i // 2]
        )
        pieces[r] = swap_depth(mixed, r) if r else mixed
    kept, sent = call(pack_kernel, (array(4, block, HD),) * 2, "vvvv")(*[pieces[r] for r in range(4)])
    context = call(gather_kernel, array(block, HEADS * HD), "vv")(kept, swap_core(sent))
    return context.reshape(time_len, site_len, HEADS * HD)


def from_behind(value, axis, by):
    devices = lax.axis_size(axis)
    pairs = [(i, i + by) for i in range(devices) if 0 <= i + by < devices]
    return lax.ppermute(value, axis, pairs)


def head_attend(query_head, key_head, value_head, allowed):
    inv_root = 1.0 / math.sqrt(HD)
    scores = (
        jnp.einsum("qd,kd->qk", query_head, key_head, preferred_element_type=jnp.float32) * inv_root
    )
    scores = jnp.where(allowed, scores, -1e30)
    row_max = jnp.max(scores, axis=-1, keepdims=True)
    powers = jnp.exp(scores - row_max)
    weights = (powers / jnp.sum(powers, axis=-1, keepdims=True)).astype(jnp.bfloat16)
    return jnp.dot(weights, value_head, preferred_element_type=jnp.float32).astype(jnp.bfloat16)


def per_device(raw, stream, conv_w, gain, w_qkv, mask):
    time_len, site_len, _ = raw.shape
    tok_rows = time_len * site_len
    normed = normed_tokens(padded_2(raw, (("depth", 1),), 1), stream, conv_w, gain)
    columns = lax.all_gather(w_qkv, "depth", axis=1, tiled=True)
    projected = jnp.dot(
        normed,
        lax.all_gather(columns, "tm", axis=0, tiled=True),
        preferred_element_type=jnp.float32,
    ).astype(jnp.bfloat16)
    head_cols = projected.shape[1] // 3
    queries = projected[:, :head_cols]
    keyvals = projected[:, head_cols:]
    earlier = []
    later = []
    moving_back = keyvals
    moving_ahead = keyvals
    for hop_index in range(RD):
        moving_back = from_behind(moving_back, "tm", 1)
        moving_ahead = from_behind(moving_ahead, "tm", -1)
        earlier.insert(0, moving_back)
        later.append(moving_ahead)
    gathered = jnp.concatenate(earlier + [keyvals] + later, axis=0)
    block_rows = BT * PP
    own_blocks = tok_rows // block_rows
    span_blocks = gathered.shape[0] // block_rows
    local_mask = mask[0]
    query_ids = jnp.arange(own_blocks, dtype=jnp.int32)[:, None]
    key_ids = jnp.arange(span_blocks, dtype=jnp.int32)[None, :]
    entry_ids = key_ids - query_ids
    picks = entry_ids[:, :, None] == jnp.arange(local_mask.shape[1], dtype=jnp.int32)[None, None, :]
    block_allowed = jnp.sum(jnp.where(picks, local_mask[:, None, :], 0), axis=-1) > 0
    allowed = jnp.repeat(jnp.repeat(block_allowed, block_rows, axis=0), block_rows, axis=1)
    query_heads = queries.reshape(tok_rows, HEADS, HD).transpose(1, 0, 2)
    key_heads = gathered[:, :head_cols].reshape(gathered.shape[0], HEADS, HD).transpose(1, 0, 2)
    value_heads = gathered[:, head_cols:].reshape(gathered.shape[0], HEADS, HD).transpose(1, 0, 2)
    context = lax.map(
        lambda operands: head_attend(operands[0], operands[1], operands[2], allowed),
        (query_heads, key_heads, value_heads),
    )
    return context.transpose(1, 0, 2).reshape(time_len, site_len, head_cols)


def solution(mesh):
    in_specs = (
        P("tm", "depth", None),
        P("tm", "depth", None),
        P(),
        P(),
        P("tm", "depth"),
        P("depth", "tm", None),
    )
    out_specs = P("tm", "depth", None)
    fits = mesh.shape["depth"] == 4 and mesh.shape["tm"] == 8
    return jax.shard_map(
        plane_device if fits else per_device, mesh=mesh, in_specs=in_specs, out_specs=out_specs, check_vma=False
    )
```

```python
import functools
import math

import jax
import jax.numpy as jnp
from jax import lax
from jax.experimental import pallas as pl
from jax.experimental.pallas import tpu as pltpu
from jax.sharding import PartitionSpec as P

HEADS = 8
HD = 128
BT = 16
PP = 8
RD = 2
VMEM = pltpu.VMEM
SMEM = pltpu.SMEM


def padded_2(value, sides, width):
    for axis, dim in sides:
        devices, length = (lax.axis_size(axis), value.shape[dim])
        up = [(i, (i + 1) % devices) for i in range(devices - 1)]
        down = [(j, i) for i, j in up]
        last = lax.slice_in_dim(value, length - width, length, axis=dim)
        leading = lax.slice_in_dim(value, 0, width, axis=dim)
        before = lax.ppermute(last, axis, up)
        after = lax.ppermute(leading, axis, down)
        value = jnp.concatenate([before, value, after], axis=dim)
    return value


def normed_tokens(padded, stream, conv_w, gain):
    time_len, site_len, width = stream.shape
    tok_rows = time_len * site_len
    embedded = stream.reshape(tok_rows, width).astype(jnp.float32)
    for offset in range(3):
        window = padded[:, offset : offset + site_len].reshape(tok_rows, padded.shape[2])
        embedded = embedded + jnp.dot(window, conv_w[offset], preferred_element_type=jnp.float32)
    scale = lax.rsqrt(jnp.mean(embedded * embedded, axis=-1, keepdims=True) + 1e-05)
    return (embedded * scale * gain).astype(jnp.bfloat16)


PAIR = 2 * HD
V_ORDER = (3, 1, 2, 0)
EXTRA = 16


def hop(value, fn):
    pairs = []
    for z in range(4):
        for core in range(2):
            for depth in range(4):
                to = fn(z, core, depth)
                if to is not None:
                    pairs.append(((2 * z + core) * 4 + depth, (2 * to[0] + to[1]) * 4 + to[2]))
    return lax.ppermute(value, ("tm", "depth"), pairs)


def swap_core(value):
    return hop(value, lambda z, c, d: (z, 1 - c, d))


def swap_depth(value, bits):
    return hop(value, lambda z, c, d: (z, c, d ^ bits))


def swap_z(value, bits):
    return hop(value, lambda z, c, d: (z ^ bits, c, d))


def swap_middle(value):
    return hop(value, lambda z, c, d: (z ^ 3, c, d) if z in (1, 2) else None)


def after(value, *others):
    return lax.optimization_barrier((value, *others))[0]


def where_am_i():
    tm = lax.axis_index("tm")
    return tm >> 1, tm & 1, lax.axis_index("depth")


def split_kernel(w, raw, to_x, to_y, to_across, keep):
    _, _, depth = where_am_i()
    even = (depth & 1) == 0
    size, half = w.shape[0], (raw.shape[0] - EXTRA) // 2
    low, high = w[:, :PAIR], w[:, 2 * PAIR :]
    to_x[:size] = w[:, PAIR : 2 * PAIR]
    to_y[:size] = jnp.where(even, high, low)
    keep[...] = jnp.where(even, low, high)
    for ref, at in ((to_x, size), (to_y, size), (to_across, 0)):
        for i in range(2):
            here = slice(i * HD, (i + 1) * HD)
            ref[at : at + half, here] = raw[i * half : (i + 1) * half]
            ref[at + half :, here] = raw[2 * half :]


def sorted_groups(kept, from_x, from_y):
    _, core, depth = where_am_i()
    first, even = core == 0, (depth & 1) == 0
    size = kept.shape[0]
    low = jnp.where(even, kept[...], from_y[:size])
    high = jnp.where(even, from_y[:size], kept[...])
    groups = (low, from_x[:size], high)
    turn = jnp.where(depth == 3, 0, depth)
    for third in range(3):
        group = jnp.where(turn == 0, groups[third], jnp.where(turn == 1, groups[(third + 1) % 3], groups[(third + 2) % 3]))
        yield third, jnp.where(first, group[:, :HD], group[:, HD:]), jnp.where(first, group[:, HD:], group[:, :HD])


def sort_kernel(kept, from_x, from_y, out_ref):
    for third, mine, other in sorted_groups(kept, from_x, from_y):
        out_ref[:, third * HD : (third + 1) * HD] = mine
        out_ref[:, (3 + third) * HD : (4 + third) * HD] = other


def sort_far_kernel(kept, from_x, from_y, plane_x, plane_y, across, raw, keep_ref, send_ref, flags_ref):
    for third, mine, other in sorted_groups(kept, from_x, from_y):
        send_ref[:, third * HD : (third + 1) * HD] = other
        keep_ref[:, third * HD : (third + 1) * HD] = mine
    row = lax.broadcasted_iota(jnp.int32, (EXTRA, HD), 0)
    flags = raw[raw.shape[0] - EXTRA :].astype(jnp.float32)
    for r, ref in enumerate((plane_x, plane_y, across)):
        flags = jnp.where(row == r + 1, ref[ref.shape[0] - EXTRA :, :HD].astype(jnp.float32), flags)
    flags = flags.astype(jnp.bfloat16)
    for k in range(3):
        flags_ref[:, k * HD : (k + 1) * HD] = flags


def other_kernel(own, near, flags, out_ref):
    size, width = own.shape[0], 3 * HD
    out_ref[:size] = own[:, width:]
    out_ref[size : 2 * size] = near[:, width:]
    out_ref[2 * size :] = flags[...]


def embed_kernel(rs, more, raw, plane_x, plane_y, across, conv_w, gain, *refs):
    count = len(rs)
    halves = 2 if rs == (3,) else 1
    count *= halves
    streams, finished, (out_ref, *onward, acc) = refs[:count], refs[count : count + more], refs[count + more :]
    for ref in finished:
        out_ref[: ref.shape[0]] = ref[...]
    if len(rs) > 1:
        for i, ref in enumerate(onward):
            half = ref.shape[1]
            ref[...] = streams[i][:, i * half : (i + 1) * half]
    _, _, depth = where_am_i()
    rows, width = raw.shape[0] - EXTRA, conv_w.shape[1]
    raws = [raw[:rows]]
    for ref in (plane_x, plane_y, across):
        at = ref.shape[0] - EXTRA - rows // 2
        raws.append(jnp.concatenate([ref[at : at + rows // 2, :HD], ref[at : at + rows // 2, HD:]], axis=0))
    raws = [value.astype(jnp.float32).reshape(rows // PP, PP, HD) for value in raws]
    done = out_ref.shape[0] - len(rs) * rows
    for i, r in enumerate(rs):
        place = depth ^ r
        even = (place & 1) == 0
        side, far = raws[r ^ 1], raws[r ^ 3]
        before = jnp.where(even, jnp.where(place == 2, far[:, PP - 1 :], 0.0), side[:, PP - 1 :])
        behind = jnp.where(even, side[:, :1], jnp.where(place == 1, far[:, :1], 0.0))
        padded = jnp.concatenate([before, raws[r], behind], axis=1)
        windows = [padded[:, j : j + PP].reshape(rows, HD).astype(jnp.bfloat16) for j in range(3)]
        windows = jnp.concatenate(windows, axis=1)
        total, step = jnp.zeros((rows, 1), jnp.float32), width // 4
        for at in range(0, width, step):
            here = slice(at, at + step)
            part = jnp.dot(windows, conv_w[:, here], preferred_element_type=jnp.float32)
            each = width // halves
            part += streams[i + at // each][:, at % each : at % each + step].astype(jnp.float32)
            acc[:, here] = part
            total += jnp.sum(part * part, axis=1, keepdims=True)
        scale = lax.rsqrt(total / width + 1e-05)
        normed = (acc[...] * scale * gain[...]).astype(jnp.bfloat16)
        out_ref[done + i * rows : done + (i + 1) * rows] = normed
        if halves > 1:
            cut = onward[0].shape[0]
            onward[0][...], onward[1][...] = normed[:cut], normed[cut:]


def take(refs, source, core, rows):
    half = rows // 2
    cuts = [pl.ds(pl.multiple_of(source * rows + c * half, half), half) for c in (core, 1 - core)]
    return jnp.concatenate([jnp.concatenate([ref[:, at] for at in cuts], axis=1) for ref in refs], axis=0)


def three_shards(x_refs, own, near, received, far):
    z, core, _ = where_am_i()
    size, width = own.shape[0], 3 * HD
    w = [own[:, :width], received[:size], far[...]]
    w = jnp.concatenate(w + [near[:, :width], received[size : 2 * size]], axis=0)
    x = [take(x_refs, source, core, 2 * size) for source in (z, z ^ 2, z ^ 1)]
    return jnp.dot(jnp.concatenate(x, axis=1), w, preferred_element_type=jnp.float32)


def partial_kernel(*refs):
    refs[-1][...] = three_shards(refs[:2], *refs[2:-1])


def diagonal_kernel(mine, top, bottom, *refs):
    weights, (acc_ref, x_ref) = refs[:-2], refs[-2:]
    at = 0
    for ref in (mine, top, bottom):
        x_ref[at : at + ref.shape[0]] = ref[...]
        at += ref.shape[0]
    acc_ref[...] = three_shards([x_ref], *weights)


ROW_ORDER = ((0, 1, 2, 6), (3, 4, 5, 7))


def finish_kernel(thirds, *refs):
    x_refs, (last, acc_in, acc_diagonal), out_refs = refs[:3], refs[3:6], refs[6:]
    z, core, _ = where_am_i()
    early = acc_in.shape[0]
    block = early // 6
    x = take(x_refs, z ^ 3, core, last.shape[0])
    for third in thirds:
        columns = slice(third * HD, (third + 1) * HD)
        value = jnp.dot(x, last[:, columns], preferred_element_type=jnp.float32)
        value = [acc_in[:, columns] + value[:early], acc_diagonal[:, columns] + value[early:]]
        value = jnp.concatenate(value, axis=0).astype(jnp.bfloat16)
        for rel in range(2):
            at = pl.ds(pl.multiple_of((core ^ rel) * block, block), block)
            for r in range(4):
                mine = value[ROW_ORDER[rel][r] * block : (ROW_ORDER[rel][r] + 1) * block]
                v_at = V_ORDER.index(r)
                if third == 2:
                    out_refs[1 + v_at // 2][v_at % 2, at, :] = mine
                else:
                    out_refs[0][r, at, :] = mine


def spans(u):
    return ((0, u, 2), (1, 0, 2), (2, 0, 1 + u))


def neighbours(outer, own, middle, index):
    z, _, _ = where_am_i()
    odd = (z & 1) == 1
    outer, middle = outer[index], middle[index]
    return jnp.where(odd, outer, middle), own[index], jnp.where(odd, middle, outer)


def weigh_kernel(q_ref, outer, own, middle, own_flags, received, out_ref):
    _, core, _ = where_am_i()
    block = q_ref.shape[1] // 2
    inv_root = 1.0 / math.sqrt(HD)
    flags = [own_flags[:, :HD].astype(jnp.float32), received[-EXTRA:, :HD].astype(jnp.float32)]
    flags = [jnp.where(core == u, flags[0], flags[1]) for u in range(2)]
    bias = [(f - 1.0) * 1e30 for f in flags]
    for r in range(4):
        keys = neighbours(outer, own, middle, r)
        for u in range(2):
            q = q_ref[r, u * block : (u + 1) * block]
            scores = []
            for side, first, last in spans(u):
                k = keys[side][first * block : last * block]
                s = lax.dot_general(q, k, (((1,), (1,)), ((), ())), preferred_element_type=jnp.float32)
                for v in range(last - first):
                    entry = len(scores)
                    shut = jnp.broadcast_to(bias[u][r : r + 1, entry : entry + 1], (block, block))
                    scores.append(s[:, v * block : (v + 1) * block] * inv_root + shut)
            top = jnp.max(functools.reduce(jnp.maximum, scores), axis=1, keepdims=True)
            powers = [jnp.exp(s - top) for s in scores]
            inverse = 1.0 / jnp.sum(functools.reduce(jnp.add, powers), axis=1, keepdims=True)
            for entry, p in enumerate(powers):
                here = slice(entry * block, (entry + 1) * block)
                out_ref[r, u * block : (u + 1) * block, here] = (p * inverse).astype(jnp.bfloat16)


def mix_kernel(r, weights, outer, own, middle, out_ref):
    block = weights.shape[1] // 2
    values = neighbours(outer, own, middle, V_ORDER.index(r) % 2)
    for u in range(2):
        w = weights[r, u * block : (u + 1) * block]
        v = [values[side][first * block : last * block] for side, first, last in spans(u)]
        result = jnp.dot(w, jnp.concatenate(v, axis=0), preferred_element_type=jnp.float32)
        out_ref[u * block : (u + 1) * block] = result.astype(jnp.bfloat16)


def pack_kernel(*refs):
    keep_ref, send_ref = refs[4:]
    _, core, _ = where_am_i()
    block = keep_ref.shape[1]
    for r, ref in enumerate(refs[:4]):
        for rel, out_ref in enumerate((keep_ref, send_ref)):
            out_ref[r] = ref[pl.ds(pl.multiple_of((core ^ rel) * block, block), block), :]


def gather_kernel(mine, other, out_ref):
    _, core, depth = where_am_i()
    for rel, ref in enumerate((mine, other)):
        for r in range(4):
            at = pl.multiple_of((2 * (depth ^ r) + (core ^ rel)) * HD, HD)
            out_ref[:, pl.ds(at, HD)] = ref[r]


def call(kernel, outs, places, scratch=(), macs=0, limit=32):
    spaces = {"v": VMEM}
    return pl.pallas_call(
        kernel,
        out_shape=outs,
        in_specs=[pl.BlockSpec(memory_space=spaces[place]) for place in places],
        out_specs=jax.tree.map(lambda _: pl.BlockSpec(memory_space=VMEM), outs),
        scratch_shapes=list(scratch),
        cost_estimate=pl.CostEstimate(flops=2 * macs, bytes_accessed=0, transcendentals=0),
        compiler_params=pltpu.CompilerParams(vmem_limit_bytes=limit * 2**20),
    )


def plane_device(raw, stream, conv_w, gain, w_qkv, mask):
    time_len, site_len, feat_len = raw.shape
    block, width = time_len * site_len, stream.shape[2]
    half, size = width // 2, w_qkv.shape[0]
    bf16, f32 = jnp.bfloat16, jnp.float32

    def array(*shape, kind=bf16):
        return jax.ShapeDtypeStruct(shape, kind)

    far_raw = swap_z(w_qkv, 2)

    mask_row = jnp.pad(mask.reshape(1, mask.shape[2]), ((0, 0), (0, feat_len - mask.shape[2]))).astype(bf16)
    raw = jnp.concatenate([raw.reshape(block, feat_len), jnp.broadcast_to(mask_row, (EXTRA, feat_len))], axis=0)
    stream = stream.reshape(block, width)
    conv_w, gain = conv_w.reshape(3 * feat_len, width), gain.reshape(1, width)
    more = block // 2 + EXTRA
    *to, kept = call(
        split_kernel,
        (array(size + more, PAIR), array(size + more, PAIR), array(more, PAIR), array(size, PAIR)),
        "vv",
    )(w_qkv, raw)
    plane = [swap_depth(t, r) for t, r in zip(to, (1, 2, 3))]
    own = call(sort_kernel, array(size, 6 * HD), "vvv")(kept, *plane[:2])
    near = swap_z(own, 1)
    far_raw = after(far_raw, own)

    piece = block // 2
    def embed(rs, *streams, finished=()):
        onward = {1: (), 2: (array(block, half),) * 2}[len(rs)]
        if rs == (3,):
            onward = (array(piece, width), array(block - piece, width))
        out = (array((len(rs) + len(finished)) * block, width), *onward)
        return call(
            functools.partial(embed_kernel, rs, len(finished)),
            out,
            "v" * (6 + len(streams) + len(finished)),
            scratch=[VMEM((block, width), f32)],
            macs=len(rs) * block * 3 * feat_len * width,
        )(raw, *plane, conv_w, gain, *streams, *finished)

    tied = after(stream, to[0])
    beside, above = swap_depth(tied, 1), swap_depth(tied, 2)
    (normed,) = embed((0,), stream)

    even = (lax.axis_index("depth") & 1) == 0
    low, to_x, high = (far_raw[:, k * PAIR : (k + 1) * PAIR] for k in range(3))
    kept, to_y = jnp.where(even, low, high), jnp.where(even, high, low)
    from_x, from_y = swap_depth(to_x, 1), swap_depth(to_y, 2)
    beside, above = after(beside, to_x), after(above, to_y)
    stack, *diagonal = embed((1, 2), beside, above, finished=(normed,))
    from_x, from_y, stack, near = lax.optimization_barrier((from_x, from_y, stack, near))
    keep, send, flags = call(
        sort_far_kernel,
        (array(size, 3 * HD), array(size, 3 * HD), array(EXTRA, 3 * HD)),
        "v" * 7,
    )(kept, from_x, from_y, *plane, raw)
    diagonal = swap_depth(diagonal[0], 2), swap_depth(diagonal[1], 1)
    far = jnp.concatenate([keep, swap_core(send)], axis=0)
    last = swap_z(far, 1)
    far, near, stack = lax.optimization_barrier((far, near, stack))
    to_other = call(other_kernel, array(2 * size + EXTRA, 3 * HD), "vvv")(own, near, flags)
    received = swap_core(to_other)
    weights = (own, near, received, far)
    early = (stack, swap_core(stack))
    rows = 2 * size
    total = call(partial_kernel, array(6 * block, 3 * HD, kind=f32), "v" * 6, macs=6 * block * 3 * rows * 3 * HD)(
        *early, *weights
    )
    diagonal, *parts = embed((3,), *[after(t, total) for t in diagonal])
    swapped = [swap_core(t) for t in parts]
    total_diagonal, diagonal = call(
        diagonal_kernel,
        (array(2 * block, 3 * HD, kind=f32), array(2 * block, width)),
        "v" * 7,
        macs=2 * block * 3 * rows * 3 * HD,
    )(diagonal, *swapped, *weights)
    one_head, half_head = array(4, 2 * block, HD), array(2, 2 * block, HD)
    sums = (*early, diagonal, last, total, total_diagonal)
    macs = 8 * block * rows * HD
    (k,) = call(functools.partial(finish_kernel, (1,)), (one_head,), "v" * 6, macs=macs)(*sums)
    q, *v = call(functools.partial(finish_kernel, (0, 2)), (one_head, half_head, half_head), "v" * 6, macs=2 * macs)(*sums)

    weights = call(weigh_kernel, array(4, 2 * block, 5 * block), "v" * 6, macs=8 * block * 5 * block * HD)(
        q, swap_z(k, 1), k, swap_middle(k), flags, received
    )
    values = [(swap_z(t, 1), t, swap_middle(t)) for t in v]
    pieces = {}
    for i, r in enumerate(V_ORDER):
        mixed = call(functools.partial(mix_kernel, r), array(2 * block, HD), "vvvv", macs=2 * block * 5 * block * HD)(
            weights, *values[i // 2]
        )
        pieces[r] = swap_depth(mixed, r) if r else mixed
    kept, sent = call(pack_kernel, (array(4, block, HD),) * 2, "vvvv")(*[pieces[r] for r in range(4)])
    context = call(gather_kernel, array(block, HEADS * HD), "vv")(kept, swap_core(sent))
    return context.reshape(time_len, site_len, HEADS * HD)


def from_behind(value, axis, by):
    devices = lax.axis_size(axis)
    pairs = [(i, i + by) for i in range(devices) if 0 <= i + by < devices]
    return lax.ppermute(value, axis, pairs)


def head_attend(query_head, key_head, value_head, allowed):
    inv_root = 1.0 / math.sqrt(HD)
    scores = (
        jnp.einsum("qd,kd->qk", query_head, key_head, preferred_element_type=jnp.float32) * inv_root
    )
    scores = jnp.where(allowed, scores, -1e30)
    row_max = jnp.max(scores, axis=-1, keepdims=True)
    powers = jnp.exp(scores - row_max)
    weights = (powers / jnp.sum(powers, axis=-1, keepdims=True)).astype(jnp.bfloat16)
    return jnp.dot(weights, value_head, preferred_element_type=jnp.float32).astype(jnp.bfloat16)


def per_device(raw, stream, conv_w, gain, w_qkv, mask):
    time_len, site_len, _ = raw.shape
    tok_rows = time_len * site_len
    normed = normed_tokens(padded_2(raw, (("depth", 1),), 1), stream, conv_w, gain)
    columns = lax.all_gather(w_qkv, "depth", axis=1, tiled=True)
    projected = jnp.dot(
        normed,
        lax.all_gather(columns, "tm", axis=0, tiled=True),
        preferred_element_type=jnp.float32,
    ).astype(jnp.bfloat16)
    head_cols = projected.shape[1] // 3
    queries = projected[:, :head_cols]
    keyvals = projected[:, head_cols:]
    earlier = []
    later = []
    moving_back = keyvals
    moving_ahead = keyvals
    for hop_index in range(RD):
        moving_back = from_behind(moving_back, "tm", 1)
        moving_ahead = from_behind(moving_ahead, "tm", -1)
        earlier.insert(0, moving_back)
        later.append(moving_ahead)
    gathered = jnp.concatenate(earlier + [keyvals] + later, axis=0)
    block_rows = BT * PP
    own_blocks = tok_rows // block_rows
    span_blocks = gathered.shape[0] // block_rows
    local_mask = mask[0]
    query_ids = jnp.arange(own_blocks, dtype=jnp.int32)[:, None]
    key_ids = jnp.arange(span_blocks, dtype=jnp.int32)[None, :]
    entry_ids = key_ids - query_ids
    picks = entry_ids[:, :, None] == jnp.arange(local_mask.shape[1], dtype=jnp.int32)[None, None, :]
    block_allowed = jnp.sum(jnp.where(picks, local_mask[:, None, :], 0), axis=-1) > 0
    allowed = jnp.repeat(jnp.repeat(block_allowed, block_rows, axis=0), block_rows, axis=1)
    query_heads = queries.reshape(tok_rows, HEADS, HD).transpose(1, 0, 2)
    key_heads = gathered[:, :head_cols].reshape(gathered.shape[0], HEADS, HD).transpose(1, 0, 2)
    value_heads = gathered[:, head_cols:].reshape(gathered.shape[0], HEADS, HD).transpose(1, 0, 2)
    context = lax.map(
        lambda operands: head_attend(operands[0], operands[1], operands[2], allowed),
        (query_heads, key_heads, value_heads),
    )
    return context.transpose(1, 0, 2).reshape(time_len, site_len, head_cols)


def solution(mesh):
    in_specs = (
        P("tm", "depth", None),
        P("tm", "depth", None),
        P(),
        P(),
        P("tm", "depth"),
        P("depth", "tm", None),
    )
    out_specs = P("tm", "depth", None)
    fits = mesh.shape["depth"] == 4 and mesh.shape["tm"] == 8
    return jax.shard_map(
        plane_device if fits else per_device, mesh=mesh, in_specs=in_specs, out_specs=out_specs, check_vma=False
    )
```

```python
import functools
import math

import jax
import jax.numpy as jnp
from jax import lax
from jax.experimental import pallas as pl
from jax.experimental.pallas import tpu as pltpu
from jax.sharding import PartitionSpec as P

HEADS = 8
HD = 128
BT = 16
PP = 8
RD = 2
VMEM = pltpu.VMEM
SMEM = pltpu.SMEM


def padded_2(value, sides, width):
    for axis, dim in sides:
        devices, length = (lax.axis_size(axis), value.shape[dim])
        up = [(i, (i + 1) % devices) for i in range(devices - 1)]
        down = [(j, i) for i, j in up]
        last = lax.slice_in_dim(value, length - width, length, axis=dim)
        leading = lax.slice_in_dim(value, 0, width, axis=dim)
        before = lax.ppermute(last, axis, up)
        after = lax.ppermute(leading, axis, down)
        value = jnp.concatenate([before, value, after], axis=dim)
    return value


def normed_tokens(padded, stream, conv_w, gain):
    time_len, site_len, width = stream.shape
    tok_rows = time_len * site_len
    embedded = stream.reshape(tok_rows, width).astype(jnp.float32)
    for offset in range(3):
        window = padded[:, offset : offset + site_len].reshape(tok_rows, padded.shape[2])
        embedded = embedded + jnp.dot(window, conv_w[offset], preferred_element_type=jnp.float32)
    scale = lax.rsqrt(jnp.mean(embedded * embedded, axis=-1, keepdims=True) + 1e-05)
    return (embedded * scale * gain).astype(jnp.bfloat16)


PAIR = 2 * HD
V_ORDER = (3, 2, 1, 0)
EXTRA = 16


def hop(value, fn):
    pairs = []
    for z in range(4):
        for core in range(2):
            for depth in range(4):
                to = fn(z, core, depth)
                if to is not None:
                    pairs.append(((2 * z + core) * 4 + depth, (2 * to[0] + to[1]) * 4 + to[2]))
    return lax.ppermute(value, ("tm", "depth"), pairs)


def swap_core(value):
    return hop(value, lambda z, c, d: (z, 1 - c, d))


def swap_depth(value, bits):
    return hop(value, lambda z, c, d: (z, c, d ^ bits))


def swap_z(value, bits):
    return hop(value, lambda z, c, d: (z ^ bits, c, d))


def swap_middle(value):
    return hop(value, lambda z, c, d: (z ^ 3, c, d) if z in (1, 2) else None)


def after(value, *others):
    return lax.optimization_barrier((value, *others))[0]


def where_am_i():
    tm = lax.axis_index("tm")
    return tm >> 1, tm & 1, lax.axis_index("depth")


def split_kernel(w, raw, to_x, to_y, to_across, keep):
    _, _, depth = where_am_i()
    even = (depth & 1) == 0
    size, half = w.shape[0], (raw.shape[0] - EXTRA) // 2
    low, high = w[:, :PAIR], w[:, 2 * PAIR :]
    to_x[:size] = w[:, PAIR : 2 * PAIR]
    to_y[:size] = jnp.where(even, high, low)
    keep[...] = jnp.where(even, low, high)
    for ref, at in ((to_x, size), (to_y, size), (to_across, 0)):
        for i in range(2):
            here = slice(i * HD, (i + 1) * HD)
            ref[at : at + half, here] = raw[i * half : (i + 1) * half]
            ref[at + half :, here] = raw[2 * half :]


def sorted_groups(kept, from_x, from_y):
    _, core, depth = where_am_i()
    first, even = core == 0, (depth & 1) == 0
    size = kept.shape[0]
    low = jnp.where(even, kept[...], from_y[:size])
    high = jnp.where(even, from_y[:size], kept[...])
    groups = (low, from_x[:size], high)
    turn = jnp.where(depth == 3, 0, depth)
    for third in range(3):
        group = jnp.where(turn == 0, groups[third], jnp.where(turn == 1, groups[(third + 1) % 3], groups[(third + 2) % 3]))
        yield third, jnp.where(first, group[:, :HD], group[:, HD:]), jnp.where(first, group[:, HD:], group[:, :HD])


def sort_kernel(kept, from_x, from_y, out_ref):
    for third, mine, other in sorted_groups(kept, from_x, from_y):
        out_ref[:, third * HD : (third + 1) * HD] = mine
        out_ref[:, (3 + third) * HD : (4 + third) * HD] = other


def sort_far_kernel(kept, from_x, from_y, plane_x, plane_y, across, raw, keep_ref, send_ref, flags_ref):
    for third, mine, other in sorted_groups(kept, from_x, from_y):
        send_ref[:, third * HD : (third + 1) * HD] = other
        keep_ref[:, third * HD : (third + 1) * HD] = mine
    row = lax.broadcasted_iota(jnp.int32, (EXTRA, HD), 0)
    flags = raw[raw.shape[0] - EXTRA :].astype(jnp.float32)
    for r, ref in enumerate((plane_x, plane_y, across)):
        flags = jnp.where(row == r + 1, ref[ref.shape[0] - EXTRA :, :HD].astype(jnp.float32), flags)
    flags = flags.astype(jnp.bfloat16)
    for k in range(3):
        flags_ref[:, k * HD : (k + 1) * HD] = flags


def other_kernel(own, near, flags, out_ref):
    size, width = own.shape[0], 3 * HD
    out_ref[:size] = own[:, width:]
    out_ref[size : 2 * size] = near[:, width:]
    out_ref[2 * size :] = flags[...]


def embed_kernel(rs, more, raw, plane_x, plane_y, across, conv_w, gain, *refs):
    count = len(rs)
    halves = 2 if rs == (3,) else 1
    count *= halves
    streams, finished, (out_ref, *onward, acc) = refs[:count], refs[count : count + more], refs[count + more :]
    for ref in finished:
        out_ref[: ref.shape[0]] = ref[...]
    if len(rs) > 1:
        for i, ref in enumerate(onward):
            half = ref.shape[1]
            ref[...] = streams[i][:, i * half : (i + 1) * half]
    _, _, depth = where_am_i()
    rows, width = raw.shape[0] - EXTRA, conv_w.shape[1]
    raws = [raw[:rows]]
    for ref in (plane_x, plane_y, across):
        at = ref.shape[0] - EXTRA - rows // 2
        raws.append(jnp.concatenate([ref[at : at + rows // 2, :HD], ref[at : at + rows // 2, HD:]], axis=0))
    raws = [value.astype(jnp.float32).reshape(rows // PP, PP, HD) for value in raws]
    done = out_ref.shape[0] - len(rs) * rows
    for i, r in enumerate(rs):
        place = depth ^ r
        even = (place & 1) == 0
        side, far = raws[r ^ 1], raws[r ^ 3]
        before = jnp.where(even, jnp.where(place == 2, far[:, PP - 1 :], 0.0), side[:, PP - 1 :])
        behind = jnp.where(even, side[:, :1], jnp.where(place == 1, far[:, :1], 0.0))
        padded = jnp.concatenate([before, raws[r], behind], axis=1)
        windows = [padded[:, j : j + PP].reshape(rows, HD).astype(jnp.bfloat16) for j in range(3)]
        windows = jnp.concatenate(windows, axis=1)
        total, step = jnp.zeros((rows, 1), jnp.float32), width // 4
        for at in range(0, width, step):
            here = slice(at, at + step)
            part = jnp.dot(windows, conv_w[:, here], preferred_element_type=jnp.float32)
            each = width // halves
            part += streams[i + at // each][:, at % each : at % each + step].astype(jnp.float32)
            acc[:, here] = part
            total += jnp.sum(part * part, axis=1, keepdims=True)
        scale = lax.rsqrt(total / width + 1e-05)
        normed = (acc[...] * scale * gain[...]).astype(jnp.bfloat16)
        out_ref[done + i * rows : done + (i + 1) * rows] = normed
        if halves > 1:
            cut = onward[0].shape[0]
            onward[0][...], onward[1][...] = normed[:cut], normed[cut:]


def take(refs, source, core, rows):
    half = rows // 2
    cuts = [pl.ds(pl.multiple_of(source * rows + c * half, half), half) for c in (core, 1 - core)]
    return jnp.concatenate([jnp.concatenate([ref[:, at] for at in cuts], axis=1) for ref in refs], axis=0)


def three_shards(x_refs, own, near, received, far):
    z, core, _ = where_am_i()
    size, width = own.shape[0], 3 * HD
    w = [own[:, :width], received[:size], far[...]]
    w = jnp.concatenate(w + [near[:, :width], received[size : 2 * size]], axis=0)
    x = [take(x_refs, source, core, 2 * size) for source in (z, z ^ 2, z ^ 1)]
    return jnp.dot(jnp.concatenate(x, axis=1), w, preferred_element_type=jnp.float32)


def partial_kernel(*refs):
    refs[-1][...] = three_shards(refs[:2], *refs[2:-1])


def diagonal_kernel(mine, top, bottom, *refs):
    weights, (acc_ref, x_ref) = refs[:-2], refs[-2:]
    at = 0
    for ref in (mine, top, bottom):
        x_ref[at : at + ref.shape[0]] = ref[...]
        at += ref.shape[0]
    acc_ref[...] = three_shards([x_ref], *weights)


ROW_ORDER = ((0, 1, 2, 6), (3, 4, 5, 7))


def finish_kernel(thirds, *refs):
    x_refs, (last, acc_in, acc_diagonal), out_refs = refs[:3], refs[3:6], refs[6:]
    z, core, _ = where_am_i()
    early = acc_in.shape[0]
    block = early // 6
    x = take(x_refs, z ^ 3, core, last.shape[0])
    for third in thirds:
        columns = slice(third * HD, (third + 1) * HD)
        value = jnp.dot(x, last[:, columns], preferred_element_type=jnp.float32)
        value = [acc_in[:, columns] + value[:early], acc_diagonal[:, columns] + value[early:]]
        value = jnp.concatenate(value, axis=0).astype(jnp.bfloat16)
        for rel in range(2):
            at = pl.ds(pl.multiple_of((core ^ rel) * block, block), block)
            for r in range(4):
                mine = value[ROW_ORDER[rel][r] * block : (ROW_ORDER[rel][r] + 1) * block]
                v_at = V_ORDER.index(r)
                if third == 2:
                    out_refs[1 + v_at // 2][v_at % 2, at, :] = mine
                else:
                    out_refs[0][r, at, :] = mine


def spans(u):
    return ((0, u, 2), (1, 0, 2), (2, 0, 1 + u))


def neighbours(outer, own, middle, index):
    z, _, _ = where_am_i()
    odd = (z & 1) == 1
    outer, middle = outer[index], middle[index]
    return jnp.where(odd, outer, middle), own[index], jnp.where(odd, middle, outer)


def weigh_kernel(q_ref, outer, own, middle, own_flags, received, out_ref):
    _, core, _ = where_am_i()
    block = q_ref.shape[1] // 2
    inv_root = 1.0 / math.sqrt(HD)
    flags = [own_flags[:, :HD].astype(jnp.float32), received[-EXTRA:, :HD].astype(jnp.float32)]
    flags = [jnp.where(core == u, flags[0], flags[1]) for u in range(2)]
    bias = [(f - 1.0) * 1e30 for f in flags]
    for r in range(4):
        keys = neighbours(outer, own, middle, r)
        for u in range(2):
            q = q_ref[r, u * block : (u + 1) * block]
            scores = []
            for side, first, last in spans(u):
                k = keys[side][first * block : last * block]
                s = lax.dot_general(q, k, (((1,), (1,)), ((), ())), preferred_element_type=jnp.float32)
                for v in range(last - first):
                    entry = len(scores)
                    shut = jnp.broadcast_to(bias[u][r : r + 1, entry : entry + 1], (block, block))
                    scores.append(s[:, v * block : (v + 1) * block] * inv_root + shut)
            top = jnp.max(functools.reduce(jnp.maximum, scores), axis=1, keepdims=True)
            powers = [jnp.exp(s - top) for s in scores]
            inverse = 1.0 / jnp.sum(functools.reduce(jnp.add, powers), axis=1, keepdims=True)
            for entry, p in enumerate(powers):
                here = slice(entry * block, (entry + 1) * block)
                out_ref[r, u * block : (u + 1) * block, here] = (p * inverse).astype(jnp.bfloat16)


def mix_kernel(r, weights, outer, own, middle, out_ref):
    block = weights.shape[1] // 2
    values = neighbours(outer, own, middle, V_ORDER.index(r) % 2)
    for u in range(2):
        w = weights[r, u * block : (u + 1) * block]
        v = [values[side][first * block : last * block] for side, first, last in spans(u)]
        result = jnp.dot(w, jnp.concatenate(v, axis=0), preferred_element_type=jnp.float32)
        out_ref[u * block : (u + 1) * block] = result.astype(jnp.bfloat16)


def pack_kernel(*refs):
    keep_ref, send_ref = refs[4:]
    _, core, _ = where_am_i()
    block = keep_ref.shape[1]
    for r, ref in enumerate(refs[:4]):
        for rel, out_ref in enumerate((keep_ref, send_ref)):
            out_ref[r] = ref[pl.ds(pl.multiple_of((core ^ rel) * block, block), block), :]


def gather_kernel(mine, other, out_ref):
    _, core, depth = where_am_i()
    for rel, ref in enumerate((mine, other)):
        for r in range(4):
            at = pl.multiple_of((2 * (depth ^ r) + (core ^ rel)) * HD, HD)
            out_ref[:, pl.ds(at, HD)] = ref[r]


def call(kernel, outs, places, scratch=(), macs=0, limit=32):
    spaces = {"v": VMEM}
    return pl.pallas_call(
        kernel,
        out_shape=outs,
        in_specs=[pl.BlockSpec(memory_space=spaces[place]) for place in places],
        out_specs=jax.tree.map(lambda _: pl.BlockSpec(memory_space=VMEM), outs),
        scratch_shapes=list(scratch),
        cost_estimate=pl.CostEstimate(flops=2 * macs, bytes_accessed=0, transcendentals=0),
        compiler_params=pltpu.CompilerParams(vmem_limit_bytes=limit * 2**20),
    )


def plane_device(raw, stream, conv_w, gain, w_qkv, mask):
    time_len, site_len, feat_len = raw.shape
    block, width = time_len * site_len, stream.shape[2]
    half, size = width // 2, w_qkv.shape[0]
    bf16, f32 = jnp.bfloat16, jnp.float32

    def array(*shape, kind=bf16):
        return jax.ShapeDtypeStruct(shape, kind)

    far_raw = swap_z(w_qkv, 2)

    mask_row = jnp.pad(mask.reshape(1, mask.shape[2]), ((0, 0), (0, feat_len - mask.shape[2]))).astype(bf16)
    raw = jnp.concatenate([raw.reshape(block, feat_len), jnp.broadcast_to(mask_row, (EXTRA, feat_len))], axis=0)
    stream = stream.reshape(block, width)
    conv_w, gain = conv_w.reshape(3 * feat_len, width), gain.reshape(1, width)
    more = block // 2 + EXTRA
    *to, kept = call(
        split_kernel,
        (array(size + more, PAIR), array(size + more, PAIR), array(more, PAIR), array(size, PAIR)),
        "vv",
    )(w_qkv, raw)
    plane = [swap_depth(t, r) for t, r in zip(to, (1, 2, 3))]
    own = call(sort_kernel, array(size, 6 * HD), "vvv")(kept, *plane[:2])
    near = swap_z(own, 1)
    far_raw = after(far_raw, own)

    piece = 5 * block // 8
    def embed(rs, *streams, finished=()):
        onward = {1: (), 2: (array(block, half),) * 2}[len(rs)]
        if rs == (3,):
            onward = (array(piece, width), array(block - piece, width))
        out = (array((len(rs) + len(finished)) * block, width), *onward)
        return call(
            functools.partial(embed_kernel, rs, len(finished)),
            out,
            "v" * (6 + len(streams) + len(finished)),
            scratch=[VMEM((block, width), f32)],
            macs=len(rs) * block * 3 * feat_len * width,
        )(raw, *plane, conv_w, gain, *streams, *finished)

    tied = after(stream, to[0])
    beside, above = swap_depth(tied, 1), swap_depth(tied, 2)
    (normed,) = embed((0,), stream)

    even = (lax.axis_index("depth") & 1) == 0
    low, to_x, high = (far_raw[:, k * PAIR : (k + 1) * PAIR] for k in range(3))
    kept, to_y = jnp.where(even, low, high), jnp.where(even, high, low)
    from_x, from_y = swap_depth(to_x, 1), swap_depth(to_y, 2)
    beside, above = after(beside, to_x), after(above, to_y)
    stack, *diagonal = embed((1, 2), beside, above, finished=(normed,))
    from_x, from_y, stack, near = lax.optimization_barrier((from_x, from_y, stack, near))
    keep, send, flags = call(
        sort_far_kernel,
        (array(size, 3 * HD), array(size, 3 * HD), array(EXTRA, 3 * HD)),
        "v" * 7,
    )(kept, from_x, from_y, *plane, raw)
    diagonal = swap_depth(diagonal[0], 2), swap_depth(diagonal[1], 1)
    far = jnp.concatenate([keep, swap_core(send)], axis=0)
    last = swap_z(far, 1)
    far, near, stack = lax.optimization_barrier((far, near, stack))
    to_other = call(other_kernel, array(2 * size + EXTRA, 3 * HD), "vvv")(own, near, flags)
    received = swap_core(to_other)
    weights = (own, near, received, far)
    early = (stack, swap_core(stack))
    rows = 2 * size
    total = call(partial_kernel, array(6 * block, 3 * HD, kind=f32), "v" * 6, macs=6 * block * 3 * rows * 3 * HD)(
        *early, *weights
    )
    diagonal, *parts = embed((3,), *[after(t, total) for t in diagonal])
    swapped = [swap_core(t) for t in parts]
    total_diagonal, diagonal = call(
        diagonal_kernel,
        (array(2 * block, 3 * HD, kind=f32), array(2 * block, width)),
        "v" * 7,
        macs=2 * block * 3 * rows * 3 * HD,
    )(diagonal, *swapped, *weights)
    one_head, half_head = array(4, 2 * block, HD), array(2, 2 * block, HD)
    sums = (*early, diagonal, last, total, total_diagonal)
    macs = 8 * block * rows * HD
    (k,) = call(functools.partial(finish_kernel, (1,)), (one_head,), "v" * 6, macs=macs)(*sums)
    q, *v = call(functools.partial(finish_kernel, (0, 2)), (one_head, half_head, half_head), "v" * 6, macs=2 * macs)(*sums)

    weights = call(weigh_kernel, array(4, 2 * block, 5 * block), "v" * 6, macs=8 * block * 5 * block * HD)(
        q, swap_z(k, 1), k, swap_middle(k), flags, received
    )
    values = [(swap_z(t, 1), t, swap_middle(t)) for t in v]
    pieces = {}
    for i, r in enumerate(V_ORDER):
        mixed = call(functools.partial(mix_kernel, r), array(2 * block, HD), "vvvv", macs=2 * block * 5 * block * HD)(
            weights, *values[i // 2]
        )
        pieces[r] = swap_depth(mixed, r) if r else mixed
    kept, sent = call(pack_kernel, (array(4, block, HD),) * 2, "vvvv")(*[pieces[r] for r in range(4)])
    context = call(gather_kernel, array(block, HEADS * HD), "vv")(kept, swap_core(sent))
    return context.reshape(time_len, site_len, HEADS * HD)


def from_behind(value, axis, by):
    devices = lax.axis_size(axis)
    pairs = [(i, i + by) for i in range(devices) if 0 <= i + by < devices]
    return lax.ppermute(value, axis, pairs)


def head_attend(query_head, key_head, value_head, allowed):
    inv_root = 1.0 / math.sqrt(HD)
    scores = (
        jnp.einsum("qd,kd->qk", query_head, key_head, preferred_element_type=jnp.float32) * inv_root
    )
    scores = jnp.where(allowed, scores, -1e30)
    row_max = jnp.max(scores, axis=-1, keepdims=True)
    powers = jnp.exp(scores - row_max)
    weights = (powers / jnp.sum(powers, axis=-1, keepdims=True)).astype(jnp.bfloat16)
    return jnp.dot(weights, value_head, preferred_element_type=jnp.float32).astype(jnp.bfloat16)


def per_device(raw, stream, conv_w, gain, w_qkv, mask):
    time_len, site_len, _ = raw.shape
    tok_rows = time_len * site_len
    normed = normed_tokens(padded_2(raw, (("depth", 1),), 1), stream, conv_w, gain)
    columns = lax.all_gather(w_qkv, "depth", axis=1, tiled=True)
    projected = jnp.dot(
        normed,
        lax.all_gather(columns, "tm", axis=0, tiled=True),
        preferred_element_type=jnp.float32,
    ).astype(jnp.bfloat16)
    head_cols = projected.shape[1] // 3
    queries = projected[:, :head_cols]
    keyvals = projected[:, head_cols:]
    earlier = []
    later = []
    moving_back = keyvals
    moving_ahead = keyvals
    for hop_index in range(RD):
        moving_back = from_behind(moving_back, "tm", 1)
        moving_ahead = from_behind(moving_ahead, "tm", -1)
        earlier.insert(0, moving_back)
        later.append(moving_ahead)
    gathered = jnp.concatenate(earlier + [keyvals] + later, axis=0)
    block_rows = BT * PP
    own_blocks = tok_rows // block_rows
    span_blocks = gathered.shape[0] // block_rows
    local_mask = mask[0]
    query_ids = jnp.arange(own_blocks, dtype=jnp.int32)[:, None]
    key_ids = jnp.arange(span_blocks, dtype=jnp.int32)[None, :]
    entry_ids = key_ids - query_ids
    picks = entry_ids[:, :, None] == jnp.arange(local_mask.shape[1], dtype=jnp.int32)[None, None, :]
    block_allowed = jnp.sum(jnp.where(picks, local_mask[:, None, :], 0), axis=-1) > 0
    allowed = jnp.repeat(jnp.repeat(block_allowed, block_rows, axis=0), block_rows, axis=1)
    query_heads = queries.reshape(tok_rows, HEADS, HD).transpose(1, 0, 2)
    key_heads = gathered[:, :head_cols].reshape(gathered.shape[0], HEADS, HD).transpose(1, 0, 2)
    value_heads = gathered[:, head_cols:].reshape(gathered.shape[0], HEADS, HD).transpose(1, 0, 2)
    context = lax.map(
        lambda operands: head_attend(operands[0], operands[1], operands[2], allowed),
        (query_heads, key_heads, value_heads),
    )
    return context.transpose(1, 0, 2).reshape(time_len, site_len, head_cols)


def solution(mesh):
    in_specs = (
        P("tm", "depth", None),
        P("tm", "depth", None),
        P(),
        P(),
        P("tm", "depth"),
        P("depth", "tm", None),
    )
    out_specs = P("tm", "depth", None)
    fits = mesh.shape["depth"] == 4 and mesh.shape["tm"] == 8
    return jax.shard_map(
        plane_device if fits else per_device, mesh=mesh, in_specs=in_specs, out_specs=out_specs, check_vma=False
    )
```
